32 devices in a mesh: replica: 8 (over y, x, core), shard: 4 (over z).
Axes of the slice: x: 2, y: 2, z: 4, core: 2. Of those that a mesh axis runs over, the one named last changes fastest.
Arguments:
- tokens: bfloat16 [6144, 2048], P(('replica', 'shard')), may hold values from -6 to 6
- cotangent: bfloat16 [6144, 2048], P(('replica', 'shard')), may hold values from -6 to 6
- qkv_weight: bfloat16 [2048, 6144], P('shard'), may hold values from -0.125 to 0.125
- qkv_bias: bfloat16 [6144], P('shard'), may hold values from -3 to 3
- out_weight: bfloat16 [2048, 2048], P('shard'), may hold values from -1 to 1
- gate_up_weight: bfloat16 [2048, 11264], P('shard'), may hold values from -0.125 to 0.125
- down_weight: bfloat16 [5632, 2048], P('shard'), may hold values from -0.078125 to 0.078125
- norm1_gain: bfloat16 [2048], P('shard'), may hold values from 0.5 to 1.5
- norm1_shift: bfloat16 [2048], P('shard'), may hold values from -1 to 1
- norm2_gain: bfloat16 [2048], P('shard'), may hold values from 0.5 to 1.5
- norm2_shift: bfloat16 [2048], P('shard'), may hold values from -1 to 1
- seq_lengths: int32 [8, 3], P('replica'), may hold values from 1 to 766, as said below
Outputs:
- mixed: bfloat16 [6144, 2048], P(('replica', 'shard'))
- input_grad: float32 [6144, 2048], P(('replica', 'shard'))
- qkv_weight_grad: float32 [2048, 6144], P('shard')
- qkv_bias_grad: float32 [6144], P('shard')
- out_weight_grad: float32 [2048, 2048], P('shard')
- gate_up_weight_grad: float32 [2048, 11264], P('shard')
- down_weight_grad: float32 [5632, 2048], P('shard')
- norm1_gain_grad: float32 [2048], P('shard')
- norm1_shift_grad: float32 [2048], P('shard')
- norm2_gain_grad: float32 [2048], P('shard')
- norm2_shift_grad: float32 [2048], P('shard')
The draws below stay inside these ranges and needn't reach their ends.
Inputs may be any that keep to these rules, and one draw needn't show every extreme that they name: `seq_lengths`: each row lists the lengths of the 3 sequences of one group of 768 tokens; they sum to 768 and one of them is longer than 384.
All inputs are finite; a program needn't handle non-finite values.
Results may differ from the reference program's by a relative error of at most 0.02.
Values may be sent and summed in bfloat16 or wider, within the bound.
A program may use at most 512 MiB of HBM per device.

```python
from functools import partial
import jax
import jax.numpy as jnp
from jax import lax

D = 2048
FF = 5632
HEADS = 32
HEAD_DIM = 64
ROT_DIM = 16
TOK_DEV = 192
GROUPS = 8
GROUP_TOK = 768
TOKENS = 6144


def draw_seq_lengths(key, part):
    key = jax.random.fold_in(key, 7)
    shorts = jax.random.randint(jax.random.fold_in(key, 1), (GROUPS, 2), 1, TOK_DEV)
    first_row = (jnp.arange(GROUPS) == 0)[:, None]
    shorts = jnp.where(first_row, 1, shorts)
    longest = GROUP_TOK - jnp.sum(shorts, axis=1)
    placing = jax.random.randint(jax.random.fold_in(key, 2), (GROUPS, 1), 0, 3)
    columns = jnp.arange(3)[None, :]
    first_slot = jnp.where(placing == 0, 1, 0)
    lengths = jnp.where(columns == placing, longest[:, None], jnp.where(columns == first_slot, shorts[:, :1], shorts[:, 1:]))
    return lengths.astype(jnp.int32)


def steps_of(key, dims, cuts, least, top_value):
    def one(dim, shards_of):
        draws = jax.random.uniform(jax.random.fold_in(jax.random.fold_in(key, 6), dim), (shards_of,), jnp.float32, least / len(cuts), top_value / len(cuts))
        return jnp.repeat(jnp.exp(draws), dims[dim] // shards_of).reshape((-1,) + (1,) * (len(dims) - dim - 1))

    factor_of = one(*cuts[0])
    for cut in cuts[1:]:
        factor_of = factor_of * one(*cut)
    return factor_of


def normal_values(rng, dims, deviation, reach, cuts=(), kind=jnp.bfloat16):
    values = jax.random.normal(rng, dims, jnp.float32) * deviation
    if len(cuts) > 0:
        values = steps_of(rng, dims, cuts, -0.22, 0.18) * values
    return jnp.clip(values, min=-reach, max=reach).astype(kind)


def setup_inputs(seed: int = 0) -> dict:
    key_of = jax.random.split(jax.random.key(seed), 13)
    return {
        "tokens": normal_values(key_of[0], (TOKENS, D), 1.0, 6.0, ((0, 32),)),
        "cotangent": normal_values(key_of[1], (TOKENS, D), 1.0, 6.0, ((0, 32),)),
        "qkv_weight": normal_values(key_of[2], (D, 3 * D), D ** -0.5, 0.125, ((0, 4),)),
        "qkv_bias": normal_values(key_of[3], (3 * D,), 0.5, 3.0, ((0, 4),)),
        "out_weight": normal_values(key_of[4], (D, D), (D // 64) ** -0.5, 1.0, ((0, 4),)),
        "gate_up_weight": normal_values(key_of[5], (D, 2 * FF), D ** -0.5, 0.125, ((0, 4),)),
        "down_weight": normal_values(key_of[6], (FF, D), FF ** -0.5, 0.078125, ((0, 4),)),
        "norm1_gain": jnp.clip(1.0 + 0.1 * jax.random.normal(key_of[7], (D,), jnp.float32), 0.5, 1.5).astype(jnp.bfloat16),
        "norm1_shift": normal_values(key_of[8], (D,), 0.2, 1.0, ((0, 4),)),
        "norm2_gain": jnp.clip(1.0 + 0.1 * jax.random.normal(key_of[9], (D,), jnp.float32), 0.5, 1.5).astype(jnp.bfloat16),
        "norm2_shift": normal_values(key_of[10], (D,), 0.2, 1.0, ((0, 4),)),
        "seq_lengths": draw_seq_lengths(jax.random.fold_in(key_of[12], 71), 0),
    }


@jax.custom_vjp
def low(v):
    return lax.optimization_barrier(v.astype(jnp.bfloat16)).astype(jnp.float32)

@jax.custom_vjp
def low_back(v):
    return v

def low_keep(v):
    return (low(v), None)

def low_pass(kept, grad):
    return (grad,)

def back_keep(v):
    return (v, None)

def back_low(kept, grad):
    return (low(grad),)
low.defvjp(low_keep, low_pass)
low_back.defvjp(back_keep, back_low)
norm_eps = 1e-05
masked_score = -1000000000.0

def layer_norm(values, norm_gain, norm_shift):
    centered = values - lax.optimization_barrier(jnp.mean(values, axis=-1, keepdims=True))
    spread = lax.optimization_barrier(jnp.mean(centered * centered, axis=-1, keepdims=True))
    return centered * lax.rsqrt(spread + norm_eps) * norm_gain + norm_shift

def group_layout(lengths, token_index):
    seq_ends = jnp.cumsum(lengths)
    passed = (token_index[:, None] >= seq_ends[None, :]).astype(jnp.int32)
    segment = lax.optimization_barrier(jnp.sum(passed, axis=1))
    position = token_index - lax.optimization_barrier(jnp.sum(passed * lengths[None, :], axis=1))
    return (segment, position)

def rope_tables(position):
    half_rot = ROT_DIM // 2
    frequency = jnp.exp(-jnp.log(10000.0) * (2.0 * jnp.arange(half_rot, dtype=jnp.float32) / ROT_DIM))
    angles = position.astype(jnp.float32)[:, None] * frequency[None, :]
    return (jnp.cos(angles), jnp.sin(angles))

def rotate(heads, cosine, sine_value):
    half_rot = ROT_DIM // 2
    first = heads[..., :half_rot]
    second = heads[..., half_rot:ROT_DIM]
    cos_wide = cosine[:, None, :]
    sin_wide = sine_value[:, None, :]
    return jnp.concatenate([first * cos_wide - second * sin_wide, second * cos_wide + first * sin_wide, heads[..., ROT_DIM:]], axis=-1)

def head_attention(visible, pieces):
    query_head, key_head, value_head = pieces
    raw_scores = jnp.dot(query_head, key_head.T, precision=lax.Precision.HIGHEST) * HEAD_DIM ** (-0.5)
    scores = jnp.where(visible, low_back(raw_scores), masked_score)
    top = lax.optimization_barrier(jnp.max(scores, axis=-1, keepdims=True))
    weights = jnp.exp(scores - top)
    probs = weights / lax.optimization_barrier(jnp.sum(weights, axis=-1, keepdims=True))
    return jnp.dot(low(probs), value_head, precision=lax.Precision.HIGHEST)

def layer_block(inputs, weights, position, visible):
    qkv_weight, qkv_bias, out_weight, gate_up_weight, down_weight, gain_one, shift_one, gain_two, shift_two = weights
    highest = lax.Precision.HIGHEST
    length = inputs.shape[0]
    normed = low(layer_norm(inputs, gain_one, shift_one))
    projected = low_back(jnp.dot(normed, qkv_weight, precision=highest) + qkv_bias)
    cosine, sine_value = rope_tables(position)
    query = low(rotate(projected[:, :D].reshape(length, HEADS, HEAD_DIM), cosine, sine_value))
    keys = low(rotate(projected[:, D:2 * D].reshape(length, HEADS, HEAD_DIM), cosine, sine_value))
    values = low(projected[:, 2 * D:].reshape(length, HEADS, HEAD_DIM))
    context = lax.map(jax.checkpoint(partial(head_attention, visible)), (jnp.moveaxis(query, 1, 0), jnp.moveaxis(keys, 1, 0), jnp.moveaxis(values, 1, 0)))
    context = jnp.moveaxis(context, 0, 1).reshape(length, D)
    attended = low(low_back(context))
    middle = inputs + low_back(jnp.dot(attended, out_weight, precision=highest))
    normed_two = low(layer_norm(middle, gain_two, shift_two))
    gate_up = low_back(jnp.dot(normed_two, gate_up_weight, precision=highest))
    hidden = low(jax.nn.silu(gate_up[:, :FF]) * gate_up[:, FF:])
    return middle + low_back(jnp.dot(hidden, down_weight, precision=highest))

def reference(tokens, cotangent, qkv_weight, qkv_bias, out_weight, gate_up_weight, down_weight, norm1_gain, norm1_shift, norm2_gain, norm2_shift, seq_lengths):
    arguments = (qkv_weight, qkv_bias, out_weight, gate_up_weight, down_weight, norm1_gain, norm1_shift, norm2_gain, norm2_shift)
    params = tuple((argument.astype(jnp.float32) for argument in arguments))
    inputs = tokens.astype(jnp.float32).reshape(GROUPS, GROUP_TOK, D)
    upstream = cotangent.astype(jnp.float32).reshape(GROUPS, GROUP_TOK, D)
    token_index = jnp.arange(GROUP_TOK, dtype=jnp.int32)

    def group_step(totals, element):
        group_in, group_cot, lengths = element
        segment, position = group_layout(lengths, token_index)
        visible = (token_index[None, :] <= token_index[:, None]) & (segment[None, :] == segment[:, None])

        def apply_block(values, *weights):
            return layer_block(values, weights, position, visible)
        result, pullback = jax.vjp(apply_block, group_in, *params)
        gradients = pullback(group_cot)
        totals = tuple((running + added for running, added in zip(totals, gradients[1:])))
        return (totals, (result, gradients[0]))
    zeros = tuple((jnp.zeros_like(argument) for argument in params))
    totals, (results, input_grads) = lax.scan(group_step, zeros, (inputs, upstream, seq_lengths))
    mixed = results.reshape(TOKENS, D).astype(jnp.bfloat16)
    input_grad = input_grads.reshape(TOKENS, D)
    return (mixed, input_grad, totals[0], totals[1], totals[2], totals[3], totals[4], totals[5], totals[6], totals[7], totals[8])
```

```python
import jax
import jax.numpy as jnp
from jax import lax
from jax.sharding import PartitionSpec as P

D = 2048
FF = 5632
HEADS = 32
HEAD_DIM = 64
ROT_DIM = 16


norm_eps = 1e-05
masked_score = -1000000000.0


def layer_norm(values, norm_gain, norm_shift):
    centered = values - jnp.mean(values, axis=-1, keepdims=True)
    spread = jnp.mean(centered * centered, axis=-1, keepdims=True)
    return centered * lax.rsqrt(spread + norm_eps) * norm_gain + norm_shift


def group_layout(lengths, token_index):
    seq_ends = jnp.cumsum(lengths)
    passed = (token_index[:, None] >= seq_ends[None, :]).astype(jnp.int32)
    segment = jnp.sum(passed, axis=1)
    position = token_index - jnp.sum(passed * lengths[None, :], axis=1)
    return (segment, position)


def rope_tables(position):
    half_rot = ROT_DIM // 2
    frequency = jnp.exp(
        -jnp.log(10000.0) * (2.0 * jnp.arange(half_rot, dtype=jnp.float32) / ROT_DIM)
    )
    angles = position.astype(jnp.float32)[:, None] * frequency[None, :]
    return (jnp.cos(angles), jnp.sin(angles))


def rotate(heads, cosine, sine_value):
    half_rot = ROT_DIM // 2
    first = heads[..., :half_rot]
    second = heads[..., half_rot:ROT_DIM]
    cos_wide = cosine[:, None, :]
    sin_wide = sine_value[:, None, :]
    return jnp.concatenate(
        [
            first * cos_wide - second * sin_wide,
            second * cos_wide + first * sin_wide,
            heads[..., ROT_DIM:],
        ],
        axis=-1,
    )


def contract_last(left, right):
    return lax.dot_general(
        left, right, (((1,), (1,)), ((), ())), preferred_element_type=jnp.float32
    )


def contract_first(left, right):
    return lax.dot_general(
        left, right, (((0,), (0,)), ((), ())), preferred_element_type=jnp.float32
    )


def spread_rows(rows, columns):
    shards = lax.axis_size("shard")
    copies = lax.axis_size("replica")
    own = rows.shape[0] // copies
    start = lax.axis_index("replica") * own
    piece = lax.dynamic_slice_in_dim(rows, start, own, axis=0)
    piece = piece.reshape(own, columns, shards, -1).transpose(2, 0, 1, 3)
    piece = piece.reshape(shards, own, -1)
    moved = lax.all_to_all(piece, "shard", split_axis=0, concat_axis=0, tiled=True)
    full = lax.all_gather(moved, "replica", axis=0, tiled=False)
    return full.transpose(1, 0, 2, 3).reshape(shards * copies * own, -1)


def gather_rows(rows):
    copies = lax.axis_size("replica")
    own = rows.shape[0] // copies
    start = lax.axis_index("replica") * own
    piece = lax.dynamic_slice_in_dim(rows, start, own, axis=0)
    moved = lax.all_gather(piece, "shard", axis=0, tiled=False)
    full = lax.all_gather(moved, "replica", axis=0, tiled=False)
    return full.transpose(1, 0, 2, 3).reshape(-1, rows.shape[1])


def own_rows(features):
    copies = lax.axis_size("replica")
    shards = lax.axis_size("shard")
    count = features.shape[0]
    return (
        features.reshape(count, shards, copies, -1).transpose(0, 2, 1, 3).reshape(count, -1)
    )


def sum_columns(features, slopes, columns):
    shards = lax.axis_size("shard")
    copies = lax.axis_size("replica")
    term = contract_first(own_rows(features), slopes).astype(jnp.bfloat16)
    part = lax.psum_scatter(term, "replica", scatter_dimension=0, tiled=True)
    own = part.shape[0] // shards
    moved = lax.all_to_all(
        part.reshape(shards, own, -1), "shard", split_axis=0, concat_axis=0, tiled=True
    )
    moved = moved.reshape(shards, own, columns, -1).transpose(1, 2, 0, 3).reshape(own, -1)
    return lax.all_gather(moved, "replica", axis=0, tiled=True).astype(jnp.float32)


def block_scores(query, keys, visible):
    scores = (
        jnp.einsum("qhd,khd->hqk", query, keys, preferred_element_type=jnp.float32)
        * HEAD_DIM ** (-0.5)
    )
    return jnp.where(visible[None], scores, masked_score)


def attend(query, keys, values, visible):
    scores = block_scores(query, keys, visible)
    top = jnp.max(scores, axis=-1, keepdims=True)
    weights = jnp.exp(scores - top)
    totals = jnp.sum(weights, axis=-1, keepdims=True)
    probs = weights / totals
    context = jnp.einsum(
        "hqk,khd->qhd", probs.astype(jnp.bfloat16), values, preferred_element_type=jnp.float32
    )
    return (context, top, totals)


def attend_back(query, keys, values, top, totals, d_context, visible):
    scores = block_scores(query, keys, visible)
    probs = jnp.exp(scores - top) / totals
    d_probs = jnp.einsum("qhd,khd->hqk", d_context, values, preferred_element_type=jnp.float32)
    inner = jnp.sum(probs * d_probs, axis=-1, keepdims=True)
    d_scores = (probs * (d_probs - inner)).astype(jnp.bfloat16)
    scale = HEAD_DIM ** (-0.5)
    d_query = (
        jnp.einsum("hqk,khd->qhd", d_scores, keys, preferred_element_type=jnp.float32) * scale
    )
    d_key = jnp.einsum("hqk,qhd->khd", d_scores, query, preferred_element_type=jnp.float32) * scale
    d_value = jnp.einsum(
        "hqk,qhd->khd", probs.astype(jnp.bfloat16), d_context, preferred_element_type=jnp.float32
    )
    return (d_query, d_key, d_value)


def swiglu(gate_up):
    half = gate_up.shape[1] // 2
    return jax.nn.silu(gate_up[:, :half]) * gate_up[:, half:]


def norm_stats(values):
    mean = jnp.mean(values, axis=-1, keepdims=True)
    centered = values - mean
    inverse = lax.rsqrt(jnp.mean(centered * centered, axis=-1, keepdims=True) + norm_eps)
    return centered * inverse, inverse


def norm_back(slope, unit, inverse, gain):
    scaled = slope * gain
    return inverse * (
        scaled
        - jnp.mean(scaled, axis=-1, keepdims=True)
        - unit * jnp.mean(scaled * unit, axis=-1, keepdims=True)
    )


def on_device(
    tokens,
    cotangent,
    qkv_weight,
    qkv_bias,
    out_weight,
    gate_up_weight,
    down_weight,
    norm1_gain,
    norm1_shift,
    norm2_gain,
    norm2_shift,
    seq_lengths,
):
    shards = lax.axis_size("shard")
    here = lax.axis_index("shard")
    row_count = tokens.shape[0]
    group_rows = row_count * shards
    width = D // shards
    local_heads = HEADS // shards
    f32 = jnp.float32
    low = jnp.bfloat16

    vectors = jnp.concatenate([qkv_bias, norm1_gain, norm1_shift, norm2_gain, norm2_shift])
    vectors = lax.all_gather(vectors, "shard", axis=0, tiled=False).astype(f32)
    bias_rows = qkv_bias.shape[0]
    bias_full = vectors[:, :bias_rows].reshape(3, shards, width)
    bias = lax.dynamic_index_in_dim(bias_full, here, axis=1, keepdims=False).reshape(3 * width)
    gain_one, shift_one, gain_two, shift_two = (
        vectors[:, bias_rows + i * width : bias_rows + (i + 1) * width].reshape(D)
        for i in range(4)
    )

    group_tokens = lax.all_gather(tokens, "shard", axis=0, tiled=True)
    weight_qkv = spread_rows(qkv_weight, 3)
    weight_out = gather_rows(out_weight)
    weight_gate_up = spread_rows(gate_up_weight, 2)
    group_cotangent = lax.all_gather(cotangent, "shard", axis=0, tiled=True)

    index = jnp.arange(group_rows, dtype=jnp.int32)
    segment, position = group_layout(seq_lengths[0], index)
    visible = (index[None, :] <= index[:, None]) & (segment[None, :] == segment[:, None])
    cosine, sine_value = rope_tables(position)

    def local(array):
        return lax.dynamic_slice_in_dim(array, here * row_count, row_count, axis=0)

    inputs = group_tokens.astype(f32)
    unit_one, inverse_one = norm_stats(inputs)
    normed_low = (unit_one * gain_one + shift_one).astype(low)
    projected = jnp.dot(normed_low, weight_qkv, preferred_element_type=f32) + bias
    projected = projected.reshape(group_rows, 3, local_heads, HEAD_DIM)
    query = rotate(projected[:, 0], cosine, sine_value).astype(low)
    keys = rotate(projected[:, 1], cosine, sine_value).astype(low)
    values = projected[:, 2].astype(low)
    context, tops, totals = attend(query, keys, values, visible)
    attended = context.reshape(group_rows, width).astype(low)
    attended_full = lax.all_gather(attended, "shard", axis=1, tiled=True)
    middle = inputs + jnp.dot(attended_full, weight_out, preferred_element_type=f32)
    unit_two, inverse_two = norm_stats(middle)
    normed_two_low = (unit_two * gain_two + shift_two).astype(low)
    gate_up = jnp.dot(normed_two_low, weight_gate_up, preferred_element_type=f32)
    hidden, swiglu_pull = jax.vjp(swiglu, gate_up)
    hidden_low = hidden.astype(low)
    down_part = jnp.dot(hidden_low, down_weight, preferred_element_type=f32).astype(low)
    down_own = lax.psum_scatter(down_part, "shard", scatter_dimension=0, tiled=True)
    mixed = (local(middle) + down_own.astype(f32)).astype(low)

    d_hidden = contract_last(group_cotangent, down_weight)
    down_grad = lax.psum(
        contract_first(hidden_low, group_cotangent).astype(low), "replica"
    ).astype(f32)
    d_gate_up_low = swiglu_pull(d_hidden)[0].astype(low)
    d_normed_two_part = contract_last(d_gate_up_low, weight_gate_up).astype(low)
    gate_up_grad = sum_columns(normed_two_low, d_gate_up_low, 2)
    d_normed_two = lax.psum_scatter(
        d_normed_two_part, "shard", scatter_dimension=0, tiled=True
    ).astype(f32)
    unit_two_own = local(unit_two)
    d_middle = cotangent.astype(f32) + norm_back(
        d_normed_two, unit_two_own, local(inverse_two), gain_two
    )
    d_gain_two = jnp.sum(d_normed_two * unit_two_own, axis=0)
    d_shift_two = jnp.sum(d_normed_two, axis=0)
    d_middle_low = d_middle.astype(low)
    d_attended_own = contract_last(d_middle_low, weight_out).astype(low)
    d_attended = lax.all_to_all(
        d_attended_own, "shard", split_axis=1, concat_axis=0, tiled=True
    ).reshape(group_rows, local_heads, HEAD_DIM)
    d_middle_columns = lax.all_to_all(
        d_middle_low, "shard", split_axis=1, concat_axis=0, tiled=True
    )
    out_grad = sum_columns(attended_full, d_middle_columns, 1)
    d_query, d_key, d_value = attend_back(
        query, keys, values, tops, totals, d_attended, visible
    )
    d_projected = jnp.stack(
        [rotate(d_query, cosine, -sine_value), rotate(d_key, cosine, -sine_value), d_value], axis=1
    )
    d_projected_low = d_projected.astype(low).reshape(group_rows, 3 * width)
    d_normed_part = contract_last(d_projected_low, weight_qkv).astype(low)
    qkv_grad = sum_columns(normed_low, d_projected_low, 3)
    d_normed = lax.psum_scatter(
        d_normed_part, "shard", scatter_dimension=0, tiled=True
    ).astype(f32)
    unit_one_own = local(unit_one)
    input_grad = d_middle + norm_back(d_normed, unit_one_own, local(inverse_one), gain_one)
    d_gain_one = jnp.sum(d_normed * unit_one_own, axis=0)
    d_shift_one = jnp.sum(d_normed, axis=0)

    bias_part = jnp.sum(d_projected_low.astype(f32), axis=0).reshape(3, 1, width)
    bias_wide = lax.dynamic_update_slice(
        jnp.zeros((3, shards, width), f32), bias_part, (0, here, 0)
    ).reshape(shards, 3 * width)
    small = jnp.concatenate(
        [bias_wide]
        + [v.reshape(shards, width) for v in (d_gain_one, d_shift_one, d_gain_two, d_shift_two)],
        axis=1,
    )
    small = lax.psum(small, ("replica", "shard"))
    small = lax.dynamic_index_in_dim(small, here, axis=0, keepdims=False)
    return (
        mixed,
        input_grad,
        qkv_grad,
        small[:bias_rows],
        out_grad,
        gate_up_grad,
        down_grad,
    ) + tuple(small[bias_rows + i * width : bias_rows + (i + 1) * width] for i in range(4))


def solution(mesh):
    placed = (
        P(("replica", "shard"), None),
        P(("replica", "shard"), None),
        P("shard", None),
        P("shard"),
        P("shard", None),
        P("shard", None),
        P("shard", None),
        P("shard"),
        P("shard"),
        P("shard"),
        P("shard"),
        P("replica", None),
    )
    return jax.shard_map(
        on_device,
        mesh=mesh,
        in_specs=placed,
        out_specs=(
            P(("replica", "shard"), None),
            P(("replica", "shard"), None),
            P("shard", None),
            P("shard"),
            P("shard", None),
            P("shard", None),
            P("shard", None),
            P("shard"),
            P("shard"),
            P("shard"),
            P("shard"),
        ),
        check_vma=False,
    )
```

```python
import functools

import jax
import jax.numpy as jnp
from jax import lax
from jax.experimental import pallas as pl
from jax.experimental.pallas import tpu as pltpu
from jax.sharding import PartitionSpec as P

D = 2048
FF = 5632
HEADS = 32
HEAD_DIM = 64
ROT_DIM = 16
MESH = pl.DeviceIdType.MESH


norm_eps = 1e-05
masked_score = -1000000000.0


def group_layout(lengths, token_index):
    seq_ends = jnp.cumsum(lengths)
    passed = (token_index[:, None] >= seq_ends[None, :]).astype(jnp.int32)
    segment = jnp.sum(passed, axis=1)
    position = token_index - jnp.sum(passed * lengths[None, :], axis=1)
    return (segment, position)


def rope_tables(position):
    half_rot = ROT_DIM // 2
    frequency = jnp.exp(
        -jnp.log(10000.0) * (2.0 * jnp.arange(half_rot, dtype=jnp.float32) / ROT_DIM)
    )
    angles = position.astype(jnp.float32)[:, None] * frequency[None, :]
    return (jnp.cos(angles), jnp.sin(angles))


def contract_last(left, right):
    return lax.dot_general(
        left, right, (((1,), (1,)), ((), ())), preferred_element_type=jnp.float32
    )


def aligned(value, unit):
    return pl.multiple_of(value * unit, unit)


def greet(partners, count):
    barrier = pltpu.get_barrier_semaphore()
    for there, device in partners:
        @pl.when(there)
        def _():
            pl.semaphore_signal(barrier, inc=1, device_id=device, device_id_type=MESH)
    pl.semaphore_wait(barrier, count)


def greet_line(z, shards):
    count = (z + shards - 1) // shards + (2 * shards - 2 - z) // shards
    greet([(z >= 1, {"shard": z - 1}), (z + 1 < shards, {"shard": z + 1})], count)


def remote(source, target, send, recv, device):
    return pltpu.make_async_remote_copy(
        src_ref=source, dst_ref=target, send_sem=send, recv_sem=recv,
        device_id=device, device_id_type=MESH,
    )


def start_kernel(shards, tokens, vectors, weight, cosine, minus, plus,
                 all_tokens, all_vectors, normed, qkv, kept_weight,
                 x_buf, v_buf, w_buf, n_buf, out_buf,
                 x_send, x_recv, v_send, v_recv, w_send, w_recv, xy_send, xy_recv, c_send, c_recv, loc):
    z = lax.axis_index("shard")
    r = lax.axis_index("replica")
    rows = tokens.shape[0]
    depth = weight.shape[0]
    share = depth // 8
    half = share // 2
    width = w_buf.shape[1] // 3
    core, x, y = r % 2, (r // 2) % 2, r // 4
    xr, yr, cr = r + 2 - 4 * x, r + 4 - 8 * y, r + 1 - 2 * core
    dr = 4 * (1 - y) + 2 * (1 - x) + core
    true = z >= 0
    greet(
        [((z != o), {"shard": o}) for o in range(shards)]
        + [(true, {"replica": d}) for d in (xr, yr, cr)],
        shards + 2,
    )

    def w_rows(owner, replica):
        return pl.ds(aligned(owner * 8 + replica, share), share)

    def vec_copy(o):
        return remote(vectors, v_buf.at[z], v_send.at[o], v_recv.at[z], {"shard": o})

    def w_copy(o, part):
        return remote(
            weight.at[pl.ds(aligned(r, share), share), pl.ds(aligned(part * shards + o, width), width)],
            w_buf.at[w_rows(z, r), pl.ds(part * width, width)],
            w_send.at[o, part], w_recv.at[z, part], {"shard": o},
        )

    def w_arrival(o, part):
        block = w_buf.at[w_rows(o, r), pl.ds(part * width, width)]
        return remote(block, block, w_send.at[o, part], w_recv.at[o, part], {"shard": o})

    def v_arrival(o):
        return remote(vectors, v_buf.at[o], v_send.at[o], v_recv.at[o], {"shard": o})

    def x_copy(way, step):
        target = z + 1 if way == 0 else z - 1
        chunk = z - step if way == 0 else z + step
        source = tokens if step == 0 else x_buf.at[chunk]
        return remote(source, x_buf.at[chunk], x_send.at[way, step], x_recv.at[way, step], {"shard": target})

    def x_sends(way, step):
        if way == 0:
            return (z + 1 < shards) & (z - step >= 0)
        return (z >= 1) & (z + step < shards)

    def x_gets(way, step):
        return (z - step >= 1) if way == 0 else (z + step + 1 < shards)

    for o in range(shards):
        @pl.when(z != o)
        def _():
            vec_copy(o).start()
            for part in range(3):
                w_copy(o, part).start()
    for way in (0, 1):
        @pl.when(x_sends(way, 0))
        def _():
            x_copy(way, 0).start()
    own_x = pltpu.make_async_copy(tokens, x_buf.at[z], loc.at[0])
    own_x.start()
    own_v = pltpu.make_async_copy(vectors, v_buf.at[z], loc.at[1])
    own_v.start()
    own_w = [
        pltpu.make_async_copy(
            weight.at[pl.ds(aligned(r, share), share), pl.ds(aligned(part * shards + z, width), width)],
            w_buf.at[w_rows(z, r), pl.ds(part * width, width)], loc.at[2 + part],
        )
        for part in range(3)
    ]
    for copy in own_w:
        copy.start()

    def to_x(o):
        block = w_buf.at[w_rows(o, r)]
        return remote(block, block, xy_send.at[0, o], xy_recv.at[0, o], {"replica": xr})

    def to_y(o):
        block = w_buf.at[w_rows(o, r)]
        return remote(block, block, xy_send.at[1, o], xy_recv.at[1, o], {"replica": yr})

    def on_to_y(o):
        block = w_buf.at[pl.ds(aligned((o * 8 + xr) * 2, half), half)]
        return remote(block, block, xy_send.at[2, o], xy_recv.at[2, o], {"replica": yr})

    def on_to_x(o):
        block = w_buf.at[pl.ds(aligned((o * 8 + yr) * 2 + 1, half), half)]
        return remote(block, block, xy_send.at[3, o], xy_recv.at[3, o], {"replica": xr})

    def to_core(o, kind):
        whose = (r, xr, yr, dr)[kind]
        block = w_buf.at[w_rows(o, whose)]
        return remote(block, block, c_send.at[kind, o], c_recv.at[kind, o], {"replica": cr})

    for copy in own_w:
        copy.wait()
    for step in range(shards):
        for o in range(shards):
            @pl.when((z - o == step) | (o - z == step))
            def _():
                if step > 0:
                    for part in range(3):
                        w_arrival(o, part).wait_recv()
                to_x(o).start()
                to_y(o).start()
                to_core(o, 0).start()
        if step + 1 < shards:
            for way in (0, 1):
                @pl.when(x_gets(way, step))
                def _():
                    x_copy(way, step).wait_recv()
                @pl.when(x_sends(way, step + 1))
                def _():
                    x_copy(way, step + 1).start()
    for o in range(shards):
        to_x(o).wait_recv()
        on_to_y(o).start()
        to_core(o, 1).start()
        to_y(o).wait_recv()
        on_to_x(o).start()
        to_core(o, 2).start()
    own_x.wait()
    own_v.wait()
    for o in range(shards):
        @pl.when(z != o)
        def _():
            v_arrival(o).wait_recv()

    keep_x = pltpu.make_async_copy(x_buf, all_tokens, loc.at[5])
    keep_x.start()
    keep_v = pltpu.make_async_copy(v_buf, all_vectors, loc.at[6])
    keep_v.start()
    gain = jnp.concatenate([v_buf[o, 3:4, :] for o in range(shards)], axis=1)
    shift = jnp.concatenate([v_buf[o, 4:5, :] for o in range(shards)], axis=1)
    for o in range(shards):
        @pl.loop(0, rows, step=32)
        def _(at):
            block = pl.ds(pl.multiple_of(at, 32), 32)
            values = x_buf[o, block, :].astype(jnp.float32)
            centered = values - jnp.mean(values, axis=-1, keepdims=True)
            spread = jnp.mean(centered * centered, axis=-1, keepdims=True)
            out = centered * lax.rsqrt(spread + norm_eps) * gain + shift
            n_buf[pl.ds(pl.multiple_of(o * rows + at, 32), 32), :] = out.astype(jnp.bfloat16)
    keep_n = pltpu.make_async_copy(n_buf, normed, loc.at[7])
    keep_n.start()

    for o in range(shards):
        on_to_y(o).wait_recv()
        on_to_x(o).wait_recv()
        to_core(o, 3).start()
    for o in range(shards):
        for kind in range(4):
            to_core(o, kind).wait_recv()
    keep_w = pltpu.make_async_copy(w_buf, kept_weight, loc.at[8])
    keep_w.start()

    tile = 256
    per_part = width // tile

    @pl.loop(0, 3 * per_part)
    def _(t):
        columns = pl.ds(aligned(t, tile), tile)
        bias_row = bias_piece(v_buf, z, t, tile, shards, per_part)
        value = jnp.dot(n_buf[...], w_buf[:, columns], preferred_element_type=jnp.float32) + bias_row

        @pl.when(t < 2 * per_part)
        def _():
            wide = jnp.concatenate([cosine[...]] * (tile // 128), axis=1)
            wide_minus = jnp.concatenate([minus[...]] * (tile // 128), axis=1)
            wide_plus = jnp.concatenate([plus[...]] * (tile // 128), axis=1)
            turned = value * wide + pltpu.roll(value, tile - 8, 1) * wide_minus + pltpu.roll(value, 8, 1) * wide_plus
            out_buf[:, columns] = turned.astype(jnp.bfloat16)

        @pl.when(t >= 2 * per_part)
        def _():
            out_buf[:, columns] = value.astype(jnp.bfloat16)
    keep_q = pltpu.make_async_copy(out_buf, qkv, loc.at[9])
    keep_q.start()

    for o in range(shards):
        @pl.when(z != o)
        def _():
            vec_copy(o).wait_send()
            for part in range(3):
                w_copy(o, part).wait_send()
        to_x(o).wait_send()
        to_y(o).wait_send()
        on_to_y(o).wait_send()
        on_to_x(o).wait_send()
        for kind in range(4):
            to_core(o, kind).wait_send()
    for step in range(shards - 1):
        for way in (0, 1):
            @pl.when(x_sends(way, step))
            def _():
                x_copy(way, step).wait_send()
    for copy in (keep_x, keep_v, keep_n, keep_w, keep_q):
        copy.wait()


def bias_piece(v_buf, z, t, tile, shards, per_part):
    part = t // per_part
    at = t % per_part
    flat = part * shards + z
    return v_buf[flat // 3, pl.ds(flat % 3, 1), pl.ds(aligned(at, tile), tile)]


def start_call(shards, tokens, vectors, weight, cosine, minus, plus):
    rows = tokens.shape[0]
    group = rows * shards
    depth = weight.shape[0]
    width = weight.shape[1] // shards
    any_ = pl.BlockSpec(memory_space=pl.ANY)
    vm = pl.BlockSpec(memory_space=pltpu.VMEM)
    low = jnp.bfloat16
    dma = pltpu.SemaphoreType.DMA
    return pl.pallas_call(
        functools.partial(start_kernel, shards),
        out_shape=[
            jax.ShapeDtypeStruct((shards, rows, D), low),
            jax.ShapeDtypeStruct((shards,) + vectors.shape, vectors.dtype),
            jax.ShapeDtypeStruct((group, D), low),
            jax.ShapeDtypeStruct((group, width), low),
            jax.ShapeDtypeStruct((depth * shards, width), low),
        ],
        in_specs=[any_, any_, any_, vm, vm, vm],
        out_specs=[any_] * 5,
        scratch_shapes=[
            pltpu.VMEM((shards, rows, D), low),
            pltpu.VMEM((shards,) + vectors.shape, vectors.dtype),
            pltpu.VMEM((depth * shards, width), low),
            pltpu.VMEM((group, D), low),
            pltpu.VMEM((group, width), low),
            dma((2, shards)), dma((2, shards)),
            dma((shards,)), dma((shards,)),
            dma((shards, 3)), dma((shards, 3)),
            dma((4, shards)), dma((4, shards)),
            dma((4, shards)), dma((4, shards)),
            dma((10,)),
        ],
        compiler_params=pltpu.CompilerParams(
            collective_id=1, has_side_effects=True, vmem_limit_bytes=48 * 2**20
        ),
        name="start",
        cost_estimate=pl.CostEstimate(flops=2 * group * D * width, bytes_accessed=150 * 10**6, transcendentals=0),
    )(tokens, vectors, weight, cosine, minus, plus)


def head_mask(even, rows):
    lane = lax.broadcasted_iota(jnp.int32, (rows, 128), 1)
    return (lane < HEAD_DIM) if even else (lane >= HEAD_DIM)


def only(values, keep):
    return jnp.where(keep, values.astype(jnp.float32), 0.0).astype(jnp.bfloat16)


def block_visible(at, rows, seg_rows, seg_columns):
    count = at + rows
    row = lax.broadcasted_iota(jnp.int32, (rows, count), 0) + at
    column = lax.broadcasted_iota(jnp.int32, (rows, count), 1)
    return (column <= row) & (seg_rows[at : at + rows, :1] == seg_columns[:1, :count])


def line_sends(z, shards, way, step):
    if way == 0:
        return (z + 1 < shards) & (z - step >= 0)
    return (z >= 1) & (z + step < shards)


def line_gets(z, shards, way, step):
    return (z - step >= 1) if way == 0 else (z + step + 1 < shards)


def attend_kernel(shards, rows, qkv, seg_rows, seg_columns, attended, stats,
                  a_buf, a_send, a_recv, loc):
    z = lax.axis_index("shard")
    width = qkv.shape[1] // 3
    group = qkv.shape[0]
    pairs = width // 128
    greet_line(z, shards)

    def a_copy(way, step, block):
        target = z + 1 if way == 0 else z - 1
        owner = z - step if way == 0 else z + step
        piece = a_buf.at[owner, pl.ds(block * rows, rows)]
        return remote(piece, piece, a_send.at[way, step, block], a_recv.at[way, step, block], {"shard": target})

    scale = HEAD_DIM ** (-0.5)
    blocks = group // rows
    for block in range(blocks):
        at = block * rows
        count = at + rows
        seen = block_visible(at, rows, seg_rows, seg_columns)
        for pair in range(pairs):
            lanes = slice(128 * pair, 128 * pair + 128)
            query = qkv[at:count, lanes]
            keys = qkv[:count, width + 128 * pair : width + 128 * pair + 128]
            values = qkv[:count, 2 * width + 128 * pair : 2 * width + 128 * pair + 128]
            results = []
            for odd in (0, 1):
                keep = head_mask(odd == 0, rows)
                scores = contract_last(only(query, keep), keys) * scale
                scores = jnp.where(seen, scores, masked_score)
                top = jnp.max(scores, axis=-1, keepdims=True)
                weights = jnp.exp(scores - top)
                total = jnp.sum(weights, axis=-1, keepdims=True)
                probs = (weights * (1.0 / total)).astype(jnp.bfloat16)
                results.append(jnp.dot(probs, values, preferred_element_type=jnp.float32))
                head = 2 * pair + odd
                stats[at:count, head : head + 1] = top
                stats[at:count, 64 + head : 65 + head] = 1.0 / total
            merged = jnp.where(head_mask(True, rows), results[0], results[1])
            a_buf[z, at:count, lanes] = merged.astype(jnp.bfloat16)
        for way in (0, 1):
            @pl.when(line_sends(z, shards, way, 0))
            def _():
                a_copy(way, 0, block).start()
    for step in range(shards - 1):
        for block in range(blocks):
            for way in (0, 1):
                @pl.when(line_gets(z, shards, way, step))
                def _():
                    a_copy(way, step, block).wait_recv()
                if step + 1 < shards - 1:
                    @pl.when(line_sends(z, shards, way, step + 1))
                    def _():
                        a_copy(way, step + 1, block).start()
    keep_a = [pltpu.make_async_copy(a_buf.at[o], attended.at[:, pl.ds(o * width, width)], loc.at[o]) for o in range(shards)]
    for copy in keep_a:
        copy.start()
    for step in range(shards - 1):
        for block in range(blocks):
            for way in (0, 1):
                @pl.when(line_sends(z, shards, way, step))
                def _():
                    a_copy(way, step, block).wait_send()
    for copy in keep_a:
        copy.wait()


def attend_call(shards, rows, qkv, seg_rows, seg_columns):
    group = qkv.shape[0]
    width = qkv.shape[1] // 3
    blocks = group // rows
    vm = pl.BlockSpec(memory_space=pltpu.VMEM)
    any_ = pl.BlockSpec(memory_space=pl.ANY)
    dma = pltpu.SemaphoreType.DMA
    return pl.pallas_call(
        functools.partial(attend_kernel, shards, rows),
        out_shape=[
            jax.ShapeDtypeStruct((group, shards * width), jnp.bfloat16),
            jax.ShapeDtypeStruct((group, 128), jnp.float32),
        ],
        in_specs=[vm, vm, vm],
        out_specs=[any_, vm],
        scratch_shapes=[
            pltpu.VMEM((shards, group, width), jnp.bfloat16),
            dma((2, shards - 1, blocks)), dma((2, shards - 1, blocks)), dma((shards,)),
        ],
        compiler_params=pltpu.CompilerParams(
            collective_id=2, has_side_effects=True, vmem_limit_bytes=48 * 2**20
        ),
        name="attend",
        cost_estimate=pl.CostEstimate(flops=10**9, bytes_accessed=150 * 10**6, transcendentals=0),
    )(qkv, seg_rows, seg_columns)


def attend_back_kernel(rows, qkv, d_attended, stats, seg_rows, seg_columns, cosine, minus, plus,
                       d_qkv, bias_grad, d_keys, d_values):
    width = qkv.shape[1] // 3
    group = qkv.shape[0]
    blocks = group // rows
    pairs = width // 128
    scale = HEAD_DIM ** (-0.5)

    def turned(value, at, count):
        return (value * cosine[at:count, :] - pltpu.roll(value, 120, 1) * minus[at:count, :]
                - pltpu.roll(value, 8, 1) * plus[at:count, :])

    for block in reversed(range(blocks)):
        at = block * rows
        count = at + rows
        seen = block_visible(at, rows, seg_rows, seg_columns)
        for pair in range(pairs):
            lanes = slice(128 * pair, 128 * pair + 128)
            query = qkv[at:count, lanes]
            keys = qkv[:count, width + 128 * pair : width + 128 * pair + 128]
            values = qkv[:count, 2 * width + 128 * pair : 2 * width + 128 * pair + 128]
            slope = d_attended[at:count, lanes]
            d_query, d_key, d_value = [], [], []
            for odd in (0, 1):
                keep = head_mask(odd == 0, rows)
                head = 2 * pair + odd
                own_query = only(query, keep)
                own_slope = only(slope, keep)
                scores = contract_last(own_query, keys) * scale
                scores = jnp.where(seen, scores, masked_score)
                probs = jnp.exp(scores - stats[at:count, head : head + 1]) * stats[at:count, 64 + head : 65 + head]
                d_probs = contract_last(own_slope, values)
                inner = jnp.sum(probs * d_probs, axis=-1, keepdims=True)
                d_scores = (probs * (d_probs - inner)).astype(jnp.bfloat16)
                d_query.append(jnp.dot(d_scores, keys, preferred_element_type=jnp.float32))
                d_key.append(contract_first(d_scores, own_query))
                d_value.append(contract_first(probs.astype(jnp.bfloat16), own_slope))
            keep = head_mask(True, rows)
            d_q = jnp.where(keep, d_query[0], d_query[1]) * scale
            d_q = turned(d_q, at, count).astype(jnp.bfloat16)
            d_qkv[at:count, lanes] = d_q
            d_k = (d_key[0] + d_key[1]) * scale
            d_v = d_value[0] + d_value[1]
            if block == blocks - 1:
                d_keys[:, lanes] = d_k
                d_values[:, lanes] = d_v
            else:
                d_keys[:count, lanes] += d_k
                d_values[:count, lanes] += d_v
            k_out = turned(d_keys[at:count, lanes], at, count).astype(jnp.bfloat16)
            d_qkv[at:count, width + 128 * pair : width + 128 * pair + 128] = k_out
            v_out = d_values[at:count, lanes].astype(jnp.bfloat16)
            d_qkv[at:count, 2 * width + 128 * pair : 2 * width + 128 * pair + 128] = v_out
    for part in range(3 * pairs):
        lanes = slice(128 * part, 128 * part + 128)
        bias_grad[:, lanes] = jnp.broadcast_to(
            jnp.sum(d_qkv[:, lanes].astype(jnp.float32), axis=0, keepdims=True), (8, 128))


def contract_first(left, right):
    return lax.dot_general(
        left, right, (((0,), (0,)), ((), ())), preferred_element_type=jnp.float32
    )


def attend_back_call(rows, qkv, d_attended, stats, seg_rows, seg_columns, cosine, minus, plus):
    group = qkv.shape[0]
    width = qkv.shape[1] // 3
    vm = pl.BlockSpec(memory_space=pltpu.VMEM)
    return pl.pallas_call(
        functools.partial(attend_back_kernel, rows),
        out_shape=[
            jax.ShapeDtypeStruct((group, 3 * width), jnp.bfloat16),
            jax.ShapeDtypeStruct((8, 3 * width), jnp.float32),
        ],
        in_specs=[vm] * 8,
        out_specs=[vm, vm],
        scratch_shapes=[pltpu.VMEM((group, width), jnp.float32), pltpu.VMEM((group, width), jnp.float32)],
        compiler_params=pltpu.CompilerParams(vmem_limit_bytes=48 * 2**20),
        name="attend_back",
        cost_estimate=pl.CostEstimate(flops=3 * 10**9, bytes_accessed=100 * 10**6, transcendentals=0),
    )(qkv, d_attended, stats, seg_rows, seg_columns, cosine, minus, plus)


def scatter_kernel(shards, cuts, parts, total, own, got, load, send, recv):
    z = lax.axis_index("shard")
    rows = parts.shape[1]
    step_rows = rows // cuts
    greet_line(z, shards)

    def piece(cut):
        return pl.ds(cut * step_rows, step_rows)

    def moved(way, block, cut):
        target = z + 1 if way == 0 else z - 1
        place = got.at[way, block, piece(cut)]
        return remote(place, place, send.at[way, block, cut], recv.at[way, block, cut], {"shard": target})

    loads = [pltpu.make_async_copy(parts.at[j], own.at[j], load.at[j]) for j in range(shards)]
    for copy in loads:
        copy.start()
    for copy in loads:
        copy.wait()
    for far in range(shards - 1):
        for cut in range(cuts):
            for way in (0, 1):
                block = shards - 1 - far if way == 0 else far
                sends = z < block if way == 0 else z > block
                first = z == 0 if way == 0 else z == shards - 1

                @pl.when(sends)
                def _():
                    @pl.when(first)
                    def _():
                        got[way, block, piece(cut)] = own[block, piece(cut)]

                    @pl.when(jnp.logical_not(first))
                    def _():
                        moved(way, block, cut).wait_recv()
                        got[way, block, piece(cut)] = (
                            got[way, block, piece(cut)].astype(jnp.float32)
                            + own[block, piece(cut)].astype(jnp.float32)
                        ).astype(got.dtype)
                    moved(way, block, cut).start()
    total[...] = own[z].astype(jnp.float32)
    for way in (0, 1):
        @pl.when(z >= 1 if way == 0 else z + 1 < shards)
        def _():
            for cut in range(cuts):
                moved(way, z, cut).wait_recv()
            total[...] += got[way, z].astype(jnp.float32)
    for far in range(shards - 1):
        for cut in range(cuts):
            for way in (0, 1):
                block = shards - 1 - far if way == 0 else far

                @pl.when(z < block if way == 0 else z > block)
                def _():
                    moved(way, block, cut).wait_send()


def scatter_call(shards, parts, number):
    _, rows, columns = parts.shape
    cuts = 3
    dma = pltpu.SemaphoreType.DMA
    return pl.pallas_call(
        functools.partial(scatter_kernel, shards, cuts),
        out_shape=jax.ShapeDtypeStruct((rows, columns), jnp.float32),
        in_specs=[pl.BlockSpec(memory_space=pl.ANY)],
        out_specs=pl.BlockSpec(memory_space=pltpu.VMEM),
        scratch_shapes=[
            pltpu.VMEM(parts.shape, parts.dtype),
            pltpu.VMEM((2,) + parts.shape, parts.dtype),
            dma((shards,)), dma((2, shards, cuts)), dma((2, shards, cuts)),
        ],
        compiler_params=pltpu.CompilerParams(
            collective_id=number, has_side_effects=True, vmem_limit_bytes=32 * 2**20
        ),
        name="scatter",
        cost_estimate=pl.CostEstimate(flops=0, bytes_accessed=200 * 10**6, transcendentals=0),
    )(parts)


def exchange_kernel(shards, first, second, first_out, second_out, send, recv, loc):
    z = lax.axis_index("shard")
    width = first.shape[1] // shards
    greet([((z != o), {"shard": o}) for o in range(shards)], shards - 1)
    arrays = ((first, first_out), (second, second_out))

    def move(k, o):
        source, target = arrays[k]
        return remote(source.at[:, pl.ds(o * width, width)], target.at[z], send.at[k, o], recv.at[k, z], {"shard": o})

    def arrival(k, o):
        source, target = arrays[k]
        return remote(target.at[o], target.at[o], send.at[k, o], recv.at[k, o], {"shard": o})

    for k in (0, 1):
        for o in range(shards):
            @pl.when(z != o)
            def _():
                move(k, o).start()

            @pl.when(z == o)
            def _():
                source, target = arrays[k]
                pltpu.make_async_copy(source.at[:, pl.ds(o * width, width)], target.at[o], loc.at[k]).start()
    for k in (0, 1):
        for o in range(shards):
            @pl.when(z != o)
            def _():
                arrival(k, o).wait_recv()
                move(k, o).wait_send()

            @pl.when(z == o)
            def _():
                source, target = arrays[k]
                pltpu.make_async_copy(source.at[:, pl.ds(o * width, width)], target.at[o], loc.at[k]).wait()


def exchange_call(shards, first, second):
    rows, columns = first.shape
    shape = jax.ShapeDtypeStruct((shards, rows, columns // shards), first.dtype)
    any_ = pl.BlockSpec(memory_space=pl.ANY)
    dma = pltpu.SemaphoreType.DMA
    return pl.pallas_call(
        functools.partial(exchange_kernel, shards),
        out_shape=[shape, shape],
        in_specs=[any_, any_],
        out_specs=[any_, any_],
        scratch_shapes=[dma((2, shards)), dma((2, shards)), dma((2,))],
        compiler_params=pltpu.CompilerParams(collective_id=5, has_side_effects=True),
        name="exchange",
        cost_estimate=pl.CostEstimate(flops=0, bytes_accessed=100 * 10**6, transcendentals=0),
    )(first, second)


def swap_pieces(pieces):
    shards = lax.axis_size("shard")
    here = lax.axis_index("shard")
    out = pieces
    for k in range(1, shards):
        partner = jnp.bitwise_xor(here, k)
        piece = lax.dynamic_index_in_dim(pieces, partner, axis=0, keepdims=True)
        piece = lax.ppermute(piece, "shard", [(i, i ^ k) for i in range(shards)])
        out = lax.dynamic_update_slice_in_dim(out, piece, partner, axis=0)
    return out


def own_share(rows):
    own = rows.shape[0] // lax.axis_size("replica")
    return lax.dynamic_slice_in_dim(rows, lax.axis_index("replica") * own, own, axis=0)


def spread_rows(rows, columns):
    shards = lax.axis_size("shard")
    piece = own_share(rows)
    own = piece.shape[0]
    piece = piece.reshape(own, columns, shards, -1).transpose(2, 0, 1, 3).reshape(shards, own, -1)
    full = lax.all_gather(swap_pieces(piece), "replica", axis=0, tiled=False)
    return full.transpose(1, 0, 2, 3).reshape(rows.shape[0] * shards, -1)


def gather_rows(rows):
    shards = lax.axis_size("shard")
    piece = own_share(rows)
    moved = swap_pieces(jnp.broadcast_to(piece[None], (shards,) + piece.shape))
    full = lax.all_gather(moved, "replica", axis=0, tiled=False)
    return full.transpose(1, 0, 2, 3).reshape(rows.shape[0] * shards, -1)


def own_rows(features):
    copies = lax.axis_size("replica")
    shards = lax.axis_size("shard")
    count = features.shape[0]
    return (
        features.reshape(count, shards, copies, -1).transpose(0, 2, 1, 3).reshape(count, -1)
    )


def sum_columns(features, slopes, columns):
    shards = lax.axis_size("shard")
    term = contract_first(own_rows(features), slopes).astype(jnp.bfloat16)
    part = lax.psum_scatter(term, "replica", scatter_dimension=0, tiled=True)
    own = part.shape[0] // shards
    moved = swap_pieces(part.reshape(shards, own, -1))
    moved = moved.reshape(shards, own, columns, -1).transpose(1, 2, 0, 3).reshape(own, -1)
    return lax.all_gather(moved, "replica", axis=0, tiled=True).astype(jnp.float32)


def swiglu(gate_up):
    half = gate_up.shape[1] // 2
    return jax.nn.silu(gate_up[:, :half]) * gate_up[:, half:]


def norm_stats(values):
    mean = jnp.mean(values, axis=-1, keepdims=True)
    centered = values - mean
    inverse = lax.rsqrt(jnp.mean(centered * centered, axis=-1, keepdims=True) + norm_eps)
    return centered * inverse, inverse


def norm_back(slope, unit, inverse, gain):
    scaled = slope * gain
    return inverse * (
        scaled
        - jnp.mean(scaled, axis=-1, keepdims=True)
        - unit * jnp.mean(scaled * unit, axis=-1, keepdims=True)
    )


def start_plain(tokens, vectors, qkv_weight, cosine, minus, plus):
    shards = lax.axis_size("shard")
    here = lax.axis_index("shard")
    all_tokens = lax.all_gather(tokens, "shard", axis=0, tiled=False)
    all_vectors = lax.all_gather(vectors, "shard", axis=0, tiled=False)
    weight = spread_rows(qkv_weight, 3)
    width = D // shards
    gain, shift = (all_vectors[:, 3 + i].reshape(D) for i in (0, 1))
    unit, _ = norm_stats(all_tokens.reshape(-1, D).astype(jnp.float32))
    normed = (unit * gain + shift).astype(jnp.bfloat16)
    bias = all_vectors[:, :3].reshape(3, shards, width)
    bias = lax.dynamic_index_in_dim(bias, here, axis=1, keepdims=False).reshape(3 * width)
    value = jnp.dot(normed, weight, preferred_element_type=jnp.float32) + bias
    turned = value[:, : 2 * width]
    wide = [jnp.tile(t, (1, 2 * width // 128)) for t in (cosine, minus, plus)]
    turned = (
        turned * wide[0] + jnp.roll(turned, -8, 1) * wide[1] + jnp.roll(turned, 8, 1) * wide[2]
    )
    qkv = jnp.concatenate([turned, value[:, 2 * width :]], axis=1).astype(jnp.bfloat16)
    return all_tokens, all_vectors, normed, qkv, weight


def on_device(
    tokens,
    cotangent,
    qkv_weight,
    qkv_bias,
    out_weight,
    gate_up_weight,
    down_weight,
    norm1_gain,
    norm1_shift,
    norm2_gain,
    norm2_shift,
    seq_lengths,
):
    shards = lax.axis_size("shard")
    copies = lax.axis_size("replica")
    here = lax.axis_index("shard")
    row_count = tokens.shape[0]
    group_rows = row_count * shards
    width = D // shards
    f32 = jnp.float32
    low = jnp.bfloat16

    index = jnp.arange(group_rows, dtype=jnp.int32)
    segment, position = group_layout(seq_lengths[0], index)
    seg_rows = jnp.broadcast_to(segment[:, None], (group_rows, 128))
    seg_columns = jnp.broadcast_to(segment[None, :], (8, group_rows))
    cosine, sine_value = rope_tables(position)
    half_rot = ROT_DIM // 2
    rest = HEAD_DIM - ROT_DIM
    none = jnp.zeros((group_rows, half_rot), f32)
    empty = jnp.zeros((group_rows, rest), f32)
    cosine = jnp.tile(jnp.concatenate([cosine, cosine, empty + 1.0], axis=1), (1, 2))
    minus = jnp.tile(jnp.concatenate([-sine_value, none, empty], axis=1), (1, 2))
    plus = jnp.tile(jnp.concatenate([none, sine_value, empty], axis=1), (1, 2))

    vectors = jnp.concatenate(
        [qkv_bias, norm1_gain, norm1_shift, norm2_gain, norm2_shift, jnp.zeros((width,), low)]
    )
    vectors = vectors.astype(f32).reshape(8, width)
    weight_out = gather_rows(out_weight)
    weight_gate_up = spread_rows(gate_up_weight, 2)
    begin = functools.partial(start_call, shards) if copies == 8 else start_plain
    all_tokens, all_vectors, normed_low, qkv, weight_qkv = begin(
        tokens, vectors, qkv_weight, cosine, minus, plus
    )
    gain_one, shift_one, gain_two, shift_two = (
        all_vectors[:, 3 + i].reshape(D) for i in range(4)
    )
    cotangent_later, qkv = lax.optimization_barrier((cotangent, qkv))
    group_cotangent = lax.all_gather(cotangent_later, "shard", axis=0, tiled=True)

    def local(array):
        return lax.dynamic_slice_in_dim(array, here * row_count, row_count, axis=0)

    attended, stats = attend_call(shards, row_count, qkv, seg_rows, seg_columns)
    inputs = all_tokens.reshape(group_rows, D).astype(f32)
    middle = inputs + jnp.dot(attended, weight_out, preferred_element_type=f32)
    unit_two, inverse_two = norm_stats(middle)
    normed_two_low = (unit_two * gain_two + shift_two).astype(low)
    gate_up = jnp.dot(normed_two_low, weight_gate_up, preferred_element_type=f32)
    hidden, swiglu_pull = jax.vjp(swiglu, gate_up)
    hidden_low = hidden.astype(low)
    d_hidden = contract_last(group_cotangent, down_weight)
    d_gate_up_low = swiglu_pull(d_hidden)[0].astype(low)
    d_normed_two_part = contract_last(d_gate_up_low, weight_gate_up).astype(low)
    d_normed_two = scatter_call(shards, d_normed_two_part.reshape(shards, row_count, D), 3)
    unit_two_own = local(unit_two)
    d_middle = cotangent.astype(f32) + norm_back(
        d_normed_two, unit_two_own, local(inverse_two), gain_two
    )
    d_gain_two = jnp.sum(d_normed_two * unit_two_own, axis=0)
    d_shift_two = jnp.sum(d_normed_two, axis=0)
    d_middle_low = d_middle.astype(low)
    d_attended_own = contract_last(d_middle_low, weight_out).astype(low)
    d_attended, d_middle_columns = exchange_call(shards, d_attended_own, d_middle_low)
    d_projected_low, bias_part = attend_back_call(
        row_count, qkv, d_attended.reshape(group_rows, width), stats, seg_rows, seg_columns,
        cosine, minus, plus,
    )
    d_normed_part = contract_last(d_projected_low, weight_qkv).astype(low)
    d_normed = scatter_call(shards, d_normed_part.reshape(shards, row_count, D), 4)
    unit_one, inverse_one = norm_stats(tokens.astype(f32))
    input_grad = d_middle + norm_back(d_normed, unit_one, inverse_one, gain_one)
    d_gain_one = jnp.sum(d_normed * unit_one, axis=0)
    d_shift_one = jnp.sum(d_normed, axis=0)

    down_part = jnp.dot(hidden_low, down_weight, preferred_element_type=f32).astype(low)
    down_own = lax.psum_scatter(down_part, "shard", scatter_dimension=0, tiled=True)
    mixed = (local(middle) + down_own.astype(f32)).astype(low)
    down_grad = lax.psum(
        contract_first(hidden_low, group_cotangent).astype(low), "replica"
    ).astype(f32)
    gate_up_grad = sum_columns(normed_two_low, d_gate_up_low, 2)
    out_grad = sum_columns(attended, d_middle_columns.reshape(group_rows, width), 1)
    qkv_grad = sum_columns(normed_low, d_projected_low, 3)

    bias_part = bias_part[0].reshape(3, 1, width)
    bias_wide = lax.dynamic_update_slice(
        jnp.zeros((3, shards, width), f32), bias_part, (0, here, 0)
    ).reshape(shards, 3 * width)
    small = jnp.concatenate(
        [bias_wide]
        + [v.reshape(shards, width) for v in (d_gain_one, d_shift_one, d_gain_two, d_shift_two)],
        axis=1,
    )
    small = lax.psum(small, ("replica", "shard"))
    small = lax.dynamic_index_in_dim(small, here, axis=0, keepdims=False)
    bias_rows = 3 * width
    return (
        mixed,
        input_grad,
        qkv_grad,
        small[:bias_rows],
        out_grad,
        gate_up_grad,
        down_grad,
    ) + tuple(small[bias_rows + i * width : bias_rows + (i + 1) * width] for i in range(4))


def solution(mesh):
    placed = (
        P(("replica", "shard"), None),
        P(("replica", "shard"), None),
        P("shard", None),
        P("shard"),
        P("shard", None),
        P("shard", None),
        P("shard", None),
        P("shard"),
        P("shard"),
        P("shard"),
        P("shard"),
        P("replica", None),
    )
    return jax.shard_map(
        on_device,
        mesh=mesh,
        in_specs=placed,
        out_specs=(
            P(("replica", "shard"), None),
            P(("replica", "shard"), None),
            P("shard", None),
            P("shard"),
            P("shard", None),
            P("shard", None),
            P("shard", None),
            P("shard"),
            P("shard"),
            P("shard"),
            P("shard"),
        ),
        check_vma=False,
    )
```

```python
import functools

import jax
import jax.numpy as jnp
from jax import lax
from jax.experimental import pallas as pl
from jax.experimental.pallas import tpu as pltpu
from jax.sharding import PartitionSpec as P

D = 2048
FF = 5632
HEADS = 32
HEAD_DIM = 64
ROT_DIM = 16
MESH = pl.DeviceIdType.MESH


norm_eps = 1e-05
masked_score = -1000000000.0


def group_layout(lengths, token_index):
    seq_ends = jnp.cumsum(lengths)
    passed = (token_index[:, None] >= seq_ends[None, :]).astype(jnp.int32)
    segment = jnp.sum(passed, axis=1)
    position = token_index - jnp.sum(passed * lengths[None, :], axis=1)
    return (segment, position)


def rope_tables(position):
    half_rot = ROT_DIM // 2
    frequency = jnp.exp(
        -jnp.log(10000.0) * (2.0 * jnp.arange(half_rot, dtype=jnp.float32) / ROT_DIM)
    )
    angles = position.astype(jnp.float32)[:, None] * frequency[None, :]
    return (jnp.cos(angles), jnp.sin(angles))


def contract_last(left, right):
    return lax.dot_general(
        left, right, (((1,), (1,)), ((), ())), preferred_element_type=jnp.float32
    )


def aligned(value, unit):
    return pl.multiple_of(value * unit, unit)


def greet(partners, count):
    barrier = pltpu.get_barrier_semaphore()
    for there, device in partners:
        @pl.when(there)
        def _():
            pl.semaphore_signal(barrier, inc=1, device_id=device, device_id_type=MESH)
    pl.semaphore_wait(barrier, count)


def greet_line(z, shards):
    count = (z + shards - 1) // shards + (2 * shards - 2 - z) // shards
    greet([(z >= 1, {"shard": z - 1}), (z + 1 < shards, {"shard": z + 1})], count)


def remote(source, target, send, recv, device):
    return pltpu.make_async_remote_copy(
        src_ref=source, dst_ref=target, send_sem=send, recv_sem=recv,
        device_id=device, device_id_type=MESH,
    )


def start_kernel(shards, tokens, vectors, weight, cosine, minus, plus,
                 all_tokens, all_vectors, normed, qkv, kept_weight,
                 x_buf, v_buf, w_buf, n_buf, out_buf,
                 x_send, x_recv, v_send, v_recv, w_send, w_recv, xy_send, xy_recv, c_send, c_recv, loc):
    z = lax.axis_index("shard")
    r = lax.axis_index("replica")
    rows = tokens.shape[0]
    depth = weight.shape[0]
    share = depth // 8
    half = share // 2
    width = w_buf.shape[1] // 3
    core, x, y = r % 2, (r // 2) % 2, r // 4
    xr, yr, cr = r + 2 - 4 * x, r + 4 - 8 * y, r + 1 - 2 * core
    dr = 4 * (1 - y) + 2 * (1 - x) + core
    true = z >= 0
    greet(
        [((z != o), {"shard": o}) for o in range(shards)]
        + [(true, {"replica": d}) for d in (xr, yr, cr)],
        shards + 2,
    )

    def w_rows(owner, replica):
        return pl.ds(aligned(owner * 8 + replica, share), share)

    def vec_copy(o):
        return remote(vectors, v_buf.at[z], v_send.at[o], v_recv.at[z], {"shard": o})

    def w_copy(o, part):
        return remote(
            weight.at[pl.ds(aligned(r, share), share), pl.ds(aligned(part * shards + o, width), width)],
            w_buf.at[w_rows(z, r), pl.ds(part * width, width)],
            w_send.at[o, part], w_recv.at[z, part], {"shard": o},
        )

    def w_arrival(o, part):
        block = w_buf.at[w_rows(o, r), pl.ds(part * width, width)]
        return remote(block, block, w_send.at[o, part], w_recv.at[o, part], {"shard": o})

    def v_arrival(o):
        return remote(vectors, v_buf.at[o], v_send.at[o], v_recv.at[o], {"shard": o})

    def x_copy(way, step):
        target = z + 1 if way == 0 else z - 1
        chunk = z - step if way == 0 else z + step
        source = tokens if step == 0 else x_buf.at[chunk]
        return remote(source, x_buf.at[chunk], x_send.at[way, step], x_recv.at[way, step], {"shard": target})

    def x_sends(way, step):
        if way == 0:
            return (z + 1 < shards) & (z - step >= 0)
        return (z >= 1) & (z + step < shards)

    def x_gets(way, step):
        return (z - step >= 1) if way == 0 else (z + step + 1 < shards)

    for o in range(shards):
        @pl.when(z != o)
        def _():
            vec_copy(o).start()
            for part in range(3):
                w_copy(o, part).start()
    for way in (0, 1):
        @pl.when(x_sends(way, 0))
        def _():
            x_copy(way, 0).start()
    own_x = pltpu.make_async_copy(tokens, x_buf.at[z], loc.at[0])
    own_x.start()
    own_v = pltpu.make_async_copy(vectors, v_buf.at[z], loc.at[1])
    own_v.start()
    own_w = [
        pltpu.make_async_copy(
            weight.at[pl.ds(aligned(r, share), share), pl.ds(aligned(part * shards + z, width), width)],
            w_buf.at[w_rows(z, r), pl.ds(part * width, width)], loc.at[2 + part],
        )
        for part in range(3)
    ]
    for copy in own_w:
        copy.start()

    def to_x(o):
        block = w_buf.at[w_rows(o, r)]
        return remote(block, block, xy_send.at[0, o], xy_recv.at[0, o], {"replica": xr})

    def to_y(o):
        block = w_buf.at[w_rows(o, r)]
        return remote(block, block, xy_send.at[1, o], xy_recv.at[1, o], {"replica": yr})

    def on_to_y(o):
        block = w_buf.at[pl.ds(aligned((o * 8 + xr) * 2, half), half)]
        return remote(block, block, xy_send.at[2, o], xy_recv.at[2, o], {"replica": yr})

    def on_to_x(o):
        block = w_buf.at[pl.ds(aligned((o * 8 + yr) * 2 + 1, half), half)]
        return remote(block, block, xy_send.at[3, o], xy_recv.at[3, o], {"replica": xr})

    def to_core(o, kind):
        whose = (r, xr, yr, dr)[kind]
        block = w_buf.at[w_rows(o, whose)]
        return remote(block, block, c_send.at[kind, o], c_recv.at[kind, o], {"replica": cr})

    for copy in own_w:
        copy.wait()
    for step in range(shards):
        for o in range(shards):
            @pl.when((z - o == step) | (o - z == step))
            def _():
                if step > 0:
                    for part in range(3):
                        w_arrival(o, part).wait_recv()
                to_x(o).start()
                to_y(o).start()
                to_core(o, 0).start()
        if step + 1 < shards:
            for way in (0, 1):
                @pl.when(x_gets(way, step))
                def _():
                    x_copy(way, step).wait_recv()
                @pl.when(x_sends(way, step + 1))
                def _():
                    x_copy(way, step + 1).start()
    for o in range(shards):
        to_x(o).wait_recv()
        on_to_y(o).start()
        to_core(o, 1).start()
        to_y(o).wait_recv()
        on_to_x(o).start()
        to_core(o, 2).start()
    own_x.wait()
    own_v.wait()
    for o in range(shards):
        @pl.when(z != o)
        def _():
            v_arrival(o).wait_recv()

    keep_x = pltpu.make_async_copy(x_buf, all_tokens, loc.at[5])
    keep_x.start()
    keep_v = pltpu.make_async_copy(v_buf, all_vectors, loc.at[6])
    keep_v.start()
    gain = jnp.concatenate([v_buf[o, 3:4, :] for o in range(shards)], axis=1)
    shift = jnp.concatenate([v_buf[o, 4:5, :] for o in range(shards)], axis=1)
    for o in range(shards):
        @pl.loop(0, rows, step=32)
        def _(at):
            block = pl.ds(pl.multiple_of(at, 32), 32)
            values = x_buf[o, block, :].astype(jnp.float32)
            centered = values - jnp.mean(values, axis=-1, keepdims=True)
            spread = jnp.mean(centered * centered, axis=-1, keepdims=True)
            out = centered * lax.rsqrt(spread + norm_eps) * gain + shift
            n_buf[pl.ds(pl.multiple_of(o * rows + at, 32), 32), :] = out.astype(jnp.bfloat16)
    keep_n = pltpu.make_async_copy(n_buf, normed, loc.at[7])
    keep_n.start()

    for o in range(shards):
        on_to_y(o).wait_recv()
        on_to_x(o).wait_recv()
        to_core(o, 3).start()
    for o in range(shards):
        for kind in range(4):
            to_core(o, kind).wait_recv()
    keep_w = pltpu.make_async_copy(w_buf, kept_weight, loc.at[8])
    keep_w.start()

    tile = 256
    per_part = width // tile

    @pl.loop(0, 3 * per_part)
    def _(t):
        columns = pl.ds(aligned(t, tile), tile)
        bias_row = bias_piece(v_buf, z, t, tile, shards, per_part)
        value = jnp.dot(n_buf[...], w_buf[:, columns], preferred_element_type=jnp.float32) + bias_row

        @pl.when(t < 2 * per_part)
        def _():
            wide = jnp.concatenate([cosine[...]] * (tile // 128), axis=1)
            wide_minus = jnp.concatenate([minus[...]] * (tile // 128), axis=1)
            wide_plus = jnp.concatenate([plus[...]] * (tile // 128), axis=1)
            turned = value * wide + pltpu.roll(value, tile - 8, 1) * wide_minus + pltpu.roll(value, 8, 1) * wide_plus
            out_buf[:, columns] = turned.astype(jnp.bfloat16)

        @pl.when(t >= 2 * per_part)
        def _():
            out_buf[:, columns] = value.astype(jnp.bfloat16)
    keep_q = pltpu.make_async_copy(out_buf, qkv, loc.at[9])
    keep_q.start()

    for o in range(shards):
        @pl.when(z != o)
        def _():
            vec_copy(o).wait_send()
            for part in range(3):
                w_copy(o, part).wait_send()
        to_x(o).wait_send()
        to_y(o).wait_send()
        on_to_y(o).wait_send()
        on_to_x(o).wait_send()
        for kind in range(4):
            to_core(o, kind).wait_send()
    for step in range(shards - 1):
        for way in (0, 1):
            @pl.when(x_sends(way, step))
            def _():
                x_copy(way, step).wait_send()
    for copy in (keep_x, keep_v, keep_n, keep_w, keep_q):
        copy.wait()


def bias_piece(v_buf, z, t, tile, shards, per_part):
    part = t // per_part
    at = t % per_part
    flat = part * shards + z
    return v_buf[flat // 3, pl.ds(flat % 3, 1), pl.ds(aligned(at, tile), tile)]


def start_call(shards, tokens, vectors, weight, cosine, minus, plus):
    rows = tokens.shape[0]
    group = rows * shards
    depth = weight.shape[0]
    width = weight.shape[1] // shards
    any_ = pl.BlockSpec(memory_space=pl.ANY)
    vm = pl.BlockSpec(memory_space=pltpu.VMEM)
    low = jnp.bfloat16
    dma = pltpu.SemaphoreType.DMA
    return pl.pallas_call(
        functools.partial(start_kernel, shards),
        out_shape=[
            jax.ShapeDtypeStruct((shards, rows, D), low),
            jax.ShapeDtypeStruct((shards,) + vectors.shape, vectors.dtype),
            jax.ShapeDtypeStruct((group, D), low),
            jax.ShapeDtypeStruct((group, width), low),
            jax.ShapeDtypeStruct((depth * shards, width), low),
        ],
        in_specs=[any_, any_, any_, vm, vm, vm],
        out_specs=[any_] * 5,
        scratch_shapes=[
            pltpu.VMEM((shards, rows, D), low),
            pltpu.VMEM((shards,) + vectors.shape, vectors.dtype),
            pltpu.VMEM((depth * shards, width), low),
            pltpu.VMEM((group, D), low),
            pltpu.VMEM((group, width), low),
            dma((2, shards)), dma((2, shards)),
            dma((shards,)), dma((shards,)),
            dma((shards, 3)), dma((shards, 3)),
            dma((4, shards)), dma((4, shards)),
            dma((4, shards)), dma((4, shards)),
            dma((10,)),
        ],
        compiler_params=pltpu.CompilerParams(
            collective_id=1, has_side_effects=True, vmem_limit_bytes=48 * 2**20
        ),
        name="start",
        cost_estimate=pl.CostEstimate(flops=2 * group * D * width, bytes_accessed=150 * 10**6, transcendentals=0),
    )(tokens, vectors, weight, cosine, minus, plus)


def head_mask(even, rows):
    lane = lax.broadcasted_iota(jnp.int32, (rows, 128), 1)
    return (lane < HEAD_DIM) if even else (lane >= HEAD_DIM)


def only(values, keep):
    return jnp.where(keep, values.astype(jnp.float32), 0.0).astype(jnp.bfloat16)


def block_visible(at, rows, seg_rows, seg_columns):
    count = at + rows
    row = lax.broadcasted_iota(jnp.int32, (rows, count), 0) + at
    column = lax.broadcasted_iota(jnp.int32, (rows, count), 1)
    return (column <= row) & (seg_rows[at : at + rows, :1] == seg_columns[:1, :count])


def line_sends(z, shards, way, step):
    if way == 0:
        return (z + 1 < shards) & (z - step >= 0)
    return (z >= 1) & (z + step < shards)


def line_gets(z, shards, way, step):
    return (z - step >= 1) if way == 0 else (z + step + 1 < shards)


def attend_kernel(shards, rows, qkv, seg_rows, seg_columns, attended, stats,
                  a_buf, a_send, a_recv, loc):
    z = lax.axis_index("shard")
    width = qkv.shape[1] // 3
    group = qkv.shape[0]
    pairs = width // 128
    greet_line(z, shards)

    def a_copy(way, step, block):
        target = z + 1 if way == 0 else z - 1
        owner = z - step if way == 0 else z + step
        piece = a_buf.at[owner, pl.ds(block * rows, rows)]
        return remote(piece, piece, a_send.at[way, step, block], a_recv.at[way, step, block], {"shard": target})

    scale = HEAD_DIM ** (-0.5)
    blocks = group // rows
    for block in range(blocks):
        at = block * rows
        count = at + rows
        seen = block_visible(at, rows, seg_rows, seg_columns)
        for pair in range(pairs):
            lanes = slice(128 * pair, 128 * pair + 128)
            query = qkv[at:count, lanes]
            keys = qkv[:count, width + 128 * pair : width + 128 * pair + 128]
            values = qkv[:count, 2 * width + 128 * pair : 2 * width + 128 * pair + 128]
            results = []
            for odd in (0, 1):
                keep = head_mask(odd == 0, rows)
                scores = contract_last(only(query, keep), keys) * scale
                scores = jnp.where(seen, scores, masked_score)
                top = jnp.max(scores, axis=-1, keepdims=True)
                weights = jnp.exp(scores - top)
                total = jnp.sum(weights, axis=-1, keepdims=True)
                probs = (weights * (1.0 / total)).astype(jnp.bfloat16)
                results.append(jnp.dot(probs, values, preferred_element_type=jnp.float32))
                head = 2 * pair + odd
                stats[at:count, head : head + 1] = top
                stats[at:count, 64 + head : 65 + head] = 1.0 / total
            merged = jnp.where(head_mask(True, rows), results[0], results[1])
            a_buf[z, at:count, lanes] = merged.astype(jnp.bfloat16)
        for way in (0, 1):
            @pl.when(line_sends(z, shards, way, 0))
            def _():
                a_copy(way, 0, block).start()
    for step in range(shards - 1):
        for block in range(blocks):
            for way in (0, 1):
                @pl.when(line_gets(z, shards, way, step))
                def _():
                    a_copy(way, step, block).wait_recv()
                if step + 1 < shards - 1:
                    @pl.when(line_sends(z, shards, way, step + 1))
                    def _():
                        a_copy(way, step + 1, block).start()
    keep_a = [pltpu.make_async_copy(a_buf.at[o], attended.at[:, pl.ds(o * width, width)], loc.at[o]) for o in range(shards)]
    for copy in keep_a:
        copy.start()
    for step in range(shards - 1):
        for block in range(blocks):
            for way in (0, 1):
                @pl.when(line_sends(z, shards, way, step))
                def _():
                    a_copy(way, step, block).wait_send()
    for copy in keep_a:
        copy.wait()


def attend_call(shards, rows, qkv, seg_rows, seg_columns):
    group = qkv.shape[0]
    width = qkv.shape[1] // 3
    blocks = group // rows
    vm = pl.BlockSpec(memory_space=pltpu.VMEM)
    any_ = pl.BlockSpec(memory_space=pl.ANY)
    dma = pltpu.SemaphoreType.DMA
    return pl.pallas_call(
        functools.partial(attend_kernel, shards, rows),
        out_shape=[
            jax.ShapeDtypeStruct((group, shards * width), jnp.bfloat16),
            jax.ShapeDtypeStruct((group, 128), jnp.float32),
        ],
        in_specs=[vm, vm, vm],
        out_specs=[any_, vm],
        scratch_shapes=[
            pltpu.VMEM((shards, group, width), jnp.bfloat16),
            dma((2, shards - 1, blocks)), dma((2, shards - 1, blocks)), dma((shards,)),
        ],
        compiler_params=pltpu.CompilerParams(
            collective_id=2, has_side_effects=True, vmem_limit_bytes=48 * 2**20
        ),
        name="attend",
        cost_estimate=pl.CostEstimate(flops=10**9, bytes_accessed=150 * 10**6, transcendentals=0),
    )(qkv, seg_rows, seg_columns)


def attend_back_kernel(rows, *refs):
    attend_back_body(rows, *refs, [])


def attend_back_body(rows, qkv, d_attended, stats, seg_rows, seg_columns, cosine, minus, plus,
                     d_qkv, bias_grad, d_keys, d_values, steps):
    width = qkv.shape[1] // 3
    group = qkv.shape[0]
    blocks = group // rows
    pairs = width // 128
    scale = HEAD_DIM ** (-0.5)

    def turned(value, at, count):
        return (value * cosine[at:count, :] - pltpu.roll(value, 120, 1) * minus[at:count, :]
                - pltpu.roll(value, 8, 1) * plus[at:count, :])

    for block in reversed(range(blocks)):
        at = block * rows
        count = at + rows
        seen = block_visible(at, rows, seg_rows, seg_columns)
        for pair in range(pairs):
            lanes = slice(128 * pair, 128 * pair + 128)
            query = qkv[at:count, lanes]
            keys = qkv[:count, width + 128 * pair : width + 128 * pair + 128]
            values = qkv[:count, 2 * width + 128 * pair : 2 * width + 128 * pair + 128]
            slope = d_attended[at:count, lanes]
            d_query, d_key, d_value = [], [], []
            for odd in (0, 1):
                keep = head_mask(odd == 0, rows)
                head = 2 * pair + odd
                own_query = only(query, keep)
                own_slope = only(slope, keep)
                scores = contract_last(own_query, keys) * scale
                scores = jnp.where(seen, scores, masked_score)
                probs = jnp.exp(scores - stats[at:count, head : head + 1]) * stats[at:count, 64 + head : 65 + head]
                d_probs = contract_last(own_slope, values)
                inner = jnp.sum(probs * d_probs, axis=-1, keepdims=True)
                d_scores = (probs * (d_probs - inner)).astype(jnp.bfloat16)
                d_query.append(jnp.dot(d_scores, keys, preferred_element_type=jnp.float32))
                d_key.append(contract_first(d_scores, own_query))
                d_value.append(contract_first(probs.astype(jnp.bfloat16), own_slope))
            keep = head_mask(True, rows)
            d_q = jnp.where(keep, d_query[0], d_query[1]) * scale
            d_q = turned(d_q, at, count).astype(jnp.bfloat16)
            d_qkv[at:count, lanes] = d_q
            d_k = (d_key[0] + d_key[1]) * scale
            d_v = d_value[0] + d_value[1]
            if block == blocks - 1:
                d_keys[:, lanes] = d_k
                d_values[:, lanes] = d_v
            else:
                d_keys[:count, lanes] += d_k
                d_values[:count, lanes] += d_v
            k_out = turned(d_keys[at:count, lanes], at, count).astype(jnp.bfloat16)
            d_qkv[at:count, width + 128 * pair : width + 128 * pair + 128] = k_out
            v_out = d_values[at:count, lanes].astype(jnp.bfloat16)
            d_qkv[at:count, 2 * width + 128 * pair : 2 * width + 128 * pair + 128] = v_out
            if steps:
                steps.pop(0)()
    for part in range(3 * pairs):
        lanes = slice(128 * part, 128 * part + 128)
        bias_grad[:, lanes] = jnp.broadcast_to(
            jnp.sum(d_qkv[:, lanes].astype(jnp.float32), axis=0, keepdims=True), (8, 128))


def contract_first(left, right):
    return lax.dot_general(
        left, right, (((0,), (0,)), ((), ())), preferred_element_type=jnp.float32
    )


def attend_back_call(rows, qkv, d_attended, stats, seg_rows, seg_columns, cosine, minus, plus):
    group = qkv.shape[0]
    width = qkv.shape[1] // 3
    vm = pl.BlockSpec(memory_space=pltpu.VMEM)
    return pl.pallas_call(
        functools.partial(attend_back_kernel, rows),
        out_shape=[
            jax.ShapeDtypeStruct((group, 3 * width), jnp.bfloat16),
            jax.ShapeDtypeStruct((8, 3 * width), jnp.float32),
        ],
        in_specs=[vm] * 8,
        out_specs=[vm, vm],
        scratch_shapes=[pltpu.VMEM((group, width), jnp.float32), pltpu.VMEM((group, width), jnp.float32)],
        compiler_params=pltpu.CompilerParams(vmem_limit_bytes=48 * 2**20),
        name="attend_back",
        cost_estimate=pl.CostEstimate(flops=3 * 10**9, bytes_accessed=100 * 10**6, transcendentals=0),
    )(qkv, d_attended, stats, seg_rows, seg_columns, cosine, minus, plus)


def scatter_kernel(shards, cuts, parts, total, own, got, load, send, recv):
    z = lax.axis_index("shard")
    rows = parts.shape[1]
    step_rows = rows // cuts
    greet_line(z, shards)

    def piece(cut):
        return pl.ds(cut * step_rows, step_rows)

    def moved(way, block, cut):
        target = z + 1 if way == 0 else z - 1
        place = got.at[way, block, piece(cut)]
        return remote(place, place, send.at[way, block, cut], recv.at[way, block, cut], {"shard": target})

    loads = [pltpu.make_async_copy(parts.at[j], own.at[j], load.at[j]) for j in range(shards)]
    for copy in loads:
        copy.start()
    for copy in loads:
        copy.wait()
    for far in range(shards - 1):
        for cut in range(cuts):
            for way in (0, 1):
                block = shards - 1 - far if way == 0 else far
                sends = z < block if way == 0 else z > block
                first = z == 0 if way == 0 else z == shards - 1

                @pl.when(sends)
                def _():
                    @pl.when(first)
                    def _():
                        got[way, block, piece(cut)] = own[block, piece(cut)]

                    @pl.when(jnp.logical_not(first))
                    def _():
                        moved(way, block, cut).wait_recv()
                        got[way, block, piece(cut)] = (
                            got[way, block, piece(cut)].astype(jnp.float32)
                            + own[block, piece(cut)].astype(jnp.float32)
                        ).astype(got.dtype)
                    moved(way, block, cut).start()
    total[...] = own[z].astype(jnp.float32)
    for way in (0, 1):
        @pl.when(z >= 1 if way == 0 else z + 1 < shards)
        def _():
            for cut in range(cuts):
                moved(way, z, cut).wait_recv()
            total[...] += got[way, z].astype(jnp.float32)
    for far in range(shards - 1):
        for cut in range(cuts):
            for way in (0, 1):
                block = shards - 1 - far if way == 0 else far

                @pl.when(z < block if way == 0 else z > block)
                def _():
                    moved(way, block, cut).wait_send()


def scatter_call(shards, parts, number):
    _, rows, columns = parts.shape
    cuts = 3
    dma = pltpu.SemaphoreType.DMA
    return pl.pallas_call(
        functools.partial(scatter_kernel, shards, cuts),
        out_shape=jax.ShapeDtypeStruct((rows, columns), jnp.float32),
        in_specs=[pl.BlockSpec(memory_space=pl.ANY)],
        out_specs=pl.BlockSpec(memory_space=pltpu.VMEM),
        scratch_shapes=[
            pltpu.VMEM(parts.shape, parts.dtype),
            pltpu.VMEM((2,) + parts.shape, parts.dtype),
            dma((shards,)), dma((2, shards, cuts)), dma((2, shards, cuts)),
        ],
        compiler_params=pltpu.CompilerParams(
            collective_id=number, has_side_effects=True, vmem_limit_bytes=32 * 2**20
        ),
        name="scatter",
        cost_estimate=pl.CostEstimate(flops=0, bytes_accessed=200 * 10**6, transcendentals=0),
    )(parts)


def exchange_kernel(shards, first, second, first_out, second_out, send, recv, loc):
    z = lax.axis_index("shard")
    width = first.shape[1] // shards
    greet([((z != o), {"shard": o}) for o in range(shards)], shards - 1)
    arrays = ((first, first_out), (second, second_out))

    def move(k, o):
        source, target = arrays[k]
        return remote(source.at[:, pl.ds(o * width, width)], target.at[z], send.at[k, o], recv.at[k, z], {"shard": o})

    def arrival(k, o):
        source, target = arrays[k]
        return remote(target.at[o], target.at[o], send.at[k, o], recv.at[k, o], {"shard": o})

    for k in (0, 1):
        for o in range(shards):
            @pl.when(z != o)
            def _():
                move(k, o).start()

            @pl.when(z == o)
            def _():
                source, target = arrays[k]
                pltpu.make_async_copy(source.at[:, pl.ds(o * width, width)], target.at[o], loc.at[k]).start()
    for k in (0, 1):
        for o in range(shards):
            @pl.when(z != o)
            def _():
                arrival(k, o).wait_recv()
                move(k, o).wait_send()

            @pl.when(z == o)
            def _():
                source, target = arrays[k]
                pltpu.make_async_copy(source.at[:, pl.ds(o * width, width)], target.at[o], loc.at[k]).wait()


def exchange_call(shards, first, second):
    rows, columns = first.shape
    shape = jax.ShapeDtypeStruct((shards, rows, columns // shards), first.dtype)
    any_ = pl.BlockSpec(memory_space=pl.ANY)
    dma = pltpu.SemaphoreType.DMA
    return pl.pallas_call(
        functools.partial(exchange_kernel, shards),
        out_shape=[shape, shape],
        in_specs=[any_, any_],
        out_specs=[any_, any_],
        scratch_shapes=[dma((2, shards)), dma((2, shards)), dma((2,))],
        compiler_params=pltpu.CompilerParams(collective_id=5, has_side_effects=True),
        name="exchange",
        cost_estimate=pl.CostEstimate(flops=0, bytes_accessed=100 * 10**6, transcendentals=0),
    )(first, second)


class Cube:
    def __init__(self):
        r = lax.axis_index("replica")
        self.core, self.x, self.y = r % 2, (r // 2) % 2, r // 4
        self.place = 2 * self.y + self.x
        self.to_x = {"replica": r + 2 - 4 * self.x}
        self.to_y = {"replica": r + 4 - 8 * self.y}
        self.to_core = {"replica": r + 1 - 2 * self.core}

    def partners(self, shards):
        z = lax.axis_index("shard")
        return [((z != o), {"shard": o}) for o in range(shards)] + [
            (z >= 0, d) for d in (self.to_x, self.to_y, self.to_core)
        ]


def rows_of(ref, start, unit, count):
    return ref.at[pl.ds(pl.multiple_of(start, unit), count)]


def add_rows(target, source, count):
    step = 16

    @pl.loop(0, count // step)
    def _(i):
        block = pl.ds(aligned(i, step), step)
        target[block, :] = (
            target[block, :].astype(jnp.float32) + source[block, :].astype(jnp.float32)
        ).astype(target.dtype)


class Reducer:
    def __init__(self, cube, share, term, core, near, last, send, recv):
        self.cube, self.share = cube, share
        self.cut = 16 * ((share // 16 + 1) // 2)
        self.term, self.core, self.near, self.last = term, core, near, last
        self.send, self.recv = send, recv
        self.chunks = term.shape[0]

    def share_rows(self, chunk, place, half):
        first, count = (0, self.cut) if half == 0 else (self.cut, self.share - self.cut)
        start = self.cube.core * 4 * self.share + place * self.share + first
        return rows_of(self.term.at[chunk], start, 16, count)

    def own(self, chunk):
        start = (self.cube.core * 4 + self.cube.place) * self.share
        return rows_of(self.term.at[chunk], start, 16, self.share)

    def core_copy(self, chunk):
        source = rows_of(self.term.at[chunk], (1 - self.cube.core) * 4 * self.share, 16, 4 * self.share)
        return remote(source, self.core.at[chunk], self.send.at[chunk, 0], self.recv.at[chunk, 0], self.cube.to_core)

    def near_place(self, half, other):
        c = self.cube
        if half == 0:
            return 2 * other + (1 - c.x), 2 * other + c.x
        return 2 * (1 - c.y) + other, 2 * c.y + other

    def near_slot(self, chunk, half, other):
        count = self.cut if half == 0 else self.share - self.cut
        start = other * count + (2 * self.cut if half == 1 else 0)
        return self.near.at[chunk, pl.ds(start, count)]

    def near_copy(self, chunk, half, other):
        source = self.share_rows(chunk, self.near_place(half, other)[0], half)
        slot = 1 + 2 * half + other
        device = self.cube.to_x if half == 0 else self.cube.to_y
        return remote(source, self.near_slot(chunk, half, other), self.send.at[chunk, slot], self.recv.at[chunk, slot], device)

    def last_slot(self, chunk, half):
        first, count = (0, self.cut) if half == 0 else (self.cut, self.share - self.cut)
        return self.last.at[chunk, pl.ds(first, count)]

    def last_copy(self, chunk, half):
        c = self.cube
        place = 2 * (1 - c.y) + c.x if half == 0 else 2 * c.y + (1 - c.x)
        device = c.to_y if half == 0 else c.to_x
        source = self.share_rows(chunk, place, half)
        return remote(source, self.last_slot(chunk, half), self.send.at[chunk, 5 + half], self.recv.at[chunk, 5 + half], device)

    def start(self, chunk):
        self.core_copy(chunk).start()

    def after_core(self, chunk):
        self.core_copy(chunk).wait_recv()
        mine = rows_of(self.term.at[chunk], self.cube.core * 4 * self.share, 16, 4 * self.share)
        add_rows(mine, self.core.at[chunk], 4 * self.share)
        for half in (0, 1):
            for other in (0, 1):
                self.near_copy(chunk, half, other).start()

    def after_near(self, chunk):
        for half in (0, 1):
            count = self.cut if half == 0 else self.share - self.cut
            for other in (0, 1):
                self.near_copy(chunk, half, other).wait_recv()
                stays = self.share_rows(chunk, self.near_place(half, other)[1], half)
                add_rows(stays, self.near_slot(chunk, half, other), count)
            self.last_copy(chunk, half).start()

    def after_last(self, chunk):
        c = self.cube
        for half in (0, 1):
            count = self.cut if half == 0 else self.share - self.cut
            self.last_copy(chunk, half).wait_recv()
            add_rows(self.share_rows(chunk, c.place, half), self.last_slot(chunk, half), count)

    def finish(self, chunk):
        self.core_copy(chunk).wait_send()
        for half in (0, 1):
            for other in (0, 1):
                self.near_copy(chunk, half, other).wait_send()
            self.last_copy(chunk, half).wait_send()


class Owners:
    def __init__(self, cube, shards, share, parts, reducer, out, send, recv, loc):
        self.cube, self.shards, self.share, self.parts = cube, shards, share, parts
        self.source, self.out, self.send, self.recv, self.loc = reducer, out, send, recv, loc
        self.z = lax.axis_index("shard")

    def target(self, shard, part):
        width = self.out.shape[1] // (self.shards * self.parts)
        start = (self.cube.core * 4 + self.cube.place) * self.share
        return self.out.at[
            pl.ds(pl.multiple_of(start, 16), self.share), pl.ds(aligned(part * self.shards + shard, width), width)
        ]

    def piece(self, o, part):
        width = self.out.shape[1] // (self.shards * self.parts)
        return self.source(o).at[:, pl.ds(part * width, width)]

    def copy(self, o, part):
        return remote(self.piece(o, part), self.target(self.z, part), self.send.at[o, part], self.recv.at[self.z, part], {"shard": o})

    def arrival(self, o, part):
        place = self.target(o, part)
        return remote(place, place, self.send.at[o, part], self.recv.at[o, part], {"shard": o})

    def local(self, o, part):
        return pltpu.make_async_copy(self.piece(o, part), self.target(o, part), self.loc.at[part])

    def start(self, o):
        for part in range(self.parts):
            @pl.when(self.z != o)
            def _():
                self.copy(o, part).start()

            @pl.when(self.z == o)
            def _():
                self.local(o, part).start()

    def arrive(self):
        for o in range(self.shards):
            for part in range(self.parts):
                @pl.when(self.z != o)
                def _():
                    self.arrival(o, part).wait_recv()

                @pl.when(self.z == o)
                def _():
                    self.local(o, part).wait()

    def finish(self):
        for o in range(self.shards):
            for part in range(self.parts):
                @pl.when(self.z != o)
                def _():
                    self.copy(o, part).wait_send()


class Gatherer:
    def __init__(self, cube, share, out, send, recv):
        self.cube, self.share, self.out, self.send, self.recv = cube, share, out, send, recv
        self.cut = 16 * ((share // 16 + 1) // 2)

    def rows(self, place, half=None):
        first, count = {None: (0, self.share), 0: (0, self.cut), 1: (self.cut, self.share - self.cut)}[half]
        start = (self.cube.core * 4 + place) * self.share + first
        return rows_of(self.out, start, 16, count)

    def copy(self, kind):
        c = self.cube
        at_x, at_y = 2 * c.y + 1 - c.x, 2 * (1 - c.y) + c.x
        block, device = (
            (self.rows(c.place), c.to_x),
            (self.rows(c.place), c.to_y),
            (self.rows(at_x, 0), c.to_y),
            (self.rows(at_y, 1), c.to_x),
            (self.rows(c.place), c.to_core),
            (self.rows(at_x), c.to_core),
            (self.rows(at_y), c.to_core),
            (self.rows(3 - c.place), c.to_core),
        )[kind]
        return remote(block, block, self.send.at[kind], self.recv.at[kind], device)

    def start(self):
        for kind in (0, 1, 4):
            self.copy(kind).start()

    def pass_on(self):
        self.copy(0).wait_recv()
        self.copy(2).start()
        self.copy(1).wait_recv()
        self.copy(3).start()
        self.copy(5).start()
        self.copy(6).start()

    def pass_last(self):
        self.copy(2).wait_recv()
        self.copy(3).wait_recv()
        self.copy(7).start()

    def finish(self):
        for kind in (4, 5, 6, 7):
            self.copy(kind).wait_recv()
        for kind in range(8):
            self.copy(kind).wait_send()


class LineSum:
    def __init__(self, shards, cuts, own, got, send, recv):
        self.z = lax.axis_index("shard")
        self.shards, self.cuts, self.own, self.got, self.send, self.recv = shards, cuts, own, got, send, recv
        self.step = own.shape[1] // cuts

    def piece(self, cut):
        return pl.ds(cut * self.step, self.step)

    def copy(self, way, block, cut, source=None):
        target = self.z + 1 if way == 0 else self.z - 1
        place = self.got.at[way, block, self.piece(cut)]
        return remote(place if source is None else source, place, self.send.at[way, block, cut], self.recv.at[way, block, cut], {"shard": target})

    def order(self, t):
        last = self.z // (self.shards - 1)
        return self.shards - 1 - t + last * (2 * t - self.shards + 1)

    def ready(self, block):
        for way in (0, 1):
            @pl.when((self.z == (0 if way == 0 else self.shards - 1)) & (block != self.z))
            def _():
                for cut in range(self.cuts):
                    self.copy(way, block, cut, self.own.at[block, self.piece(cut)]).start()

    def step_on(self, far, cut):
        for way in (0, 1):
            block = self.shards - 1 - far if way == 0 else far
            sends = (self.z < block) & (self.z > 0) if way == 0 else (self.z > block) & (self.z < self.shards - 1)

            @pl.when(sends)
            def _():
                self.copy(way, block, cut).wait_recv()
                place = self.got.at[way, block, self.piece(cut)]
                add_rows(place, self.own.at[block, self.piece(cut)], self.step)
                self.copy(way, block, cut).start()

    def result(self, total):
        rows = self.own.shape[1]
        for way in (0, 1):
            @pl.when(self.z >= 1 if way == 0 else self.z + 1 < self.shards)
            def _():
                for cut in range(self.cuts):
                    self.copy(way, self.z, cut).wait_recv()

        @pl.loop(0, rows // 16)
        def _(i):
            block = pl.ds(aligned(i, 16), 16)
            total[block, :] = self.own[self.z, block, :].astype(jnp.float32)

            @pl.when(self.z >= 1)
            def _():
                total[block, :] += self.got[0, self.z, block, :].astype(jnp.float32)

            @pl.when(self.z + 1 < self.shards)
            def _():
                total[block, :] += self.got[1, self.z, block, :].astype(jnp.float32)

    def finish(self):
        for far in range(self.shards - 1):
            for cut in range(self.cuts):
                for way in (0, 1):
                    block = self.shards - 1 - far if way == 0 else far

                    @pl.when(self.z < block if way == 0 else self.z > block)
                    def _():
                        self.copy(way, block, cut).wait_send()


def line_scratch(shards, rows, columns, cuts):
    dma = pltpu.SemaphoreType.DMA
    return [
        pltpu.VMEM((shards, rows, columns), jnp.bfloat16),
        pltpu.VMEM((2, shards, rows, columns), jnp.bfloat16),
        dma((2, shards, cuts)), dma((2, shards, cuts)),
    ]


def reducer_scratch(chunks, share, columns):
    dma = pltpu.SemaphoreType.DMA
    return [pltpu.VMEM((chunks, n * share, columns), jnp.bfloat16) for n in (8, 4, 2, 1)] + [
        dma((chunks, 7)), dma((chunks, 7)),
    ]


def block_product(own, block, slopes, weight, tile=256):
    rows = own.shape[1]

    @pl.loop(0, own.shape[2] // tile)
    def _(t):
        columns = pl.ds(aligned(t, tile), tile)
        value = contract_last(slopes[pl.ds(aligned(block, rows), rows), :], weight[columns, :])
        own[block, :, columns] = value.astype(own.dtype)


def term_product(term, chunk, left, right, tile):
    columns = right.shape[1]

    @pl.loop(0, columns // tile)
    def _(t):
        place = pl.ds(aligned(t, tile), tile)
        term[chunk, :, place] = contract_first(left[...], right[:, place]).astype(term.dtype)


def hidden_back_kernel(shards, slopes, weight, hidden, cotangent, total, down_grad,
                       own, got, z_send, z_recv, term, core, near, last, r_send, r_recv,
                       share_send, share_recv, loc):
    cube = Cube()
    z = lax.axis_index("shard")
    greet(cube.partners(shards), shards + 2)
    line = LineSum(shards, 3, own, got, z_send, z_recv)
    share = hidden.shape[1] // 8
    chunks = term.shape[0]
    columns = term.shape[2]
    reducer = Reducer(cube, share, term, core, near, last, r_send, r_recv)
    gatherer = Gatherer(cube, share, down_grad, share_send, share_recv)
    for k in range(chunks):
        term[k] = contract_first(hidden[...], cotangent[:, k * columns : (k + 1) * columns]).astype(term.dtype)
        reducer.start(k)
    for t in range(shards):
        block = line.order(t)
        block_product(own, block, slopes, weight)
        line.ready(block)
        if t < chunks:
            reducer.after_core(t)
    for t in range(shards, chunks):
        reducer.after_core(t)
    steps = [functools.partial(reducer.after_near, k) for k in range(chunks)]
    steps += [functools.partial(reducer.after_last, k) for k in range(chunks)]
    moves = [functools.partial(line.step_on, far, cut) for far in range(shards - 1) for cut in range(3)]
    for i in range(max(len(steps), len(moves))):
        if i < len(moves):
            moves[i]()
        if i < len(steps):
            steps[i]()
    keep = []
    for k in range(chunks):
        target = down_grad.at[pl.ds(pl.multiple_of((cube.core * 4 + cube.place) * share, 16), share), pl.ds(k * columns, columns)]
        copy = pltpu.make_async_copy(reducer.own(k), target, loc.at[k])
        copy.start()
        keep.append(copy)
    for copy in keep:
        copy.wait()
    gatherer.start()
    line.result(total)
    gatherer.pass_on()
    gatherer.pass_last()
    line.finish()
    for k in range(chunks):
        reducer.finish(k)
    gatherer.finish()


def hidden_back_call(shards, slopes, weight, hidden, cotangent):
    group, inner = hidden.shape
    rows = group // shards
    share = inner // 8
    chunks = 4
    vm = pl.BlockSpec(memory_space=pltpu.VMEM)
    dma = pltpu.SemaphoreType.DMA
    return pl.pallas_call(
        functools.partial(hidden_back_kernel, shards),
        out_shape=[jax.ShapeDtypeStruct((rows, D), jnp.float32), jax.ShapeDtypeStruct((inner, D), jnp.bfloat16)],
        in_specs=[vm] * 4,
        out_specs=[vm, pl.BlockSpec(memory_space=pl.ANY)],
        scratch_shapes=line_scratch(shards, rows, D, 3) + reducer_scratch(chunks, share, D // chunks)
        + [dma((8,)), dma((8,)), dma((chunks,))],
        compiler_params=pltpu.CompilerParams(collective_id=6, has_side_effects=True, vmem_limit_bytes=56 * 2**20),
        name="hidden_back",
        cost_estimate=pl.CostEstimate(flops=10**10, bytes_accessed=200 * 10**6, transcendentals=0),
    )(slopes, weight, hidden, cotangent)


def heads_back_kernel(shards, rows, d_attended_own, d_middle_own, qkv, stats, seg_rows, seg_columns, cosine, minus, plus,
                      normed_two, slopes, d_qkv, bias_grad, d_middle_columns, share_out,
                      d_keys, d_values, d_attended, term, core, near, last, r_send, r_recv, e_send, e_recv, loc):
    cube = Cube()
    z = lax.axis_index("shard")
    greet(cube.partners(shards), shards + 2)
    width = D // shards
    arrays = ((d_attended_own, d_attended), (d_middle_own, d_middle_columns))

    def move(k, o):
        source, target = arrays[k]
        return remote(source.at[:, pl.ds(o * width, width)], target.at[pl.ds(aligned(z, rows), rows)],
                      e_send.at[k, o], e_recv.at[k, z], {"shard": o})

    def arrival(k, o):
        place = arrays[k][1].at[pl.ds(o * rows, rows)]
        return remote(place, place, e_send.at[k, o], e_recv.at[k, o], {"shard": o})

    def here(k, o):
        source, target = arrays[k]
        return pltpu.make_async_copy(source.at[:, pl.ds(o * width, width)], target.at[pl.ds(o * rows, rows)], loc.at[k])

    for k in (0, 1):
        for o in range(shards):
            @pl.when(z != o)
            def _():
                move(k, o).start()

            @pl.when(z == o)
            def _():
                here(k, o).start()
    share = D // shards // 8
    reducer = Reducer(cube, share, term, core, near, last, r_send, r_recv)
    for k in range(shards):
        term_product(term, k, normed_two.at[:, pl.ds(k * width, width)], slopes, 256)
        reducer.start(k)
    for k in (0, 1):
        for o in range(shards):
            @pl.when(z != o)
            def _():
                arrival(k, o).wait_recv()

            @pl.when(z == o)
            def _():
                here(k, o).wait()
    steps = [functools.partial(reducer.after_core, k) for k in range(shards)]
    steps += [functools.partial(reducer.after_near, k) for k in range(shards)]
    steps += [functools.partial(reducer.after_last, k) for k in range(shards)]
    attend_back_body(rows, qkv, d_attended, stats, seg_rows, seg_columns, cosine, minus, plus,
                     d_qkv, bias_grad, d_keys, d_values, steps)
    for step in steps:
        step()
    keep = [pltpu.make_async_copy(reducer.own(k), share_out.at[k], loc.at[2 + k]) for k in range(shards)]
    for copy in keep:
        copy.start()
    for k in (0, 1):
        for o in range(shards):
            @pl.when(z != o)
            def _():
                move(k, o).wait_send()
    for k in range(shards):
        reducer.finish(k)
    for copy in keep:
        copy.wait()


def heads_back_call(shards, rows, d_attended_own, d_middle_own, qkv, stats, seg_rows, seg_columns, cosine, minus, plus, normed_two, slopes):
    group = qkv.shape[0]
    width = D // shards
    share = width // 8
    columns = slopes.shape[1]
    vm = pl.BlockSpec(memory_space=pltpu.VMEM)
    any_ = pl.BlockSpec(memory_space=pl.ANY)
    dma = pltpu.SemaphoreType.DMA
    low = jnp.bfloat16
    return pl.pallas_call(
        functools.partial(heads_back_kernel, shards, rows),
        out_shape=[
            jax.ShapeDtypeStruct((group, 3 * width), low),
            jax.ShapeDtypeStruct((8, 3 * width), jnp.float32),
            jax.ShapeDtypeStruct((group, width), low),
            jax.ShapeDtypeStruct((shards, share, columns), low),
        ],
        in_specs=[any_, any_] + [vm] * 9,
        out_specs=[vm, vm, any_, any_],
        scratch_shapes=[
            pltpu.VMEM((group, width), jnp.float32), pltpu.VMEM((group, width), jnp.float32),
            pltpu.VMEM((group, width), low),
        ] + reducer_scratch(shards, share, columns) + [dma((2, shards)), dma((2, shards)), dma((2 + shards,))],
        compiler_params=pltpu.CompilerParams(collective_id=7, has_side_effects=True, vmem_limit_bytes=56 * 2**20),
        name="heads_back",
        cost_estimate=pl.CostEstimate(flops=10**10, bytes_accessed=200 * 10**6, transcendentals=0),
    )(d_attended_own, d_middle_own, qkv, stats, seg_rows, seg_columns, cosine, minus, plus, normed_two, slopes)


def input_back_kernel(shards, slopes, weight, normed, attended, d_middle, gate_up_share,
                      total, qkv_grad, out_grad, gate_up_grad,
                      own, got, z_send, z_recv,
                      term, core, near, last, r_send, r_recv,
                      o_term, o_core, o_near, o_last, o_send, o_recv,
                      t_send, t_recv, loc, g_send, g_recv):
    cube = Cube()
    greet(cube.partners(shards), shards + 2)
    width = D // shards
    share = width // 8
    line = LineSum(shards, 3, own, got, z_send, z_recv)
    reducer = Reducer(cube, share, term, core, near, last, r_send, r_recv)
    o_reducer = Reducer(cube, share, o_term, o_core, o_near, o_last, o_send, o_recv)
    sources = (lambda o: gate_up_share.at[o], o_reducer.own, reducer.own)
    outs = (gate_up_grad, out_grad, qkv_grad)
    owners = [Owners(cube, shards, share, p, s, out, t_send.at[i], t_recv.at[i], loc.at[i])
              for i, (p, s, out) in enumerate(zip((2, 1, 3), sources, outs))]
    gatherers = [Gatherer(cube, share, out, g_send.at[i], g_recv.at[i]) for i, out in enumerate(outs)]
    for o in range(shards):
        owners[0].start(o)
    for k in range(shards):
        term_product(term, k, normed.at[:, pl.ds(k * width, width)], slopes, 256)
        reducer.start(k)
    for t in range(shards):
        block = line.order(t)
        block_product(own, block, slopes, weight)
        line.ready(block)
        if t == 0:
            owners[0].arrive()
            gatherers[0].start()
        reducer.after_core(t)
    for k in range(shards):
        term_product(o_term, k, attended.at[:, pl.ds(k * width, width)], d_middle, width)
        o_reducer.start(k)
    steps = [gatherers[0].pass_on]
    steps += [functools.partial(reducer.after_near, k) for k in range(shards)]
    steps += [functools.partial(o_reducer.after_core, k) for k in range(shards)]
    steps += [gatherers[0].pass_last]
    for k in range(shards):
        steps += [functools.partial(reducer.after_last, k), functools.partial(owners[2].start, k)]
    steps += [functools.partial(o_reducer.after_near, k) for k in range(shards)]
    for k in range(shards):
        steps += [functools.partial(o_reducer.after_last, k), functools.partial(owners[1].start, k)]
    moves = [functools.partial(line.step_on, far, cut) for far in range(shards - 1) for cut in range(3)]
    for i in range(max(len(steps), len(moves))):
        if i < len(moves):
            moves[i]()
        if i < len(steps):
            steps[i]()
    line.result(total)
    for i in (2, 1):
        owners[i].arrive()
        gatherers[i].start()
    for i in (2, 1):
        gatherers[i].pass_on()
    for i in (2, 1):
        gatherers[i].pass_last()
    line.finish()
    for k in range(shards):
        reducer.finish(k)
        o_reducer.finish(k)
    for i in range(3):
        owners[i].finish()
        gatherers[i].finish()


def input_back_call(shards, slopes, weight, normed, attended, d_middle, gate_up_share):
    group = slopes.shape[0]
    rows = group // shards
    width = D // shards
    share = width // 8
    vm = pl.BlockSpec(memory_space=pltpu.VMEM)
    any_ = pl.BlockSpec(memory_space=pl.ANY)
    dma = pltpu.SemaphoreType.DMA
    low = jnp.bfloat16
    return pl.pallas_call(
        functools.partial(input_back_kernel, shards),
        out_shape=[
            jax.ShapeDtypeStruct((rows, D), jnp.float32),
            jax.ShapeDtypeStruct((width, 3 * D), low),
            jax.ShapeDtypeStruct((width, D), low),
            jax.ShapeDtypeStruct((width, shards * gate_up_share.shape[2]), low),
        ],
        in_specs=[vm] * 5 + [any_],
        out_specs=[vm, any_, any_, any_],
        scratch_shapes=line_scratch(shards, rows, D, 3)
        + reducer_scratch(shards, share, 3 * width) + reducer_scratch(shards, share, width)
        + [dma((3, shards, 3)), dma((3, shards, 3)), dma((3, 3)), dma((3, 8)), dma((3, 8))],
        compiler_params=pltpu.CompilerParams(collective_id=8, has_side_effects=True, vmem_limit_bytes=60 * 2**20),
        name="input_back",
        cost_estimate=pl.CostEstimate(flops=10**10, bytes_accessed=200 * 10**6, transcendentals=0),
    )(slopes, weight, normed, attended, d_middle, gate_up_share)


def swap_pieces(pieces):
    shards = lax.axis_size("shard")
    here = lax.axis_index("shard")
    out = pieces
    for k in range(1, shards):
        partner = jnp.bitwise_xor(here, k)
        piece = lax.dynamic_index_in_dim(pieces, partner, axis=0, keepdims=True)
        piece = lax.ppermute(piece, "shard", [(i, i ^ k) for i in range(shards)])
        out = lax.dynamic_update_slice_in_dim(out, piece, partner, axis=0)
    return out


def own_share(rows):
    own = rows.shape[0] // lax.axis_size("replica")
    return lax.dynamic_slice_in_dim(rows, lax.axis_index("replica") * own, own, axis=0)


def spread_rows(rows, columns):
    shards = lax.axis_size("shard")
    piece = own_share(rows)
    own = piece.shape[0]
    piece = piece.reshape(own, columns, shards, -1).transpose(2, 0, 1, 3).reshape(shards, own, -1)
    full = lax.all_gather(swap_pieces(piece), "replica", axis=0, tiled=False)
    return full.transpose(1, 0, 2, 3).reshape(rows.shape[0] * shards, -1)


def gather_rows(rows):
    shards = lax.axis_size("shard")
    piece = own_share(rows)
    moved = swap_pieces(jnp.broadcast_to(piece[None], (shards,) + piece.shape))
    full = lax.all_gather(moved, "replica", axis=0, tiled=False)
    return full.transpose(1, 0, 2, 3).reshape(rows.shape[0] * shards, -1)


def own_rows(features):
    copies = lax.axis_size("replica")
    shards = lax.axis_size("shard")
    count = features.shape[0]
    return (
        features.reshape(count, shards, copies, -1).transpose(0, 2, 1, 3).reshape(count, -1)
    )


def sum_columns(features, slopes, columns):
    shards = lax.axis_size("shard")
    term = contract_first(own_rows(features), slopes).astype(jnp.bfloat16)
    part = lax.psum_scatter(term, "replica", scatter_dimension=0, tiled=True)
    own = part.shape[0] // shards
    moved = swap_pieces(part.reshape(shards, own, -1))
    moved = moved.reshape(shards, own, columns, -1).transpose(1, 2, 0, 3).reshape(own, -1)
    return lax.all_gather(moved, "replica", axis=0, tiled=True)


def swiglu(gate_up):
    half = gate_up.shape[1] // 2
    return jax.nn.silu(gate_up[:, :half]) * gate_up[:, half:]


def norm_stats(values):
    mean = jnp.mean(values, axis=-1, keepdims=True)
    centered = values - mean
    inverse = lax.rsqrt(jnp.mean(centered * centered, axis=-1, keepdims=True) + norm_eps)
    return centered * inverse, inverse


def norm_back(slope, unit, inverse, gain):
    scaled = slope * gain
    return inverse * (
        scaled
        - jnp.mean(scaled, axis=-1, keepdims=True)
        - unit * jnp.mean(scaled * unit, axis=-1, keepdims=True)
    )


def start_plain(tokens, vectors, qkv_weight, cosine, minus, plus):
    shards = lax.axis_size("shard")
    here = lax.axis_index("shard")
    all_tokens = lax.all_gather(tokens, "shard", axis=0, tiled=False)
    all_vectors = lax.all_gather(vectors, "shard", axis=0, tiled=False)
    weight = spread_rows(qkv_weight, 3)
    width = D // shards
    gain, shift = (all_vectors[:, 3 + i].reshape(D) for i in (0, 1))
    unit, _ = norm_stats(all_tokens.reshape(-1, D).astype(jnp.float32))
    normed = (unit * gain + shift).astype(jnp.bfloat16)
    bias = all_vectors[:, :3].reshape(3, shards, width)
    bias = lax.dynamic_index_in_dim(bias, here, axis=1, keepdims=False).reshape(3 * width)
    value = jnp.dot(normed, weight, preferred_element_type=jnp.float32) + bias
    turned = value[:, : 2 * width]
    wide = [jnp.tile(t, (1, 2 * width // 128)) for t in (cosine, minus, plus)]
    turned = (
        turned * wide[0] + jnp.roll(turned, -8, 1) * wide[1] + jnp.roll(turned, 8, 1) * wide[2]
    )
    qkv = jnp.concatenate([turned, value[:, 2 * width :]], axis=1).astype(jnp.bfloat16)
    return all_tokens, all_vectors, normed, qkv, weight


def on_device(
    tokens,
    cotangent,
    qkv_weight,
    qkv_bias,
    out_weight,
    gate_up_weight,
    down_weight,
    norm1_gain,
    norm1_shift,
    norm2_gain,
    norm2_shift,
    seq_lengths,
):
    shards = lax.axis_size("shard")
    copies = lax.axis_size("replica")
    here = lax.axis_index("shard")
    row_count = tokens.shape[0]
    group_rows = row_count * shards
    width = D // shards
    f32 = jnp.float32
    low = jnp.bfloat16

    index = jnp.arange(group_rows, dtype=jnp.int32)
    segment, position = group_layout(seq_lengths[0], index)
    seg_rows = jnp.broadcast_to(segment[:, None], (group_rows, 128))
    seg_columns = jnp.broadcast_to(segment[None, :], (8, group_rows))
    cosine, sine_value = rope_tables(position)
    half_rot = ROT_DIM // 2
    rest = HEAD_DIM - ROT_DIM
    none = jnp.zeros((group_rows, half_rot), f32)
    empty = jnp.zeros((group_rows, rest), f32)
    cosine = jnp.tile(jnp.concatenate([cosine, cosine, empty + 1.0], axis=1), (1, 2))
    minus = jnp.tile(jnp.concatenate([-sine_value, none, empty], axis=1), (1, 2))
    plus = jnp.tile(jnp.concatenate([none, sine_value, empty], axis=1), (1, 2))

    vectors = jnp.concatenate(
        [qkv_bias, norm1_gain, norm1_shift, norm2_gain, norm2_shift, jnp.zeros((width,), low)]
    )
    vectors = vectors.astype(f32).reshape(8, width)
    weight_out = gather_rows(out_weight)
    weight_gate_up = spread_rows(gate_up_weight, 2)
    begin = functools.partial(start_call, shards) if copies == 8 else start_plain
    all_tokens, all_vectors, normed_low, qkv, weight_qkv = begin(
        tokens, vectors, qkv_weight, cosine, minus, plus
    )
    gain_one, shift_one, gain_two, shift_two = (
        all_vectors[:, 3 + i].reshape(D) for i in range(4)
    )
    cotangent_later, qkv = lax.optimization_barrier((cotangent, qkv))
    group_cotangent = lax.all_gather(cotangent_later, "shard", axis=0, tiled=True)

    def local(array):
        return lax.dynamic_slice_in_dim(array, here * row_count, row_count, axis=0)

    attended, stats = attend_call(shards, row_count, qkv, seg_rows, seg_columns)
    inputs = all_tokens.reshape(group_rows, D).astype(f32)
    middle = inputs + jnp.dot(attended, weight_out, preferred_element_type=f32)
    unit_two, inverse_two = norm_stats(middle)
    normed_two_low = (unit_two * gain_two + shift_two).astype(low)
    gate_up = jnp.dot(normed_two_low, weight_gate_up, preferred_element_type=f32)
    hidden, swiglu_pull = jax.vjp(swiglu, gate_up)
    hidden_low = hidden.astype(low)
    d_hidden = contract_last(group_cotangent, down_weight)
    d_gate_up_low = swiglu_pull(d_hidden)[0].astype(low)
    down_part = jnp.dot(hidden_low, down_weight, preferred_element_type=f32).astype(low)
    unit_two_own = local(unit_two)
    inverse_two_own = local(inverse_two)
    middle_own = local(middle)

    if copies == 8:
        d_normed_two, down_grad = hidden_back_call(
            shards, d_gate_up_low, weight_gate_up, hidden_low, group_cotangent
        )
    else:
        d_normed_two_part = contract_last(d_gate_up_low, weight_gate_up).astype(low)
        d_normed_two = scatter_call(shards, d_normed_two_part.reshape(shards, row_count, D), 3)
        down_grad = lax.psum(contract_first(hidden_low, group_cotangent).astype(low), "replica")
    d_middle = cotangent.astype(f32) + norm_back(
        d_normed_two, unit_two_own, inverse_two_own, gain_two
    )
    d_gain_two = jnp.sum(d_normed_two * unit_two_own, axis=0)
    d_shift_two = jnp.sum(d_normed_two, axis=0)
    d_middle_low = d_middle.astype(low)
    d_attended_own = contract_last(d_middle_low, weight_out).astype(low)
    if copies == 8:
        d_projected_low, bias_part, d_middle_columns, gate_up_share = heads_back_call(
            shards, row_count, d_attended_own, d_middle_low, qkv, stats, seg_rows, seg_columns,
            cosine, minus, plus, normed_two_low, d_gate_up_low,
        )
        down_part, d_projected_low = lax.optimization_barrier((down_part, d_projected_low))
    else:
        d_attended, d_middle_columns = exchange_call(shards, d_attended_own, d_middle_low)
        d_projected_low, bias_part = attend_back_call(
            row_count, qkv, d_attended.reshape(group_rows, width), stats, seg_rows, seg_columns,
            cosine, minus, plus,
        )
    down_own = lax.psum_scatter(down_part, "shard", scatter_dimension=0, tiled=True)
    mixed = (middle_own + down_own.astype(f32)).astype(low)
    if copies == 8:
        d_normed, qkv_grad, out_grad, gate_up_grad = input_back_call(
            shards, d_projected_low, weight_qkv, normed_low, attended, d_middle_columns, gate_up_share
        )
    else:
        d_normed_part = contract_last(d_projected_low, weight_qkv).astype(low)
        d_normed = scatter_call(shards, d_normed_part.reshape(shards, row_count, D), 4)
        gate_up_grad = sum_columns(normed_two_low, d_gate_up_low, 2)
        out_grad = sum_columns(attended, d_middle_columns.reshape(group_rows, width), 1)
        qkv_grad = sum_columns(normed_low, d_projected_low, 3)
    unit_one, inverse_one = norm_stats(tokens.astype(f32))
    input_grad = d_middle + norm_back(d_normed, unit_one, inverse_one, gain_one)
    d_gain_one = jnp.sum(d_normed * unit_one, axis=0)
    d_shift_one = jnp.sum(d_normed, axis=0)

    bias_part = bias_part[0].reshape(3, 1, width)
    bias_wide = lax.dynamic_update_slice(
        jnp.zeros((3, shards, width), f32), bias_part, (0, here, 0)
    ).reshape(shards, 3 * width)
    small = jnp.concatenate(
        [bias_wide]
        + [v.reshape(shards, width) for v in (d_gain_one, d_shift_one, d_gain_two, d_shift_two)],
        axis=1,
    )
    small = lax.psum(small, ("replica", "shard"))
    small = lax.dynamic_index_in_dim(small, here, axis=0, keepdims=False)
    bias_rows = 3 * width
    return (
        mixed,
        input_grad,
        qkv_grad.astype(f32),
        small[:bias_rows],
        out_grad.astype(f32),
        gate_up_grad.astype(f32),
        down_grad.astype(f32),
    ) + tuple(small[bias_rows + i * width : bias_rows + (i + 1) * width] for i in range(4))


def solution(mesh):
    placed = (
        P(("replica", "shard"), None),
        P(("replica", "shard"), None),
        P("shard", None),
        P("shard"),
        P("shard", None),
        P("shard", None),
        P("shard", None),
        P("shard"),
        P("shard"),
        P("shard"),
        P("shard"),
        P("replica", None),
    )
    return jax.shard_map(
        on_device,
        mesh=mesh,
        in_specs=placed,
        out_specs=(
            P(("replica", "shard"), None),
            P(("replica", "shard"), None),
            P("shard", None),
            P("shard"),
            P("shard", None),
            P("shard", None),
            P("shard", None),
            P("shard"),
            P("shard"),
            P("shard"),
            P("shard"),
        ),
        check_vma=False,
    )
```

```python
import functools

import jax
import jax.numpy as jnp
from jax import lax
from jax.experimental import pallas as pl
from jax.experimental.pallas import tpu as pltpu
from jax.sharding import PartitionSpec as P

D = 2048
FF = 5632
HEADS = 32
HEAD_DIM = 64
ROT_DIM = 16
MESH = pl.DeviceIdType.MESH


norm_eps = 1e-05
masked_score = -1000000000.0


def group_layout(lengths, token_index):
    seq_ends = jnp.cumsum(lengths)
    passed = (token_index[:, None] >= seq_ends[None, :]).astype(jnp.int32)
    segment = jnp.sum(passed, axis=1)
    position = token_index - jnp.sum(passed * lengths[None, :], axis=1)
    return (segment, position)


def rope_tables(position):
    half_rot = ROT_DIM // 2
    frequency = jnp.exp(
        -jnp.log(10000.0) * (2.0 * jnp.arange(half_rot, dtype=jnp.float32) / ROT_DIM)
    )
    angles = position.astype(jnp.float32)[:, None] * frequency[None, :]
    return (jnp.cos(angles), jnp.sin(angles))


def contract_last(left, right):
    return lax.dot_general(
        left, right, (((1,), (1,)), ((), ())), preferred_element_type=jnp.float32
    )


def aligned(value, unit):
    return pl.multiple_of(value * unit, unit)


def greet(partners, count):
    barrier = pltpu.get_barrier_semaphore()
    for there, device in partners:
        @pl.when(there)
        def _():
            pl.semaphore_signal(barrier, inc=1, device_id=device, device_id_type=MESH)
    pl.semaphore_wait(barrier, count)


def greet_line(z, shards):
    count = (z + shards - 1) // shards + (2 * shards - 2 - z) // shards
    greet([(z >= 1, {"shard": z - 1}), (z + 1 < shards, {"shard": z + 1})], count)


def remote(source, target, send, recv, device):
    return pltpu.make_async_remote_copy(
        src_ref=source, dst_ref=target, send_sem=send, recv_sem=recv,
        device_id=device, device_id_type=MESH,
    )


class Cube:
    def __init__(self):
        r = lax.axis_index("replica")
        self.core, self.x, self.y = r % 2, (r // 2) % 2, r // 4
        self.place = 2 * self.y + self.x
        self.to_x = {"replica": r + 2 - 4 * self.x}
        self.to_y = {"replica": r + 4 - 8 * self.y}
        self.to_core = {"replica": r + 1 - 2 * self.core}

    def partners(self, shards):
        z = lax.axis_index("shard")
        return [((z != o), {"shard": o}) for o in range(shards)] + [
            (z >= 0, d) for d in (self.to_x, self.to_y, self.to_core)
        ]


def rows_of(ref, start, unit, count):
    return ref.at[pl.ds(pl.multiple_of(start, unit), count)]


class Spreader:
    def __init__(self, cube, shards, share, parts, source, out, sems):
        self.cube, self.shards, self.share, self.parts = cube, shards, share, parts
        self.source, self.out = source, out
        self.z_send, self.z_recv, self.send, self.recv, self.loc = sems
        self.cut = 16 * ((share // 16 + 1) // 2)
        self.z = lax.axis_index("shard")
        r = lax.axis_index("replica")
        self.who = (r, r + 2 - 4 * cube.x, r + 4 - 8 * cube.y, 4 * (1 - cube.y) + 2 * (1 - cube.x) + cube.core)

    def rows(self, o, kind, half=None):
        first, count = {None: (0, self.share), 0: (0, self.cut), 1: (self.cut, self.share - self.cut)}[half]
        return rows_of(self.out, (o * 8 + self.who[kind]) * self.share + first, 16, count)

    def target(self, o, part):
        width = self.out.shape[1] // self.parts
        return self.rows(o, 0).at[:, pl.ds(part * width, width)]

    def z_copy(self, o, part):
        return remote(self.source(o, part), self.target(self.z, part), self.z_send.at[o, part], self.z_recv.at[self.z, part], {"shard": o})

    def z_arrival(self, o, part):
        place = self.target(o, part)
        return remote(place, place, self.z_send.at[o, part], self.z_recv.at[o, part], {"shard": o})

    def local(self, o, part):
        return pltpu.make_async_copy(self.source(o, part), self.target(o, part), self.loc.at[part])

    def start_own(self):
        for part in range(self.parts):
            self.local(self.z, part).start()

    def start(self):
        for o in range(self.shards):
            for part in range(self.parts):
                @pl.when(self.z != o)
                def _():
                    self.z_copy(o, part).start()

    def sent(self):
        for o in range(self.shards):
            for part in range(self.parts):
                @pl.when(self.z != o)
                def _():
                    self.z_copy(o, part).wait_send()

    def copy(self, kind, o):
        c = self.cube
        block, device = (
            (self.rows(o, 0), c.to_x),
            (self.rows(o, 0), c.to_y),
            (self.rows(o, 1, 0), c.to_y),
            (self.rows(o, 2, 1), c.to_x),
            (self.rows(o, 0), c.to_core),
            (self.rows(o, 1), c.to_core),
            (self.rows(o, 2), c.to_core),
            (self.rows(o, 3), c.to_core),
        )[kind]
        return remote(block, block, self.send.at[kind, o], self.recv.at[kind, o], device)

    def arrive(self, distance):
        for o in range(self.shards):
            @pl.when((self.z - o == distance) | (o - self.z == distance))
            def _():
                for part in range(self.parts):
                    if distance == 0:
                        self.local(o, part).wait()
                    else:
                        self.z_arrival(o, part).wait_recv()
                for kind in (0, 1, 4):
                    self.copy(kind, o).start()

    def pass_on(self, o):
        self.copy(0, o).wait_recv()
        self.copy(2, o).start()
        self.copy(5, o).start()
        self.copy(1, o).wait_recv()
        self.copy(3, o).start()
        self.copy(6, o).start()

    def pass_last(self, o):
        self.copy(2, o).wait_recv()
        self.copy(3, o).wait_recv()
        self.copy(7, o).start()

    def landed(self):
        for o in range(self.shards):
            for kind in (4, 5, 6, 7):
                self.copy(kind, o).wait_recv()

    def finish(self):
        for o in range(self.shards):
            for kind in range(8):
                self.copy(kind, o).wait_send()


def spread_sems(shards, parts):
    dma = pltpu.SemaphoreType.DMA
    return [dma((shards, parts)), dma((shards, parts)), dma((8, shards)), dma((8, shards)), dma((parts,))]


class Line:
    def __init__(self, shards, pieces, own, buf, send, recv):
        self.z = lax.axis_index("shard")
        self.shards, self.pieces, self.own, self.buf, self.send, self.recv = shards, pieces, own, buf, send, recv
        self.rows = buf.shape[1] // pieces

    def copy(self, way, step, piece):
        target = self.z + 1 if way == 0 else self.z - 1
        owner = self.z - step if way == 0 else self.z + step
        block = pl.ds(piece * self.rows, self.rows)
        place = self.buf.at[owner, block]
        source = self.own.at[block] if step == 0 and self.own is not None else place
        return remote(source, place, self.send.at[way, step, piece], self.recv.at[way, step, piece], {"shard": target})

    def sends(self, way, step):
        if way == 0:
            return (self.z + 1 < self.shards) & (self.z - step >= 0)
        return (self.z >= 1) & (self.z + step < self.shards)

    def gets(self, way, step):
        return (self.z - step >= 1) if way == 0 else (self.z + step + 1 < self.shards)

    def start(self, piece):
        for way in (0, 1):
            @pl.when(self.sends(way, 0))
            def _():
                self.copy(way, 0, piece).start()

    def relay(self, step, piece):
        for way in (0, 1):
            @pl.when(self.gets(way, step))
            def _():
                self.copy(way, step, piece).wait_recv()
            if step + 1 < self.shards - 1:
                @pl.when(self.sends(way, step + 1))
                def _():
                    self.copy(way, step + 1, piece).start()

    def finish(self):
        for step in range(self.shards - 1):
            for piece in range(self.pieces):
                for way in (0, 1):
                    @pl.when(self.sends(way, step))
                    def _():
                        self.copy(way, step, piece).wait_send()


def line_sems(shards, pieces):
    dma = pltpu.SemaphoreType.DMA
    return [dma((2, shards - 1, pieces)), dma((2, shards - 1, pieces))]


def layer_norm_rows(values, gain, shift):
    centered = values - jnp.mean(values, axis=-1, keepdims=True)
    spread = jnp.mean(centered * centered, axis=-1, keepdims=True)
    return (centered * lax.rsqrt(spread + norm_eps) * gain + shift).astype(jnp.bfloat16)


def bias_piece(v_buf, z, t, tile, shards, per_part):
    flat = (t // per_part) * shards + z
    return v_buf[flat // 3, pl.ds(flat % 3, 1), pl.ds(aligned(t % per_part, tile), tile)]


def start_kernel(shards, tokens, vectors, weight, out_weight, cosine, minus, plus,
                 all_tokens, all_vectors, normed, qkv, kept_weight, all_out,
                 x_buf, v_buf, w_buf, n_buf, q_buf, *sems):
    cube = Cube()
    z = lax.axis_index("shard")
    r = lax.axis_index("replica")
    rows = tokens.shape[0]
    share = weight.shape[0] // 8
    width = w_buf.shape[1] // 3
    x_send, x_recv, v_send, v_recv, loc = sems[:5]
    line = Line(shards, 1, tokens, x_buf, x_send, x_recv)
    mine = pl.ds(aligned(r, share), share)
    spread = Spreader(
        cube, shards, share, 3,
        lambda o, part: weight.at[mine, pl.ds(aligned(part * shards + o, width), width)], w_buf, sems[5:10],
    )
    spread_out = Spreader(cube, shards, share, 1, lambda o, part: out_weight.at[mine], all_out, sems[10:15])
    greet(cube.partners(shards), shards + 2)

    def v_copy(o):
        return remote(vectors, v_buf.at[z], v_send.at[o], v_recv.at[z], {"shard": o})

    def v_arrival(o):
        return remote(vectors, v_buf.at[o], v_send.at[o], v_recv.at[o], {"shard": o})

    own_x = pltpu.make_async_copy(tokens, x_buf.at[z], loc.at[0, 0])
    own_v = pltpu.make_async_copy(vectors, v_buf.at[z], loc.at[1, 0])
    own_x.start()
    own_v.start()
    for o in range(shards):
        @pl.when(z != o)
        def _():
            v_copy(o).start()
    spread.start_own()
    spread_out.start_own()
    spread.start()
    spread.arrive(0)
    spread_out.arrive(0)
    line.start(0)
    spread_out.start()
    for distance in range(1, shards):
        spread.arrive(distance)
    own_x.wait()
    own_v.wait()
    for o in range(shards):
        @pl.when(z != o)
        def _():
            v_arrival(o).wait_recv()
    keep_v = pltpu.make_async_copy(v_buf, all_vectors, loc.at[2, 0])
    keep_v.start()
    gain = jnp.concatenate([v_buf[o, 3:4, :] for o in range(shards)], axis=1)
    shift = jnp.concatenate([v_buf[o, 4:5, :] for o in range(shards)], axis=1)

    def put(source, target, o, i):
        block = pl.ds(aligned(o, rows), rows)
        copy = pltpu.make_async_copy(source.at[block], target.at[block], loc.at[4 + i, o])
        copy.start()

    def normalize(o):
        @pl.loop(0, rows // 32)
        def _(i):
            values = x_buf[o, pl.ds(aligned(i, 32), 32), :].astype(jnp.float32)
            n_buf[pl.ds(pl.multiple_of(o * rows + i * 32, 32), 32), :] = layer_norm_rows(values, gain, shift)
        put(n_buf, normed, o, 0)
        pltpu.make_async_copy(x_buf.at[o], all_tokens.at[o], loc.at[6, o]).start()

    tile = 256
    per_part = width // tile

    def project(o):
        block = pl.ds(aligned(o, rows), rows)

        @pl.loop(0, 3 * per_part)
        def _(t):
            columns = pl.ds(aligned(t, tile), tile)
            value = jnp.dot(n_buf[block, :], w_buf[:, columns], preferred_element_type=jnp.float32)
            value = value + bias_piece(v_buf, z, t, tile, shards, per_part)

            @pl.when(t < 2 * per_part)
            def _():
                wide, wide_minus, wide_plus = (
                    jnp.concatenate([table[block, :]] * (tile // 128), axis=1) for table in (cosine, minus, plus)
                )
                turned = value * wide + pltpu.roll(value, tile - 8, 1) * wide_minus + pltpu.roll(value, 8, 1) * wide_plus
                q_buf[block, columns] = turned.astype(jnp.bfloat16)

            @pl.when(t >= 2 * per_part)
            def _():
                q_buf[block, columns] = value.astype(jnp.bfloat16)
        put(q_buf, qkv, o, 1)

    normalize(z)
    line.relay(0, 0)
    for o in range(shards):
        spread.pass_on(o)
    for o in range(shards):
        spread.pass_last(o)
    spread.landed()
    keep_w = pltpu.make_async_copy(w_buf, kept_weight, loc.at[3, 0])
    keep_w.start()
    project(z)
    for distance in range(1, shards):
        spread_out.arrive(distance)
    for step in range(shards - 1):
        if step > 0:
            line.relay(step, 0)
        for way in (0, 1):
            owner = z - step - 1 if way == 0 else z + step + 1

            @pl.when(line.gets(way, step))
            def _():
                normalize(owner)
                project(owner)
        if step == min(1, shards - 2):
            for o in range(shards):
                spread_out.pass_on(o)
    for o in range(shards):
        spread_out.pass_last(o)
    spread_out.landed()
    line.finish()
    spread.sent()
    spread.finish()
    spread_out.sent()
    spread_out.finish()
    for o in range(shards):
        block = pl.ds(o * rows, rows)

        @pl.when(z != o)
        def _():
            v_copy(o).wait_send()
        pltpu.make_async_copy(n_buf.at[block], normed.at[block], loc.at[4, o]).wait()
        pltpu.make_async_copy(q_buf.at[block], qkv.at[block], loc.at[5, o]).wait()
        pltpu.make_async_copy(x_buf.at[o], all_tokens.at[o], loc.at[6, o]).wait()
    keep_v.wait()
    keep_w.wait()


def start_call(shards, tokens, vectors, weight, out_weight, cosine, minus, plus):
    rows = tokens.shape[0]
    group = rows * shards
    depth = weight.shape[0]
    width = weight.shape[1] // shards
    any_ = pl.BlockSpec(memory_space=pl.ANY)
    vm = pl.BlockSpec(memory_space=pltpu.VMEM)
    low = jnp.bfloat16
    dma = pltpu.SemaphoreType.DMA
    return pl.pallas_call(
        functools.partial(start_kernel, shards),
        out_shape=[
            jax.ShapeDtypeStruct((shards, rows, D), low),
            jax.ShapeDtypeStruct((shards,) + vectors.shape, vectors.dtype),
            jax.ShapeDtypeStruct((group, D), low),
            jax.ShapeDtypeStruct((group, width), low),
            jax.ShapeDtypeStruct((depth * shards, width), low),
            jax.ShapeDtypeStruct((depth * shards, D), low),
        ],
        in_specs=[any_] * 4 + [vm] * 3,
        out_specs=[any_] * 6,
        scratch_shapes=[
            pltpu.VMEM((shards, rows, D), low),
            pltpu.VMEM((shards,) + vectors.shape, vectors.dtype),
            pltpu.VMEM((depth * shards, width), low),
            pltpu.VMEM((group, D), low),
            pltpu.VMEM((group, width), low),
        ] + line_sems(shards, 1) + [dma((shards,)), dma((shards,)), dma((7, shards))]
        + spread_sems(shards, 3) + spread_sems(shards, 1),
        compiler_params=pltpu.CompilerParams(
            collective_id=1, has_side_effects=True, vmem_limit_bytes=48 * 2**20
        ),
        name="start",
        cost_estimate=pl.CostEstimate(flops=2 * group * D * width, bytes_accessed=150 * 10**6, transcendentals=0),
    )(tokens, vectors, weight, out_weight, cosine, minus, plus)


def attend_spread_kernel(shards, rows, qkv, seg_rows, seg_columns, gate_up, attended, stats, all_gate_up, a_buf, *sems):
    cube = Cube()
    z = lax.axis_index("shard")
    r = lax.axis_index("replica")
    width = qkv.shape[1] // 3
    blocks = qkv.shape[0] // rows
    share = gate_up.shape[0] // 8
    half = all_gate_up.shape[1] // 2
    mine = pl.ds(aligned(r, share), share)
    spread = Spreader(
        cube, shards, share, 2,
        lambda o, part: gate_up.at[mine, pl.ds(aligned((part * shards + o) * (half // 128), 128), half)], all_gate_up, sems[3:8],
    )
    line = Line(shards, blocks, None, a_buf, sems[0], sems[1])
    loc = sems[2]
    greet(cube.partners(shards), shards + 2)
    spread.start_own()
    spread.start()
    spread.arrive(0)

    def done(block):
        line.start(block)
        if 0 < block < shards:
            spread.arrive(block)

    attend_body(rows, qkv, seg_rows, seg_columns, a_buf, stats, done)
    moves = [functools.partial(line.relay, step, block) for step in range(shards - 1) for block in range(blocks)]
    steps = [functools.partial(spread.pass_on, o) for o in range(shards)]
    steps += [functools.partial(spread.pass_last, o) for o in range(shards)]
    for i in range(max(len(moves), len(steps))):
        if i < len(moves):
            moves[i]()
        if i < len(steps):
            steps[i]()
    keep = [pltpu.make_async_copy(a_buf.at[o], attended.at[:, pl.ds(o * width, width)], loc.at[o]) for o in range(shards)]
    for copy in keep:
        copy.start()
    spread.landed()
    line.finish()
    spread.sent()
    spread.finish()
    for copy in keep:
        copy.wait()


def attend_spread_call(shards, rows, qkv, seg_rows, seg_columns, gate_up):
    group = qkv.shape[0]
    width = qkv.shape[1] // 3
    blocks = group // rows
    vm = pl.BlockSpec(memory_space=pltpu.VMEM)
    any_ = pl.BlockSpec(memory_space=pl.ANY)
    dma = pltpu.SemaphoreType.DMA
    low = jnp.bfloat16
    return pl.pallas_call(
        functools.partial(attend_spread_kernel, shards, rows),
        out_shape=[
            jax.ShapeDtypeStruct((group, shards * width), low),
            jax.ShapeDtypeStruct((group, 128), jnp.float32),
            jax.ShapeDtypeStruct((gate_up.shape[0] * shards, gate_up.shape[1] // shards), low),
        ],
        in_specs=[vm, vm, vm, any_],
        out_specs=[any_, vm, any_],
        scratch_shapes=[pltpu.VMEM((shards, group, width), low)] + line_sems(shards, blocks) + [dma((shards,))]
        + spread_sems(shards, 2),
        compiler_params=pltpu.CompilerParams(
            collective_id=2, has_side_effects=True, vmem_limit_bytes=48 * 2**20
        ),
        name="attend_spread",
        cost_estimate=pl.CostEstimate(flops=10**9, bytes_accessed=150 * 10**6, transcendentals=0),
    )(qkv, seg_rows, seg_columns, gate_up)


def hidden_kernel(shards, attended, tokens, out_weight, gate_up_weight, down_weight, cotangent, gain, shift,
                  middle_own, normed_two, hidden, slopes, all_cotangent, down_part,
                  a_buf, x_buf, o_buf, g_buf, d_buf, c_buf, mid, n_buf, gu, h_buf, s_buf, c_send, c_recv, loc):
    z = lax.axis_index("shard")
    greet_line(z, shards)
    rows = cotangent.shape[0]
    group = rows * shards
    inner = h_buf.shape[1]
    line = Line(shards, 1, cotangent, c_buf, c_send, c_recv)
    line.start(0)
    load = [pltpu.make_async_copy(source, target, loc.at[i]) for i, (source, target) in enumerate((
        (attended, a_buf), (out_weight, o_buf), (tokens, x_buf), (gate_up_weight, g_buf), (down_weight, d_buf),
        (cotangent, c_buf.at[z])))]
    for copy in load:
        copy.start()
    for copy in load[:3]:
        copy.wait()
    tile = 256
    span = 2 * rows
    for part in range(group // span):
        at = part * span

        @pl.loop(0, D // tile)
        def _(t):
            columns = pl.ds(aligned(t, tile), tile)
            value = jnp.dot(a_buf[at : at + span, :], o_buf[:, columns], preferred_element_type=jnp.float32)
            for k in range(2):
                mid[k * rows : (k + 1) * rows, columns] = (
                    value[k * rows : (k + 1) * rows] + x_buf[2 * part + k, :, columns].astype(jnp.float32)
                )

        @pl.loop(0, span // 32)
        def _(i):
            block = pl.ds(aligned(i, 32), 32)
            n_buf[pl.ds(pl.multiple_of(at + i * 32, 32), 32), :] = layer_norm_rows(mid[block, :], gain[...], shift[...])
        for k in range(2):
            @pl.when(z == 2 * part + k)
            def _():
                middle_own[...] = mid[k * rows : (k + 1) * rows, :]
    keep_n = pltpu.make_async_copy(n_buf, normed_two, loc.at[6])
    keep_n.start()
    line.relay(0, 0)
    load[3].wait()

    @pl.loop(0, 2 * inner // tile)
    def _(t):
        columns = pl.ds(aligned(t, tile), tile)
        gu[:, columns] = jnp.dot(n_buf[...], g_buf[:, columns], preferred_element_type=jnp.float32)

    @pl.loop(0, group // 32)
    def _(i):
        block = pl.ds(aligned(i, 32), 32)
        gate = gu[block, :inner]
        h_buf[block, :] = (gate / (1.0 + jnp.exp(-gate)) * gu[block, inner:]).astype(jnp.bfloat16)
    keep_h = pltpu.make_async_copy(h_buf, hidden, loc.at[7])
    keep_h.start()
    if shards > 2:
        line.relay(1, 0)
    load[4].wait()

    @pl.loop(0, D // tile)
    def _(t):
        columns = pl.ds(aligned(t, tile), tile)
        a_buf[:, columns] = jnp.dot(h_buf[...], d_buf[:, columns], preferred_element_type=jnp.float32).astype(jnp.bfloat16)
    keep_p = pltpu.make_async_copy(a_buf, down_part, loc.at[8])
    keep_p.start()
    load[5].wait()

    def back(o):
        mid[:rows, :inner] = contract_last(c_buf[o], d_buf[...])

        @pl.loop(0, rows // 32)
        def _(i):
            value = mid[pl.ds(aligned(i, 32), 32), :inner]
            place = pl.ds(pl.multiple_of(o * rows + i * 32, 32), 32)
            gate = gu[place, :inner]
            up = gu[place, inner:]
            sigmoid = 1.0 / (1.0 + jnp.exp(-gate))
            s_buf[place, :inner] = (value * up * (sigmoid * (1.0 + gate * (1.0 - sigmoid)))).astype(jnp.bfloat16)
            s_buf[place, inner:] = (value * (gate * sigmoid)).astype(jnp.bfloat16)

    back(z)
    for step in range(shards - 1):
        if step >= 2:
            line.relay(step, 0)
        for way in (0, 1):
            owner = z - step - 1 if way == 0 else z + step + 1

            @pl.when(line.gets(way, step))
            def _():
                back(owner)
    keep = [pltpu.make_async_copy(c_buf, all_cotangent, loc.at[9]), pltpu.make_async_copy(s_buf, slopes, loc.at[10])]
    for copy in keep:
        copy.start()
    line.finish()
    for copy in keep + [keep_n, keep_h, keep_p]:
        copy.wait()


def hidden_call(shards, attended, tokens, out_weight, gate_up_weight, down_weight, cotangent, gain, shift):
    rows = cotangent.shape[0]
    group = rows * shards
    inner = down_weight.shape[0]
    low = jnp.bfloat16
    f32 = jnp.float32
    vm = pl.BlockSpec(memory_space=pltpu.VMEM)
    any_ = pl.BlockSpec(memory_space=pl.ANY)
    return pl.pallas_call(
        functools.partial(hidden_kernel, shards),
        out_shape=[
            jax.ShapeDtypeStruct((rows, D), f32),
            jax.ShapeDtypeStruct((group, D), low),
            jax.ShapeDtypeStruct((group, inner), low),
            jax.ShapeDtypeStruct((group, 2 * inner), low),
            jax.ShapeDtypeStruct((shards, rows, D), low),
            jax.ShapeDtypeStruct((group, D), low),
        ],
        in_specs=[any_] * 6 + [vm, vm],
        out_specs=[vm] + [any_] * 5,
        scratch_shapes=[
            pltpu.VMEM((group, D), low),
            pltpu.VMEM((shards, rows, D), low),
            pltpu.VMEM(out_weight.shape, low),
            pltpu.VMEM(gate_up_weight.shape, low),
            pltpu.VMEM(down_weight.shape, low),
            pltpu.VMEM((shards, rows, D), low),
            pltpu.VMEM((2 * rows, D), f32),
            pltpu.VMEM((group, D), low),
            pltpu.VMEM((group, 2 * inner), f32),
            pltpu.VMEM((group, inner), low),
            pltpu.VMEM((group, 2 * inner), low),
        ] + line_sems(shards, 1) + [pltpu.SemaphoreType.DMA((11,))],
        compiler_params=pltpu.CompilerParams(
            collective_id=9, has_side_effects=True, vmem_limit_bytes=63 * 2**20
        ),
        name="hidden",
        cost_estimate=pl.CostEstimate(flops=24 * 10**9, bytes_accessed=150 * 10**6, transcendentals=0),
    )(attended, tokens, out_weight, gate_up_weight, down_weight, cotangent, gain, shift)


def head_mask(even, rows):
    lane = lax.broadcasted_iota(jnp.int32, (rows, 128), 1)
    return (lane < HEAD_DIM) if even else (lane >= HEAD_DIM)


def only(values, keep):
    return jnp.where(keep, values.astype(jnp.float32), 0.0).astype(jnp.bfloat16)


def block_visible(at, rows, seg_rows, seg_columns):
    count = at + rows
    row = lax.broadcasted_iota(jnp.int32, (rows, count), 0) + at
    column = lax.broadcasted_iota(jnp.int32, (rows, count), 1)
    return (column <= row) & (seg_rows[at : at + rows, :1] == seg_columns[:1, :count])


def attend_body(rows, qkv, seg_rows, seg_columns, a_buf, stats, done):
    z = lax.axis_index("shard")
    width = qkv.shape[1] // 3
    pairs = width // 128
    scale = HEAD_DIM ** (-0.5)
    for block in range(qkv.shape[0] // rows):
        at = block * rows
        count = at + rows
        seen = block_visible(at, rows, seg_rows, seg_columns)
        for pair in range(pairs):
            lanes = slice(128 * pair, 128 * pair + 128)
            query = qkv[at:count, lanes]
            keys = qkv[:count, width + 128 * pair : width + 128 * pair + 128]
            values = qkv[:count, 2 * width + 128 * pair : 2 * width + 128 * pair + 128]
            results = []
            for odd in (0, 1):
                keep = head_mask(odd == 0, rows)
                scores = contract_last(only(query, keep), keys) * scale
                scores = jnp.where(seen, scores, masked_score)
                top = jnp.max(scores, axis=-1, keepdims=True)
                weights = jnp.exp(scores - top)
                total = jnp.sum(weights, axis=-1, keepdims=True)
                probs = (weights * (1.0 / total)).astype(jnp.bfloat16)
                results.append(jnp.dot(probs, values, preferred_element_type=jnp.float32))
                head = 2 * pair + odd
                stats[at:count, head : head + 1] = top
                stats[at:count, 64 + head : 65 + head] = 1.0 / total
            merged = jnp.where(head_mask(True, rows), results[0], results[1])
            a_buf[z, at:count, lanes] = merged.astype(jnp.bfloat16)
        done(block)


def attend_kernel(shards, rows, qkv, seg_rows, seg_columns, attended, stats, a_buf, a_send, a_recv, loc):
    z = lax.axis_index("shard")
    width = qkv.shape[1] // 3
    blocks = qkv.shape[0] // rows
    greet_line(z, shards)
    line = Line(shards, blocks, None, a_buf, a_send, a_recv)
    attend_body(rows, qkv, seg_rows, seg_columns, a_buf, stats, line.start)
    for step in range(shards - 1):
        for block in range(blocks):
            line.relay(step, block)
    keep = [pltpu.make_async_copy(a_buf.at[o], attended.at[:, pl.ds(o * width, width)], loc.at[o]) for o in range(shards)]
    for copy in keep:
        copy.start()
    line.finish()
    for copy in keep:
        copy.wait()


def attend_call(shards, rows, qkv, seg_rows, seg_columns):
    group = qkv.shape[0]
    width = qkv.shape[1] // 3
    blocks = group // rows
    vm = pl.BlockSpec(memory_space=pltpu.VMEM)
    any_ = pl.BlockSpec(memory_space=pl.ANY)
    dma = pltpu.SemaphoreType.DMA
    return pl.pallas_call(
        functools.partial(attend_kernel, shards, rows),
        out_shape=[
            jax.ShapeDtypeStruct((group, shards * width), jnp.bfloat16),
            jax.ShapeDtypeStruct((group, 128), jnp.float32),
        ],
        in_specs=[vm, vm, vm],
        out_specs=[any_, vm],
        scratch_shapes=[
            pltpu.VMEM((shards, group, width), jnp.bfloat16),
            dma((2, shards - 1, blocks)), dma((2, shards - 1, blocks)), dma((shards,)),
        ],
        compiler_params=pltpu.CompilerParams(
            collective_id=2, has_side_effects=True, vmem_limit_bytes=48 * 2**20
        ),
        name="attend",
        cost_estimate=pl.CostEstimate(flops=10**9, bytes_accessed=150 * 10**6, transcendentals=0),
    )(qkv, seg_rows, seg_columns)


def attend_back_kernel(rows, *refs):
    attend_back_body(rows, *refs, [])


def attend_back_body(rows, qkv, d_attended, stats, seg_rows, seg_columns, cosine, minus, plus,
                     d_qkv, bias_grad, d_keys, d_values, steps):
    width = qkv.shape[1] // 3
    group = qkv.shape[0]
    blocks = group // rows
    pairs = width // 128
    scale = HEAD_DIM ** (-0.5)

    def turned(value, at, count):
        return (value * cosine[at:count, :] - pltpu.roll(value, 120, 1) * minus[at:count, :]
                - pltpu.roll(value, 8, 1) * plus[at:count, :])

    for block in reversed(range(blocks)):
        at = block * rows
        count = at + rows
        seen = block_visible(at, rows, seg_rows, seg_columns)
        for pair in range(pairs):
            lanes = slice(128 * pair, 128 * pair + 128)
            query = qkv[at:count, lanes]
            keys = qkv[:count, width + 128 * pair : width + 128 * pair + 128]
            values = qkv[:count, 2 * width + 128 * pair : 2 * width + 128 * pair + 128]
            slope = d_attended[at:count, lanes]
            d_query, d_key, d_value = [], [], []
            for odd in (0, 1):
                keep = head_mask(odd == 0, rows)
                head = 2 * pair + odd
                own_query = only(query, keep)
                own_slope = only(slope, keep)
                scores = contract_last(own_query, keys) * scale
                scores = jnp.where(seen, scores, masked_score)
                probs = jnp.exp(scores - stats[at:count, head : head + 1]) * stats[at:count, 64 + head : 65 + head]
                d_probs = contract_last(own_slope, values)
                inner = jnp.sum(probs * d_probs, axis=-1, keepdims=True)
                d_scores = (probs * (d_probs - inner)).astype(jnp.bfloat16)
                d_query.append(jnp.dot(d_scores, keys, preferred_element_type=jnp.float32))
                d_key.append(contract_first(d_scores, own_query))
                d_value.append(contract_first(probs.astype(jnp.bfloat16), own_slope))
            keep = head_mask(True, rows)
            d_q = jnp.where(keep, d_query[0], d_query[1]) * scale
            d_q = turned(d_q, at, count).astype(jnp.bfloat16)
            d_qkv[at:count, lanes] = d_q
            d_k = (d_key[0] + d_key[1]) * scale
            d_v = d_value[0] + d_value[1]
            if block == blocks - 1:
                d_keys[:, lanes] = d_k
                d_values[:, lanes] = d_v
            else:
                d_keys[:count, lanes] += d_k
                d_values[:count, lanes] += d_v
            k_out = turned(d_keys[at:count, lanes], at, count).astype(jnp.bfloat16)
            d_qkv[at:count, width + 128 * pair : width + 128 * pair + 128] = k_out
            v_out = d_values[at:count, lanes].astype(jnp.bfloat16)
            d_qkv[at:count, 2 * width + 128 * pair : 2 * width + 128 * pair + 128] = v_out
            if steps:
                steps.pop(0)()
    for part in range(3 * pairs):
        lanes = slice(128 * part, 128 * part + 128)
        bias_grad[:, lanes] = jnp.broadcast_to(
            jnp.sum(d_qkv[:, lanes].astype(jnp.float32), axis=0, keepdims=True), (8, 128))


def contract_first(left, right):
    return lax.dot_general(
        left, right, (((0,), (0,)), ((), ())), preferred_element_type=jnp.float32
    )


def attend_back_call(rows, qkv, d_attended, stats, seg_rows, seg_columns, cosine, minus, plus):
    group = qkv.shape[0]
    width = qkv.shape[1] // 3
    vm = pl.BlockSpec(memory_space=pltpu.VMEM)
    return pl.pallas_call(
        functools.partial(attend_back_kernel, rows),
        out_shape=[
            jax.ShapeDtypeStruct((group, 3 * width), jnp.bfloat16),
            jax.ShapeDtypeStruct((8, 3 * width), jnp.float32),
        ],
        in_specs=[vm] * 8,
        out_specs=[vm, vm],
        scratch_shapes=[pltpu.VMEM((group, width), jnp.float32), pltpu.VMEM((group, width), jnp.float32)],
        compiler_params=pltpu.CompilerParams(vmem_limit_bytes=48 * 2**20),
        name="attend_back",
        cost_estimate=pl.CostEstimate(flops=3 * 10**9, bytes_accessed=100 * 10**6, transcendentals=0),
    )(qkv, d_attended, stats, seg_rows, seg_columns, cosine, minus, plus)


def scatter_kernel(shards, cuts, parts, total, own, got, load, send, recv):
    z = lax.axis_index("shard")
    rows = parts.shape[1]
    step_rows = rows // cuts
    greet_line(z, shards)

    def piece(cut):
        return pl.ds(cut * step_rows, step_rows)

    def moved(way, block, cut):
        target = z + 1 if way == 0 else z - 1
        place = got.at[way, block, piece(cut)]
        return remote(place, place, send.at[way, block, cut], recv.at[way, block, cut], {"shard": target})

    loads = [pltpu.make_async_copy(parts.at[j], own.at[j], load.at[j]) for j in range(shards)]
    for copy in loads:
        copy.start()
    for copy in loads:
        copy.wait()
    for far in range(shards - 1):
        for cut in range(cuts):
            for way in (0, 1):
                block = shards - 1 - far if way == 0 else far
                sends = z < block if way == 0 else z > block
                first = z == 0 if way == 0 else z == shards - 1

                @pl.when(sends)
                def _():
                    @pl.when(first)
                    def _():
                        got[way, block, piece(cut)] = own[block, piece(cut)]

                    @pl.when(jnp.logical_not(first))
                    def _():
                        moved(way, block, cut).wait_recv()
                        got[way, block, piece(cut)] = (
                            got[way, block, piece(cut)].astype(jnp.float32)
                            + own[block, piece(cut)].astype(jnp.float32)
                        ).astype(got.dtype)
                    moved(way, block, cut).start()
    total[...] = own[z].astype(jnp.float32)
    for way in (0, 1):
        @pl.when(z >= 1 if way == 0 else z + 1 < shards)
        def _():
            for cut in range(cuts):
                moved(way, z, cut).wait_recv()
            total[...] += got[way, z].astype(jnp.float32)
    for far in range(shards - 1):
        for cut in range(cuts):
            for way in (0, 1):
                block = shards - 1 - far if way == 0 else far

                @pl.when(z < block if way == 0 else z > block)
                def _():
                    moved(way, block, cut).wait_send()


def scatter_call(shards, parts, number):
    _, rows, columns = parts.shape
    cuts = 3
    dma = pltpu.SemaphoreType.DMA
    return pl.pallas_call(
        functools.partial(scatter_kernel, shards, cuts),
        out_shape=jax.ShapeDtypeStruct((rows, columns), jnp.float32),
        in_specs=[pl.BlockSpec(memory_space=pl.ANY)],
        out_specs=pl.BlockSpec(memory_space=pltpu.VMEM),
        scratch_shapes=[
            pltpu.VMEM(parts.shape, parts.dtype),
            pltpu.VMEM((2,) + parts.shape, parts.dtype),
            dma((shards,)), dma((2, shards, cuts)), dma((2, shards, cuts)),
        ],
        compiler_params=pltpu.CompilerParams(
            collective_id=number, has_side_effects=True, vmem_limit_bytes=32 * 2**20
        ),
        name="scatter",
        cost_estimate=pl.CostEstimate(flops=0, bytes_accessed=200 * 10**6, transcendentals=0),
    )(parts)


def exchange_kernel(shards, first, second, first_out, second_out, send, recv, loc):
    z = lax.axis_index("shard")
    width = first.shape[1] // shards
    greet([((z != o), {"shard": o}) for o in range(shards)], shards - 1)
    arrays = ((first, first_out), (second, second_out))

    def move(k, o):
        source, target = arrays[k]
        return remote(source.at[:, pl.ds(o * width, width)], target.at[z], send.at[k, o], recv.at[k, z], {"shard": o})

    def arrival(k, o):
        source, target = arrays[k]
        return remote(target.at[o], target.at[o], send.at[k, o], recv.at[k, o], {"shard": o})

    for k in (0, 1):
        for o in range(shards):
            @pl.when(z != o)
            def _():
                move(k, o).start()

            @pl.when(z == o)
            def _():
                source, target = arrays[k]
                pltpu.make_async_copy(source.at[:, pl.ds(o * width, width)], target.at[o], loc.at[k]).start()
    for k in (0, 1):
        for o in range(shards):
            @pl.when(z != o)
            def _():
                arrival(k, o).wait_recv()
                move(k, o).wait_send()

            @pl.when(z == o)
            def _():
                source, target = arrays[k]
                pltpu.make_async_copy(source.at[:, pl.ds(o * width, width)], target.at[o], loc.at[k]).wait()


def exchange_call(shards, first, second):
    rows, columns = first.shape
    shape = jax.ShapeDtypeStruct((shards, rows, columns // shards), first.dtype)
    any_ = pl.BlockSpec(memory_space=pl.ANY)
    dma = pltpu.SemaphoreType.DMA
    return pl.pallas_call(
        functools.partial(exchange_kernel, shards),
        out_shape=[shape, shape],
        in_specs=[any_, any_],
        out_specs=[any_, any_],
        scratch_shapes=[dma((2, shards)), dma((2, shards)), dma((2,))],
        compiler_params=pltpu.CompilerParams(collective_id=5, has_side_effects=True),
        name="exchange",
        cost_estimate=pl.CostEstimate(flops=0, bytes_accessed=100 * 10**6, transcendentals=0),
    )(first, second)


def add_rows(target, source, count):
    step = 16

    @pl.loop(0, count // step)
    def _(i):
        block = pl.ds(aligned(i, step), step)
        target[block, :] = (
            target[block, :].astype(jnp.float32) + source[block, :].astype(jnp.float32)
        ).astype(target.dtype)


class Reducer:
    def __init__(self, cube, share, term, core, near, last, send, recv):
        self.cube, self.share = cube, share
        self.cut = 16 * ((share // 16 + 1) // 2)
        self.term, self.core, self.near, self.last = term, core, near, last
        self.send, self.recv = send, recv
        self.chunks = term.shape[0]

    def share_rows(self, chunk, place, half):
        first, count = (0, self.cut) if half == 0 else (self.cut, self.share - self.cut)
        start = self.cube.core * 4 * self.share + place * self.share + first
        return rows_of(self.term.at[chunk], start, 16, count)

    def own(self, chunk):
        start = (self.cube.core * 4 + self.cube.place) * self.share
        return rows_of(self.term.at[chunk], start, 16, self.share)

    def core_copy(self, chunk):
        source = rows_of(self.term.at[chunk], (1 - self.cube.core) * 4 * self.share, 16, 4 * self.share)
        return remote(source, self.core.at[chunk], self.send.at[chunk, 0], self.recv.at[chunk, 0], self.cube.to_core)

    def near_place(self, half, other):
        c = self.cube
        if half == 0:
            return 2 * other + (1 - c.x), 2 * other + c.x
        return 2 * (1 - c.y) + other, 2 * c.y + other

    def near_slot(self, chunk, half, other):
        count = self.cut if half == 0 else self.share - self.cut
        start = other * count + (2 * self.cut if half == 1 else 0)
        return self.near.at[chunk, pl.ds(start, count)]

    def near_copy(self, chunk, half, other):
        source = self.share_rows(chunk, self.near_place(half, other)[0], half)
        slot = 1 + 2 * half + other
        device = self.cube.to_x if half == 0 else self.cube.to_y
        return remote(source, self.near_slot(chunk, half, other), self.send.at[chunk, slot], self.recv.at[chunk, slot], device)

    def last_slot(self, chunk, half):
        first, count = (0, self.cut) if half == 0 else (self.cut, self.share - self.cut)
        return self.last.at[chunk, pl.ds(first, count)]

    def last_copy(self, chunk, half):
        c = self.cube
        place = 2 * (1 - c.y) + c.x if half == 0 else 2 * c.y + (1 - c.x)
        device = c.to_y if half == 0 else c.to_x
        source = self.share_rows(chunk, place, half)
        return remote(source, self.last_slot(chunk, half), self.send.at[chunk, 5 + half], self.recv.at[chunk, 5 + half], device)

    def start(self, chunk):
        self.core_copy(chunk).start()

    def after_core(self, chunk):
        self.core_copy(chunk).wait_recv()
        mine = rows_of(self.term.at[chunk], self.cube.core * 4 * self.share, 16, 4 * self.share)
        add_rows(mine, self.core.at[chunk], 4 * self.share)
        for half in (0, 1):
            for other in (0, 1):
                self.near_copy(chunk, half, other).start()

    def after_near(self, chunk):
        for half in (0, 1):
            count = self.cut if half == 0 else self.share - self.cut
            for other in (0, 1):
                self.near_copy(chunk, half, other).wait_recv()
                stays = self.share_rows(chunk, self.near_place(half, other)[1], half)
                add_rows(stays, self.near_slot(chunk, half, other), count)
            self.last_copy(chunk, half).start()

    def after_last(self, chunk):
        c = self.cube
        for half in (0, 1):
            count = self.cut if half == 0 else self.share - self.cut
            self.last_copy(chunk, half).wait_recv()
            add_rows(self.share_rows(chunk, c.place, half), self.last_slot(chunk, half), count)

    def finish(self, chunk):
        self.core_copy(chunk).wait_send()
        for half in (0, 1):
            for other in (0, 1):
                self.near_copy(chunk, half, other).wait_send()
            self.last_copy(chunk, half).wait_send()


class Owners:
    def __init__(self, shards, parts, source, out, send, recv, loc):
        self.shards, self.parts, self.source, self.out = shards, parts, source, out
        self.send, self.recv, self.loc = send, recv, loc
        self.z = lax.axis_index("shard")
        self.width = out.shape[1] // (shards * parts)

    def target(self, shard, part):
        return self.out.at[:, pl.ds(aligned((part * self.shards + shard) * (self.width // 128), 128), self.width)]

    def piece(self, o, part):
        return self.source(o).at[:, pl.ds(part * self.width, self.width)]

    def copy(self, o, part):
        return remote(self.piece(o, part), self.target(self.z, part), self.send.at[o, part], self.recv.at[self.z, part], {"shard": o})

    def arrival(self, o, part):
        place = self.target(o, part)
        return remote(place, place, self.send.at[o, part], self.recv.at[o, part], {"shard": o})

    def local(self, o, part):
        return pltpu.make_async_copy(self.piece(o, part), self.target(o, part), self.loc.at[part])

    def start(self, o):
        for part in range(self.parts):
            @pl.when(self.z != o)
            def _():
                self.copy(o, part).start()

            @pl.when(self.z == o)
            def _():
                self.local(o, part).start()

    def arrive(self):
        for o in range(self.shards):
            for part in range(self.parts):
                @pl.when(self.z != o)
                def _():
                    self.arrival(o, part).wait_recv()

                @pl.when(self.z == o)
                def _():
                    self.local(o, part).wait()

    def finish(self):
        for o in range(self.shards):
            for part in range(self.parts):
                @pl.when(self.z != o)
                def _():
                    self.copy(o, part).wait_send()


def owner_sems(shards, parts):
    dma = pltpu.SemaphoreType.DMA
    return [dma((shards, parts)), dma((shards, parts)), dma((parts,))]


class Gatherer:
    def __init__(self, cube, share, out, sems):
        self.cube, self.share, self.out = cube, share, out
        self.send, self.recv, self.loc = sems
        self.count = share.shape[0]
        self.cut = 16 * ((self.count // 16 + 1) // 2)

    def rows(self, place, half=None):
        first, count = {None: (0, self.count), 0: (0, self.cut), 1: (self.cut, self.count - self.cut)}[half]
        return rows_of(self.out, (self.cube.core * 4 + place) * self.count + first, 16, count)

    def copy(self, kind):
        c = self.cube
        at_x, at_y = 2 * c.y + 1 - c.x, 2 * (1 - c.y) + c.x
        block, device = (
            (self.rows(c.place), c.to_x),
            (self.rows(c.place), c.to_y),
            (self.rows(at_x, 0), c.to_y),
            (self.rows(at_y, 1), c.to_x),
            (self.rows(c.place), c.to_core),
            (self.rows(at_x), c.to_core),
            (self.rows(at_y), c.to_core),
            (self.rows(3 - c.place), c.to_core),
        )[kind]
        source = self.share if kind in (0, 1, 4) else block
        return remote(source, block, self.send.at[kind], self.recv.at[kind], device)

    def local(self):
        return pltpu.make_async_copy(self.share, self.rows(self.cube.place), self.loc.at[0])

    def start(self):
        for kind in (0, 1, 4):
            self.copy(kind).start()
        self.local().start()

    def pass_on(self):
        self.copy(0).wait_recv()
        self.copy(2).start()
        self.copy(5).start()
        self.copy(1).wait_recv()
        self.copy(3).start()
        self.copy(6).start()

    def pass_last(self):
        self.copy(2).wait_recv()
        self.copy(3).wait_recv()
        self.copy(7).start()

    def finish(self):
        for kind in (4, 5, 6, 7):
            self.copy(kind).wait_recv()
        for kind in range(8):
            self.copy(kind).wait_send()
        self.local().wait()


def gatherer_sems():
    dma = pltpu.SemaphoreType.DMA
    return [dma((8,)), dma((8,)), dma((1,))]


class LineSum:
    def __init__(self, shards, cuts, own, got, send, recv):
        self.z = lax.axis_index("shard")
        self.shards, self.cuts, self.own, self.got, self.send, self.recv = shards, cuts, own, got, send, recv
        self.step = own.shape[1] // cuts

    def piece(self, cut):
        return pl.ds(cut * self.step, self.step)

    def copy(self, way, block, cut, source=None):
        target = self.z + 1 if way == 0 else self.z - 1
        place = self.got.at[way, block, self.piece(cut)]
        return remote(place if source is None else source, place, self.send.at[way, block, cut], self.recv.at[way, block, cut], {"shard": target})

    def pair(self, t):
        half = self.shards // 2
        upper = self.z // half
        return half - 1 - t + upper * (2 * t - half + 1)

    def ready(self, pair):
        for way in (0, 1):
            for i in (0, 1):
                block = 2 * pair + (1 - i if way == 0 else i)

                @pl.when((self.z == (0 if way == 0 else self.shards - 1)) & (block != self.z))
                def _():
                    for cut in range(self.cuts):
                        self.copy(way, block, cut, self.own.at[block, self.piece(cut)]).start()

    def step_on(self, far, cut):
        for way in (0, 1):
            block = self.shards - 1 - far if way == 0 else far
            sends = (self.z < block) & (self.z > 0) if way == 0 else (self.z > block) & (self.z < self.shards - 1)

            @pl.when(sends)
            def _():
                self.copy(way, block, cut).wait_recv()
                place = self.got.at[way, block, self.piece(cut)]
                add_rows(place, self.own.at[block, self.piece(cut)], self.step)
                self.copy(way, block, cut).start()

    def result(self, total):
        rows = self.own.shape[1]
        for way in (0, 1):
            @pl.when(self.z >= 1 if way == 0 else self.z + 1 < self.shards)
            def _():
                for cut in range(self.cuts):
                    self.copy(way, self.z, cut).wait_recv()

        @pl.loop(0, rows // 16)
        def _(i):
            block = pl.ds(aligned(i, 16), 16)
            total[block, :] = self.own[self.z, block, :].astype(jnp.float32)

            @pl.when(self.z >= 1)
            def _():
                total[block, :] += self.got[0, self.z, block, :].astype(jnp.float32)

            @pl.when(self.z + 1 < self.shards)
            def _():
                total[block, :] += self.got[1, self.z, block, :].astype(jnp.float32)

    def finish(self):
        for far in range(self.shards - 1):
            for cut in range(self.cuts):
                for way in (0, 1):
                    block = self.shards - 1 - far if way == 0 else far

                    @pl.when(self.z < block if way == 0 else self.z > block)
                    def _():
                        self.copy(way, block, cut).wait_send()


def line_scratch(shards, rows, columns, cuts):
    dma = pltpu.SemaphoreType.DMA
    return [
        pltpu.VMEM((shards, rows, columns), jnp.bfloat16),
        pltpu.VMEM((2, shards, rows, columns), jnp.bfloat16),
        dma((2, shards, cuts)), dma((2, shards, cuts)),
    ]


def reducer_scratch(chunks, share, columns):
    dma = pltpu.SemaphoreType.DMA
    return [pltpu.VMEM((chunks, n * share, columns), jnp.bfloat16) for n in (8, 4, 2, 1)] + [
        dma((chunks, 7)), dma((chunks, 7)),
    ]


def pair_product(own, pair, slopes, weight, tile=512):
    rows = own.shape[1]

    @pl.loop(0, own.shape[2] // tile)
    def _(t):
        columns = pl.ds(aligned(t, tile), tile)
        value = contract_last(slopes[pl.ds(aligned(pair, 2 * rows), 2 * rows), :], weight[columns, :])
        own[2 * pair, :, columns] = value[:rows].astype(own.dtype)
        own[2 * pair + 1, :, columns] = value[rows:].astype(own.dtype)


def term_product(term, chunk, left, right):
    term[chunk] = contract_first(left[...], right[...]).astype(term.dtype)


def interleave(moves, steps):
    for i in range(max(len(moves), len(steps))):
        if i < len(moves):
            moves[i]()
        if i < len(steps):
            steps[i]()


def load_all(pairs, loc):
    copies = [pltpu.make_async_copy(source, target, loc.at[i]) for i, (source, target) in enumerate(pairs)]
    for copy in copies:
        copy.start()
    return copies


def hidden_back_kernel(shards, slopes, weight, hidden, cotangent, normed_two, total, down_share, gate_up_share,
                       s_buf, w_buf, h_buf, c_buf, n_buf, own, got, z_send, z_recv,
                       term, core, near, last, r_send, r_recv,
                       g_term, g_core, g_near, g_last, g_send, g_recv, loc):
    cube = Cube()
    loads = load_all(((slopes, s_buf), (weight, w_buf), (hidden, h_buf), (cotangent, c_buf), (normed_two, n_buf)), loc)
    greet(cube.partners(shards), shards + 2)
    line = LineSum(shards, 3, own, got, z_send, z_recv)
    share = hidden.shape[1] // 8
    width = D // shards
    chunks, _, columns = term.shape
    early = g_term.shape[0]
    reducer = Reducer(cube, share, term, core, near, last, r_send, r_recv)
    g_reducer = Reducer(cube, width // 8, g_term, g_core, g_near, g_last, g_send, g_recv)
    for copy in loads[:2]:
        copy.wait()
    for t in range(shards // 2):
        pair = line.pair(t)
        pair_product(own, pair, s_buf, w_buf)
        line.ready(pair)
        if t == 0:
            for copy in loads[2:]:
                copy.wait()
            for k in range(chunks):
                term_product(term, k, h_buf, c_buf.at[:, pl.ds(k * columns, columns)])
                reducer.start(k)
    for k in range(chunks):
        reducer.after_core(k)
    for k in range(early):
        term_product(g_term, k, n_buf.at[:, pl.ds(k * width, width)], s_buf)
        g_reducer.start(k)
    keep = []

    def keep_down(k):
        copy = pltpu.make_async_copy(reducer.own(k), down_share.at[:, pl.ds(k * columns, columns)], loc.at[5 + k])
        copy.start()
        keep.append(copy)

    def keep_gate_up(k):
        copy = pltpu.make_async_copy(g_reducer.own(k), gate_up_share.at[k], loc.at[5 + chunks + k])
        copy.start()
        keep.append(copy)

    steps = [functools.partial(reducer.after_near, k) for k in range(chunks)]
    steps += [functools.partial(g_reducer.after_core, k) for k in range(early)]
    for k in range(chunks):
        steps += [functools.partial(reducer.after_last, k), functools.partial(keep_down, k)]
    steps += [functools.partial(g_reducer.after_near, k) for k in range(early)]
    for k in range(early):
        steps += [functools.partial(g_reducer.after_last, k), functools.partial(keep_gate_up, k)]
    moves = [functools.partial(line.step_on, far, cut) for far in range(shards - 1) for cut in range(3)]
    interleave(moves, steps)
    line.result(total)
    line.finish()
    for k in range(chunks):
        reducer.finish(k)
    for k in range(early):
        g_reducer.finish(k)
    for copy in keep:
        copy.wait()


def hidden_back_call(shards, slopes, weight, hidden, cotangent, normed_two):
    group, inner = hidden.shape
    rows = group // shards
    share = inner // 8
    chunks = 4
    early = shards // 2
    width = D // shards
    low = jnp.bfloat16
    any_ = pl.BlockSpec(memory_space=pl.ANY)
    dma = pltpu.SemaphoreType.DMA
    return pl.pallas_call(
        functools.partial(hidden_back_kernel, shards),
        out_shape=[
            jax.ShapeDtypeStruct((rows, D), jnp.float32),
            jax.ShapeDtypeStruct((share, D), low),
            jax.ShapeDtypeStruct((early, width // 8, 2 * inner), low),
        ],
        in_specs=[any_] * 5,
        out_specs=[pl.BlockSpec(memory_space=pltpu.VMEM), any_, any_],
        scratch_shapes=[pltpu.VMEM(a.shape, low) for a in (slopes, weight, hidden, cotangent, normed_two)]
        + line_scratch(shards, rows, D, 3) + reducer_scratch(chunks, share, D // chunks)
        + reducer_scratch(early, width // 8, 2 * inner) + [dma((5 + chunks + early,))],
        compiler_params=pltpu.CompilerParams(collective_id=6, has_side_effects=True, vmem_limit_bytes=63 * 2**20),
        name="hidden_back",
        cost_estimate=pl.CostEstimate(flops=10**10, bytes_accessed=200 * 10**6, transcendentals=0),
    )(slopes, weight, hidden, cotangent, normed_two)


def norm_back_rows(slope, values, gain):
    centered = values - jnp.mean(values, axis=-1, keepdims=True)
    inverse = lax.rsqrt(jnp.mean(centered * centered, axis=-1, keepdims=True) + norm_eps)
    unit = centered * inverse
    scaled = slope * gain
    back = inverse * (
        scaled
        - jnp.mean(scaled, axis=-1, keepdims=True)
        - unit * jnp.mean(scaled * unit, axis=-1, keepdims=True)
    )
    return back, unit


def heads_back_kernel(shards, rows, d_normed_two, middle, cotangent, gain, out_weight, qkv, stats, seg_rows, seg_columns,
                      cosine, minus, plus, normed_two, slopes, attended, down_share, gate_up_first,
                      d_middle, norm_grads, d_qkv, bias_grad, gate_up_rows, out_rows, down_grad,
                      o_buf, n_buf, s_buf, a_buf, m_low, da_own, d_attended, m_columns, d_keys, d_values,
                      g_term, g_core, g_near, g_last, g_send, g_recv,
                      o_term, o_core, o_near, o_last, o_send, o_recv,
                      e_send, e_recv, loc, *sems):
    cube = Cube()
    z = lax.axis_index("shard")
    loads = load_all(((out_weight, o_buf), (normed_two, n_buf), (slopes, s_buf), (attended, a_buf)), loc)
    greet(cube.partners(shards), shards + 2)
    width = D // shards
    share = width // 8
    first = gate_up_first.shape[0]
    gatherer = Gatherer(cube, down_share, down_grad, sems[0:3])
    g_reducer = Reducer(cube, share, g_term, g_core, g_near, g_last, g_send, g_recv)
    o_reducer = Reducer(cube, share, o_term, o_core, o_near, o_last, o_send, o_recv)
    owners = Owners(shards, 2, lambda o: gate_up_first.at[o] if o < first else g_reducer.own(o - first), gate_up_rows, *sems[3:6])
    o_owners = Owners(shards, 1, o_reducer.own, out_rows, *sems[6:9])
    gatherer.start()
    arrays = ((da_own, d_attended), (m_low, m_columns))

    def move(k, o):
        source, target = arrays[k]
        return remote(source.at[:, pl.ds(o * width, width)], target.at[pl.ds(aligned(z, rows), rows)],
                      e_send.at[k, o], e_recv.at[k, z], {"shard": o})

    def arrival(k, o):
        place = arrays[k][1].at[pl.ds(o * rows, rows)]
        return remote(place, place, e_send.at[k, o], e_recv.at[k, o], {"shard": o})

    def here(k, o):
        source, target = arrays[k]
        return pltpu.make_async_copy(source.at[:, pl.ds(o * width, width)], target.at[pl.ds(o * rows, rows)], loc.at[4 + k])

    def begin(k, o):
        @pl.when(z != o)
        def _():
            move(k, o).start()

        @pl.when(z == o)
        def _():
            here(k, o).start()

    def arrive(k):
        for o in range(shards):
            @pl.when(z != o)
            def _():
                arrival(k, o).wait_recv()

            @pl.when(z == o)
            def _():
                here(k, o).wait()

    norm_grads[...] = jnp.zeros_like(norm_grads)

    @pl.loop(0, rows // 16)
    def _(i):
        block = pl.ds(aligned(i, 16), 16)
        slope = d_normed_two[block, :]
        back, unit = norm_back_rows(slope, middle[block, :], gain[...])
        value = cotangent[block, :].astype(jnp.float32) + back
        d_middle[block, :] = value
        m_low[block, :] = value.astype(jnp.bfloat16)
        norm_grads[0:8, :] += (slope * unit).reshape(2, 8, D).sum(axis=0)
        norm_grads[8:16, :] += slope.reshape(2, 8, D).sum(axis=0)

    loads[0].wait()
    for o in range(shards):
        da_own[:, o * width : (o + 1) * width] = contract_last(
            m_low[...], o_buf[o * width : (o + 1) * width, :]).astype(jnp.bfloat16)
        begin(0, o)
    for o in range(shards):
        begin(1, o)
    loads[1].wait()
    loads[2].wait()
    gatherer.pass_on()
    for k in range(shards - first):
        at = (first + k) * width
        term_product(g_term, k, n_buf.at[:, pl.ds(at, width)], s_buf)
        g_reducer.start(k)
    gatherer.pass_last()
    for k in range(shards - first):
        g_reducer.after_core(k)
    arrive(0)
    for o in range(first):
        owners.start(o)
    steps = []

    def out_term(k):
        if k == 0:
            loads[3].wait()
            arrive(1)
        term_product(o_term, k, a_buf.at[:, pl.ds(k * width, width)], m_columns)
        o_reducer.start(k)

    for k in range(shards - first):
        steps.append(functools.partial(g_reducer.after_near, k))
    for k in range(shards):
        steps.append(functools.partial(out_term, k))
    for k in range(shards):
        steps.append(functools.partial(o_reducer.after_core, k))
    for k in range(shards - first):
        steps += [functools.partial(g_reducer.after_last, k), functools.partial(owners.start, first + k)]
    for k in range(shards):
        steps.append(functools.partial(o_reducer.after_near, k))
    for k in range(shards):
        steps += [functools.partial(o_reducer.after_last, k), functools.partial(o_owners.start, k)]
    attend_back_body(rows, qkv, d_attended, stats, seg_rows, seg_columns, cosine, minus, plus,
                     d_qkv, bias_grad, d_keys, d_values, steps)
    for step in steps:
        step()
    owners.arrive()
    o_owners.arrive()
    for k in (0, 1):
        for o in range(shards):
            @pl.when(z != o)
            def _():
                move(k, o).wait_send()
    for k in range(shards - first):
        g_reducer.finish(k)
    for k in range(shards):
        o_reducer.finish(k)
    owners.finish()
    o_owners.finish()
    gatherer.finish()


def heads_back_call(shards, rows, d_normed_two, middle, cotangent, gain, out_weight, qkv, stats, seg_rows, seg_columns,
                    cosine, minus, plus, normed_two, slopes, attended, down_share, gate_up_first):
    group = qkv.shape[0]
    width = D // shards
    share = width // 8
    columns = slopes.shape[1]
    late = shards - gate_up_first.shape[0]
    vm = pl.BlockSpec(memory_space=pltpu.VMEM)
    any_ = pl.BlockSpec(memory_space=pl.ANY)
    dma = pltpu.SemaphoreType.DMA
    low = jnp.bfloat16
    f32 = jnp.float32
    return pl.pallas_call(
        functools.partial(heads_back_kernel, shards, rows),
        out_shape=[
            jax.ShapeDtypeStruct((rows, D), f32),
            jax.ShapeDtypeStruct((16, D), f32),
            jax.ShapeDtypeStruct((group, 3 * width), low),
            jax.ShapeDtypeStruct((8, 3 * width), f32),
            jax.ShapeDtypeStruct((share, shards * columns), low),
            jax.ShapeDtypeStruct((share, D), low),
            jax.ShapeDtypeStruct((8 * down_share.shape[0], D), low),
        ],
        in_specs=[vm] * 4 + [any_] + [vm] * 7 + [any_] * 5,
        out_specs=[vm, vm, vm, vm, any_, any_, any_],
        scratch_shapes=[
            pltpu.VMEM(out_weight.shape, low), pltpu.VMEM(normed_two.shape, low), pltpu.VMEM(slopes.shape, low),
            pltpu.VMEM(attended.shape, low),
            pltpu.VMEM((rows, D), low), pltpu.VMEM((rows, D), low),
            pltpu.VMEM((group, width), low), pltpu.VMEM((group, width), low),
            pltpu.VMEM((group, width), f32), pltpu.VMEM((group, width), f32),
        ] + reducer_scratch(late, share, columns) + reducer_scratch(shards, share, width)
        + [dma((2, shards)), dma((2, shards)), dma((6,))] + gatherer_sems() + owner_sems(shards, 2) + owner_sems(shards, 1),
        compiler_params=pltpu.CompilerParams(collective_id=7, has_side_effects=True, vmem_limit_bytes=63 * 2**20),
        name="heads_back",
        cost_estimate=pl.CostEstimate(flops=10**10, bytes_accessed=200 * 10**6, transcendentals=0),
    )(d_normed_two, middle, cotangent, gain, out_weight, qkv, stats, seg_rows, seg_columns, cosine, minus, plus,
      normed_two, slopes, attended, down_share, gate_up_first)


def input_back_kernel(shards, slopes, weight, normed, tokens, gain, d_middle, bias_grad, norm_grads, gate_up_rows, out_rows,
                      input_grad, small, qkv_grad, out_grad, gate_up_grad,
                      w_buf, n_buf, total, part, part_in, own, got, z_send, z_recv,
                      term, core, near, last, r_send, r_recv, qkv_rows, s_send, s_recv, loc, *sems):
    cube = Cube()
    z = lax.axis_index("shard")
    loads = load_all(((weight, w_buf), (normed, n_buf)), loc)
    greet(cube.partners(shards), shards + 2)
    rows = tokens.shape[0]
    width = D // shards
    share = width // 8
    line = LineSum(shards, 3, own, got, z_send, z_recv)
    reducer = Reducer(cube, share, term, core, near, last, r_send, r_recv)
    owners = Owners(shards, 3, reducer.own, qkv_rows, *sems[0:3])
    g_gatherer = Gatherer(cube, gate_up_rows, gate_up_grad, sems[3:6])
    o_gatherer = Gatherer(cube, out_rows, out_grad, sems[6:9])
    gatherer = Gatherer(cube, qkv_rows, qkv_grad, sems[9:12])
    loads[0].wait()
    for t in range(shards // 2):
        pair = line.pair(t)
        pair_product(own, pair, slopes, w_buf)
        line.ready(pair)
        if t == 0:
            loads[1].wait()
            for k in range(shards):
                term_product(term, k, n_buf.at[:, pl.ds(k * width, width)], slopes)
                reducer.start(k)
    steps = [functools.partial(reducer.after_core, k) for k in range(shards)]
    steps += [g_gatherer.start, o_gatherer.start]
    steps += [functools.partial(reducer.after_near, k) for k in range(shards)]
    for k in range(shards):
        steps += [functools.partial(reducer.after_last, k), functools.partial(owners.start, k)]
    steps += [o_gatherer.pass_on, g_gatherer.pass_on]
    moves = [functools.partial(line.step_on, far, cut) for far in range(shards - 1) for cut in range(3)]
    interleave(moves, steps)
    line.result(total)
    owners.arrive()
    gatherer.start()

    part[...] = jnp.zeros_like(part)

    @pl.loop(0, rows // 16)
    def _(i):
        block = pl.ds(aligned(i, 16), 16)
        slope = total[block, :]
        back, unit = norm_back_rows(slope, tokens[block, :].astype(jnp.float32), gain[...])
        input_grad[block, :] = d_middle[block, :] + back
        ones = (slope * unit).reshape(2, 8, D).sum(axis=0).sum(axis=0, keepdims=True)
        twos = slope.reshape(2, 8, D).sum(axis=0).sum(axis=0, keepdims=True)
        for o in range(shards):
            part[o, 3:4, :] += ones[:, o * width : (o + 1) * width]
            part[o, 4:5, :] += twos[:, o * width : (o + 1) * width]
    for o in range(shards):
        for k in range(2):
            part[o, 5 + k : 6 + k, :] = jnp.sum(
                norm_grads[8 * k : 8 * k + 8, o * width : (o + 1) * width], axis=0, keepdims=True)
    for k in range(3):
        flat = k * shards + z
        part[flat // 3, pl.ds(flat % 3, 1), :] = bias_grad[0:1, k * width : (k + 1) * width]

    def small_copy(o):
        return remote(part.at[o], part_in.at[z], s_send.at[o], s_recv.at[z], {"shard": o})

    def small_arrival(o):
        return remote(part.at[o], part_in.at[o], s_send.at[o], s_recv.at[o], {"shard": o})

    for o in range(shards):
        @pl.when(z != o)
        def _():
            small_copy(o).start()
    small[...] = part[z]
    for o in range(shards):
        @pl.when(z != o)
        def _():
            small_arrival(o).wait_recv()
            small[...] += part_in[o]
    sums = [remote(small, part_in.at[shards + i], s_send.at[shards + i], s_recv.at[shards + i], device)
            for i, device in enumerate((cube.to_core, cube.to_x, cube.to_y))]
    for i, copy in enumerate(sums):
        copy.start()
        copy.wait()
        small[...] += part_in[shards + i]
    g_gatherer.pass_last()
    o_gatherer.pass_last()
    gatherer.pass_on()
    gatherer.pass_last()
    for o in range(shards):
        @pl.when(z != o)
        def _():
            small_copy(o).wait_send()
    line.finish()
    for k in range(shards):
        reducer.finish(k)
    owners.finish()
    for g in (g_gatherer, o_gatherer, gatherer):
        g.finish()


def input_back_call(shards, slopes, weight, normed, tokens, gain, d_middle, bias_grad, norm_grads, gate_up_rows, out_rows):
    group = slopes.shape[0]
    rows = group // shards
    width = D // shards
    share = width // 8
    vm = pl.BlockSpec(memory_space=pltpu.VMEM)
    any_ = pl.BlockSpec(memory_space=pl.ANY)
    dma = pltpu.SemaphoreType.DMA
    low = jnp.bfloat16
    f32 = jnp.float32
    return pl.pallas_call(
        functools.partial(input_back_kernel, shards),
        out_shape=[
            jax.ShapeDtypeStruct((rows, D), f32),
            jax.ShapeDtypeStruct((8, width), f32),
            jax.ShapeDtypeStruct((width, 3 * D), low),
            jax.ShapeDtypeStruct((width, D), low),
            jax.ShapeDtypeStruct((width, gate_up_rows.shape[1]), low),
        ],
        in_specs=[vm, any_, any_, vm, vm, vm, vm, vm, any_, any_],
        out_specs=[vm, vm, any_, any_, any_],
        scratch_shapes=[
            pltpu.VMEM(weight.shape, low), pltpu.VMEM(normed.shape, low), pltpu.VMEM((rows, D), f32),
            pltpu.VMEM((shards, 8, width), f32), pltpu.VMEM((shards + 3, 8, width), f32),
        ] + line_scratch(shards, rows, D, 3) + reducer_scratch(shards, share, 3 * width)
        + [pltpu.VMEM((share, 3 * D), low), dma((shards + 3,)), dma((shards + 3,)), dma((2,))]
        + owner_sems(shards, 3) + gatherer_sems() * 3,
        compiler_params=pltpu.CompilerParams(collective_id=8, has_side_effects=True, vmem_limit_bytes=60 * 2**20),
        name="input_back",
        cost_estimate=pl.CostEstimate(flops=10**10, bytes_accessed=200 * 10**6, transcendentals=0),
    )(slopes, weight, normed, tokens, gain, d_middle, bias_grad, norm_grads, gate_up_rows, out_rows)


def swap_pieces(pieces):
    shards = lax.axis_size("shard")
    here = lax.axis_index("shard")
    out = pieces
    for k in range(1, shards):
        partner = jnp.bitwise_xor(here, k)
        piece = lax.dynamic_index_in_dim(pieces, partner, axis=0, keepdims=True)
        piece = lax.ppermute(piece, "shard", [(i, i ^ k) for i in range(shards)])
        out = lax.dynamic_update_slice_in_dim(out, piece, partner, axis=0)
    return out


def own_share(rows):
    own = rows.shape[0] // lax.axis_size("replica")
    return lax.dynamic_slice_in_dim(rows, lax.axis_index("replica") * own, own, axis=0)


def spread_rows(rows, columns):
    shards = lax.axis_size("shard")
    piece = own_share(rows)
    own = piece.shape[0]
    piece = piece.reshape(own, columns, shards, -1).transpose(2, 0, 1, 3).reshape(shards, own, -1)
    full = lax.all_gather(swap_pieces(piece), "replica", axis=0, tiled=False)
    return full.transpose(1, 0, 2, 3).reshape(rows.shape[0] * shards, -1)


def gather_rows(rows):
    shards = lax.axis_size("shard")
    piece = own_share(rows)
    moved = swap_pieces(jnp.broadcast_to(piece[None], (shards,) + piece.shape))
    full = lax.all_gather(moved, "replica", axis=0, tiled=False)
    return full.transpose(1, 0, 2, 3).reshape(rows.shape[0] * shards, -1)


def own_rows(features):
    copies = lax.axis_size("replica")
    shards = lax.axis_size("shard")
    count = features.shape[0]
    return (
        features.reshape(count, shards, copies, -1).transpose(0, 2, 1, 3).reshape(count, -1)
    )


def sum_columns(features, slopes, columns):
    shards = lax.axis_size("shard")
    term = contract_first(own_rows(features), slopes).astype(jnp.bfloat16)
    part = lax.psum_scatter(term, "replica", scatter_dimension=0, tiled=True)
    own = part.shape[0] // shards
    moved = swap_pieces(part.reshape(shards, own, -1))
    moved = moved.reshape(shards, own, columns, -1).transpose(1, 2, 0, 3).reshape(own, -1)
    return lax.all_gather(moved, "replica", axis=0, tiled=True)


def swiglu(gate_up):
    half = gate_up.shape[1] // 2
    return jax.nn.silu(gate_up[:, :half]) * gate_up[:, half:]


def norm_stats(values):
    mean = jnp.mean(values, axis=-1, keepdims=True)
    centered = values - mean
    inverse = lax.rsqrt(jnp.mean(centered * centered, axis=-1, keepdims=True) + norm_eps)
    return centered * inverse, inverse


def norm_back(slope, unit, inverse, gain):
    scaled = slope * gain
    return inverse * (
        scaled
        - jnp.mean(scaled, axis=-1, keepdims=True)
        - unit * jnp.mean(scaled * unit, axis=-1, keepdims=True)
    )


def start_plain(tokens, vectors, qkv_weight, cosine, minus, plus):
    shards = lax.axis_size("shard")
    here = lax.axis_index("shard")
    all_tokens = lax.all_gather(tokens, "shard", axis=0, tiled=False)
    all_vectors = lax.all_gather(vectors, "shard", axis=0, tiled=False)
    weight = spread_rows(qkv_weight, 3)
    width = D // shards
    gain, shift = (all_vectors[:, 3 + i].reshape(D) for i in (0, 1))
    unit, _ = norm_stats(all_tokens.reshape(-1, D).astype(jnp.float32))
    normed = (unit * gain + shift).astype(jnp.bfloat16)
    bias = all_vectors[:, :3].reshape(3, shards, width)
    bias = lax.dynamic_index_in_dim(bias, here, axis=1, keepdims=False).reshape(3 * width)
    value = jnp.dot(normed, weight, preferred_element_type=jnp.float32) + bias
    turned = value[:, : 2 * width]
    wide = [jnp.tile(t, (1, 2 * width // 128)) for t in (cosine, minus, plus)]
    turned = (
        turned * wide[0] + jnp.roll(turned, -8, 1) * wide[1] + jnp.roll(turned, 8, 1) * wide[2]
    )
    qkv = jnp.concatenate([turned, value[:, 2 * width :]], axis=1).astype(jnp.bfloat16)
    return all_tokens, all_vectors, normed, qkv, weight


def layer_kernels(shards, tokens, cotangent, weights, vectors, tables):
    qkv_weight, out_weight, gate_up_weight, down_weight = weights
    seg_rows, seg_columns, cosine, minus, plus = tables
    rows = tokens.shape[0]
    f32 = jnp.float32
    low = jnp.bfloat16
    all_tokens, all_vectors, normed, qkv, weight_qkv, weight_out = start_call(
        shards, tokens, vectors, qkv_weight, out_weight, cosine, minus, plus
    )
    gain_one, shift_one, gain_two, shift_two = (
        all_vectors[:, 3 + i].reshape(1, D) for i in range(4)
    )
    attended, stats, weight_gate_up = attend_spread_call(
        shards, rows, qkv, seg_rows, seg_columns, gate_up_weight
    )
    middle, normed_two, hidden, slopes, group_cotangent, down_part = hidden_call(
        shards, attended, all_tokens, weight_out, weight_gate_up, down_weight, cotangent, gain_two, shift_two
    )
    down_own = lax.psum_scatter(down_part, "shard", scatter_dimension=0, tiled=True)
    d_normed_two, down_share, gate_up_first = hidden_back_call(
        shards, slopes, weight_gate_up, hidden, group_cotangent.reshape(shards * rows, D), normed_two
    )
    d_middle, norm_grads, d_qkv, bias_grad, gate_up_rows, out_rows, down_grad = heads_back_call(
        shards, rows, d_normed_two, middle, cotangent, gain_two, weight_out, qkv, stats, seg_rows, seg_columns,
        cosine, minus, plus, normed_two, slopes, attended, down_share, gate_up_first,
    )
    input_grad, small, qkv_grad, out_grad, gate_up_grad = input_back_call(
        shards, d_qkv, weight_qkv, normed, tokens, gain_one, d_middle, bias_grad, norm_grads, gate_up_rows, out_rows
    )
    mixed = (middle + down_own.astype(f32)).astype(low)
    return mixed, input_grad, small, (qkv_grad, out_grad, gate_up_grad, down_grad)


def layer_plain(shards, tokens, cotangent, weights, vectors, tables):
    qkv_weight, out_weight, gate_up_weight, down_weight = weights
    seg_rows, seg_columns, cosine, minus, plus = tables
    here = lax.axis_index("shard")
    row_count = tokens.shape[0]
    group_rows = row_count * shards
    width = D // shards
    f32 = jnp.float32
    low = jnp.bfloat16
    weight_out = gather_rows(out_weight)
    weight_gate_up = spread_rows(gate_up_weight, 2)
    all_tokens, all_vectors, normed_low, qkv, weight_qkv = start_plain(
        tokens, vectors, qkv_weight, cosine, minus, plus
    )
    gain_one, shift_one, gain_two, shift_two = (
        all_vectors[:, 3 + i].reshape(D) for i in range(4)
    )
    cotangent_later, qkv = lax.optimization_barrier((cotangent, qkv))
    group_cotangent = lax.all_gather(cotangent_later, "shard", axis=0, tiled=True)

    def local(array):
        return lax.dynamic_slice_in_dim(array, here * row_count, row_count, axis=0)

    attended, stats = attend_call(shards, row_count, qkv, seg_rows, seg_columns)
    inputs = all_tokens.reshape(group_rows, D).astype(f32)
    middle = inputs + jnp.dot(attended, weight_out, preferred_element_type=f32)
    unit_two, inverse_two = norm_stats(middle)
    normed_two_low = (unit_two * gain_two + shift_two).astype(low)
    gate_up = jnp.dot(normed_two_low, weight_gate_up, preferred_element_type=f32)
    hidden, swiglu_pull = jax.vjp(swiglu, gate_up)
    hidden_low = hidden.astype(low)
    d_hidden = contract_last(group_cotangent, down_weight)
    d_gate_up_low = swiglu_pull(d_hidden)[0].astype(low)
    down_part = jnp.dot(hidden_low, down_weight, preferred_element_type=f32).astype(low)
    unit_two_own = local(unit_two)
    inverse_two_own = local(inverse_two)
    middle_own = local(middle)

    d_normed_two_part = contract_last(d_gate_up_low, weight_gate_up).astype(low)
    d_normed_two = scatter_call(shards, d_normed_two_part.reshape(shards, row_count, D), 3)
    down_grad = lax.psum(contract_first(hidden_low, group_cotangent).astype(low), "replica")
    d_middle = cotangent.astype(f32) + norm_back(
        d_normed_two, unit_two_own, inverse_two_own, gain_two
    )
    d_gain_two = jnp.sum(d_normed_two * unit_two_own, axis=0)
    d_shift_two = jnp.sum(d_normed_two, axis=0)
    d_middle_low = d_middle.astype(low)
    d_attended_own = contract_last(d_middle_low, weight_out).astype(low)
    d_attended, d_middle_columns = exchange_call(shards, d_attended_own, d_middle_low)
    d_projected_low, bias_part = attend_back_call(
        row_count, qkv, d_attended.reshape(group_rows, width), stats, seg_rows, seg_columns,
        cosine, minus, plus,
    )
    down_own = lax.psum_scatter(down_part, "shard", scatter_dimension=0, tiled=True)
    mixed = (middle_own + down_own.astype(f32)).astype(low)
    d_normed_part = contract_last(d_projected_low, weight_qkv).astype(low)
    d_normed = scatter_call(shards, d_normed_part.reshape(shards, row_count, D), 4)
    gate_up_grad = sum_columns(normed_two_low, d_gate_up_low, 2)
    out_grad = sum_columns(attended, d_middle_columns.reshape(group_rows, width), 1)
    qkv_grad = sum_columns(normed_low, d_projected_low, 3)
    unit_one, inverse_one = norm_stats(tokens.astype(f32))
    input_grad = d_middle + norm_back(d_normed, unit_one, inverse_one, gain_one)
    d_gain_one = jnp.sum(d_normed * unit_one, axis=0)
    d_shift_one = jnp.sum(d_normed, axis=0)

    bias_part = bias_part[0].reshape(3, 1, width)
    bias_wide = lax.dynamic_update_slice(
        jnp.zeros((3, shards, width), f32), bias_part, (0, here, 0)
    ).reshape(shards, 3 * width)
    small = jnp.concatenate(
        [bias_wide]
        + [v.reshape(shards, width) for v in (d_gain_one, d_shift_one, d_gain_two, d_shift_two)],
        axis=1,
    )
    small = jnp.pad(small, ((0, 0), (0, width)))
    small = lax.psum(small, ("replica", "shard"))
    small = lax.dynamic_index_in_dim(small, here, axis=0, keepdims=False)
    return mixed, input_grad, small, (qkv_grad, out_grad, gate_up_grad, down_grad)


def on_device(
    tokens,
    cotangent,
    qkv_weight,
    qkv_bias,
    out_weight,
    gate_up_weight,
    down_weight,
    norm1_gain,
    norm1_shift,
    norm2_gain,
    norm2_shift,
    seq_lengths,
):
    shards = lax.axis_size("shard")
    copies = lax.axis_size("replica")
    row_count = tokens.shape[0]
    group_rows = row_count * shards
    width = D // shards
    f32 = jnp.float32
    low = jnp.bfloat16

    index = jnp.arange(group_rows, dtype=jnp.int32)
    segment, position = group_layout(seq_lengths[0], index)
    seg_rows = jnp.broadcast_to(segment[:, None], (group_rows, 128))
    seg_columns = jnp.broadcast_to(segment[None, :], (8, group_rows))
    cosine, sine_value = rope_tables(position)
    half_rot = ROT_DIM // 2
    rest = HEAD_DIM - ROT_DIM
    none = jnp.zeros((group_rows, half_rot), f32)
    empty = jnp.zeros((group_rows, rest), f32)
    cosine = jnp.tile(jnp.concatenate([cosine, cosine, empty + 1.0], axis=1), (1, 2))
    minus = jnp.tile(jnp.concatenate([-sine_value, none, empty], axis=1), (1, 2))
    plus = jnp.tile(jnp.concatenate([none, sine_value, empty], axis=1), (1, 2))

    vectors = jnp.concatenate(
        [qkv_bias, norm1_gain, norm1_shift, norm2_gain, norm2_shift, jnp.zeros((width,), low)]
    )
    vectors = vectors.astype(f32).reshape(8, width)
    weights = (qkv_weight, out_weight, gate_up_weight, down_weight)
    tables = (seg_rows, seg_columns, cosine, minus, plus)
    if copies == 8:
        outputs = layer_kernels(shards, tokens, cotangent, weights, vectors, tables)
    else:
        outputs = layer_plain(shards, tokens, cotangent, weights, vectors, tables)
    mixed, input_grad, small, grads = outputs
    bias_rows = 3 * width
    small = small.reshape(8 * width)
    out_dtype = tuple(grad.astype(f32) for grad in grads)
    return (
        mixed,
        input_grad,
        out_dtype[0],
        small[:bias_rows],
        out_dtype[1],
        out_dtype[2],
        out_dtype[3],
    ) + tuple(small[bias_rows + i * width : bias_rows + (i + 1) * width] for i in range(4))


def solution(mesh):
    placed = (
        P(("replica", "shard"), None),
        P(("replica", "shard"), None),
        P("shard", None),
        P("shard"),
        P("shard", None),
        P("shard", None),
        P("shard", None),
        P("shard"),
        P("shard"),
        P("shard"),
        P("shard"),
        P("replica", None),
    )
    return jax.shard_map(
        on_device,
        mesh=mesh,
        in_specs=placed,
        out_specs=(
            P(("replica", "shard"), None),
            P(("replica", "shard"), None),
            P("shard", None),
            P("shard"),
            P("shard", None),
            P("shard", None),
            P("shard", None),
            P("shard"),
            P("shard"),
            P("shard"),
            P("shard"),
        ),
        check_vma=False,
    )
```

```python
import functools

import jax
import jax.numpy as jnp
from jax import lax
from jax.experimental import pallas as pl
from jax.experimental.pallas import tpu as pltpu
from jax.sharding import PartitionSpec as P

D = 2048
FF = 5632
HEADS = 32
HEAD_DIM = 64
ROT_DIM = 16
MESH = pl.DeviceIdType.MESH


norm_eps = 1e-05
masked_score = -1000000000.0


def group_layout(lengths, token_index):
    segment = jnp.zeros_like(token_index)
    position = token_index
    end = jnp.int32(0)
    for i in range(lengths.shape[0]):
        end = end + lengths[i]
        passed = (token_index >= end).astype(jnp.int32)
        segment = segment + passed
        position = position - passed * lengths[i]
    return (segment, position)


def rope_tables(position, index):
    frequency = jnp.exp(-jnp.log(10000.0) * (2.0 * index.astype(jnp.float32) / ROT_DIM))
    angles = position.astype(jnp.float32)[:, None] * frequency
    return (jnp.cos(angles), jnp.sin(angles))


def contract_last(left, right):
    return lax.dot_general(
        left, right, (((1,), (1,)), ((), ())), preferred_element_type=jnp.float32
    )


def aligned(value, unit):
    return pl.multiple_of(value * unit, unit)


def greet(partners, count):
    barrier = pltpu.get_barrier_semaphore()
    for there, device in partners:
        @pl.when(there)
        def _():
            pl.semaphore_signal(barrier, inc=1, device_id=device, device_id_type=MESH)
    pl.semaphore_wait(barrier, count)


def greet_line(z, shards):
    count = (z + shards - 1) // shards + (2 * shards - 2 - z) // shards
    greet([(z >= 1, {"shard": z - 1}), (z + 1 < shards, {"shard": z + 1})], count)


def remote(source, target, send, recv, device):
    return pltpu.make_async_remote_copy(
        src_ref=source, dst_ref=target, send_sem=send, recv_sem=recv,
        device_id=device, device_id_type=MESH,
    )


class Cube:
    def __init__(self):
        r = lax.axis_index("replica")
        self.core, self.x, self.y = r % 2, (r // 2) % 2, r // 4
        self.place = 2 * self.y + self.x
        self.to_x = {"replica": r + 2 - 4 * self.x}
        self.to_y = {"replica": r + 4 - 8 * self.y}
        self.to_core = {"replica": r + 1 - 2 * self.core}

    def partners(self, shards):
        z = lax.axis_index("shard")
        return [((z != o), {"shard": o}) for o in range(shards)] + [
            (z >= 0, d) for d in (self.to_x, self.to_y, self.to_core)
        ]


def rows_of(ref, start, unit, count):
    return ref.at[pl.ds(pl.multiple_of(start, unit), count)]


class Spreader:
    def __init__(self, cube, shards, share, parts, source, out, sems):
        self.cube, self.shards, self.share, self.parts = cube, shards, share, parts
        self.source, self.out = source, out
        self.z_send, self.z_recv, self.send, self.recv, self.loc = sems
        self.cut = 16 * ((share // 16 + 1) // 2)
        self.z = lax.axis_index("shard")
        r = lax.axis_index("replica")
        self.who = (r, r + 2 - 4 * cube.x, r + 4 - 8 * cube.y, 4 * (1 - cube.y) + 2 * (1 - cube.x) + cube.core)

    def rows(self, o, kind, half=None):
        first, count = {None: (0, self.share), 0: (0, self.cut), 1: (self.cut, self.share - self.cut)}[half]
        return rows_of(self.out, (o * 8 + self.who[kind]) * self.share + first, 16, count)

    def target(self, o, part):
        width = self.out.shape[1] // self.parts
        return self.rows(o, 0).at[:, pl.ds(part * width, width)]

    def z_copy(self, o, part):
        return remote(self.source(o, part), self.target(self.z, part), self.z_send.at[o, part], self.z_recv.at[self.z, part], {"shard": o})

    def z_arrival(self, o, part):
        place = self.target(o, part)
        return remote(place, place, self.z_send.at[o, part], self.z_recv.at[o, part], {"shard": o})

    def local(self, o, part):
        return pltpu.make_async_copy(self.source(o, part), self.target(o, part), self.loc.at[part])

    def start_own(self):
        for part in range(self.parts):
            self.local(self.z, part).start()

    def start(self):
        for o in range(self.shards):
            for part in range(self.parts):
                @pl.when(self.z != o)
                def _():
                    self.z_copy(o, part).start()

    def sent(self):
        for o in range(self.shards):
            for part in range(self.parts):
                @pl.when(self.z != o)
                def _():
                    self.z_copy(o, part).wait_send()

    def copy(self, kind, o):
        c = self.cube
        block, device = (
            (self.rows(o, 0), c.to_x),
            (self.rows(o, 0), c.to_y),
            (self.rows(o, 1, 0), c.to_y),
            (self.rows(o, 2, 1), c.to_x),
            (self.rows(o, 0), c.to_core),
            (self.rows(o, 1), c.to_core),
            (self.rows(o, 2), c.to_core),
            (self.rows(o, 3), c.to_core),
        )[kind]
        return remote(block, block, self.send.at[kind, o], self.recv.at[kind, o], device)

    def arrive(self, distance):
        for o in range(self.shards):
            @pl.when((self.z - o == distance) | (o - self.z == distance))
            def _():
                for part in range(self.parts):
                    if distance == 0:
                        self.local(o, part).wait()
                    else:
                        self.z_arrival(o, part).wait_recv()
                for kind in (0, 1, 4):
                    self.copy(kind, o).start()

    def pass_on(self, o):
        self.copy(0, o).wait_recv()
        self.copy(2, o).start()
        self.copy(5, o).start()
        self.copy(1, o).wait_recv()
        self.copy(3, o).start()
        self.copy(6, o).start()

    def pass_last(self, o):
        self.copy(2, o).wait_recv()
        self.copy(3, o).wait_recv()
        self.copy(7, o).start()

    def landed(self):
        for o in range(self.shards):
            for kind in (4, 5, 6, 7):
                self.copy(kind, o).wait_recv()

    def finish(self):
        for o in range(self.shards):
            for kind in range(8):
                self.copy(kind, o).wait_send()


def spread_sems(shards, parts):
    dma = pltpu.SemaphoreType.DMA
    return [dma((shards, parts)), dma((shards, parts)), dma((8, shards)), dma((8, shards)), dma((parts,))]


class Line:
    def __init__(self, shards, pieces, own, buf, send, recv):
        self.z = lax.axis_index("shard")
        self.shards, self.pieces, self.own, self.buf, self.send, self.recv = shards, pieces, own, buf, send, recv
        self.rows = buf.shape[1] // pieces

    def copy(self, way, step, piece):
        target = self.z + 1 if way == 0 else self.z - 1
        owner = self.z - step if way == 0 else self.z + step
        block = pl.ds(piece * self.rows, self.rows)
        place = self.buf.at[owner, block]
        source = self.own.at[block] if step == 0 and self.own is not None else place
        return remote(source, place, self.send.at[way, step, piece], self.recv.at[way, step, piece], {"shard": target})

    def sends(self, way, step):
        if way == 0:
            return (self.z + 1 < self.shards) & (self.z - step >= 0)
        return (self.z >= 1) & (self.z + step < self.shards)

    def gets(self, way, step):
        return (self.z - step >= 1) if way == 0 else (self.z + step + 1 < self.shards)

    def start(self, piece):
        for way in (0, 1):
            @pl.when(self.sends(way, 0))
            def _():
                self.copy(way, 0, piece).start()

    def relay(self, step, piece):
        for way in (0, 1):
            @pl.when(self.gets(way, step))
            def _():
                self.copy(way, step, piece).wait_recv()
            if step + 1 < self.shards - 1:
                @pl.when(self.sends(way, step + 1))
                def _():
                    self.copy(way, step + 1, piece).start()

    def finish(self):
        for step in range(self.shards - 1):
            for piece in range(self.pieces):
                for way in (0, 1):
                    @pl.when(self.sends(way, step))
                    def _():
                        self.copy(way, step, piece).wait_send()


def line_sems(shards, pieces):
    dma = pltpu.SemaphoreType.DMA
    return [dma((2, shards - 1, pieces)), dma((2, shards - 1, pieces))]


def layer_norm_rows(values, gain, shift):
    centered = values - jnp.mean(values, axis=-1, keepdims=True)
    spread = jnp.mean(centered * centered, axis=-1, keepdims=True)
    return (centered * lax.rsqrt(spread + norm_eps) * gain + shift).astype(jnp.bfloat16)


def bias_piece(v_buf, z, t, tile, shards, per_part):
    flat = (t // per_part) * shards + z
    return v_buf[flat // 3, pl.ds(flat % 3, 1), pl.ds(aligned(t % per_part, tile), tile)]


def start_kernel(shards, tokens, vectors, weight, out_weight, cosine, minus, plus,
                 all_tokens, all_vectors, normed, qkv, kept_weight, all_out,
                 x_buf, v_buf, w_buf, n_buf, q_buf, *sems):
    cube = Cube()
    z = lax.axis_index("shard")
    r = lax.axis_index("replica")
    rows = tokens.shape[0]
    share = weight.shape[0] // 8
    width = w_buf.shape[1] // 3
    x_send, x_recv, v_send, v_recv, loc = sems[:5]
    line = Line(shards, 1, tokens, x_buf, x_send, x_recv)
    mine = pl.ds(aligned(r, share), share)
    spread = Spreader(
        cube, shards, share, 3,
        lambda o, part: weight.at[mine, pl.ds(aligned(part * shards + o, width), width)], w_buf, sems[5:10],
    )
    spread_out = Spreader(cube, shards, share, 1, lambda o, part: out_weight.at[mine], all_out, sems[10:15])
    greet(cube.partners(shards), shards + 2)

    def v_copy(o):
        return remote(vectors, v_buf.at[z], v_send.at[o], v_recv.at[z], {"shard": o})

    def v_arrival(o):
        return remote(vectors, v_buf.at[o], v_send.at[o], v_recv.at[o], {"shard": o})

    own_x = pltpu.make_async_copy(tokens, x_buf.at[z], loc.at[0, 0])
    own_v = pltpu.make_async_copy(vectors, v_buf.at[z], loc.at[1, 0])
    own_x.start()
    own_v.start()
    for o in range(shards):
        @pl.when(z != o)
        def _():
            v_copy(o).start()
    spread.start_own()
    spread_out.start_own()
    spread.start()
    spread.arrive(0)
    spread_out.arrive(0)
    line.start(0)
    spread_out.start()
    for distance in range(1, shards):
        spread.arrive(distance)
    own_x.wait()
    own_v.wait()
    for o in range(shards):
        @pl.when(z != o)
        def _():
            v_arrival(o).wait_recv()
    keep_v = pltpu.make_async_copy(v_buf, all_vectors, loc.at[2, 0])
    keep_v.start()
    gain = jnp.concatenate([v_buf[o, 3:4, :] for o in range(shards)], axis=1)
    shift = jnp.concatenate([v_buf[o, 4:5, :] for o in range(shards)], axis=1)

    def put(source, target, o, i):
        block = pl.ds(aligned(o, rows), rows)
        copy = pltpu.make_async_copy(source.at[block], target.at[block], loc.at[4 + i, o])
        copy.start()

    def normalize(o):
        @pl.loop(0, rows // 32)
        def _(i):
            values = x_buf[o, pl.ds(aligned(i, 32), 32), :].astype(jnp.float32)
            n_buf[pl.ds(pl.multiple_of(o * rows + i * 32, 32), 32), :] = layer_norm_rows(values, gain, shift)
        put(n_buf, normed, o, 0)
        pltpu.make_async_copy(x_buf.at[o], all_tokens.at[o], loc.at[6, o]).start()

    tile = 256
    per_part = width // tile

    def project(o):
        block = pl.ds(aligned(o, rows), rows)

        @pl.loop(0, 3 * per_part)
        def _(t):
            columns = pl.ds(aligned(t, tile), tile)
            value = jnp.dot(n_buf[block, :], w_buf[:, columns], preferred_element_type=jnp.float32)
            value = value + bias_piece(v_buf, z, t, tile, shards, per_part)

            @pl.when(t < 2 * per_part)
            def _():
                wide, wide_minus, wide_plus = (
                    jnp.concatenate([table[block, :]] * (tile // 128), axis=1) for table in (cosine, minus, plus)
                )
                turned = value * wide + pltpu.roll(value, tile - 8, 1) * wide_minus + pltpu.roll(value, 8, 1) * wide_plus
                q_buf[block, columns] = turned.astype(jnp.bfloat16)

            @pl.when(t >= 2 * per_part)
            def _():
                q_buf[block, columns] = value.astype(jnp.bfloat16)
        put(q_buf, qkv, o, 1)

    normalize(z)
    line.relay(0, 0)
    for o in range(shards):
        spread.pass_on(o)
    for o in range(shards):
        spread.pass_last(o)
    spread.landed()
    keep_w = pltpu.make_async_copy(w_buf, kept_weight, loc.at[3, 0])
    keep_w.start()
    project(z)
    for distance in range(1, shards):
        spread_out.arrive(distance)
    for step in range(shards - 1):
        if step > 0:
            line.relay(step, 0)
        for way in (0, 1):
            owner = z - step - 1 if way == 0 else z + step + 1

            @pl.when(line.gets(way, step))
            def _():
                normalize(owner)
                project(owner)
        if step == min(1, shards - 2):
            for o in range(shards):
                spread_out.pass_on(o)
    for o in range(shards):
        spread_out.pass_last(o)
    spread_out.landed()
    line.finish()
    spread.sent()
    spread.finish()
    spread_out.sent()
    spread_out.finish()
    for o in range(shards):
        block = pl.ds(o * rows, rows)

        @pl.when(z != o)
        def _():
            v_copy(o).wait_send()
        pltpu.make_async_copy(n_buf.at[block], normed.at[block], loc.at[4, o]).wait()
        pltpu.make_async_copy(q_buf.at[block], qkv.at[block], loc.at[5, o]).wait()
        pltpu.make_async_copy(x_buf.at[o], all_tokens.at[o], loc.at[6, o]).wait()
    keep_v.wait()
    keep_w.wait()


def start_call(shards, tokens, vectors, weight, out_weight, cosine, minus, plus):
    rows = tokens.shape[0]
    group = rows * shards
    depth = weight.shape[0]
    width = weight.shape[1] // shards
    any_ = pl.BlockSpec(memory_space=pl.ANY)
    vm = pl.BlockSpec(memory_space=pltpu.VMEM)
    low = jnp.bfloat16
    dma = pltpu.SemaphoreType.DMA
    return pl.pallas_call(
        functools.partial(start_kernel, shards),
        out_shape=[
            jax.ShapeDtypeStruct((shards, rows, D), low),
            jax.ShapeDtypeStruct((shards,) + vectors.shape, vectors.dtype),
            jax.ShapeDtypeStruct((group, D), low),
            jax.ShapeDtypeStruct((group, width), low),
            jax.ShapeDtypeStruct((depth * shards, width), low),
            jax.ShapeDtypeStruct((depth * shards, D), low),
        ],
        in_specs=[any_] * 4 + [vm] * 3,
        out_specs=[any_] * 6,
        scratch_shapes=[
            pltpu.VMEM((shards, rows, D), low),
            pltpu.VMEM((shards,) + vectors.shape, vectors.dtype),
            pltpu.VMEM((depth * shards, width), low),
            pltpu.VMEM((group, D), low),
            pltpu.VMEM((group, width), low),
        ] + line_sems(shards, 1) + [dma((shards,)), dma((shards,)), dma((7, shards))]
        + spread_sems(shards, 3) + spread_sems(shards, 1),
        compiler_params=pltpu.CompilerParams(
            collective_id=1, has_side_effects=True, vmem_limit_bytes=48 * 2**20
        ),
        name="start",
        cost_estimate=pl.CostEstimate(flops=2 * group * D * width, bytes_accessed=150 * 10**6, transcendentals=0),
    )(tokens, vectors, weight, out_weight, cosine, minus, plus)


def attend_spread_kernel(shards, rows, qkv, seg_rows, seg_columns, gate_up, attended, stats, all_gate_up, a_buf, *sems):
    cube = Cube()
    z = lax.axis_index("shard")
    r = lax.axis_index("replica")
    width = qkv.shape[1] // 3
    blocks = qkv.shape[0] // rows
    share = gate_up.shape[0] // 8
    half = all_gate_up.shape[1] // 2
    mine = pl.ds(aligned(r, share), share)
    spread = Spreader(
        cube, shards, share, 2,
        lambda o, part: gate_up.at[mine, pl.ds(aligned((part * shards + o) * (half // 128), 128), half)], all_gate_up, sems[3:8],
    )
    line = Line(shards, blocks, None, a_buf, sems[0], sems[1])
    loc = sems[2]
    greet(cube.partners(shards), shards + 2)
    spread.start_own()
    spread.start()
    spread.arrive(0)

    def done(block):
        line.start(block)
        if 0 < block < shards:
            spread.arrive(block)

    attend_body(rows, qkv, seg_rows, seg_columns, a_buf, stats, done)
    moves = [functools.partial(line.relay, step, block) for step in range(shards - 1) for block in range(blocks)]
    steps = [functools.partial(spread.pass_on, o) for o in range(shards)]
    steps += [functools.partial(spread.pass_last, o) for o in range(shards)]
    for i in range(max(len(moves), len(steps))):
        if i < len(moves):
            moves[i]()
        if i < len(steps):
            steps[i]()
    keep = [pltpu.make_async_copy(a_buf.at[o], attended.at[:, pl.ds(o * width, width)], loc.at[o]) for o in range(shards)]
    for copy in keep:
        copy.start()
    spread.landed()
    line.finish()
    spread.sent()
    spread.finish()
    for copy in keep:
        copy.wait()


def attend_spread_call(shards, rows, qkv, seg_rows, seg_columns, gate_up):
    group = qkv.shape[0]
    width = qkv.shape[1] // 3
    blocks = group // rows
    vm = pl.BlockSpec(memory_space=pltpu.VMEM)
    any_ = pl.BlockSpec(memory_space=pl.ANY)
    dma = pltpu.SemaphoreType.DMA
    low = jnp.bfloat16
    return pl.pallas_call(
        functools.partial(attend_spread_kernel, shards, rows),
        out_shape=[
            jax.ShapeDtypeStruct((group, shards * width), low),
            jax.ShapeDtypeStruct((group, 128), jnp.float32),
            jax.ShapeDtypeStruct((gate_up.shape[0] * shards, gate_up.shape[1] // shards), low),
        ],
        in_specs=[vm, vm, vm, any_],
        out_specs=[any_, vm, any_],
        scratch_shapes=[pltpu.VMEM((shards, group, width), low)] + line_sems(shards, blocks) + [dma((shards,))]
        + spread_sems(shards, 2),
        compiler_params=pltpu.CompilerParams(
            collective_id=2, has_side_effects=True, vmem_limit_bytes=48 * 2**20
        ),
        name="attend_spread",
        cost_estimate=pl.CostEstimate(flops=10**9, bytes_accessed=150 * 10**6, transcendentals=0),
    )(qkv, seg_rows, seg_columns, gate_up)


def hidden_kernel(shards, attended, tokens, out_weight, gate_up_weight, down_weight, cotangent, gain, shift,
                  middle_own, normed_two, hidden, slopes, all_cotangent, down_part,
                  a_buf, x_buf, o_buf, g_buf, d_buf, c_buf, mid, n_buf, gu, h_buf, s_buf, c_send, c_recv, loc):
    z = lax.axis_index("shard")
    greet_line(z, shards)
    rows = cotangent.shape[0]
    group = rows * shards
    inner = h_buf.shape[1]
    line = Line(shards, 1, cotangent, c_buf, c_send, c_recv)
    line.start(0)
    load = [pltpu.make_async_copy(source, target, loc.at[i]) for i, (source, target) in enumerate((
        (attended, a_buf), (out_weight, o_buf), (tokens, x_buf), (gate_up_weight, g_buf), (down_weight, d_buf),
        (cotangent, c_buf.at[z])))]
    for copy in load:
        copy.start()
    for copy in load[:3]:
        copy.wait()
    tile = 256
    span = 2 * rows
    for part in range(group // span):
        at = part * span

        @pl.loop(0, D // tile)
        def _(t):
            columns = pl.ds(aligned(t, tile), tile)
            value = jnp.dot(a_buf[at : at + span, :], o_buf[:, columns], preferred_element_type=jnp.float32)
            for k in range(2):
                mid[k * rows : (k + 1) * rows, columns] = (
                    value[k * rows : (k + 1) * rows] + x_buf[2 * part + k, :, columns].astype(jnp.float32)
                )

        @pl.loop(0, span // 32)
        def _(i):
            block = pl.ds(aligned(i, 32), 32)
            n_buf[pl.ds(pl.multiple_of(at + i * 32, 32), 32), :] = layer_norm_rows(mid[block, :], gain[...], shift[...])
        for k in range(2):
            @pl.when(z == 2 * part + k)
            def _():
                middle_own[...] = mid[k * rows : (k + 1) * rows, :]
    keep_n = pltpu.make_async_copy(n_buf, normed_two, loc.at[6])
    keep_n.start()
    line.relay(0, 0)
    load[3].wait()

    @pl.loop(0, 2 * inner // tile)
    def _(t):
        columns = pl.ds(aligned(t, tile), tile)
        gu[:, columns] = jnp.dot(n_buf[...], g_buf[:, columns], preferred_element_type=jnp.float32)

    @pl.loop(0, group // 32)
    def _(i):
        block = pl.ds(aligned(i, 32), 32)
        gate = gu[block, :inner]
        h_buf[block, :] = (gate / (1.0 + jnp.exp(-gate)) * gu[block, inner:]).astype(jnp.bfloat16)
    keep_h = pltpu.make_async_copy(h_buf, hidden, loc.at[7])
    keep_h.start()
    if shards > 2:
        line.relay(1, 0)
    load[4].wait()

    @pl.loop(0, D // tile)
    def _(t):
        columns = pl.ds(aligned(t, tile), tile)
        a_buf[:, columns] = jnp.dot(h_buf[...], d_buf[:, columns], preferred_element_type=jnp.float32).astype(jnp.bfloat16)
    keep_p = pltpu.make_async_copy(a_buf, down_part, loc.at[8])
    keep_p.start()
    load[5].wait()

    def back(o):
        mid[:rows, :inner] = contract_last(c_buf[o], d_buf[...])

        @pl.loop(0, rows // 32)
        def _(i):
            value = mid[pl.ds(aligned(i, 32), 32), :inner]
            place = pl.ds(pl.multiple_of(o * rows + i * 32, 32), 32)
            gate = gu[place, :inner]
            up = gu[place, inner:]
            sigmoid = 1.0 / (1.0 + jnp.exp(-gate))
            s_buf[place, :inner] = (value * up * (sigmoid * (1.0 + gate * (1.0 - sigmoid)))).astype(jnp.bfloat16)
            s_buf[place, inner:] = (value * (gate * sigmoid)).astype(jnp.bfloat16)

    back(z)
    for step in range(shards - 1):
        if step >= 2:
            line.relay(step, 0)
        for way in (0, 1):
            owner = z - step - 1 if way == 0 else z + step + 1

            @pl.when(line.gets(way, step))
            def _():
                back(owner)
    keep = [pltpu.make_async_copy(c_buf, all_cotangent, loc.at[9]), pltpu.make_async_copy(s_buf, slopes, loc.at[10])]
    for copy in keep:
        copy.start()
    line.finish()
    for copy in keep + [keep_n, keep_h, keep_p]:
        copy.wait()


def hidden_call(shards, attended, tokens, out_weight, gate_up_weight, down_weight, cotangent, gain, shift):
    rows = cotangent.shape[0]
    group = rows * shards
    inner = down_weight.shape[0]
    low = jnp.bfloat16
    f32 = jnp.float32
    vm = pl.BlockSpec(memory_space=pltpu.VMEM)
    any_ = pl.BlockSpec(memory_space=pl.ANY)
    return pl.pallas_call(
        functools.partial(hidden_kernel, shards),
        out_shape=[
            jax.ShapeDtypeStruct((rows, D), f32),
            jax.ShapeDtypeStruct((group, D), low),
            jax.ShapeDtypeStruct((group, inner), low),
            jax.ShapeDtypeStruct((group, 2 * inner), low),
            jax.ShapeDtypeStruct((shards, rows, D), low),
            jax.ShapeDtypeStruct((group, D), low),
        ],
        in_specs=[any_] * 6 + [vm, vm],
        out_specs=[vm] + [any_] * 5,
        scratch_shapes=[
            pltpu.VMEM((group, D), low),
            pltpu.VMEM((shards, rows, D), low),
            pltpu.VMEM(out_weight.shape, low),
            pltpu.VMEM(gate_up_weight.shape, low),
            pltpu.VMEM(down_weight.shape, low),
            pltpu.VMEM((shards, rows, D), low),
            pltpu.VMEM((2 * rows, D), f32),
            pltpu.VMEM((group, D), low),
            pltpu.VMEM((group, 2 * inner), f32),
            pltpu.VMEM((group, inner), low),
            pltpu.VMEM((group, 2 * inner), low),
        ] + line_sems(shards, 1) + [pltpu.SemaphoreType.DMA((11,))],
        compiler_params=pltpu.CompilerParams(
            collective_id=9, has_side_effects=True, vmem_limit_bytes=63 * 2**20
        ),
        name="hidden",
        cost_estimate=pl.CostEstimate(flops=24 * 10**9, bytes_accessed=150 * 10**6, transcendentals=0),
    )(attended, tokens, out_weight, gate_up_weight, down_weight, cotangent, gain, shift)


def head_mask(even, rows):
    lane = lax.broadcasted_iota(jnp.int32, (rows, 128), 1)
    return (lane < HEAD_DIM) if even else (lane >= HEAD_DIM)


def only(values, keep):
    return jnp.where(keep, values.astype(jnp.float32), 0.0).astype(jnp.bfloat16)


def block_visible(at, rows, seg_rows, seg_columns):
    count = at + rows
    row = lax.broadcasted_iota(jnp.int32, (rows, count), 0) + at
    column = lax.broadcasted_iota(jnp.int32, (rows, count), 1)
    return (column <= row) & (seg_rows[at : at + rows, :1] == seg_columns[:1, :count])


def attend_body(rows, qkv, seg_rows, seg_columns, a_buf, stats, done):
    z = lax.axis_index("shard")
    width = qkv.shape[1] // 3
    pairs = width // 128
    scale = HEAD_DIM ** (-0.5)
    for block in range(qkv.shape[0] // rows):
        at = block * rows
        count = at + rows
        seen = block_visible(at, rows, seg_rows, seg_columns)
        for pair in range(pairs):
            lanes = slice(128 * pair, 128 * pair + 128)
            query = qkv[at:count, lanes]
            keys = qkv[:count, width + 128 * pair : width + 128 * pair + 128]
            values = qkv[:count, 2 * width + 128 * pair : 2 * width + 128 * pair + 128]
            results = []
            for odd in (0, 1):
                keep = head_mask(odd == 0, rows)
                scores = contract_last(only(query, keep), keys) * scale
                scores = jnp.where(seen, scores, masked_score)
                top = jnp.max(scores, axis=-1, keepdims=True)
                weights = jnp.exp(scores - top)
                total = jnp.sum(weights, axis=-1, keepdims=True)
                probs = (weights * (1.0 / total)).astype(jnp.bfloat16)
                results.append(jnp.dot(probs, values, preferred_element_type=jnp.float32))
                head = 2 * pair + odd
                stats[at:count, head : head + 1] = top
                stats[at:count, 64 + head : 65 + head] = 1.0 / total
            merged = jnp.where(head_mask(True, rows), results[0], results[1])
            a_buf[z, at:count, lanes] = merged.astype(jnp.bfloat16)
        done(block)


def attend_kernel(shards, rows, qkv, seg_rows, seg_columns, attended, stats, a_buf, a_send, a_recv, loc):
    z = lax.axis_index("shard")
    width = qkv.shape[1] // 3
    blocks = qkv.shape[0] // rows
    greet_line(z, shards)
    line = Line(shards, blocks, None, a_buf, a_send, a_recv)
    attend_body(rows, qkv, seg_rows, seg_columns, a_buf, stats, line.start)
    for step in range(shards - 1):
        for block in range(blocks):
            line.relay(step, block)
    keep = [pltpu.make_async_copy(a_buf.at[o], attended.at[:, pl.ds(o * width, width)], loc.at[o]) for o in range(shards)]
    for copy in keep:
        copy.start()
    line.finish()
    for copy in keep:
        copy.wait()


def attend_call(shards, rows, qkv, seg_rows, seg_columns):
    group = qkv.shape[0]
    width = qkv.shape[1] // 3
    blocks = group // rows
    vm = pl.BlockSpec(memory_space=pltpu.VMEM)
    any_ = pl.BlockSpec(memory_space=pl.ANY)
    dma = pltpu.SemaphoreType.DMA
    return pl.pallas_call(
        functools.partial(attend_kernel, shards, rows),
        out_shape=[
            jax.ShapeDtypeStruct((group, shards * width), jnp.bfloat16),
            jax.ShapeDtypeStruct((group, 128), jnp.float32),
        ],
        in_specs=[vm, vm, vm],
        out_specs=[any_, vm],
        scratch_shapes=[
            pltpu.VMEM((shards, group, width), jnp.bfloat16),
            dma((2, shards - 1, blocks)), dma((2, shards - 1, blocks)), dma((shards,)),
        ],
        compiler_params=pltpu.CompilerParams(
            collective_id=2, has_side_effects=True, vmem_limit_bytes=48 * 2**20
        ),
        name="attend",
        cost_estimate=pl.CostEstimate(flops=10**9, bytes_accessed=150 * 10**6, transcendentals=0),
    )(qkv, seg_rows, seg_columns)


def attend_back_kernel(rows, *refs):
    attend_back_body(rows, *refs, [])


def attend_back_body(rows, qkv, d_attended, stats, seg_rows, seg_columns, cosine, minus, plus,
                     d_qkv, bias_grad, d_keys, d_values, steps):
    width = qkv.shape[1] // 3
    group = qkv.shape[0]
    blocks = group // rows
    pairs = width // 128
    scale = HEAD_DIM ** (-0.5)

    def turned(value, at, count):
        return (value * cosine[at:count, :] - pltpu.roll(value, 120, 1) * minus[at:count, :]
                - pltpu.roll(value, 8, 1) * plus[at:count, :])

    for block in reversed(range(blocks)):
        at = block * rows
        count = at + rows
        seen = block_visible(at, rows, seg_rows, seg_columns)
        for pair in range(pairs):
            lanes = slice(128 * pair, 128 * pair + 128)
            query = qkv[at:count, lanes]
            keys = qkv[:count, width + 128 * pair : width + 128 * pair + 128]
            values = qkv[:count, 2 * width + 128 * pair : 2 * width + 128 * pair + 128]
            slope = d_attended[at:count, lanes]
            d_query, d_key, d_value = [], [], []
            for odd in (0, 1):
                keep = head_mask(odd == 0, rows)
                head = 2 * pair + odd
                own_query = only(query, keep)
                own_slope = only(slope, keep)
                scores = contract_last(own_query, keys) * scale
                scores = jnp.where(seen, scores, masked_score)
                probs = jnp.exp(scores - stats[at:count, head : head + 1]) * stats[at:count, 64 + head : 65 + head]
                d_probs = contract_last(own_slope, values)
                inner = jnp.sum(probs * d_probs, axis=-1, keepdims=True)
                d_scores = (probs * (d_probs - inner)).astype(jnp.bfloat16)
                d_query.append(jnp.dot(d_scores, keys, preferred_element_type=jnp.float32))
                d_key.append(contract_first(d_scores, own_query))
                d_value.append(contract_first(probs.astype(jnp.bfloat16), own_slope))
            keep = head_mask(True, rows)
            d_q = jnp.where(keep, d_query[0], d_query[1]) * scale
            d_q = turned(d_q, at, count).astype(jnp.bfloat16)
            d_qkv[at:count, lanes] = d_q
            d_k = (d_key[0] + d_key[1]) * scale
            d_v = d_value[0] + d_value[1]
            if block == blocks - 1:
                d_keys[:, lanes] = d_k
                d_values[:, lanes] = d_v
            else:
                d_keys[:count, lanes] += d_k
                d_values[:count, lanes] += d_v
            k_out = turned(d_keys[at:count, lanes], at, count).astype(jnp.bfloat16)
            d_qkv[at:count, width + 128 * pair : width + 128 * pair + 128] = k_out
            v_out = d_values[at:count, lanes].astype(jnp.bfloat16)
            d_qkv[at:count, 2 * width + 128 * pair : 2 * width + 128 * pair + 128] = v_out
            if steps:
                steps.pop(0)()
    for part in range(3 * pairs):
        lanes = slice(128 * part, 128 * part + 128)
        bias_grad[:, lanes] = jnp.broadcast_to(
            jnp.sum(d_qkv[:, lanes].astype(jnp.float32), axis=0, keepdims=True), (8, 128))


def contract_first(left, right):
    return lax.dot_general(
        left, right, (((0,), (0,)), ((), ())), preferred_element_type=jnp.float32
    )


def attend_back_call(rows, qkv, d_attended, stats, seg_rows, seg_columns, cosine, minus, plus):
    group = qkv.shape[0]
    width = qkv.shape[1] // 3
    vm = pl.BlockSpec(memory_space=pltpu.VMEM)
    return pl.pallas_call(
        functools.partial(attend_back_kernel, rows),
        out_shape=[
            jax.ShapeDtypeStruct((group, 3 * width), jnp.bfloat16),
            jax.ShapeDtypeStruct((8, 3 * width), jnp.float32),
        ],
        in_specs=[vm] * 8,
        out_specs=[vm, vm],
        scratch_shapes=[pltpu.VMEM((group, width), jnp.float32), pltpu.VMEM((group, width), jnp.float32)],
        compiler_params=pltpu.CompilerParams(vmem_limit_bytes=48 * 2**20),
        name="attend_back",
        cost_estimate=pl.CostEstimate(flops=3 * 10**9, bytes_accessed=100 * 10**6, transcendentals=0),
    )(qkv, d_attended, stats, seg_rows, seg_columns, cosine, minus, plus)


def scatter_kernel(shards, cuts, parts, total, own, got, load, send, recv):
    z = lax.axis_index("shard")
    rows = parts.shape[1]
    step_rows = rows // cuts
    greet_line(z, shards)

    def piece(cut):
        return pl.ds(cut * step_rows, step_rows)

    def moved(way, block, cut):
        target = z + 1 if way == 0 else z - 1
        place = got.at[way, block, piece(cut)]
        return remote(place, place, send.at[way, block, cut], recv.at[way, block, cut], {"shard": target})

    loads = [pltpu.make_async_copy(parts.at[j], own.at[j], load.at[j]) for j in range(shards)]
    for copy in loads:
        copy.start()
    for copy in loads:
        copy.wait()
    for far in range(shards - 1):
        for cut in range(cuts):
            for way in (0, 1):
                block = shards - 1 - far if way == 0 else far
                sends = z < block if way == 0 else z > block
                first = z == 0 if way == 0 else z == shards - 1

                @pl.when(sends)
                def _():
                    @pl.when(first)
                    def _():
                        got[way, block, piece(cut)] = own[block, piece(cut)]

                    @pl.when(jnp.logical_not(first))
                    def _():
                        moved(way, block, cut).wait_recv()
                        got[way, block, piece(cut)] = (
                            got[way, block, piece(cut)].astype(jnp.float32)
                            + own[block, piece(cut)].astype(jnp.float32)
                        ).astype(got.dtype)
                    moved(way, block, cut).start()
    total[...] = own[z].astype(jnp.float32)
    for way in (0, 1):
        @pl.when(z >= 1 if way == 0 else z + 1 < shards)
        def _():
            for cut in range(cuts):
                moved(way, z, cut).wait_recv()
            total[...] += got[way, z].astype(jnp.float32)
    for far in range(shards - 1):
        for cut in range(cuts):
            for way in (0, 1):
                block = shards - 1 - far if way == 0 else far

                @pl.when(z < block if way == 0 else z > block)
                def _():
                    moved(way, block, cut).wait_send()


def scatter_call(shards, parts, number):
    _, rows, columns = parts.shape
    cuts = 3
    dma = pltpu.SemaphoreType.DMA
    return pl.pallas_call(
        functools.partial(scatter_kernel, shards, cuts),
        out_shape=jax.ShapeDtypeStruct((rows, columns), jnp.float32),
        in_specs=[pl.BlockSpec(memory_space=pl.ANY)],
        out_specs=pl.BlockSpec(memory_space=pltpu.VMEM),
        scratch_shapes=[
            pltpu.VMEM(parts.shape, parts.dtype),
            pltpu.VMEM((2,) + parts.shape, parts.dtype),
            dma((shards,)), dma((2, shards, cuts)), dma((2, shards, cuts)),
        ],
        compiler_params=pltpu.CompilerParams(
            collective_id=number, has_side_effects=True, vmem_limit_bytes=32 * 2**20
        ),
        name="scatter",
        cost_estimate=pl.CostEstimate(flops=0, bytes_accessed=200 * 10**6, transcendentals=0),
    )(parts)


def exchange_kernel(shards, first, second, first_out, second_out, send, recv, loc):
    z = lax.axis_index("shard")
    width = first.shape[1] // shards
    greet([((z != o), {"shard": o}) for o in range(shards)], shards - 1)
    arrays = ((first, first_out), (second, second_out))

    def move(k, o):
        source, target = arrays[k]
        return remote(source.at[:, pl.ds(o * width, width)], target.at[z], send.at[k, o], recv.at[k, z], {"shard": o})

    def arrival(k, o):
        source, target = arrays[k]
        return remote(target.at[o], target.at[o], send.at[k, o], recv.at[k, o], {"shard": o})

    for k in (0, 1):
        for o in range(shards):
            @pl.when(z != o)
            def _():
                move(k, o).start()

            @pl.when(z == o)
            def _():
                source, target = arrays[k]
                pltpu.make_async_copy(source.at[:, pl.ds(o * width, width)], target.at[o], loc.at[k]).start()
    for k in (0, 1):
        for o in range(shards):
            @pl.when(z != o)
            def _():
                arrival(k, o).wait_recv()
                move(k, o).wait_send()

            @pl.when(z == o)
            def _():
                source, target = arrays[k]
                pltpu.make_async_copy(source.at[:, pl.ds(o * width, width)], target.at[o], loc.at[k]).wait()


def exchange_call(shards, first, second):
    rows, columns = first.shape
    shape = jax.ShapeDtypeStruct((shards, rows, columns // shards), first.dtype)
    any_ = pl.BlockSpec(memory_space=pl.ANY)
    dma = pltpu.SemaphoreType.DMA
    return pl.pallas_call(
        functools.partial(exchange_kernel, shards),
        out_shape=[shape, shape],
        in_specs=[any_, any_],
        out_specs=[any_, any_],
        scratch_shapes=[dma((2, shards)), dma((2, shards)), dma((2,))],
        compiler_params=pltpu.CompilerParams(collective_id=5, has_side_effects=True),
        name="exchange",
        cost_estimate=pl.CostEstimate(flops=0, bytes_accessed=100 * 10**6, transcendentals=0),
    )(first, second)


def add_rows(target, source, count):
    step = 16

    @pl.loop(0, count // step)
    def _(i):
        block = pl.ds(aligned(i, step), step)
        target[block, :] = (
            target[block, :].astype(jnp.float32) + source[block, :].astype(jnp.float32)
        ).astype(target.dtype)


class Reducer:
    def __init__(self, cube, share, term, core, near, last, send, recv):
        self.cube, self.share = cube, share
        self.cut = 16 * ((share // 16 + 1) // 2)
        self.term, self.core, self.near, self.last = term, core, near, last
        self.send, self.recv = send, recv
        self.chunks = term.shape[0]

    def share_rows(self, chunk, place, half):
        first, count = (0, self.cut) if half == 0 else (self.cut, self.share - self.cut)
        start = self.cube.core * 4 * self.share + place * self.share + first
        return rows_of(self.term.at[chunk], start, 16, count)

    def own(self, chunk):
        start = (self.cube.core * 4 + self.cube.place) * self.share
        return rows_of(self.term.at[chunk], start, 16, self.share)

    def core_copy(self, chunk):
        source = rows_of(self.term.at[chunk], (1 - self.cube.core) * 4 * self.share, 16, 4 * self.share)
        return remote(source, self.core.at[chunk], self.send.at[chunk, 0], self.recv.at[chunk, 0], self.cube.to_core)

    def near_place(self, half, other):
        c = self.cube
        if half == 0:
            return 2 * other + (1 - c.x), 2 * other + c.x
        return 2 * (1 - c.y) + other, 2 * c.y + other

    def near_slot(self, chunk, half, other):
        count = self.cut if half == 0 else self.share - self.cut
        start = other * count + (2 * self.cut if half == 1 else 0)
        return self.near.at[chunk, pl.ds(start, count)]

    def near_copy(self, chunk, half, other):
        source = self.share_rows(chunk, self.near_place(half, other)[0], half)
        slot = 1 + 2 * half + other
        device = self.cube.to_x if half == 0 else self.cube.to_y
        return remote(source, self.near_slot(chunk, half, other), self.send.at[chunk, slot], self.recv.at[chunk, slot], device)

    def last_slot(self, chunk, half):
        first, count = (0, self.cut) if half == 0 else (self.cut, self.share - self.cut)
        return self.last.at[chunk, pl.ds(first, count)]

    def last_copy(self, chunk, half):
        c = self.cube
        place = 2 * (1 - c.y) + c.x if half == 0 else 2 * c.y + (1 - c.x)
        device = c.to_y if half == 0 else c.to_x
        source = self.share_rows(chunk, place, half)
        return remote(source, self.last_slot(chunk, half), self.send.at[chunk, 5 + half], self.recv.at[chunk, 5 + half], device)

    def start(self, chunk):
        self.core_copy(chunk).start()

    def after_core(self, chunk):
        self.core_copy(chunk).wait_recv()
        mine = rows_of(self.term.at[chunk], self.cube.core * 4 * self.share, 16, 4 * self.share)
        add_rows(mine, self.core.at[chunk], 4 * self.share)
        for half in (0, 1):
            for other in (0, 1):
                self.near_copy(chunk, half, other).start()

    def after_near(self, chunk):
        for half in (0, 1):
            count = self.cut if half == 0 else self.share - self.cut
            for other in (0, 1):
                self.near_copy(chunk, half, other).wait_recv()
                stays = self.share_rows(chunk, self.near_place(half, other)[1], half)
                add_rows(stays, self.near_slot(chunk, half, other), count)
            self.last_copy(chunk, half).start()

    def after_last(self, chunk):
        c = self.cube
        for half in (0, 1):
            count = self.cut if half == 0 else self.share - self.cut
            self.last_copy(chunk, half).wait_recv()
            add_rows(self.share_rows(chunk, c.place, half), self.last_slot(chunk, half), count)

    def finish(self, chunk):
        self.core_copy(chunk).wait_send()
        for half in (0, 1):
            for other in (0, 1):
                self.near_copy(chunk, half, other).wait_send()
            self.last_copy(chunk, half).wait_send()


class Owners:
    def __init__(self, shards, parts, source, out, send, recv, loc):
        self.shards, self.parts, self.source, self.out = shards, parts, source, out
        self.send, self.recv, self.loc = send, recv, loc
        self.z = lax.axis_index("shard")
        self.width = out.shape[1] // (shards * parts)

    def target(self, shard, part):
        return self.out.at[:, pl.ds(aligned((part * self.shards + shard) * (self.width // 128), 128), self.width)]

    def piece(self, o, part):
        return self.source(o).at[:, pl.ds(part * self.width, self.width)]

    def copy(self, o, part):
        return remote(self.piece(o, part), self.target(self.z, part), self.send.at[o, part], self.recv.at[self.z, part], {"shard": o})

    def arrival(self, o, part):
        place = self.target(o, part)
        return remote(place, place, self.send.at[o, part], self.recv.at[o, part], {"shard": o})

    def local(self, o, part):
        return pltpu.make_async_copy(self.piece(o, part), self.target(o, part), self.loc.at[part])

    def start(self, k):
        o = lax.rem(self.z + k, self.shards)
        for part in range(self.parts):
            if k == 0:
                self.local(o, part).start()
            else:
                self.copy(o, part).start()

    def arrive(self):
        for k in range(self.shards):
            o = lax.rem(self.z + k, self.shards)
            for part in range(self.parts):
                if k == 0:
                    self.local(o, part).wait()
                else:
                    self.arrival(o, part).wait_recv()

    def finish(self):
        for k in range(1, self.shards):
            o = lax.rem(self.z + k, self.shards)
            for part in range(self.parts):
                self.copy(o, part).wait_send()


def owner_sems(shards, parts):
    dma = pltpu.SemaphoreType.DMA
    return [dma((shards, parts)), dma((shards, parts)), dma((parts,))]


class Gatherer:
    def __init__(self, cube, share, out, sems):
        self.cube, self.share, self.out = cube, share, out
        self.send, self.recv, self.loc = sems
        self.count = share.shape[0]
        self.cut = 16 * ((self.count // 16 + 1) // 2)

    def rows(self, place, half=None):
        first, count = {None: (0, self.count), 0: (0, self.cut), 1: (self.cut, self.count - self.cut)}[half]
        return rows_of(self.out, (self.cube.core * 4 + place) * self.count + first, 16, count)

    def copy(self, kind):
        c = self.cube
        at_x, at_y = 2 * c.y + 1 - c.x, 2 * (1 - c.y) + c.x
        block, device = (
            (self.rows(c.place), c.to_x),
            (self.rows(c.place), c.to_y),
            (self.rows(at_x, 0), c.to_y),
            (self.rows(at_y, 1), c.to_x),
            (self.rows(c.place), c.to_core),
            (self.rows(at_x), c.to_core),
            (self.rows(at_y), c.to_core),
            (self.rows(3 - c.place), c.to_core),
        )[kind]
        source = self.share if kind in (0, 1, 4) else block
        return remote(source, block, self.send.at[kind], self.recv.at[kind], device)

    def local(self):
        return pltpu.make_async_copy(self.share, self.rows(self.cube.place), self.loc.at[0])

    def start(self):
        for kind in (0, 1, 4):
            self.copy(kind).start()
        self.local().start()

    def pass_on(self):
        self.copy(0).wait_recv()
        self.copy(2).start()
        self.copy(5).start()
        self.copy(1).wait_recv()
        self.copy(3).start()
        self.copy(6).start()

    def pass_last(self):
        self.copy(2).wait_recv()
        self.copy(3).wait_recv()
        self.copy(7).start()

    def finish(self):
        for kind in (4, 5, 6, 7):
            self.copy(kind).wait_recv()
        for kind in range(8):
            self.copy(kind).wait_send()
        self.local().wait()


def gatherer_sems():
    dma = pltpu.SemaphoreType.DMA
    return [dma((8,)), dma((8,)), dma((1,))]


class LineSum:
    def __init__(self, shards, cuts, own, got, send, recv):
        self.z = lax.axis_index("shard")
        self.shards, self.cuts, self.own, self.got, self.send, self.recv = shards, cuts, own, got, send, recv
        self.step = own.shape[1] // cuts

    def piece(self, cut):
        return pl.ds(cut * self.step, self.step)

    def copy(self, way, block, cut, source=None):
        target = self.z + 1 if way == 0 else self.z - 1
        place = self.got.at[way, block, self.piece(cut)]
        return remote(place if source is None else source, place, self.send.at[way, block, cut], self.recv.at[way, block, cut], {"shard": target})

    def pair(self, t):
        half = self.shards // 2
        upper = self.z // half
        return half - 1 - t + upper * (2 * t - half + 1)

    def ready(self, pair):
        for way in (0, 1):
            for i in (0, 1):
                block = 2 * pair + (1 - i if way == 0 else i)

                @pl.when((self.z == (0 if way == 0 else self.shards - 1)) & (block != self.z))
                def _():
                    for cut in range(self.cuts):
                        self.copy(way, block, cut, self.own.at[block, self.piece(cut)]).start()

    def nearest(self):
        for way in (0, 1):
            block = 1 if way == 0 else self.shards - 2

            @pl.when(self.z == (0 if way == 0 else self.shards - 1))
            def _():
                for cut in range(self.cuts):
                    self.copy(way, block, cut, self.own.at[block, self.piece(cut)]).start()

    def step_on(self, hop, far, cut):
        for way in (0, 1):
            block = self.shards - 1 - far if way == 0 else far

            @pl.when(self.z == (hop if way == 0 else self.shards - 1 - hop))
            def _():
                self.copy(way, block, cut).wait_recv()
                place = self.got.at[way, block, self.piece(cut)]
                add_rows(place, self.own.at[block, self.piece(cut)], self.step)
                self.copy(way, block, cut).start()

    def steps(self):
        return [
            functools.partial(self.step_on, hop, far, cut)
            for far in range(self.shards - 2)
            for hop in range(1, self.shards - 1 - far)
            for cut in range(self.cuts)
        ]

    def result(self, total):
        rows = self.own.shape[1]
        for way in (0, 1):
            @pl.when(self.z >= 1 if way == 0 else self.z + 1 < self.shards)
            def _():
                for cut in range(self.cuts):
                    self.copy(way, self.z, cut).wait_recv()

        @pl.loop(0, rows // 16)
        def _(i):
            block = pl.ds(aligned(i, 16), 16)
            total[block, :] = self.own[self.z, block, :].astype(jnp.float32)

            @pl.when(self.z >= 1)
            def _():
                total[block, :] += self.got[0, self.z, block, :].astype(jnp.float32)

            @pl.when(self.z + 1 < self.shards)
            def _():
                total[block, :] += self.got[1, self.z, block, :].astype(jnp.float32)

    def finish(self):
        for far in range(self.shards - 1):
            for cut in range(self.cuts):
                for way in (0, 1):
                    block = self.shards - 1 - far if way == 0 else far

                    @pl.when(self.z < block if way == 0 else self.z > block)
                    def _():
                        self.copy(way, block, cut).wait_send()


def line_scratch(shards, rows, columns, cuts):
    dma = pltpu.SemaphoreType.DMA
    return [
        pltpu.VMEM((shards, rows, columns), jnp.bfloat16),
        pltpu.VMEM((2, shards, rows, columns), jnp.bfloat16),
        dma((2, shards, cuts)), dma((2, shards, cuts)),
    ]


def reducer_scratch(chunks, share, columns):
    dma = pltpu.SemaphoreType.DMA
    return [pltpu.VMEM((chunks, n * share, columns), jnp.bfloat16) for n in (8, 4, 2, 1)] + [
        dma((chunks, 7)), dma((chunks, 7)),
    ]


def pair_product(own, pair, slopes, weight, tile=512):
    rows = own.shape[1]

    @pl.loop(0, own.shape[2] // tile)
    def _(t):
        columns = pl.ds(aligned(t, tile), tile)
        value = contract_last(slopes[pl.ds(aligned(pair, 2 * rows), 2 * rows), :], weight[columns, :])
        own[2 * pair, :, columns] = value[:rows].astype(own.dtype)
        own[2 * pair + 1, :, columns] = value[rows:].astype(own.dtype)


def term_product(term, chunk, left, right):
    term.at[chunk][...] = contract_first(left[...], right[...]).astype(jnp.bfloat16)


def spaced(moves, steps, every):
    moves = list(moves)
    for i, step in enumerate(steps):
        step()
        if i % every == every - 1 and moves:
            moves.pop(0)()
    for move in moves:
        move()


def interleave(moves, steps):
    for i in range(max(len(moves), len(steps))):
        if i < len(moves):
            moves[i]()
        if i < len(steps):
            steps[i]()


def load_all(pairs, loc):
    copies = [pltpu.make_async_copy(source, target, loc.at[i]) for i, (source, target) in enumerate(pairs)]
    for copy in copies:
        copy.start()
    return copies


def further(shards):
    z = lax.axis_index("shard")
    return [(k, lax.rem(z + k, shards)) for k in (*range(1, shards), 0)]


class Chunks:
    def __init__(self, ref, chunks):
        self.ref, self.shape = ref, (chunks, ref.shape[0] // chunks, ref.shape[1])

    @property
    def at(self):
        return self

    def __getitem__(self, chunk):
        return self.ref.at[pl.ds(aligned(chunk, self.shape[1]), self.shape[1])]


def hidden_back_kernel(shards, slopes, weight, hidden, cotangent, normed_two, total, down_share, gate_up_rows,
                       s_buf, w_buf, h_buf, c_buf, n_buf, own, got, z_send, z_recv,
                       term, core, near, last, r_send, r_recv, g_core, g_near, g_last, g_send, g_recv, loc, *sems):
    cube = Cube()
    loads = load_all(((slopes, s_buf), (weight, w_buf), (hidden, h_buf), (cotangent, c_buf), (normed_two, n_buf)), loc)
    greet(cube.partners(shards), shards + 2)
    line = LineSum(shards, 3, own, got, z_send, z_recv)
    share = hidden.shape[1] // 8
    width = D // shards
    chunks, _, columns = term.shape
    g_term = Chunks(w_buf, shards)
    reducer = Reducer(cube, share, term, core, near, last, r_send, r_recv)
    g_reducer = Reducer(cube, width // 8, g_term, g_core, g_near, g_last, g_send, g_recv)
    owners = Owners(shards, 2, g_reducer.own, gate_up_rows, *sems)
    for copy in loads[:2]:
        copy.wait()
    for t in range(shards // 2):
        pair = line.pair(t)
        pair_product(own, pair, s_buf, w_buf)
        line.ready(pair)
    for copy in loads[2:]:
        copy.wait()

    def down_term(k):
        term_product(term, k, h_buf, c_buf.at[:, pl.ds(k * columns, columns)])
        reducer.start(k)

    def gate_up_term(k):
        term_product(g_term, k, n_buf.at[:, pl.ds(aligned(k, width), width)], s_buf)
        g_reducer.start(k)

    keep = []

    def keep_down(k):
        copy = pltpu.make_async_copy(reducer.own(k), down_share.at[:, pl.ds(k * columns, columns)], loc.at[5 + k])
        copy.start()
        keep.append(copy)

    def of(call, count):
        return [functools.partial(call, k) for k in range(count)]

    turn = further(shards)

    def each(call):
        return [functools.partial(call, o) for _, o in turn]

    moves = line.steps()

    def down_ending(k):
        reducer.after_last(k)
        keep_down(k)

    def g_ending(k, o):
        g_reducer.after_last(o)
        owners.start(k)

    cores = of(reducer.after_core, chunks) + each(g_reducer.after_core)
    nears = of(reducer.after_near, chunks) + each(g_reducer.after_near)
    lasts = of(down_ending, chunks) + [functools.partial(g_ending, k, o) for k, o in turn]
    g_terms = each(gate_up_term)
    sequence = of(down_term, chunks) + cores[:2] + g_terms[:2] + nears[:1] + cores[2:3] + g_terms[2:] + nears[1:2] + lasts[:1]
    sequence += cores[3:4] + moves[:5]
    for i in range(2, chunks + shards):
        sequence += nears[i : i + 1] + lasts[i - 1 : i] + cores[i + 2 : i + 3] + moves[i + 3 : i + 4]
    sequence += lasts[-1:] + moves[chunks + shards + 3 :]
    for step in sequence:
        step()
    line.result(total)
    line.finish()
    owners.arrive()
    for k in range(chunks):
        reducer.finish(k)
    for k in range(shards):
        g_reducer.finish(k)
    owners.finish()
    for copy in keep:
        copy.wait()


def hidden_back_call(shards, slopes, weight, hidden, cotangent, normed_two):
    group, inner = hidden.shape
    rows = group // shards
    share = inner // 8
    chunks = 4
    width = D // shards
    low = jnp.bfloat16
    any_ = pl.BlockSpec(memory_space=pl.ANY)
    dma = pltpu.SemaphoreType.DMA
    return pl.pallas_call(
        functools.partial(hidden_back_kernel, shards),
        out_shape=[
            jax.ShapeDtypeStruct((rows, D), jnp.float32),
            jax.ShapeDtypeStruct((share, D), low),
            jax.ShapeDtypeStruct((width // 8, shards * 2 * inner), low),
        ],
        in_specs=[any_] * 5,
        out_specs=[pl.BlockSpec(memory_space=pltpu.VMEM), any_, any_],
        scratch_shapes=[pltpu.VMEM(a.shape, low) for a in (slopes, weight, hidden, cotangent, normed_two)]
        + line_scratch(shards, rows, D, 3) + reducer_scratch(chunks, share, D // chunks)
        + reducer_scratch(shards, width // 8, 2 * inner)[1:] + [dma((5 + chunks,))] + owner_sems(shards, 2),
        compiler_params=pltpu.CompilerParams(collective_id=6, has_side_effects=True, vmem_limit_bytes=63 * 2**20),
        name="hidden_back",
        cost_estimate=pl.CostEstimate(flops=10**10, bytes_accessed=200 * 10**6, transcendentals=0),
    )(slopes, weight, hidden, cotangent, normed_two)


def norm_back_rows(slope, values, gain):
    centered = values - jnp.mean(values, axis=-1, keepdims=True)
    inverse = lax.rsqrt(jnp.mean(centered * centered, axis=-1, keepdims=True) + norm_eps)
    unit = centered * inverse
    scaled = slope * gain
    back = inverse * (
        scaled
        - jnp.mean(scaled, axis=-1, keepdims=True)
        - unit * jnp.mean(scaled * unit, axis=-1, keepdims=True)
    )
    return back, unit


def heads_back_kernel(shards, rows, d_normed_two, middle, cotangent, gain, out_weight, qkv, stats, seg_rows, seg_columns,
                      cosine, minus, plus, down_share, gate_up_rows,
                      d_middle, norm_grads, d_qkv, bias_grad, m_columns, down_grad, gate_up_grad,
                      o_buf, m_low, da_own, d_attended, d_keys, d_values, e_send, e_recv, loc, *sems):
    cube = Cube()
    z = lax.axis_index("shard")
    loads = load_all(((out_weight, o_buf),), loc)
    greet(cube.partners(shards), shards + 2)
    width = D // shards
    half = gate_up_rows.shape[1] // 2
    gatherers = [Gatherer(cube, down_share, down_grad, sems[0:3])] + [
        Gatherer(cube, gate_up_rows.at[:, pl.ds(i * half, half)], gate_up_grad.at[:, pl.ds(i * half, half)], sems[3 * i + 3 : 3 * i + 6])
        for i in (0, 1)
    ]
    gatherers[0].start()
    gatherers[1].start()
    arrays = ((da_own, d_attended), (m_low, m_columns))

    def move(k, o):
        source, target = arrays[k]
        return remote(source.at[:, pl.ds(o * width, width)], target.at[pl.ds(aligned(z, rows), rows)],
                      e_send.at[k, o], e_recv.at[k, z], {"shard": o})

    def arrival(k, o):
        place = arrays[k][1].at[pl.ds(o * rows, rows)]
        return remote(place, place, e_send.at[k, o], e_recv.at[k, o], {"shard": o})

    def here(k, o):
        source, target = arrays[k]
        return pltpu.make_async_copy(source.at[:, pl.ds(o * width, width)], target.at[pl.ds(o * rows, rows)], loc.at[1 + k])

    def begin(k, o):
        @pl.when(z != o)
        def _():
            move(k, o).start()

        @pl.when(z == o)
        def _():
            here(k, o).start()

    def arrive(k):
        for o in range(shards):
            @pl.when(z != o)
            def _():
                arrival(k, o).wait_recv()

            @pl.when(z == o)
            def _():
                here(k, o).wait()

    norm_grads[...] = jnp.zeros_like(norm_grads)

    @pl.loop(0, rows // 16)
    def _(i):
        block = pl.ds(aligned(i, 16), 16)
        slope = d_normed_two[block, :]
        back, unit = norm_back_rows(slope, middle[block, :], gain[...])
        value = cotangent[block, :].astype(jnp.float32) + back
        d_middle[block, :] = value
        m_low[block, :] = value.astype(jnp.bfloat16)
        norm_grads[0:8, :] += (slope * unit).reshape(2, 8, D).sum(axis=0)
        norm_grads[8:16, :] += slope.reshape(2, 8, D).sum(axis=0)

    loads[0].wait()
    for o in range(shards):
        da_own[:, o * width : (o + 1) * width] = contract_last(
            m_low[...], o_buf[o * width : (o + 1) * width, :]).astype(jnp.bfloat16)
        begin(0, o)
    for o in range(shards):
        begin(1, o)
    arrive(0)
    gatherers[0].pass_on()

    def nothing():
        pass

    steps = [nothing, gatherers[1].pass_on, gatherers[2].start] + [nothing] * 4 + [gatherers[0].pass_last] + [nothing] * 3
    steps += [gatherers[1].pass_last]
    attend_back_body(rows, qkv, d_attended, stats, seg_rows, seg_columns, cosine, minus, plus,
                     d_qkv, bias_grad, d_keys, d_values, steps)
    for step in steps:
        step()
    gatherers[2].pass_on()
    arrive(1)
    gatherers[2].pass_last()
    for k in (0, 1):
        for o in range(shards):
            @pl.when(z != o)
            def _():
                move(k, o).wait_send()
    for gatherer in gatherers:
        gatherer.finish()


def heads_back_call(shards, rows, d_normed_two, middle, cotangent, gain, out_weight, qkv, stats, seg_rows, seg_columns,
                    cosine, minus, plus, down_share, gate_up_rows):
    group = qkv.shape[0]
    width = D // shards
    vm = pl.BlockSpec(memory_space=pltpu.VMEM)
    any_ = pl.BlockSpec(memory_space=pl.ANY)
    dma = pltpu.SemaphoreType.DMA
    low = jnp.bfloat16
    f32 = jnp.float32
    return pl.pallas_call(
        functools.partial(heads_back_kernel, shards, rows),
        out_shape=[
            jax.ShapeDtypeStruct((rows, D), f32),
            jax.ShapeDtypeStruct((16, D), f32),
            jax.ShapeDtypeStruct((group, 3 * width), low),
            jax.ShapeDtypeStruct((8, 3 * width), f32),
            jax.ShapeDtypeStruct((group, width), low),
            jax.ShapeDtypeStruct((8 * down_share.shape[0], D), low),
            jax.ShapeDtypeStruct((8 * gate_up_rows.shape[0], gate_up_rows.shape[1]), low),
        ],
        in_specs=[vm] * 4 + [any_] + [vm] * 7 + [any_] * 2,
        out_specs=[vm, vm, vm, vm, any_, any_, any_],
        scratch_shapes=[
            pltpu.VMEM(out_weight.shape, low), pltpu.VMEM((rows, D), low), pltpu.VMEM((rows, D), low),
            pltpu.VMEM((group, width), low),
            pltpu.VMEM((group, width), f32), pltpu.VMEM((group, width), f32),
        ] + [dma((2, shards)), dma((2, shards)), dma((3,))] + gatherer_sems() * 3,
        compiler_params=pltpu.CompilerParams(collective_id=7, has_side_effects=True, vmem_limit_bytes=56 * 2**20),
        name="heads_back",
        cost_estimate=pl.CostEstimate(flops=10**10, bytes_accessed=200 * 10**6, transcendentals=0),
    )(d_normed_two, middle, cotangent, gain, out_weight, qkv, stats, seg_rows, seg_columns, cosine, minus, plus,
      down_share, gate_up_rows)


def input_back_kernel(shards, slopes, weight, normed, attended, d_middle_columns, tokens, gain, d_middle, bias_grad, norm_grads,
                      input_grad, small, qkv_grad, out_grad,
                      w_buf, n_buf, a_buf, m_buf, total, part, part_in, own, got, z_send, z_recv,
                      term, core, near, last, r_send, r_recv, o_term, o_core, o_near, o_last, o_send, o_recv,
                      qkv_rows, out_rows, s_send, s_recv, loc, *sems):
    cube = Cube()
    z = lax.axis_index("shard")
    loads = load_all(((attended, a_buf), (d_middle_columns, m_buf), (weight, w_buf), (normed, n_buf)), loc)
    greet(cube.partners(shards), shards + 2)
    rows = tokens.shape[0]
    width = D // shards
    share = width // 8
    line = LineSum(shards, 3, own, got, z_send, z_recv)
    reducer = Reducer(cube, share, term, core, near, last, r_send, r_recv)
    o_reducer = Reducer(cube, share, o_term, o_core, o_near, o_last, o_send, o_recv)
    owners = Owners(shards, 3, reducer.own, qkv_rows, *sems[0:3])
    o_owners = Owners(shards, 1, o_reducer.own, out_rows, *sems[3:6])
    gatherer = Gatherer(cube, qkv_rows, qkv_grad, sems[6:9])
    o_gatherer = Gatherer(cube, out_rows, out_grad, sems[9:12])

    def qkv_term(o):
        term_product(term, o, n_buf.at[:, pl.ds(aligned(o, width), width)], slopes)
        reducer.start(o)

    def out_term(o):
        term_product(o_term, o, a_buf.at[:, pl.ds(aligned(o, width), width)], m_buf)
        o_reducer.start(o)

    def product(t):
        pair = line.pair(t)
        pair_product(own, pair, slopes, w_buf)
        if t + 1 < shards // 2:
            line.ready(pair)

    turn = further(shards)

    def each(call):
        return [functools.partial(call, o) for _, o in turn]

    def ending(red, own_, k, o):
        red.after_last(o)
        own_.start(k)

    loads[0].wait()
    loads[1].wait()
    for _, o in turn:
        out_term(o)
    loads[2].wait()
    moves = line.steps()
    cores, nears = each(reducer.after_core), each(reducer.after_near)
    lasts = [functools.partial(ending, reducer, owners, k, o) for k, o in turn]
    terms = each(qkv_term)
    sequence = [functools.partial(product, 0)] + each(o_reducer.after_core)
    sequence += [functools.partial(product, t) for t in range(1, shards // 2)] + [loads[3].wait] + each(o_reducer.after_near)
    sequence += terms[:2] + cores[:1] + terms[2:3] + cores[1:2] + terms[3:]
    sequence += [functools.partial(ending, o_reducer, o_owners, k, o) for k, o in turn]
    sequence += moves[:2] + nears[:1] + cores[2:3] + moves[2:4] + nears[1:2] + lasts[:1] + cores[3:] + moves[4:6]
    for i in range(2, shards):
        sequence += nears[i : i + 1] + lasts[i - 1 : i] + moves[i + 4 : i + 5]
    sequence += lasts[-1:] + [line.nearest] + moves[shards + 4 :]
    sequence += [o_owners.arrive, o_gatherer.start]
    for step in sequence:
        step()
    line.result(total)
    owners.arrive()
    gatherer.start()

    part[...] = jnp.zeros_like(part)

    @pl.loop(0, rows // 16)
    def _(i):
        block = pl.ds(aligned(i, 16), 16)
        slope = total[block, :]
        back, unit = norm_back_rows(slope, tokens[block, :].astype(jnp.float32), gain[...])
        input_grad[block, :] = d_middle[block, :] + back
        ones = (slope * unit).reshape(2, 8, D).sum(axis=0).sum(axis=0, keepdims=True)
        twos = slope.reshape(2, 8, D).sum(axis=0).sum(axis=0, keepdims=True)
        for o in range(shards):
            part[o, 3:4, :] += ones[:, o * width : (o + 1) * width]
            part[o, 4:5, :] += twos[:, o * width : (o + 1) * width]
    for o in range(shards):
        for k in range(2):
            part[o, 5 + k : 6 + k, :] = jnp.sum(
                norm_grads[8 * k : 8 * k + 8, o * width : (o + 1) * width], axis=0, keepdims=True)
    for k in range(3):
        flat = k * shards + z
        part[flat // 3, pl.ds(flat % 3, 1), :] = bias_grad[0:1, k * width : (k + 1) * width]

    def small_copy(o):
        return remote(part.at[o], part_in.at[z], s_send.at[o], s_recv.at[z], {"shard": o})

    def small_arrival(o):
        return remote(part.at[o], part_in.at[o], s_send.at[o], s_recv.at[o], {"shard": o})

    for o in range(shards):
        @pl.when(z != o)
        def _():
            small_copy(o).start()
    small[...] = part[z]
    for o in range(shards):
        @pl.when(z != o)
        def _():
            small_arrival(o).wait_recv()
            small[...] += part_in[o]
    sums = [remote(small, part_in.at[shards + i], s_send.at[shards + i], s_recv.at[shards + i], device)
            for i, device in enumerate((cube.to_core, cube.to_x, cube.to_y))]
    for i, copy in enumerate(sums):
        copy.start()
        copy.wait()
        small[...] += part_in[shards + i]
    o_gatherer.pass_on()
    gatherer.pass_on()
    o_gatherer.pass_last()
    gatherer.pass_last()
    for o in range(shards):
        @pl.when(z != o)
        def _():
            small_copy(o).wait_send()
    line.finish()
    for k in range(shards):
        reducer.finish(k)
        o_reducer.finish(k)
    owners.finish()
    o_owners.finish()
    gatherer.finish()
    o_gatherer.finish()


def input_back_call(shards, slopes, weight, normed, attended, d_middle_columns, tokens, gain, d_middle, bias_grad, norm_grads):
    group = slopes.shape[0]
    rows = group // shards
    width = D // shards
    share = width // 8
    vm = pl.BlockSpec(memory_space=pltpu.VMEM)
    any_ = pl.BlockSpec(memory_space=pl.ANY)
    dma = pltpu.SemaphoreType.DMA
    low = jnp.bfloat16
    f32 = jnp.float32
    return pl.pallas_call(
        functools.partial(input_back_kernel, shards),
        out_shape=[
            jax.ShapeDtypeStruct((rows, D), f32),
            jax.ShapeDtypeStruct((8, width), f32),
            jax.ShapeDtypeStruct((width, 3 * D), low),
            jax.ShapeDtypeStruct((width, D), low),
        ],
        in_specs=[vm] + [any_] * 4 + [vm] * 5,
        out_specs=[vm, vm, any_, any_],
        scratch_shapes=[
            pltpu.VMEM(weight.shape, low), pltpu.VMEM(normed.shape, low), pltpu.VMEM(attended.shape, low),
            pltpu.VMEM(d_middle_columns.shape, low), pltpu.VMEM((rows, D), f32),
            pltpu.VMEM((shards, 8, width), f32), pltpu.VMEM((shards + 3, 8, width), f32),
        ] + line_scratch(shards, rows, D, 3) + reducer_scratch(shards, share, 3 * width) + reducer_scratch(shards, share, width)
        + [pltpu.VMEM((share, 3 * D), low), pltpu.VMEM((share, D), low), dma((shards + 3,)), dma((shards + 3,)), dma((4,))]
        + owner_sems(shards, 3) + owner_sems(shards, 1) + gatherer_sems() * 2,
        compiler_params=pltpu.CompilerParams(collective_id=8, has_side_effects=True, vmem_limit_bytes=60 * 2**20),
        name="input_back",
        cost_estimate=pl.CostEstimate(flops=10**10, bytes_accessed=200 * 10**6, transcendentals=0),
    )(slopes, weight, normed, attended, d_middle_columns, tokens, gain, d_middle, bias_grad, norm_grads)


def swap_pieces(pieces):
    shards = lax.axis_size("shard")
    here = lax.axis_index("shard")
    out = pieces
    for k in range(1, shards):
        partner = jnp.bitwise_xor(here, k)
        piece = lax.dynamic_index_in_dim(pieces, partner, axis=0, keepdims=True)
        piece = lax.ppermute(piece, "shard", [(i, i ^ k) for i in range(shards)])
        out = lax.dynamic_update_slice_in_dim(out, piece, partner, axis=0)
    return out


def own_share(rows):
    own = rows.shape[0] // lax.axis_size("replica")
    return lax.dynamic_slice_in_dim(rows, lax.axis_index("replica") * own, own, axis=0)


def spread_rows(rows, columns):
    shards = lax.axis_size("shard")
    piece = own_share(rows)
    own = piece.shape[0]
    piece = piece.reshape(own, columns, shards, -1).transpose(2, 0, 1, 3).reshape(shards, own, -1)
    full = lax.all_gather(swap_pieces(piece), "replica", axis=0, tiled=False)
    return full.transpose(1, 0, 2, 3).reshape(rows.shape[0] * shards, -1)


def gather_rows(rows):
    shards = lax.axis_size("shard")
    piece = own_share(rows)
    moved = swap_pieces(jnp.broadcast_to(piece[None], (shards,) + piece.shape))
    full = lax.all_gather(moved, "replica", axis=0, tiled=False)
    return full.transpose(1, 0, 2, 3).reshape(rows.shape[0] * shards, -1)


def own_rows(features):
    copies = lax.axis_size("replica")
    shards = lax.axis_size("shard")
    count = features.shape[0]
    return (
        features.reshape(count, shards, copies, -1).transpose(0, 2, 1, 3).reshape(count, -1)
    )


def sum_columns(features, slopes, columns):
    shards = lax.axis_size("shard")
    term = contract_first(own_rows(features), slopes).astype(jnp.bfloat16)
    part = lax.psum_scatter(term, "replica", scatter_dimension=0, tiled=True)
    own = part.shape[0] // shards
    moved = swap_pieces(part.reshape(shards, own, -1))
    moved = moved.reshape(shards, own, columns, -1).transpose(1, 2, 0, 3).reshape(own, -1)
    return lax.all_gather(moved, "replica", axis=0, tiled=True)


def swiglu(gate_up):
    half = gate_up.shape[1] // 2
    return jax.nn.silu(gate_up[:, :half]) * gate_up[:, half:]


def norm_stats(values):
    mean = jnp.mean(values, axis=-1, keepdims=True)
    centered = values - mean
    inverse = lax.rsqrt(jnp.mean(centered * centered, axis=-1, keepdims=True) + norm_eps)
    return centered * inverse, inverse


def norm_back(slope, unit, inverse, gain):
    scaled = slope * gain
    return inverse * (
        scaled
        - jnp.mean(scaled, axis=-1, keepdims=True)
        - unit * jnp.mean(scaled * unit, axis=-1, keepdims=True)
    )


def start_plain(tokens, vectors, qkv_weight, cosine, minus, plus):
    shards = lax.axis_size("shard")
    here = lax.axis_index("shard")
    all_tokens = lax.all_gather(tokens, "shard", axis=0, tiled=False)
    all_vectors = lax.all_gather(vectors, "shard", axis=0, tiled=False)
    weight = spread_rows(qkv_weight, 3)
    width = D // shards
    gain, shift = (all_vectors[:, 3 + i].reshape(D) for i in (0, 1))
    unit, _ = norm_stats(all_tokens.reshape(-1, D).astype(jnp.float32))
    normed = (unit * gain + shift).astype(jnp.bfloat16)
    bias = all_vectors[:, :3].reshape(3, shards, width)
    bias = lax.dynamic_index_in_dim(bias, here, axis=1, keepdims=False).reshape(3 * width)
    value = jnp.dot(normed, weight, preferred_element_type=jnp.float32) + bias
    turned = value[:, : 2 * width]
    wide = [jnp.tile(t, (1, 2 * width // 128)) for t in (cosine, minus, plus)]
    turned = (
        turned * wide[0] + jnp.roll(turned, -8, 1) * wide[1] + jnp.roll(turned, 8, 1) * wide[2]
    )
    qkv = jnp.concatenate([turned, value[:, 2 * width :]], axis=1).astype(jnp.bfloat16)
    return all_tokens, all_vectors, normed, qkv, weight


def layer_kernels(shards, tokens, cotangent, weights, vectors, tables):
    qkv_weight, out_weight, gate_up_weight, down_weight = weights
    seg_rows, seg_columns, cosine, minus, plus = tables
    rows = tokens.shape[0]
    f32 = jnp.float32
    low = jnp.bfloat16
    all_tokens, all_vectors, normed, qkv, weight_qkv, weight_out = start_call(
        shards, tokens, vectors, qkv_weight, out_weight, cosine, minus, plus
    )
    gain_one, shift_one, gain_two, shift_two = (
        all_vectors[:, 3 + i].reshape(1, D) for i in range(4)
    )
    attended, stats, weight_gate_up = attend_spread_call(
        shards, rows, qkv, seg_rows, seg_columns, gate_up_weight
    )
    middle, normed_two, hidden, slopes, group_cotangent, down_part = hidden_call(
        shards, attended, all_tokens, weight_out, weight_gate_up, down_weight, cotangent, gain_two, shift_two
    )
    d_normed_two, down_share, gate_up_rows = hidden_back_call(
        shards, slopes, weight_gate_up, hidden, group_cotangent.reshape(shards * rows, D), normed_two
    )
    down_part, d_normed_two = lax.optimization_barrier((down_part, d_normed_two))
    down_own = lax.psum_scatter(down_part, "shard", scatter_dimension=0, tiled=True)
    d_middle, norm_grads, d_qkv, bias_grad, d_middle_columns, down_grad, gate_up_grad = heads_back_call(
        shards, rows, d_normed_two, middle, cotangent, gain_two, weight_out, qkv, stats, seg_rows, seg_columns,
        cosine, minus, plus, down_share, gate_up_rows,
    )
    input_grad, small, qkv_grad, out_grad = input_back_call(
        shards, d_qkv, weight_qkv, normed, attended, d_middle_columns, tokens, gain_one, d_middle, bias_grad, norm_grads
    )
    mixed = (middle + down_own.astype(f32)).astype(low)
    return mixed, input_grad, small, (qkv_grad, out_grad, gate_up_grad, down_grad)


def layer_plain(shards, tokens, cotangent, weights, vectors, tables):
    qkv_weight, out_weight, gate_up_weight, down_weight = weights
    seg_rows, seg_columns, cosine, minus, plus = tables
    here = lax.axis_index("shard")
    row_count = tokens.shape[0]
    group_rows = row_count * shards
    width = D // shards
    f32 = jnp.float32
    low = jnp.bfloat16
    weight_out = gather_rows(out_weight)
    weight_gate_up = spread_rows(gate_up_weight, 2)
    all_tokens, all_vectors, normed_low, qkv, weight_qkv = start_plain(
        tokens, vectors, qkv_weight, cosine, minus, plus
    )
    gain_one, shift_one, gain_two, shift_two = (
        all_vectors[:, 3 + i].reshape(D) for i in range(4)
    )
    cotangent_later, qkv = lax.optimization_barrier((cotangent, qkv))
    group_cotangent = lax.all_gather(cotangent_later, "shard", axis=0, tiled=True)

    def local(array):
        return lax.dynamic_slice_in_dim(array, here * row_count, row_count, axis=0)

    attended, stats = attend_call(shards, row_count, qkv, seg_rows, seg_columns)
    inputs = all_tokens.reshape(group_rows, D).astype(f32)
    middle = inputs + jnp.dot(attended, weight_out, preferred_element_type=f32)
    unit_two, inverse_two = norm_stats(middle)
    normed_two_low = (unit_two * gain_two + shift_two).astype(low)
    gate_up = jnp.dot(normed_two_low, weight_gate_up, preferred_element_type=f32)
    hidden, swiglu_pull = jax.vjp(swiglu, gate_up)
    hidden_low = hidden.astype(low)
    d_hidden = contract_last(group_cotangent, down_weight)
    d_gate_up_low = swiglu_pull(d_hidden)[0].astype(low)
    down_part = jnp.dot(hidden_low, down_weight, preferred_element_type=f32).astype(low)
    unit_two_own = local(unit_two)
    inverse_two_own = local(inverse_two)
    middle_own = local(middle)

    d_normed_two_part = contract_last(d_gate_up_low, weight_gate_up).astype(low)
    d_normed_two = scatter_call(shards, d_normed_two_part.reshape(shards, row_count, D), 3)
    down_grad = lax.psum(contract_first(hidden_low, group_cotangent).astype(low), "replica")
    d_middle = cotangent.astype(f32) + norm_back(
        d_normed_two, unit_two_own, inverse_two_own, gain_two
    )
    d_gain_two = jnp.sum(d_normed_two * unit_two_own, axis=0)
    d_shift_two = jnp.sum(d_normed_two, axis=0)
    d_middle_low = d_middle.astype(low)
    d_attended_own = contract_last(d_middle_low, weight_out).astype(low)
    d_attended, d_middle_columns = exchange_call(shards, d_attended_own, d_middle_low)
    d_projected_low, bias_part = attend_back_call(
        row_count, qkv, d_attended.reshape(group_rows, width), stats, seg_rows, seg_columns,
        cosine, minus, plus,
    )
    down_own = lax.psum_scatter(down_part, "shard", scatter_dimension=0, tiled=True)
    mixed = (middle_own + down_own.astype(f32)).astype(low)
    d_normed_part = contract_last(d_projected_low, weight_qkv).astype(low)
    d_normed = scatter_call(shards, d_normed_part.reshape(shards, row_count, D), 4)
    gate_up_grad = sum_columns(normed_two_low, d_gate_up_low, 2)
    out_grad = sum_columns(attended, d_middle_columns.reshape(group_rows, width), 1)
    qkv_grad = sum_columns(normed_low, d_projected_low, 3)
    unit_one, inverse_one = norm_stats(tokens.astype(f32))
    input_grad = d_middle + norm_back(d_normed, unit_one, inverse_one, gain_one)
    d_gain_one = jnp.sum(d_normed * unit_one, axis=0)
    d_shift_one = jnp.sum(d_normed, axis=0)

    bias_part = bias_part[0].reshape(3, 1, width)
    bias_wide = lax.dynamic_update_slice(
        jnp.zeros((3, shards, width), f32), bias_part, (0, here, 0)
    ).reshape(shards, 3 * width)
    small = jnp.concatenate(
        [bias_wide]
        + [v.reshape(shards, width) for v in (d_gain_one, d_shift_one, d_gain_two, d_shift_two)],
        axis=1,
    )
    small = jnp.pad(small, ((0, 0), (0, width)))
    small = lax.psum(small, ("replica", "shard"))
    small = lax.dynamic_index_in_dim(small, here, axis=0, keepdims=False)
    return mixed, input_grad, small, (qkv_grad, out_grad, gate_up_grad, down_grad)


def on_device(
    tokens,
    cotangent,
    qkv_weight,
    qkv_bias,
    out_weight,
    gate_up_weight,
    down_weight,
    norm1_gain,
    norm1_shift,
    norm2_gain,
    norm2_shift,
    seq_lengths,
):
    shards = lax.axis_size("shard")
    copies = lax.axis_size("replica")
    row_count = tokens.shape[0]
    group_rows = row_count * shards
    width = D // shards
    f32 = jnp.float32
    low = jnp.bfloat16

    segment, position = group_layout(seq_lengths[0], jnp.arange(group_rows, dtype=jnp.int32))
    seg_rows = jnp.broadcast_to(segment[:, None], (group_rows, 128))
    seg_columns = jnp.broadcast_to(segment[None, :], (8, group_rows))
    lane = jnp.arange(128, dtype=jnp.int32)[None, :] % HEAD_DIM
    cosine, sine_value = rope_tables(position, lane % (ROT_DIM // 2))
    cosine = jnp.where(lane < ROT_DIM, cosine, 1.0)
    minus = jnp.where(lane < ROT_DIM // 2, -sine_value, 0.0)
    plus = jnp.where((lane >= ROT_DIM // 2) & (lane < ROT_DIM), sine_value, 0.0)

    def rows_at(vector, first):
        block = vector.astype(f32).reshape(-1, width)
        return jnp.pad(block, ((first, 8 - first - block.shape[0]), (0, 0)))

    vectors = rows_at(qkv_bias, 0)
    for i, vector in enumerate((norm1_gain, norm1_shift, norm2_gain, norm2_shift)):
        vectors = vectors + rows_at(vector, 3 + i)
    weights = (qkv_weight, out_weight, gate_up_weight, down_weight)
    tables = (seg_rows, seg_columns, cosine, minus, plus)
    if copies == 8:
        outputs = layer_kernels(shards, tokens, cotangent, weights, vectors, tables)
    else:
        outputs = layer_plain(shards, tokens, cotangent, weights, vectors, tables)
    mixed, input_grad, small, grads = outputs
    bias_rows = 3 * width
    small = small.reshape(8 * width)
    out_dtype = tuple(grad.astype(f32) for grad in grads)
    return (
        mixed,
        input_grad,
        out_dtype[0],
        small[:bias_rows],
        out_dtype[1],
        out_dtype[2],
        out_dtype[3],
    ) + tuple(small[bias_rows + i * width : bias_rows + (i + 1) * width] for i in range(4))


def solution(mesh):
    placed = (
        P(("replica", "shard"), None),
        P(("replica", "shard"), None),
        P("shard", None),
        P("shard"),
        P("shard", None),
        P("shard", None),
        P("shard", None),
        P("shard"),
        P("shard"),
        P("shard"),
        P("shard"),
        P("replica", None),
    )
    return jax.shard_map(
        on_device,
        mesh=mesh,
        in_specs=placed,
        out_specs=(
            P(("replica", "shard"), None),
            P(("replica", "shard"), None),
            P("shard", None),
            P("shard"),
            P("shard", None),
            P("shard", None),
            P("shard", None),
            P("shard"),
            P("shard"),
            P("shard"),
            P("shard"),
        ),
        check_vma=False,
    )
```

```python
import functools

import jax
import jax.numpy as jnp
from jax import lax
from jax.experimental import pallas as pl
from jax.experimental.pallas import tpu as pltpu
from jax.sharding import PartitionSpec as P

D = 2048
FF = 5632
HEADS = 32
HEAD_DIM = 64
ROT_DIM = 16
MESH = pl.DeviceIdType.MESH


norm_eps = 1e-05
masked_score = -1000000000.0


def group_layout(lengths, token_index):
    segment = jnp.zeros_like(token_index)
    position = token_index
    end = jnp.int32(0)
    for i in range(lengths.shape[0]):
        end = end + lengths[i]
        passed = (token_index >= end).astype(jnp.int32)
        segment = segment + passed
        position = position - passed * lengths[i]
    return (segment, position)


def rope_tables(position, index):
    frequency = jnp.exp(-jnp.log(10000.0) * (2.0 * index.astype(jnp.float32) / ROT_DIM))
    angles = position.astype(jnp.float32)[:, None] * frequency
    return (jnp.cos(angles), jnp.sin(angles))


def contract_last(left, right):
    return lax.dot_general(
        left, right, (((1,), (1,)), ((), ())), preferred_element_type=jnp.float32
    )


def aligned(value, unit):
    return pl.multiple_of(value * unit, unit)


def greet(partners, count):
    barrier = pltpu.get_barrier_semaphore()
    for there, device in partners:
        @pl.when(there)
        def _():
            pl.semaphore_signal(barrier, inc=1, device_id=device, device_id_type=MESH)
    pl.semaphore_wait(barrier, count)


def greet_line(z, shards):
    count = (z + shards - 1) // shards + (2 * shards - 2 - z) // shards
    greet([(z >= 1, {"shard": z - 1}), (z + 1 < shards, {"shard": z + 1})], count)


def remote(source, target, send, recv, device):
    return pltpu.make_async_remote_copy(
        src_ref=source, dst_ref=target, send_sem=send, recv_sem=recv,
        device_id=device, device_id_type=MESH,
    )


class Cube:
    def __init__(self):
        r = lax.axis_index("replica")
        self.core, self.x, self.y = r % 2, (r // 2) % 2, r // 4
        self.place = 2 * self.y + self.x
        self.to_x = {"replica": r + 2 - 4 * self.x}
        self.to_y = {"replica": r + 4 - 8 * self.y}
        self.to_core = {"replica": r + 1 - 2 * self.core}

    def partners(self, shards):
        z = lax.axis_index("shard")
        return [((z != o), {"shard": o}) for o in range(shards)] + [
            (z >= 0, d) for d in (self.to_x, self.to_y, self.to_core)
        ]


def rows_of(ref, start, unit, count):
    return ref.at[pl.ds(pl.multiple_of(start, unit), count)]


class Spreader:
    def __init__(self, cube, shards, share, parts, source, out, sems):
        self.cube, self.shards, self.share, self.parts = cube, shards, share, parts
        self.source, self.out = source, out
        self.z_send, self.z_recv, self.send, self.recv, self.loc = sems
        self.cut = 16 * ((share // 16 + 1) // 2)
        self.z = lax.axis_index("shard")
        r = lax.axis_index("replica")
        self.who = (r, r + 2 - 4 * cube.x, r + 4 - 8 * cube.y, 4 * (1 - cube.y) + 2 * (1 - cube.x) + cube.core)

    def rows(self, o, kind, half=None):
        first, count = {None: (0, self.share), 0: (0, self.cut), 1: (self.cut, self.share - self.cut)}[half]
        return rows_of(self.out, (o * 8 + self.who[kind]) * self.share + first, 16, count)

    def target(self, o, part):
        width = self.out.shape[1] // self.parts
        return self.rows(o, 0).at[:, pl.ds(part * width, width)]

    def z_copy(self, o, part):
        return remote(self.source(o, part), self.target(self.z, part), self.z_send.at[o, part], self.z_recv.at[self.z, part], {"shard": o})

    def z_arrival(self, o, part):
        place = self.target(o, part)
        return remote(place, place, self.z_send.at[o, part], self.z_recv.at[o, part], {"shard": o})

    def local(self, o, part):
        return pltpu.make_async_copy(self.source(o, part), self.target(o, part), self.loc.at[part])

    def start_own(self):
        for part in range(self.parts):
            self.local(self.z, part).start()

    def start(self):
        for o in range(self.shards):
            for part in range(self.parts):
                @pl.when(self.z != o)
                def _():
                    self.z_copy(o, part).start()

    def sent(self):
        for o in range(self.shards):
            for part in range(self.parts):
                @pl.when(self.z != o)
                def _():
                    self.z_copy(o, part).wait_send()

    def copy(self, kind, o):
        c = self.cube
        block, device = (
            (self.rows(o, 0), c.to_x),
            (self.rows(o, 0), c.to_y),
            (self.rows(o, 1, 0), c.to_y),
            (self.rows(o, 2, 1), c.to_x),
            (self.rows(o, 0), c.to_core),
            (self.rows(o, 1), c.to_core),
            (self.rows(o, 2), c.to_core),
            (self.rows(o, 3), c.to_core),
        )[kind]
        return remote(block, block, self.send.at[kind, o], self.recv.at[kind, o], device)

    def arrive(self, distance):
        for o in range(self.shards):
            @pl.when((self.z - o == distance) | (o - self.z == distance))
            def _():
                for part in range(self.parts):
                    if distance == 0:
                        self.local(o, part).wait()
                    else:
                        self.z_arrival(o, part).wait_recv()
                for kind in (0, 1, 4):
                    self.copy(kind, o).start()

    def pass_on(self, o):
        self.copy(0, o).wait_recv()
        self.copy(2, o).start()
        self.copy(5, o).start()
        self.copy(1, o).wait_recv()
        self.copy(3, o).start()
        self.copy(6, o).start()

    def pass_last(self, o):
        self.copy(2, o).wait_recv()
        self.copy(3, o).wait_recv()
        self.copy(7, o).start()

    def landed(self):
        for o in range(self.shards):
            for kind in (4, 5, 6, 7):
                self.copy(kind, o).wait_recv()

    def finish(self):
        for o in range(self.shards):
            for kind in range(8):
                self.copy(kind, o).wait_send()


def spread_sems(shards, parts):
    dma = pltpu.SemaphoreType.DMA
    return [dma((shards, parts)), dma((shards, parts)), dma((8, shards)), dma((8, shards)), dma((parts,))]


class Line:
    def __init__(self, shards, pieces, own, buf, send, recv):
        self.z = lax.axis_index("shard")
        self.shards, self.pieces, self.own, self.buf, self.send, self.recv = shards, pieces, own, buf, send, recv
        self.rows = buf.shape[1] // pieces

    def copy(self, way, step, piece):
        target = self.z + 1 if way == 0 else self.z - 1
        owner = self.z - step if way == 0 else self.z + step
        block = pl.ds(piece * self.rows, self.rows)
        place = self.buf.at[owner, block]
        source = self.own.at[block] if step == 0 and self.own is not None else place
        return remote(source, place, self.send.at[way, step, piece], self.recv.at[way, step, piece], {"shard": target})

    def sends(self, way, step):
        if way == 0:
            return (self.z + 1 < self.shards) & (self.z - step >= 0)
        return (self.z >= 1) & (self.z + step < self.shards)

    def gets(self, way, step):
        return (self.z - step >= 1) if way == 0 else (self.z + step + 1 < self.shards)

    def start(self, piece):
        for way in (0, 1):
            @pl.when(self.sends(way, 0))
            def _():
                self.copy(way, 0, piece).start()

    def relay(self, step, piece):
        for way in (0, 1):
            @pl.when(self.gets(way, step))
            def _():
                self.copy(way, step, piece).wait_recv()
            if step + 1 < self.shards - 1:
                @pl.when(self.sends(way, step + 1))
                def _():
                    self.copy(way, step + 1, piece).start()

    def finish(self):
        for step in range(self.shards - 1):
            for piece in range(self.pieces):
                for way in (0, 1):
                    @pl.when(self.sends(way, step))
                    def _():
                        self.copy(way, step, piece).wait_send()


def line_sems(shards, pieces):
    dma = pltpu.SemaphoreType.DMA
    return [dma((2, shards - 1, pieces)), dma((2, shards - 1, pieces))]


def layer_norm_rows(values, gain, shift):
    centered = values - jnp.mean(values, axis=-1, keepdims=True)
    spread = jnp.mean(centered * centered, axis=-1, keepdims=True)
    return (centered * lax.rsqrt(spread + norm_eps) * gain + shift).astype(jnp.bfloat16)


def bias_piece(v_buf, z, t, tile, shards, per_part):
    flat = (t // per_part) * shards + z
    return v_buf[flat // 3, pl.ds(flat % 3, 1), pl.ds(aligned(t % per_part, tile), tile)]


def start_kernel(shards, tokens, vectors, weight, out_weight, cosine, minus, plus,
                 all_tokens, all_vectors, normed, qkv, kept_weight, all_out,
                 x_buf, v_buf, w_buf, n_buf, q_buf, *sems):
    cube = Cube()
    z = lax.axis_index("shard")
    r = lax.axis_index("replica")
    rows = tokens.shape[0]
    share = weight.shape[0] // 8
    width = w_buf.shape[1] // 3
    x_send, x_recv, v_send, v_recv, loc = sems[:5]
    line = Line(shards, 1, tokens, x_buf, x_send, x_recv)
    mine = pl.ds(aligned(r, share), share)
    spread = Spreader(
        cube, shards, share, 3,
        lambda o, part: weight.at[mine, pl.ds(aligned(part * shards + o, width), width)], w_buf, sems[5:10],
    )
    spread_out = Spreader(cube, shards, share, 1, lambda o, part: out_weight.at[mine], all_out, sems[10:15])
    greet(cube.partners(shards), shards + 2)

    def v_copy(o):
        return remote(vectors, v_buf.at[z], v_send.at[o], v_recv.at[z], {"shard": o})

    def v_arrival(o):
        return remote(vectors, v_buf.at[o], v_send.at[o], v_recv.at[o], {"shard": o})

    own_x = pltpu.make_async_copy(tokens, x_buf.at[z], loc.at[0, 0])
    own_v = pltpu.make_async_copy(vectors, v_buf.at[z], loc.at[1, 0])
    own_x.start()
    own_v.start()
    for o in range(shards):
        @pl.when(z != o)
        def _():
            v_copy(o).start()
    spread.start_own()
    spread_out.start_own()
    spread.start()
    spread.arrive(0)
    spread_out.arrive(0)
    line.start(0)
    spread_out.start()
    for distance in range(1, shards):
        spread.arrive(distance)
    own_x.wait()
    own_v.wait()
    for o in range(shards):
        @pl.when(z != o)
        def _():
            v_arrival(o).wait_recv()
    keep_v = pltpu.make_async_copy(v_buf, all_vectors, loc.at[2, 0])
    keep_v.start()
    gain = jnp.concatenate([v_buf[o, 3:4, :] for o in range(shards)], axis=1)
    shift = jnp.concatenate([v_buf[o, 4:5, :] for o in range(shards)], axis=1)

    def put(source, target, o, i):
        block = pl.ds(aligned(o, rows), rows)
        copy = pltpu.make_async_copy(source.at[block], target.at[block], loc.at[4 + i, o])
        copy.start()

    def normalize(o):
        @pl.loop(0, rows // 32)
        def _(i):
            values = x_buf[o, pl.ds(aligned(i, 32), 32), :].astype(jnp.float32)
            n_buf[pl.ds(pl.multiple_of(o * rows + i * 32, 32), 32), :] = layer_norm_rows(values, gain, shift)
        put(n_buf, normed, o, 0)
        pltpu.make_async_copy(x_buf.at[o], all_tokens.at[o], loc.at[6, o]).start()

    tile = 256
    per_part = width // tile

    def project(o):
        block = pl.ds(aligned(o, rows), rows)

        @pl.loop(0, 3 * per_part)
        def _(t):
            columns = pl.ds(aligned(t, tile), tile)
            value = jnp.dot(n_buf[block, :], w_buf[:, columns], preferred_element_type=jnp.float32)
            value = value + bias_piece(v_buf, z, t, tile, shards, per_part)

            @pl.when(t < 2 * per_part)
            def _():
                wide, wide_minus, wide_plus = (
                    jnp.concatenate([table[block, :]] * (tile // 128), axis=1) for table in (cosine, minus, plus)
                )
                turned = value * wide + pltpu.roll(value, tile - 8, 1) * wide_minus + pltpu.roll(value, 8, 1) * wide_plus
                q_buf[block, columns] = turned.astype(jnp.bfloat16)

            @pl.when(t >= 2 * per_part)
            def _():
                q_buf[block, columns] = value.astype(jnp.bfloat16)
        put(q_buf, qkv, o, 1)

    normalize(z)
    line.relay(0, 0)
    for o in range(shards):
        spread.pass_on(o)
    for o in range(shards):
        spread.pass_last(o)
    spread.landed()
    keep_w = pltpu.make_async_copy(w_buf, kept_weight, loc.at[3, 0])
    keep_w.start()
    project(z)
    for distance in range(1, shards):
        spread_out.arrive(distance)
    for step in range(shards - 1):
        if step > 0:
            line.relay(step, 0)
        for way in (0, 1):
            owner = z - step - 1 if way == 0 else z + step + 1

            @pl.when(line.gets(way, step))
            def _():
                normalize(owner)
                project(owner)
        if step == min(1, shards - 2):
            for o in range(shards):
                spread_out.pass_on(o)
    for o in range(shards):
        spread_out.pass_last(o)
    spread_out.landed()
    line.finish()
    spread.sent()
    spread.finish()
    spread_out.sent()
    spread_out.finish()
    for o in range(shards):
        block = pl.ds(o * rows, rows)

        @pl.when(z != o)
        def _():
            v_copy(o).wait_send()
        pltpu.make_async_copy(n_buf.at[block], normed.at[block], loc.at[4, o]).wait()
        pltpu.make_async_copy(q_buf.at[block], qkv.at[block], loc.at[5, o]).wait()
        pltpu.make_async_copy(x_buf.at[o], all_tokens.at[o], loc.at[6, o]).wait()
    keep_v.wait()
    keep_w.wait()


def start_call(shards, tokens, vectors, weight, out_weight, cosine, minus, plus):
    rows = tokens.shape[0]
    group = rows * shards
    depth = weight.shape[0]
    width = weight.shape[1] // shards
    any_ = pl.BlockSpec(memory_space=pl.ANY)
    vm = pl.BlockSpec(memory_space=pltpu.VMEM)
    low = jnp.bfloat16
    dma = pltpu.SemaphoreType.DMA
    return pl.pallas_call(
        functools.partial(start_kernel, shards),
        out_shape=[
            jax.ShapeDtypeStruct((shards, rows, D), low),
            jax.ShapeDtypeStruct((shards,) + vectors.shape, vectors.dtype),
            jax.ShapeDtypeStruct((group, D), low),
            jax.ShapeDtypeStruct((group, width), low),
            jax.ShapeDtypeStruct((depth * shards, width), low),
            jax.ShapeDtypeStruct((depth * shards, D), low),
        ],
        in_specs=[any_] * 4 + [vm] * 3,
        out_specs=[any_] * 6,
        scratch_shapes=[
            pltpu.VMEM((shards, rows, D), low),
            pltpu.VMEM((shards,) + vectors.shape, vectors.dtype),
            pltpu.VMEM((depth * shards, width), low),
            pltpu.VMEM((group, D), low),
            pltpu.VMEM((group, width), low),
        ] + line_sems(shards, 1) + [dma((shards,)), dma((shards,)), dma((7, shards))]
        + spread_sems(shards, 3) + spread_sems(shards, 1),
        compiler_params=pltpu.CompilerParams(
            collective_id=1, has_side_effects=True, vmem_limit_bytes=62 * 2**20
        ),
        name="start",
        cost_estimate=pl.CostEstimate(flops=2 * group * D * width, bytes_accessed=150 * 10**6, transcendentals=0),
    )(tokens, vectors, weight, out_weight, cosine, minus, plus)


def attend_spread_kernel(shards, rows, qkv, seg_rows, seg_columns, gate_up, attended, stats, all_gate_up, a_buf, *sems):
    cube = Cube()
    z = lax.axis_index("shard")
    r = lax.axis_index("replica")
    width = qkv.shape[1] // 3
    blocks = qkv.shape[0] // rows
    share = gate_up.shape[0] // 8
    half = all_gate_up.shape[1] // 2
    mine = pl.ds(aligned(r, share), share)
    spread = Spreader(
        cube, shards, share, 2,
        lambda o, part: gate_up.at[mine, pl.ds(aligned((part * shards + o) * (half // 128), 128), half)], all_gate_up, sems[3:8],
    )
    line = Line(shards, blocks, None, a_buf, sems[0], sems[1])
    loc = sems[2]
    greet(cube.partners(shards), shards + 2)
    spread.start_own()
    spread.start()
    spread.arrive(0)

    def done(block):
        line.start(block)
        if 0 < block < shards:
            spread.arrive(block)

    attend_body(rows, qkv, seg_rows, seg_columns, a_buf, stats, done)
    moves = [functools.partial(line.relay, step, block) for step in range(shards - 1) for block in range(blocks)]
    steps = [functools.partial(spread.pass_on, o) for o in range(shards)]
    steps += [functools.partial(spread.pass_last, o) for o in range(shards)]
    for i in range(max(len(moves), len(steps))):
        if i < len(moves):
            moves[i]()
        if i < len(steps):
            steps[i]()
    keep = [pltpu.make_async_copy(a_buf.at[o], attended.at[:, pl.ds(o * width, width)], loc.at[o]) for o in range(shards)]
    for copy in keep:
        copy.start()
    spread.landed()
    line.finish()
    spread.sent()
    spread.finish()
    for copy in keep:
        copy.wait()


def attend_spread_call(shards, rows, qkv, seg_rows, seg_columns, gate_up):
    group = qkv.shape[0]
    width = qkv.shape[1] // 3
    blocks = group // rows
    vm = pl.BlockSpec(memory_space=pltpu.VMEM)
    any_ = pl.BlockSpec(memory_space=pl.ANY)
    dma = pltpu.SemaphoreType.DMA
    low = jnp.bfloat16
    return pl.pallas_call(
        functools.partial(attend_spread_kernel, shards, rows),
        out_shape=[
            jax.ShapeDtypeStruct((group, shards * width), low),
            jax.ShapeDtypeStruct((group, 128), jnp.float32),
            jax.ShapeDtypeStruct((gate_up.shape[0] * shards, gate_up.shape[1] // shards), low),
        ],
        in_specs=[vm, vm, vm, any_],
        out_specs=[any_, vm, any_],
        scratch_shapes=[pltpu.VMEM((shards, group, width), low)] + line_sems(shards, blocks) + [dma((shards,))]
        + spread_sems(shards, 2),
        compiler_params=pltpu.CompilerParams(
            collective_id=2, has_side_effects=True, vmem_limit_bytes=48 * 2**20
        ),
        name="attend_spread",
        cost_estimate=pl.CostEstimate(flops=10**9, bytes_accessed=150 * 10**6, transcendentals=0),
    )(qkv, seg_rows, seg_columns, gate_up)


def hidden_kernel(shards, attended, tokens, out_weight, gate_up_weight, down_weight, cotangent, gain, shift,
                  middle_own, normed_two, hidden, slopes, all_cotangent, down_part,
                  a_buf, x_buf, o_buf, g_buf, d_buf, c_buf, mid, n_buf, gu, h_buf, s_buf, c_send, c_recv, loc):
    z = lax.axis_index("shard")
    greet_line(z, shards)
    rows = cotangent.shape[0]
    group = rows * shards
    inner = h_buf.shape[1]
    line = Line(shards, 1, cotangent, c_buf, c_send, c_recv)
    line.start(0)
    load = [pltpu.make_async_copy(source, target, loc.at[i]) for i, (source, target) in enumerate((
        (attended, a_buf), (out_weight, o_buf), (tokens, x_buf), (gate_up_weight, g_buf), (down_weight, d_buf),
        (cotangent, c_buf.at[z])))]
    for copy in load:
        copy.start()
    for copy in load[:3]:
        copy.wait()
    tile = 256
    span = 2 * rows
    for part in range(group // span):
        at = part * span

        @pl.loop(0, D // tile)
        def _(t):
            columns = pl.ds(aligned(t, tile), tile)
            value = jnp.dot(a_buf[at : at + span, :], o_buf[:, columns], preferred_element_type=jnp.float32)
            for k in range(2):
                mid[k * rows : (k + 1) * rows, columns] = (
                    value[k * rows : (k + 1) * rows] + x_buf[2 * part + k, :, columns].astype(jnp.float32)
                )

        @pl.loop(0, span // 32)
        def _(i):
            block = pl.ds(aligned(i, 32), 32)
            n_buf[pl.ds(pl.multiple_of(at + i * 32, 32), 32), :] = layer_norm_rows(mid[block, :], gain[...], shift[...])
        for k in range(2):
            @pl.when(z == 2 * part + k)
            def _():
                middle_own[...] = mid[k * rows : (k + 1) * rows, :]
    keep_n = pltpu.make_async_copy(n_buf, normed_two, loc.at[6])
    keep_n.start()
    line.relay(0, 0)
    load[3].wait()

    @pl.loop(0, 2 * inner // tile)
    def _(t):
        columns = pl.ds(aligned(t, tile), tile)
        gu[:, columns] = jnp.dot(n_buf[...], g_buf[:, columns], preferred_element_type=jnp.float32)

    @pl.loop(0, group // 32)
    def _(i):
        block = pl.ds(aligned(i, 32), 32)
        gate = gu[block, :inner]
        h_buf[block, :] = (gate / (1.0 + jnp.exp(-gate)) * gu[block, inner:]).astype(jnp.bfloat16)
    keep_h = pltpu.make_async_copy(h_buf, hidden, loc.at[7])
    keep_h.start()
    if shards > 2:
        line.relay(1, 0)
    load[4].wait()

    @pl.loop(0, D // tile)
    def _(t):
        columns = pl.ds(aligned(t, tile), tile)
        a_buf[:, columns] = jnp.dot(h_buf[...], d_buf[:, columns], preferred_element_type=jnp.float32).astype(jnp.bfloat16)
    keep_p = pltpu.make_async_copy(a_buf, down_part, loc.at[8])
    keep_p.start()
    load[5].wait()

    def back(o):
        mid[:rows, :inner] = contract_last(c_buf[o], d_buf[...])

        @pl.loop(0, rows // 32)
        def _(i):
            value = mid[pl.ds(aligned(i, 32), 32), :inner]
            place = pl.ds(pl.multiple_of(o * rows + i * 32, 32), 32)
            gate = gu[place, :inner]
            up = gu[place, inner:]
            sigmoid = 1.0 / (1.0 + jnp.exp(-gate))
            s_buf[place, :inner] = (value * up * (sigmoid * (1.0 + gate * (1.0 - sigmoid)))).astype(jnp.bfloat16)
            s_buf[place, inner:] = (value * (gate * sigmoid)).astype(jnp.bfloat16)

    back(z)
    for step in range(shards - 1):
        if step >= 2:
            line.relay(step, 0)
        for way in (0, 1):
            owner = z - step - 1 if way == 0 else z + step + 1

            @pl.when(line.gets(way, step))
            def _():
                back(owner)
    keep = [pltpu.make_async_copy(c_buf, all_cotangent, loc.at[9]), pltpu.make_async_copy(s_buf, slopes, loc.at[10])]
    for copy in keep:
        copy.start()
    line.finish()
    for copy in keep + [keep_n, keep_h, keep_p]:
        copy.wait()


def hidden_call(shards, attended, tokens, out_weight, gate_up_weight, down_weight, cotangent, gain, shift):
    rows = cotangent.shape[0]
    group = rows * shards
    inner = down_weight.shape[0]
    low = jnp.bfloat16
    f32 = jnp.float32
    vm = pl.BlockSpec(memory_space=pltpu.VMEM)
    any_ = pl.BlockSpec(memory_space=pl.ANY)
    return pl.pallas_call(
        functools.partial(hidden_kernel, shards),
        out_shape=[
            jax.ShapeDtypeStruct((rows, D), f32),
            jax.ShapeDtypeStruct((group, D), low),
            jax.ShapeDtypeStruct((group, inner), low),
            jax.ShapeDtypeStruct((group, 2 * inner), low),
            jax.ShapeDtypeStruct((shards, rows, D), low),
            jax.ShapeDtypeStruct((group, D), low),
        ],
        in_specs=[any_] * 6 + [vm, vm],
        out_specs=[vm] + [any_] * 5,
        scratch_shapes=[
            pltpu.VMEM((group, D), low),
            pltpu.VMEM((shards, rows, D), low),
            pltpu.VMEM(out_weight.shape, low),
            pltpu.VMEM(gate_up_weight.shape, low),
            pltpu.VMEM(down_weight.shape, low),
            pltpu.VMEM((shards, rows, D), low),
            pltpu.VMEM((2 * rows, D), f32),
            pltpu.VMEM((group, D), low),
            pltpu.VMEM((group, 2 * inner), f32),
            pltpu.VMEM((group, inner), low),
            pltpu.VMEM((group, 2 * inner), low),
        ] + line_sems(shards, 1) + [pltpu.SemaphoreType.DMA((11,))],
        compiler_params=pltpu.CompilerParams(
            collective_id=9, has_side_effects=True, vmem_limit_bytes=63 * 2**20
        ),
        name="hidden",
        cost_estimate=pl.CostEstimate(flops=24 * 10**9, bytes_accessed=150 * 10**6, transcendentals=0),
    )(attended, tokens, out_weight, gate_up_weight, down_weight, cotangent, gain, shift)


def head_mask(even, rows):
    lane = lax.broadcasted_iota(jnp.int32, (rows, 128), 1)
    return (lane < HEAD_DIM) if even else (lane >= HEAD_DIM)


def only(values, keep):
    return jnp.where(keep, values.astype(jnp.float32), 0.0).astype(jnp.bfloat16)


def block_visible(at, rows, seg_rows, seg_columns):
    count = at + rows
    row = lax.broadcasted_iota(jnp.int32, (rows, count), 0) + at
    column = lax.broadcasted_iota(jnp.int32, (rows, count), 1)
    return (column <= row) & (seg_rows[at : at + rows, :1] == seg_columns[:1, :count])


def attend_body(rows, qkv, seg_rows, seg_columns, a_buf, stats, done):
    z = lax.axis_index("shard")
    width = qkv.shape[1] // 3
    pairs = width // 128
    scale = HEAD_DIM ** (-0.5)
    for block in range(qkv.shape[0] // rows):
        at = block * rows
        count = at + rows
        seen = block_visible(at, rows, seg_rows, seg_columns)
        for pair in range(pairs):
            lanes = slice(128 * pair, 128 * pair + 128)
            query = qkv[at:count, lanes]
            keys = qkv[:count, width + 128 * pair : width + 128 * pair + 128]
            values = qkv[:count, 2 * width + 128 * pair : 2 * width + 128 * pair + 128]
            results = []
            for odd in (0, 1):
                keep = head_mask(odd == 0, rows)
                scores = contract_last(only(query, keep), keys) * scale
                scores = jnp.where(seen, scores, masked_score)
                top = jnp.max(scores, axis=-1, keepdims=True)
                weights = jnp.exp(scores - top)
                total = jnp.sum(weights, axis=-1, keepdims=True)
                probs = (weights * (1.0 / total)).astype(jnp.bfloat16)
                results.append(jnp.dot(probs, values, preferred_element_type=jnp.float32))
                head = 2 * pair + odd
                stats[at:count, head : head + 1] = top
                stats[at:count, 64 + head : 65 + head] = 1.0 / total
            merged = jnp.where(head_mask(True, rows), results[0], results[1])
            a_buf[z, at:count, lanes] = merged.astype(jnp.bfloat16)
        done(block)


def attend_kernel(shards, rows, qkv, seg_rows, seg_columns, attended, stats, a_buf, a_send, a_recv, loc):
    z = lax.axis_index("shard")
    width = qkv.shape[1] // 3
    blocks = qkv.shape[0] // rows
    greet_line(z, shards)
    line = Line(shards, blocks, None, a_buf, a_send, a_recv)
    attend_body(rows, qkv, seg_rows, seg_columns, a_buf, stats, line.start)
    for step in range(shards - 1):
        for block in range(blocks):
            line.relay(step, block)
    keep = [pltpu.make_async_copy(a_buf.at[o], attended.at[:, pl.ds(o * width, width)], loc.at[o]) for o in range(shards)]
    for copy in keep:
        copy.start()
    line.finish()
    for copy in keep:
        copy.wait()


def attend_call(shards, rows, qkv, seg_rows, seg_columns):
    group = qkv.shape[0]
    width = qkv.shape[1] // 3
    blocks = group // rows
    vm = pl.BlockSpec(memory_space=pltpu.VMEM)
    any_ = pl.BlockSpec(memory_space=pl.ANY)
    dma = pltpu.SemaphoreType.DMA
    return pl.pallas_call(
        functools.partial(attend_kernel, shards, rows),
        out_shape=[
            jax.ShapeDtypeStruct((group, shards * width), jnp.bfloat16),
            jax.ShapeDtypeStruct((group, 128), jnp.float32),
        ],
        in_specs=[vm, vm, vm],
        out_specs=[any_, vm],
        scratch_shapes=[
            pltpu.VMEM((shards, group, width), jnp.bfloat16),
            dma((2, shards - 1, blocks)), dma((2, shards - 1, blocks)), dma((shards,)),
        ],
        compiler_params=pltpu.CompilerParams(
            collective_id=2, has_side_effects=True, vmem_limit_bytes=48 * 2**20
        ),
        name="attend",
        cost_estimate=pl.CostEstimate(flops=10**9, bytes_accessed=150 * 10**6, transcendentals=0),
    )(qkv, seg_rows, seg_columns)


def attend_back_kernel(rows, *refs):
    attend_back_body(rows, *refs, [])


def attend_back_body(rows, qkv, d_attended, stats, seg_rows, seg_columns, cosine, minus, plus,
                     d_qkv, bias_grad, d_keys, d_values, steps):
    width = qkv.shape[1] // 3
    group = qkv.shape[0]
    blocks = group // rows
    pairs = width // 128
    scale = HEAD_DIM ** (-0.5)

    def turned(value, at, count):
        return (value * cosine[at:count, :] - pltpu.roll(value, 120, 1) * minus[at:count, :]
                - pltpu.roll(value, 8, 1) * plus[at:count, :])

    for block in reversed(range(blocks)):
        at = block * rows
        count = at + rows
        seen = block_visible(at, rows, seg_rows, seg_columns)
        for pair in range(pairs):
            lanes = slice(128 * pair, 128 * pair + 128)
            query = qkv[at:count, lanes]
            keys = qkv[:count, width + 128 * pair : width + 128 * pair + 128]
            values = qkv[:count, 2 * width + 128 * pair : 2 * width + 128 * pair + 128]
            slope = d_attended[at:count, lanes]
            d_query, d_key, d_value = [], [], []
            for odd in (0, 1):
                keep = head_mask(odd == 0, rows)
                head = 2 * pair + odd
                own_query = only(query, keep)
                own_slope = only(slope, keep)
                scores = contract_last(own_query, keys) * scale
                scores = jnp.where(seen, scores, masked_score)
                probs = jnp.exp(scores - stats[at:count, head : head + 1]) * stats[at:count, 64 + head : 65 + head]
                d_probs = contract_last(own_slope, values)
                inner = jnp.sum(probs * d_probs, axis=-1, keepdims=True)
                d_scores = (probs * (d_probs - inner)).astype(jnp.bfloat16)
                d_query.append(jnp.dot(d_scores, keys, preferred_element_type=jnp.float32))
                d_key.append(contract_first(d_scores, own_query))
                d_value.append(contract_first(probs.astype(jnp.bfloat16), own_slope))
            keep = head_mask(True, rows)
            d_q = jnp.where(keep, d_query[0], d_query[1]) * scale
            d_q = turned(d_q, at, count).astype(jnp.bfloat16)
            d_qkv[at:count, lanes] = d_q
            d_k = (d_key[0] + d_key[1]) * scale
            d_v = d_value[0] + d_value[1]
            if block == blocks - 1:
                d_keys[:, lanes] = d_k
                d_values[:, lanes] = d_v
            else:
                d_keys[:count, lanes] += d_k
                d_values[:count, lanes] += d_v
            k_out = turned(d_keys[at:count, lanes], at, count).astype(jnp.bfloat16)
            d_qkv[at:count, width + 128 * pair : width + 128 * pair + 128] = k_out
            v_out = d_values[at:count, lanes].astype(jnp.bfloat16)
            d_qkv[at:count, 2 * width + 128 * pair : 2 * width + 128 * pair + 128] = v_out
            if steps:
                steps.pop(0)()
    for part in range(3 * pairs):
        lanes = slice(128 * part, 128 * part + 128)
        bias_grad[:, lanes] = jnp.broadcast_to(
            jnp.sum(d_qkv[:, lanes].astype(jnp.float32), axis=0, keepdims=True), (8, 128))


def contract_first(left, right):
    return lax.dot_general(
        left, right, (((0,), (0,)), ((), ())), preferred_element_type=jnp.float32
    )


def attend_back_call(rows, qkv, d_attended, stats, seg_rows, seg_columns, cosine, minus, plus):
    group = qkv.shape[0]
    width = qkv.shape[1] // 3
    vm = pl.BlockSpec(memory_space=pltpu.VMEM)
    return pl.pallas_call(
        functools.partial(attend_back_kernel, rows),
        out_shape=[
            jax.ShapeDtypeStruct((group, 3 * width), jnp.bfloat16),
            jax.ShapeDtypeStruct((8, 3 * width), jnp.float32),
        ],
        in_specs=[vm] * 8,
        out_specs=[vm, vm],
        scratch_shapes=[pltpu.VMEM((group, width), jnp.float32), pltpu.VMEM((group, width), jnp.float32)],
        compiler_params=pltpu.CompilerParams(vmem_limit_bytes=48 * 2**20),
        name="attend_back",
        cost_estimate=pl.CostEstimate(flops=3 * 10**9, bytes_accessed=100 * 10**6, transcendentals=0),
    )(qkv, d_attended, stats, seg_rows, seg_columns, cosine, minus, plus)


def scatter_kernel(shards, cuts, parts, total, own, got, load, send, recv):
    z = lax.axis_index("shard")
    rows = parts.shape[1]
    step_rows = rows // cuts
    greet_line(z, shards)

    def piece(cut):
        return pl.ds(cut * step_rows, step_rows)

    def moved(way, block, cut):
        target = z + 1 if way == 0 else z - 1
        place = got.at[way, block, piece(cut)]
        return remote(place, place, send.at[way, block, cut], recv.at[way, block, cut], {"shard": target})

    loads = [pltpu.make_async_copy(parts.at[j], own.at[j], load.at[j]) for j in range(shards)]
    for copy in loads:
        copy.start()
    for copy in loads:
        copy.wait()
    for far in range(shards - 1):
        for cut in range(cuts):
            for way in (0, 1):
                block = shards - 1 - far if way == 0 else far
                sends = z < block if way == 0 else z > block
                first = z == 0 if way == 0 else z == shards - 1

                @pl.when(sends)
                def _():
                    @pl.when(first)
                    def _():
                        got[way, block, piece(cut)] = own[block, piece(cut)]

                    @pl.when(jnp.logical_not(first))
                    def _():
                        moved(way, block, cut).wait_recv()
                        got[way, block, piece(cut)] = (
                            got[way, block, piece(cut)].astype(jnp.float32)
                            + own[block, piece(cut)].astype(jnp.float32)
                        ).astype(got.dtype)
                    moved(way, block, cut).start()
    total[...] = own[z].astype(jnp.float32)
    for way in (0, 1):
        @pl.when(z >= 1 if way == 0 else z + 1 < shards)
        def _():
            for cut in range(cuts):
                moved(way, z, cut).wait_recv()
            total[...] += got[way, z].astype(jnp.float32)
    for far in range(shards - 1):
        for cut in range(cuts):
            for way in (0, 1):
                block = shards - 1 - far if way == 0 else far

                @pl.when(z < block if way == 0 else z > block)
                def _():
                    moved(way, block, cut).wait_send()


def scatter_call(shards, parts, number):
    _, rows, columns = parts.shape
    cuts = 3
    dma = pltpu.SemaphoreType.DMA
    return pl.pallas_call(
        functools.partial(scatter_kernel, shards, cuts),
        out_shape=jax.ShapeDtypeStruct((rows, columns), jnp.float32),
        in_specs=[pl.BlockSpec(memory_space=pl.ANY)],
        out_specs=pl.BlockSpec(memory_space=pltpu.VMEM),
        scratch_shapes=[
            pltpu.VMEM(parts.shape, parts.dtype),
            pltpu.VMEM((2,) + parts.shape, parts.dtype),
            dma((shards,)), dma((2, shards, cuts)), dma((2, shards, cuts)),
        ],
        compiler_params=pltpu.CompilerParams(
            collective_id=number, has_side_effects=True, vmem_limit_bytes=32 * 2**20
        ),
        name="scatter",
        cost_estimate=pl.CostEstimate(flops=0, bytes_accessed=200 * 10**6, transcendentals=0),
    )(parts)


def exchange_kernel(shards, first, second, first_out, second_out, send, recv, loc):
    z = lax.axis_index("shard")
    width = first.shape[1] // shards
    greet([((z != o), {"shard": o}) for o in range(shards)], shards - 1)
    arrays = ((first, first_out), (second, second_out))

    def move(k, o):
        source, target = arrays[k]
        return remote(source.at[:, pl.ds(o * width, width)], target.at[z], send.at[k, o], recv.at[k, z], {"shard": o})

    def arrival(k, o):
        source, target = arrays[k]
        return remote(target.at[o], target.at[o], send.at[k, o], recv.at[k, o], {"shard": o})

    for k in (0, 1):
        for o in range(shards):
            @pl.when(z != o)
            def _():
                move(k, o).start()

            @pl.when(z == o)
            def _():
                source, target = arrays[k]
                pltpu.make_async_copy(source.at[:, pl.ds(o * width, width)], target.at[o], loc.at[k]).start()
    for k in (0, 1):
        for o in range(shards):
            @pl.when(z != o)
            def _():
                arrival(k, o).wait_recv()
                move(k, o).wait_send()

            @pl.when(z == o)
            def _():
                source, target = arrays[k]
                pltpu.make_async_copy(source.at[:, pl.ds(o * width, width)], target.at[o], loc.at[k]).wait()


def exchange_call(shards, first, second):
    rows, columns = first.shape
    shape = jax.ShapeDtypeStruct((shards, rows, columns // shards), first.dtype)
    any_ = pl.BlockSpec(memory_space=pl.ANY)
    dma = pltpu.SemaphoreType.DMA
    return pl.pallas_call(
        functools.partial(exchange_kernel, shards),
        out_shape=[shape, shape],
        in_specs=[any_, any_],
        out_specs=[any_, any_],
        scratch_shapes=[dma((2, shards)), dma((2, shards)), dma((2,))],
        compiler_params=pltpu.CompilerParams(collective_id=5, has_side_effects=True),
        name="exchange",
        cost_estimate=pl.CostEstimate(flops=0, bytes_accessed=100 * 10**6, transcendentals=0),
    )(first, second)


def add_rows(target, source, count):
    step = 16

    @pl.loop(0, count // step)
    def _(i):
        block = pl.ds(aligned(i, step), step)
        target[block, :] = (
            target[block, :].astype(jnp.float32) + source[block, :].astype(jnp.float32)
        ).astype(target.dtype)


class Reducer:
    def __init__(self, cube, share, term, core, near, last, send, recv):
        self.cube, self.share = cube, share
        self.cut = 16 * ((share // 16 + 1) // 2)
        self.term, self.core, self.near, self.last = term, core, near, last
        self.send, self.recv = send, recv
        self.chunks = term.shape[0]

    def share_rows(self, chunk, place, half):
        first, count = (0, self.cut) if half == 0 else (self.cut, self.share - self.cut)
        start = self.cube.core * 4 * self.share + place * self.share + first
        return rows_of(self.term.at[chunk], start, 16, count)

    def own(self, chunk):
        start = (self.cube.core * 4 + self.cube.place) * self.share
        return rows_of(self.term.at[chunk], start, 16, self.share)

    def core_copy(self, chunk):
        source = rows_of(self.term.at[chunk], (1 - self.cube.core) * 4 * self.share, 16, 4 * self.share)
        return remote(source, self.core.at[chunk], self.send.at[chunk, 0], self.recv.at[chunk, 0], self.cube.to_core)

    def near_place(self, half, other):
        c = self.cube
        if half == 0:
            return 2 * other + (1 - c.x), 2 * other + c.x
        return 2 * (1 - c.y) + other, 2 * c.y + other

    def near_slot(self, chunk, half, other):
        count = self.cut if half == 0 else self.share - self.cut
        start = other * count + (2 * self.cut if half == 1 else 0)
        return self.near.at[chunk, pl.ds(start, count)]

    def near_copy(self, chunk, half, other):
        source = self.share_rows(chunk, self.near_place(half, other)[0], half)
        slot = 1 + 2 * half + other
        device = self.cube.to_x if half == 0 else self.cube.to_y
        return remote(source, self.near_slot(chunk, half, other), self.send.at[chunk, slot], self.recv.at[chunk, slot], device)

    def last_slot(self, chunk, half):
        first, count = (0, self.cut) if half == 0 else (self.cut, self.share - self.cut)
        return self.last.at[chunk, pl.ds(first, count)]

    def last_copy(self, chunk, half):
        c = self.cube
        place = 2 * (1 - c.y) + c.x if half == 0 else 2 * c.y + (1 - c.x)
        device = c.to_y if half == 0 else c.to_x
        source = self.share_rows(chunk, place, half)
        return remote(source, self.last_slot(chunk, half), self.send.at[chunk, 5 + half], self.recv.at[chunk, 5 + half], device)

    def start(self, chunk):
        self.core_copy(chunk).start()

    def after_core(self, chunk):
        self.core_copy(chunk).wait_recv()
        mine = rows_of(self.term.at[chunk], self.cube.core * 4 * self.share, 16, 4 * self.share)
        add_rows(mine, self.core.at[chunk], 4 * self.share)
        for half in (0, 1):
            for other in (0, 1):
                self.near_copy(chunk, half, other).start()

    def after_near(self, chunk):
        for half in (0, 1):
            count = self.cut if half == 0 else self.share - self.cut
            for other in (0, 1):
                self.near_copy(chunk, half, other).wait_recv()
                stays = self.share_rows(chunk, self.near_place(half, other)[1], half)
                add_rows(stays, self.near_slot(chunk, half, other), count)
            self.last_copy(chunk, half).start()

    def after_last(self, chunk):
        c = self.cube
        for half in (0, 1):
            count = self.cut if half == 0 else self.share - self.cut
            self.last_copy(chunk, half).wait_recv()
            add_rows(self.share_rows(chunk, c.place, half), self.last_slot(chunk, half), count)

    def finish(self, chunk):
        self.core_copy(chunk).wait_send()
        for half in (0, 1):
            for other in (0, 1):
                self.near_copy(chunk, half, other).wait_send()
            self.last_copy(chunk, half).wait_send()


class Owners:
    def __init__(self, shards, parts, source, out, send, recv, loc):
        self.shards, self.parts, self.source, self.out = shards, parts, source, out
        self.send, self.recv, self.loc = send, recv, loc
        self.z = lax.axis_index("shard")
        self.width = out.shape[1] // (shards * parts)

    def target(self, shard, part):
        return self.out.at[:, pl.ds(aligned((part * self.shards + shard) * (self.width // 128), 128), self.width)]

    def piece(self, o, part):
        return self.source(o).at[:, pl.ds(part * self.width, self.width)]

    def copy(self, o, part):
        return remote(self.piece(o, part), self.target(self.z, part), self.send.at[o, part], self.recv.at[self.z, part], {"shard": o})

    def arrival(self, o, part):
        place = self.target(o, part)
        return remote(place, place, self.send.at[o, part], self.recv.at[o, part], {"shard": o})

    def local(self, o, part):
        return pltpu.make_async_copy(self.piece(o, part), self.target(o, part), self.loc.at[part])

    def start(self, k):
        o = lax.rem(self.z + k, self.shards)
        for part in range(self.parts):
            if k == 0:
                self.local(o, part).start()
            else:
                self.copy(o, part).start()

    def arrive(self):
        for k in range(self.shards):
            o = lax.rem(self.z + k, self.shards)
            for part in range(self.parts):
                if k == 0:
                    self.local(o, part).wait()
                else:
                    self.arrival(o, part).wait_recv()

    def finish(self):
        for k in range(1, self.shards):
            o = lax.rem(self.z + k, self.shards)
            for part in range(self.parts):
                self.copy(o, part).wait_send()


def owner_sems(shards, parts):
    dma = pltpu.SemaphoreType.DMA
    return [dma((shards, parts)), dma((shards, parts)), dma((parts,))]


class Gatherer:
    def __init__(self, cube, share, out, sems):
        self.cube, self.share, self.out = cube, share, out
        self.send, self.recv, self.loc = sems
        self.count = share.shape[0]
        self.cut = 16 * ((self.count // 16 + 1) // 2)

    def rows(self, place, half=None):
        first, count = {None: (0, self.count), 0: (0, self.cut), 1: (self.cut, self.count - self.cut)}[half]
        return rows_of(self.out, (self.cube.core * 4 + place) * self.count + first, 16, count)

    def copy(self, kind):
        c = self.cube
        at_x, at_y = 2 * c.y + 1 - c.x, 2 * (1 - c.y) + c.x
        block, device = (
            (self.rows(c.place), c.to_x),
            (self.rows(c.place), c.to_y),
            (self.rows(at_x, 0), c.to_y),
            (self.rows(at_y, 1), c.to_x),
            (self.rows(c.place), c.to_core),
            (self.rows(at_x), c.to_core),
            (self.rows(at_y), c.to_core),
            (self.rows(3 - c.place), c.to_core),
        )[kind]
        source = self.share if kind in (0, 1, 4) else block
        return remote(source, block, self.send.at[kind], self.recv.at[kind], device)

    def local(self):
        return pltpu.make_async_copy(self.share, self.rows(self.cube.place), self.loc.at[0])

    def start(self):
        for kind in (0, 1, 4):
            self.copy(kind).start()
        self.local().start()

    def pass_on(self):
        self.copy(0).wait_recv()
        self.copy(2).start()
        self.copy(5).start()
        self.copy(1).wait_recv()
        self.copy(3).start()
        self.copy(6).start()

    def pass_last(self):
        self.copy(2).wait_recv()
        self.copy(3).wait_recv()
        self.copy(7).start()

    def finish(self):
        for kind in (4, 5, 6, 7):
            self.copy(kind).wait_recv()
        for kind in range(8):
            self.copy(kind).wait_send()
        self.local().wait()


def gatherer_sems():
    dma = pltpu.SemaphoreType.DMA
    return [dma((8,)), dma((8,)), dma((1,))]


class LineSum:
    def __init__(self, shards, cuts, own, got, send, recv):
        self.z = lax.axis_index("shard")
        self.shards, self.cuts, self.own, self.got, self.send, self.recv = shards, cuts, own, got, send, recv
        self.step = own.shape[1] // cuts

    def piece(self, cut):
        return pl.ds(cut * self.step, self.step)

    def copy(self, way, block, cut, source=None):
        target = self.z + 1 if way == 0 else self.z - 1
        place = self.got.at[way, block, self.piece(cut)]
        return remote(place if source is None else source, place, self.send.at[way, block, cut], self.recv.at[way, block, cut], {"shard": target})

    def pair(self, t):
        half = self.shards // 2
        upper = self.z // half
        return half - 1 - t + upper * (2 * t - half + 1)

    def ready(self, pair):
        for way in (0, 1):
            for i in (0, 1):
                block = 2 * pair + (1 - i if way == 0 else i)

                @pl.when((self.z == (0 if way == 0 else self.shards - 1)) & (block != self.z))
                def _():
                    for cut in range(self.cuts):
                        self.copy(way, block, cut, self.own.at[block, self.piece(cut)]).start()

    def nearest(self):
        for way in (0, 1):
            block = 1 if way == 0 else self.shards - 2

            @pl.when(self.z == (0 if way == 0 else self.shards - 1))
            def _():
                for cut in range(self.cuts):
                    self.copy(way, block, cut, self.own.at[block, self.piece(cut)]).start()

    def step_on(self, hop, far, cut):
        for way in (0, 1):
            block = self.shards - 1 - far if way == 0 else far

            @pl.when(self.z == (hop if way == 0 else self.shards - 1 - hop))
            def _():
                self.copy(way, block, cut).wait_recv()
                place = self.got.at[way, block, self.piece(cut)]
                add_rows(place, self.own.at[block, self.piece(cut)], self.step)
                self.copy(way, block, cut).start()

    def steps(self):
        return [
            functools.partial(self.step_on, hop, far, cut)
            for far in range(self.shards - 2)
            for hop in range(1, self.shards - 1 - far)
            for cut in range(self.cuts)
        ]

    def result(self, total):
        rows = self.own.shape[1]
        for way in (0, 1):
            @pl.when(self.z >= 1 if way == 0 else self.z + 1 < self.shards)
            def _():
                for cut in range(self.cuts):
                    self.copy(way, self.z, cut).wait_recv()

        @pl.loop(0, rows // 16)
        def _(i):
            block = pl.ds(aligned(i, 16), 16)
            total[block, :] = self.own[self.z, block, :].astype(jnp.float32)

            @pl.when(self.z >= 1)
            def _():
                total[block, :] += self.got[0, self.z, block, :].astype(jnp.float32)

            @pl.when(self.z + 1 < self.shards)
            def _():
                total[block, :] += self.got[1, self.z, block, :].astype(jnp.float32)

    def finish(self):
        for far in range(self.shards - 1):
            for cut in range(self.cuts):
                for way in (0, 1):
                    block = self.shards - 1 - far if way == 0 else far

                    @pl.when(self.z < block if way == 0 else self.z > block)
                    def _():
                        self.copy(way, block, cut).wait_send()


def line_scratch(shards, rows, columns, cuts):
    dma = pltpu.SemaphoreType.DMA
    return [
        pltpu.VMEM((shards, rows, columns), jnp.bfloat16),
        pltpu.VMEM((2, shards, rows, columns), jnp.bfloat16),
        dma((2, shards, cuts)), dma((2, shards, cuts)),
    ]


def reducer_scratch(chunks, share, columns):
    dma = pltpu.SemaphoreType.DMA
    return [pltpu.VMEM((chunks, n * share, columns), jnp.bfloat16) for n in (8, 4, 2, 1)] + [
        dma((chunks, 7)), dma((chunks, 7)),
    ]


def pair_product(own, pair, slopes, weight, tile=512):
    rows = own.shape[1]

    @pl.loop(0, own.shape[2] // tile)
    def _(t):
        columns = pl.ds(aligned(t, tile), tile)
        value = contract_last(slopes[pl.ds(aligned(pair, 2 * rows), 2 * rows), :], weight[columns, :])
        own[2 * pair, :, columns] = value[:rows].astype(own.dtype)
        own[2 * pair + 1, :, columns] = value[rows:].astype(own.dtype)


def term_product(term, chunk, left, right):
    term.at[chunk][...] = contract_first(left[...], right[...]).astype(jnp.bfloat16)


def spaced(moves, steps, every):
    moves = list(moves)
    for i, step in enumerate(steps):
        step()
        if i % every == every - 1 and moves:
            moves.pop(0)()
    for move in moves:
        move()


def interleave(moves, steps):
    for i in range(max(len(moves), len(steps))):
        if i < len(moves):
            moves[i]()
        if i < len(steps):
            steps[i]()


def load_all(pairs, loc):
    copies = [pltpu.make_async_copy(source, target, loc.at[i]) for i, (source, target) in enumerate(pairs)]
    for copy in copies:
        copy.start()
    return copies


def further(shards):
    z = lax.axis_index("shard")
    return [(k, lax.rem(z + k, shards)) for k in (*range(1, shards), 0)]


class Chunks:
    def __init__(self, ref, chunks):
        self.ref, self.shape = ref, (chunks, ref.shape[0] // chunks, ref.shape[1])

    @property
    def at(self):
        return self

    def __getitem__(self, chunk):
        return self.ref.at[pl.ds(aligned(chunk, self.shape[1]), self.shape[1])]


def hidden_back_kernel(shards, slopes, weight, hidden, cotangent, normed_two, total, down_share, gate_up_rows,
                       s_buf, w_buf, h_buf, c_buf, n_buf, own, got, z_send, z_recv,
                       term, core, near, last, r_send, r_recv, g_core, g_near, g_last, g_send, g_recv, loc, *sems):
    cube = Cube()
    loads = load_all(((slopes, s_buf), (weight, w_buf), (hidden, h_buf), (cotangent, c_buf), (normed_two, n_buf)), loc)
    greet(cube.partners(shards), shards + 2)
    line = LineSum(shards, 3, own, got, z_send, z_recv)
    share = hidden.shape[1] // 8
    width = D // shards
    chunks, _, columns = term.shape
    g_term = Chunks(w_buf, shards)
    reducer = Reducer(cube, share, term, core, near, last, r_send, r_recv)
    g_reducer = Reducer(cube, width // 8, g_term, g_core, g_near, g_last, g_send, g_recv)
    owners = Owners(shards, 2, g_reducer.own, gate_up_rows, *sems)
    for copy in loads[:2]:
        copy.wait()
    for t in range(shards // 2):
        pair = line.pair(t)
        pair_product(own, pair, s_buf, w_buf)
        line.ready(pair)
    for copy in loads[2:]:
        copy.wait()

    def down_term(k):
        term_product(term, k, h_buf, c_buf.at[:, pl.ds(k * columns, columns)])
        reducer.start(k)

    def gate_up_term(k):
        term_product(g_term, k, n_buf.at[:, pl.ds(aligned(k, width), width)], s_buf)
        g_reducer.start(k)

    keep = []

    def keep_down(k):
        copy = pltpu.make_async_copy(reducer.own(k), down_share.at[:, pl.ds(k * columns, columns)], loc.at[5 + k])
        copy.start()
        keep.append(copy)

    def of(call, count):
        return [functools.partial(call, k) for k in range(count)]

    turn = further(shards)

    def each(call):
        return [functools.partial(call, o) for _, o in turn]

    moves = line.steps()

    def down_ending(k):
        reducer.after_last(k)
        keep_down(k)

    def g_ending(k, o):
        g_reducer.after_last(o)
        owners.start(k)

    cores = of(reducer.after_core, chunks) + each(g_reducer.after_core)
    nears = of(reducer.after_near, chunks) + each(g_reducer.after_near)
    lasts = of(down_ending, chunks) + [functools.partial(g_ending, k, o) for k, o in turn]
    g_terms = each(gate_up_term)
    sequence = of(down_term, chunks) + cores[:2] + g_terms[:2] + nears[:1] + cores[2:3] + g_terms[2:] + nears[1:2] + lasts[:1]
    sequence += cores[3:4] + moves[:5]
    for i in range(2, chunks + shards):
        sequence += nears[i : i + 1] + lasts[i - 1 : i] + cores[i + 2 : i + 3] + moves[i + 3 : i + 4]
    sequence += lasts[-1:] + moves[chunks + shards + 3 :]
    for step in sequence:
        step()
    line.result(total)
    line.finish()
    owners.arrive()
    for k in range(chunks):
        reducer.finish(k)
    for k in range(shards):
        g_reducer.finish(k)
    owners.finish()
    for copy in keep:
        copy.wait()


def hidden_back_call(shards, slopes, weight, hidden, cotangent, normed_two):
    group, inner = hidden.shape
    rows = group // shards
    share = inner // 8
    chunks = 4
    width = D // shards
    low = jnp.bfloat16
    any_ = pl.BlockSpec(memory_space=pl.ANY)
    dma = pltpu.SemaphoreType.DMA
    return pl.pallas_call(
        functools.partial(hidden_back_kernel, shards),
        out_shape=[
            jax.ShapeDtypeStruct((rows, D), jnp.float32),
            jax.ShapeDtypeStruct((share, D), low),
            jax.ShapeDtypeStruct((width // 8, shards * 2 * inner), low),
        ],
        in_specs=[any_] * 5,
        out_specs=[pl.BlockSpec(memory_space=pltpu.VMEM), any_, any_],
        scratch_shapes=[pltpu.VMEM(a.shape, low) for a in (slopes, weight, hidden, cotangent, normed_two)]
        + line_scratch(shards, rows, D, 3) + reducer_scratch(chunks, share, D // chunks)
        + reducer_scratch(shards, width // 8, 2 * inner)[1:] + [dma((5 + chunks,))] + owner_sems(shards, 2),
        compiler_params=pltpu.CompilerParams(collective_id=6, has_side_effects=True, vmem_limit_bytes=63 * 2**20),
        name="hidden_back",
        cost_estimate=pl.CostEstimate(flops=10**10, bytes_accessed=200 * 10**6, transcendentals=0),
    )(slopes, weight, hidden, cotangent, normed_two)


def norm_back_rows(slope, values, gain):
    centered = values - jnp.mean(values, axis=-1, keepdims=True)
    inverse = lax.rsqrt(jnp.mean(centered * centered, axis=-1, keepdims=True) + norm_eps)
    unit = centered * inverse
    scaled = slope * gain
    back = inverse * (
        scaled
        - jnp.mean(scaled, axis=-1, keepdims=True)
        - unit * jnp.mean(scaled * unit, axis=-1, keepdims=True)
    )
    return back, unit


def heads_back_kernel(shards, rows, d_normed_two, middle, cotangent, gain, out_weight, qkv, stats, seg_rows, seg_columns,
                      cosine, minus, plus, down_share, gate_up_rows,
                      d_middle, norm_grads, d_qkv, bias_grad, m_columns, down_grad, gate_up_grad,
                      o_buf, m_low, da_own, d_attended, d_keys, d_values, e_send, e_recv, loc, *sems):
    cube = Cube()
    z = lax.axis_index("shard")
    loads = load_all(((out_weight, o_buf),), loc)
    greet(cube.partners(shards), shards + 2)
    width = D // shards
    half = gate_up_rows.shape[1] // 2
    gatherers = [Gatherer(cube, down_share, down_grad, sems[0:3])] + [
        Gatherer(cube, gate_up_rows.at[:, pl.ds(i * half, half)], gate_up_grad.at[:, pl.ds(i * half, half)], sems[3 * i + 3 : 3 * i + 6])
        for i in (0, 1)
    ]
    gatherers[0].start()
    gatherers[1].start()
    arrays = ((da_own, d_attended), (m_low, m_columns))

    def move(k, o):
        source, target = arrays[k]
        return remote(source.at[:, pl.ds(o * width, width)], target.at[pl.ds(aligned(z, rows), rows)],
                      e_send.at[k, o], e_recv.at[k, z], {"shard": o})

    def arrival(k, o):
        place = arrays[k][1].at[pl.ds(o * rows, rows)]
        return remote(place, place, e_send.at[k, o], e_recv.at[k, o], {"shard": o})

    def here(k, o):
        source, target = arrays[k]
        return pltpu.make_async_copy(source.at[:, pl.ds(o * width, width)], target.at[pl.ds(o * rows, rows)], loc.at[1 + k])

    def begin(k, o):
        @pl.when(z != o)
        def _():
            move(k, o).start()

        @pl.when(z == o)
        def _():
            here(k, o).start()

    def arrive(k):
        for o in range(shards):
            @pl.when(z != o)
            def _():
                arrival(k, o).wait_recv()

            @pl.when(z == o)
            def _():
                here(k, o).wait()

    norm_grads[...] = jnp.zeros_like(norm_grads)

    @pl.loop(0, rows // 16)
    def _(i):
        block = pl.ds(aligned(i, 16), 16)
        slope = d_normed_two[block, :]
        back, unit = norm_back_rows(slope, middle[block, :], gain[...])
        value = cotangent[block, :].astype(jnp.float32) + back
        d_middle[block, :] = value
        m_low[block, :] = value.astype(jnp.bfloat16)
        norm_grads[0:8, :] += (slope * unit).reshape(2, 8, D).sum(axis=0)
        norm_grads[8:16, :] += slope.reshape(2, 8, D).sum(axis=0)

    loads[0].wait()
    for o in range(shards):
        da_own[:, o * width : (o + 1) * width] = contract_last(
            m_low[...], o_buf[o * width : (o + 1) * width, :]).astype(jnp.bfloat16)
        begin(0, o)
    for o in range(shards):
        begin(1, o)
    arrive(0)
    gatherers[0].pass_on()

    def nothing():
        pass

    steps = [nothing, gatherers[1].pass_on, gatherers[2].start] + [nothing] * 4 + [gatherers[0].pass_last] + [nothing] * 3
    steps += [gatherers[1].pass_last]
    attend_back_body(rows, qkv, d_attended, stats, seg_rows, seg_columns, cosine, minus, plus,
                     d_qkv, bias_grad, d_keys, d_values, steps)
    for step in steps:
        step()
    gatherers[2].pass_on()
    arrive(1)
    gatherers[2].pass_last()
    for k in (0, 1):
        for o in range(shards):
            @pl.when(z != o)
            def _():
                move(k, o).wait_send()
    for gatherer in gatherers:
        gatherer.finish()


def heads_back_call(shards, rows, d_normed_two, middle, cotangent, gain, out_weight, qkv, stats, seg_rows, seg_columns,
                    cosine, minus, plus, down_share, gate_up_rows):
    group = qkv.shape[0]
    width = D // shards
    vm = pl.BlockSpec(memory_space=pltpu.VMEM)
    any_ = pl.BlockSpec(memory_space=pl.ANY)
    dma = pltpu.SemaphoreType.DMA
    low = jnp.bfloat16
    f32 = jnp.float32
    return pl.pallas_call(
        functools.partial(heads_back_kernel, shards, rows),
        out_shape=[
            jax.ShapeDtypeStruct((rows, D), f32),
            jax.ShapeDtypeStruct((16, D), f32),
            jax.ShapeDtypeStruct((group, 3 * width), low),
            jax.ShapeDtypeStruct((8, 3 * width), f32),
            jax.ShapeDtypeStruct((group, width), low),
            jax.ShapeDtypeStruct((8 * down_share.shape[0], D), low),
            jax.ShapeDtypeStruct((8 * gate_up_rows.shape[0], gate_up_rows.shape[1]), low),
        ],
        in_specs=[vm] * 4 + [any_] + [vm] * 7 + [any_] * 2,
        out_specs=[vm, vm, vm, vm, any_, any_, any_],
        scratch_shapes=[
            pltpu.VMEM(out_weight.shape, low), pltpu.VMEM((rows, D), low), pltpu.VMEM((rows, D), low),
            pltpu.VMEM((group, width), low),
            pltpu.VMEM((group, width), f32), pltpu.VMEM((group, width), f32),
        ] + [dma((2, shards)), dma((2, shards)), dma((3,))] + gatherer_sems() * 3,
        compiler_params=pltpu.CompilerParams(collective_id=7, has_side_effects=True, vmem_limit_bytes=56 * 2**20),
        name="heads_back",
        cost_estimate=pl.CostEstimate(flops=10**10, bytes_accessed=200 * 10**6, transcendentals=0),
    )(d_normed_two, middle, cotangent, gain, out_weight, qkv, stats, seg_rows, seg_columns, cosine, minus, plus,
      down_share, gate_up_rows)


def input_back_kernel(shards, slopes, weight, normed, attended, d_middle_columns, tokens, gain, d_middle, bias_grad, norm_grads,
                      input_grad, small, qkv_grad, out_grad,
                      w_buf, n_buf, a_buf, m_buf, total, part, part_in, own, got, z_send, z_recv,
                      term, core, near, last, r_send, r_recv, o_term, o_core, o_near, o_last, o_send, o_recv,
                      qkv_rows, out_rows, s_send, s_recv, loc, *sems):
    cube = Cube()
    z = lax.axis_index("shard")
    loads = load_all(((attended, a_buf), (d_middle_columns, m_buf), (weight, w_buf), (normed, n_buf)), loc)
    greet(cube.partners(shards), shards + 2)
    rows = tokens.shape[0]
    width = D // shards
    share = width // 8
    line = LineSum(shards, 3, own, got, z_send, z_recv)
    reducer = Reducer(cube, share, term, core, near, last, r_send, r_recv)
    o_reducer = Reducer(cube, share, o_term, o_core, o_near, o_last, o_send, o_recv)
    owners = Owners(shards, 3, reducer.own, qkv_rows, *sems[0:3])
    o_owners = Owners(shards, 1, o_reducer.own, out_rows, *sems[3:6])
    gatherer = Gatherer(cube, qkv_rows, qkv_grad, sems[6:9])
    o_gatherer = Gatherer(cube, out_rows, out_grad, sems[9:12])

    def qkv_term(o):
        term_product(term, o, n_buf.at[:, pl.ds(aligned(o, width), width)], slopes)
        reducer.start(o)

    def out_term(o):
        term_product(o_term, o, a_buf.at[:, pl.ds(aligned(o, width), width)], m_buf)
        o_reducer.start(o)

    def product(t):
        pair = line.pair(t)
        pair_product(own, pair, slopes, w_buf)
        if t + 1 < shards // 2:
            line.ready(pair)

    turn = further(shards)

    def each(call):
        return [functools.partial(call, o) for _, o in turn]

    def ending(red, own_, k, o):
        red.after_last(o)
        own_.start(k)

    loads[0].wait()
    loads[1].wait()
    for _, o in turn:
        out_term(o)
    loads[2].wait()
    moves = line.steps()
    cores, nears = each(reducer.after_core), each(reducer.after_near)
    lasts = [functools.partial(ending, reducer, owners, k, o) for k, o in turn]
    terms = each(qkv_term)
    sequence = [functools.partial(product, 0)] + each(o_reducer.after_core)
    sequence += [functools.partial(product, t) for t in range(1, shards // 2)] + [loads[3].wait] + each(o_reducer.after_near)
    sequence += terms[:2] + cores[:1] + terms[2:3] + cores[1:2] + terms[3:]
    sequence += [functools.partial(ending, o_reducer, o_owners, k, o) for k, o in turn]
    sequence += moves[:2] + nears[:1] + cores[2:3] + moves[2:4] + nears[1:2] + lasts[:1] + cores[3:] + moves[4:6]
    for i in range(2, shards):
        sequence += nears[i : i + 1] + lasts[i - 1 : i] + moves[i + 4 : i + 5]
    sequence += lasts[-1:] + [line.nearest] + moves[shards + 4 :]
    sequence += [o_owners.arrive, o_gatherer.start]
    for step in sequence:
        step()
    owners.arrive()
    gatherer.start()
    line.result(total)

    part[...] = jnp.zeros_like(part)

    @pl.loop(0, rows // 16)
    def _(i):
        block = pl.ds(aligned(i, 16), 16)
        slope = total[block, :]
        back, unit = norm_back_rows(slope, tokens[block, :].astype(jnp.float32), gain[...])
        input_grad[block, :] = d_middle[block, :] + back
        ones = (slope * unit).reshape(2, 8, D).sum(axis=0).sum(axis=0, keepdims=True)
        twos = slope.reshape(2, 8, D).sum(axis=0).sum(axis=0, keepdims=True)
        for o in range(shards):
            part[o, 3:4, :] += ones[:, o * width : (o + 1) * width]
            part[o, 4:5, :] += twos[:, o * width : (o + 1) * width]
    for o in range(shards):
        for k in range(2):
            part[o, 5 + k : 6 + k, :] = jnp.sum(
                norm_grads[8 * k : 8 * k + 8, o * width : (o + 1) * width], axis=0, keepdims=True)
    for k in range(3):
        flat = k * shards + z
        part[flat // 3, pl.ds(flat % 3, 1), :] = bias_grad[0:1, k * width : (k + 1) * width]

    def small_copy(o):
        return remote(part.at[o], part_in.at[z], s_send.at[o], s_recv.at[z], {"shard": o})

    def small_arrival(o):
        return remote(part.at[o], part_in.at[o], s_send.at[o], s_recv.at[o], {"shard": o})

    for o in range(shards):
        @pl.when(z != o)
        def _():
            small_copy(o).start()
    small[...] = part[z]
    for o in range(shards):
        @pl.when(z != o)
        def _():
            small_arrival(o).wait_recv()
            small[...] += part_in[o]
    sums = [remote(small, part_in.at[shards + i], s_send.at[shards + i], s_recv.at[shards + i], device)
            for i, device in enumerate((cube.to_core, cube.to_x, cube.to_y))]

    def add_small(i):
        sums[i].start()
        sums[i].wait()
        small[...] += part_in[shards + i]

    add_small(0)
    o_gatherer.pass_on()
    gatherer.pass_on()
    add_small(1)
    add_small(2)
    o_gatherer.pass_last()
    gatherer.pass_last()
    for o in range(shards):
        @pl.when(z != o)
        def _():
            small_copy(o).wait_send()
    line.finish()
    for k in range(shards):
        reducer.finish(k)
        o_reducer.finish(k)
    owners.finish()
    o_owners.finish()
    gatherer.finish()
    o_gatherer.finish()


def input_back_call(shards, slopes, weight, normed, attended, d_middle_columns, tokens, gain, d_middle, bias_grad, norm_grads):
    group = slopes.shape[0]
    rows = group // shards
    width = D // shards
    share = width // 8
    vm = pl.BlockSpec(memory_space=pltpu.VMEM)
    any_ = pl.BlockSpec(memory_space=pl.ANY)
    dma = pltpu.SemaphoreType.DMA
    low = jnp.bfloat16
    f32 = jnp.float32
    return pl.pallas_call(
        functools.partial(input_back_kernel, shards),
        out_shape=[
            jax.ShapeDtypeStruct((rows, D), f32),
            jax.ShapeDtypeStruct((8, width), f32),
            jax.ShapeDtypeStruct((width, 3 * D), low),
            jax.ShapeDtypeStruct((width, D), low),
        ],
        in_specs=[vm] + [any_] * 4 + [vm] * 5,
        out_specs=[vm, vm, any_, any_],
        scratch_shapes=[
            pltpu.VMEM(weight.shape, low), pltpu.VMEM(normed.shape, low), pltpu.VMEM(attended.shape, low),
            pltpu.VMEM(d_middle_columns.shape, low), pltpu.VMEM((rows, D), f32),
            pltpu.VMEM((shards, 8, width), f32), pltpu.VMEM((shards + 3, 8, width), f32),
        ] + line_scratch(shards, rows, D, 3) + reducer_scratch(shards, share, 3 * width) + reducer_scratch(shards, share, width)
        + [pltpu.VMEM((share, 3 * D), low), pltpu.VMEM((share, D), low), dma((shards + 3,)), dma((shards + 3,)), dma((4,))]
        + owner_sems(shards, 3) + owner_sems(shards, 1) + gatherer_sems() * 2,
        compiler_params=pltpu.CompilerParams(collective_id=8, has_side_effects=True, vmem_limit_bytes=60 * 2**20),
        name="input_back",
        cost_estimate=pl.CostEstimate(flops=10**10, bytes_accessed=200 * 10**6, transcendentals=0),
    )(slopes, weight, normed, attended, d_middle_columns, tokens, gain, d_middle, bias_grad, norm_grads)


def swap_pieces(pieces):
    shards = lax.axis_size("shard")
    here = lax.axis_index("shard")
    out = pieces
    for k in range(1, shards):
        partner = jnp.bitwise_xor(here, k)
        piece = lax.dynamic_index_in_dim(pieces, partner, axis=0, keepdims=True)
        piece = lax.ppermute(piece, "shard", [(i, i ^ k) for i in range(shards)])
        out = lax.dynamic_update_slice_in_dim(out, piece, partner, axis=0)
    return out


def own_share(rows):
    own = rows.shape[0] // lax.axis_size("replica")
    return lax.dynamic_slice_in_dim(rows, lax.axis_index("replica") * own, own, axis=0)


def spread_rows(rows, columns):
    shards = lax.axis_size("shard")
    piece = own_share(rows)
    own = piece.shape[0]
    piece = piece.reshape(own, columns, shards, -1).transpose(2, 0, 1, 3).reshape(shards, own, -1)
    full = lax.all_gather(swap_pieces(piece), "replica", axis=0, tiled=False)
    return full.transpose(1, 0, 2, 3).reshape(rows.shape[0] * shards, -1)


def gather_rows(rows):
    shards = lax.axis_size("shard")
    piece = own_share(rows)
    moved = swap_pieces(jnp.broadcast_to(piece[None], (shards,) + piece.shape))
    full = lax.all_gather(moved, "replica", axis=0, tiled=False)
    return full.transpose(1, 0, 2, 3).reshape(rows.shape[0] * shards, -1)


def own_rows(features):
    copies = lax.axis_size("replica")
    shards = lax.axis_size("shard")
    count = features.shape[0]
    return (
        features.reshape(count, shards, copies, -1).transpose(0, 2, 1, 3).reshape(count, -1)
    )


def sum_columns(features, slopes, columns):
    shards = lax.axis_size("shard")
    term = contract_first(own_rows(features), slopes).astype(jnp.bfloat16)
    part = lax.psum_scatter(term, "replica", scatter_dimension=0, tiled=True)
    own = part.shape[0] // shards
    moved = swap_pieces(part.reshape(shards, own, -1))
    moved = moved.reshape(shards, own, columns, -1).transpose(1, 2, 0, 3).reshape(own, -1)
    return lax.all_gather(moved, "replica", axis=0, tiled=True)


def swiglu(gate_up):
    half = gate_up.shape[1] // 2
    return jax.nn.silu(gate_up[:, :half]) * gate_up[:, half:]


def norm_stats(values):
    mean = jnp.mean(values, axis=-1, keepdims=True)
    centered = values - mean
    inverse = lax.rsqrt(jnp.mean(centered * centered, axis=-1, keepdims=True) + norm_eps)
    return centered * inverse, inverse


def norm_back(slope, unit, inverse, gain):
    scaled = slope * gain
    return inverse * (
        scaled
        - jnp.mean(scaled, axis=-1, keepdims=True)
        - unit * jnp.mean(scaled * unit, axis=-1, keepdims=True)
    )


def start_plain(tokens, vectors, qkv_weight, cosine, minus, plus):
    shards = lax.axis_size("shard")
    here = lax.axis_index("shard")
    all_tokens = lax.all_gather(tokens, "shard", axis=0, tiled=False)
    all_vectors = lax.all_gather(vectors, "shard", axis=0, tiled=False)
    weight = spread_rows(qkv_weight, 3)
    width = D // shards
    gain, shift = (all_vectors[:, 3 + i].reshape(D) for i in (0, 1))
    unit, _ = norm_stats(all_tokens.reshape(-1, D).astype(jnp.float32))
    normed = (unit * gain + shift).astype(jnp.bfloat16)
    bias = all_vectors[:, :3].reshape(3, shards, width)
    bias = lax.dynamic_index_in_dim(bias, here, axis=1, keepdims=False).reshape(3 * width)
    value = jnp.dot(normed, weight, preferred_element_type=jnp.float32) + bias
    turned = value[:, : 2 * width]
    wide = [jnp.tile(t, (1, 2 * width // 128)) for t in (cosine, minus, plus)]
    turned = (
        turned * wide[0] + jnp.roll(turned, -8, 1) * wide[1] + jnp.roll(turned, 8, 1) * wide[2]
    )
    qkv = jnp.concatenate([turned, value[:, 2 * width :]], axis=1).astype(jnp.bfloat16)
    return all_tokens, all_vectors, normed, qkv, weight


def layer_kernels(shards, tokens, cotangent, weights, vectors, tables):
    qkv_weight, out_weight, gate_up_weight, down_weight = weights
    seg_rows, seg_columns, cosine, minus, plus = tables
    rows = tokens.shape[0]
    f32 = jnp.float32
    low = jnp.bfloat16
    all_tokens, all_vectors, normed, qkv, weight_qkv, weight_out = start_call(
        shards, tokens, vectors, qkv_weight, out_weight, cosine, minus, plus
    )
    gain_one, shift_one, gain_two, shift_two = (
        all_vectors[:, 3 + i].reshape(1, D) for i in range(4)
    )
    attended, stats, weight_gate_up = attend_spread_call(
        shards, rows, qkv, seg_rows, seg_columns, gate_up_weight
    )
    middle, normed_two, hidden, slopes, group_cotangent, down_part = hidden_call(
        shards, attended, all_tokens, weight_out, weight_gate_up, down_weight, cotangent, gain_two, shift_two
    )
    d_normed_two, down_share, gate_up_rows = hidden_back_call(
        shards, slopes, weight_gate_up, hidden, group_cotangent.reshape(shards * rows, D), normed_two
    )
    down_parts = down_part[:, : D // 2], down_part[:, D // 2 :]

    def sum_half(half):
        return lax.psum_scatter(half, "shard", scatter_dimension=0, tiled=True)

    first_half, d_normed_two = lax.optimization_barrier((down_parts[0], d_normed_two))
    first_half = sum_half(first_half)
    d_middle, norm_grads, d_qkv, bias_grad, d_middle_columns, down_grad, gate_up_grad = heads_back_call(
        shards, rows, d_normed_two, middle, cotangent, gain_two, weight_out, qkv, stats, seg_rows, seg_columns,
        cosine, minus, plus, down_share, gate_up_rows,
    )
    second_half, d_qkv = lax.optimization_barrier((down_parts[1], d_qkv))
    down_own = jnp.concatenate([first_half, sum_half(second_half)], axis=1)
    input_grad, small, qkv_grad, out_grad = input_back_call(
        shards, d_qkv, weight_qkv, normed, attended, d_middle_columns, tokens, gain_one, d_middle, bias_grad, norm_grads
    )
    mixed = (middle + down_own.astype(f32)).astype(low)
    return mixed, input_grad, small, (qkv_grad, out_grad, gate_up_grad, down_grad)


def layer_plain(shards, tokens, cotangent, weights, vectors, tables):
    qkv_weight, out_weight, gate_up_weight, down_weight = weights
    seg_rows, seg_columns, cosine, minus, plus = tables
    here = lax.axis_index("shard")
    row_count = tokens.shape[0]
    group_rows = row_count * shards
    width = D // shards
    f32 = jnp.float32
    low = jnp.bfloat16
    weight_out = gather_rows(out_weight)
    weight_gate_up = spread_rows(gate_up_weight, 2)
    all_tokens, all_vectors, normed_low, qkv, weight_qkv = start_plain(
        tokens, vectors, qkv_weight, cosine, minus, plus
    )
    gain_one, shift_one, gain_two, shift_two = (
        all_vectors[:, 3 + i].reshape(D) for i in range(4)
    )
    cotangent_later, qkv = lax.optimization_barrier((cotangent, qkv))
    group_cotangent = lax.all_gather(cotangent_later, "shard", axis=0, tiled=True)

    def local(array):
        return lax.dynamic_slice_in_dim(array, here * row_count, row_count, axis=0)

    attended, stats = attend_call(shards, row_count, qkv, seg_rows, seg_columns)
    inputs = all_tokens.reshape(group_rows, D).astype(f32)
    middle = inputs + jnp.dot(attended, weight_out, preferred_element_type=f32)
    unit_two, inverse_two = norm_stats(middle)
    normed_two_low = (unit_two * gain_two + shift_two).astype(low)
    gate_up = jnp.dot(normed_two_low, weight_gate_up, preferred_element_type=f32)
    hidden, swiglu_pull = jax.vjp(swiglu, gate_up)
    hidden_low = hidden.astype(low)
    d_hidden = contract_last(group_cotangent, down_weight)
    d_gate_up_low = swiglu_pull(d_hidden)[0].astype(low)
    down_part = jnp.dot(hidden_low, down_weight, preferred_element_type=f32).astype(low)
    unit_two_own = local(unit_two)
    inverse_two_own = local(inverse_two)
    middle_own = local(middle)

    d_normed_two_part = contract_last(d_gate_up_low, weight_gate_up).astype(low)
    d_normed_two = scatter_call(shards, d_normed_two_part.reshape(shards, row_count, D), 3)
    down_grad = lax.psum(contract_first(hidden_low, group_cotangent).astype(low), "replica")
    d_middle = cotangent.astype(f32) + norm_back(
        d_normed_two, unit_two_own, inverse_two_own, gain_two
    )
    d_gain_two = jnp.sum(d_normed_two * unit_two_own, axis=0)
    d_shift_two = jnp.sum(d_normed_two, axis=0)
    d_middle_low = d_middle.astype(low)
    d_attended_own = contract_last(d_middle_low, weight_out).astype(low)
    d_attended, d_middle_columns = exchange_call(shards, d_attended_own, d_middle_low)
    d_projected_low, bias_part = attend_back_call(
        row_count, qkv, d_attended.reshape(group_rows, width), stats, seg_rows, seg_columns,
        cosine, minus, plus,
    )
    down_own = lax.psum_scatter(down_part, "shard", scatter_dimension=0, tiled=True)
    mixed = (middle_own + down_own.astype(f32)).astype(low)
    d_normed_part = contract_last(d_projected_low, weight_qkv).astype(low)
    d_normed = scatter_call(shards, d_normed_part.reshape(shards, row_count, D), 4)
    gate_up_grad = sum_columns(normed_two_low, d_gate_up_low, 2)
    out_grad = sum_columns(attended, d_middle_columns.reshape(group_rows, width), 1)
    qkv_grad = sum_columns(normed_low, d_projected_low, 3)
    unit_one, inverse_one = norm_stats(tokens.astype(f32))
    input_grad = d_middle + norm_back(d_normed, unit_one, inverse_one, gain_one)
    d_gain_one = jnp.sum(d_normed * unit_one, axis=0)
    d_shift_one = jnp.sum(d_normed, axis=0)

    bias_part = bias_part[0].reshape(3, 1, width)
    bias_wide = lax.dynamic_update_slice(
        jnp.zeros((3, shards, width), f32), bias_part, (0, here, 0)
    ).reshape(shards, 3 * width)
    small = jnp.concatenate(
        [bias_wide]
        + [v.reshape(shards, width) for v in (d_gain_one, d_shift_one, d_gain_two, d_shift_two)],
        axis=1,
    )
    small = jnp.pad(small, ((0, 0), (0, width)))
    small = lax.psum(small, ("replica", "shard"))
    small = lax.dynamic_index_in_dim(small, here, axis=0, keepdims=False)
    return mixed, input_grad, small, (qkv_grad, out_grad, gate_up_grad, down_grad)


def on_device(
    tokens,
    cotangent,
    qkv_weight,
    qkv_bias,
    out_weight,
    gate_up_weight,
    down_weight,
    norm1_gain,
    norm1_shift,
    norm2_gain,
    norm2_shift,
    seq_lengths,
):
    shards = lax.axis_size("shard")
    copies = lax.axis_size("replica")
    row_count = tokens.shape[0]
    group_rows = row_count * shards
    width = D // shards
    f32 = jnp.float32
    low = jnp.bfloat16

    segment, position = group_layout(seq_lengths[0], jnp.arange(group_rows, dtype=jnp.int32))
    seg_rows = jnp.broadcast_to(segment[:, None], (group_rows, 128))
    seg_columns = jnp.broadcast_to(segment[None, :], (8, group_rows))
    lane = jnp.arange(128, dtype=jnp.int32)[None, :] % HEAD_DIM
    cosine, sine_value = rope_tables(position, lane % (ROT_DIM // 2))
    cosine = jnp.where(lane < ROT_DIM, cosine, 1.0)
    minus = jnp.where(lane < ROT_DIM // 2, -sine_value, 0.0)
    plus = jnp.where((lane >= ROT_DIM // 2) & (lane < ROT_DIM), sine_value, 0.0)

    vectors = jnp.zeros((8 * width,), f32)
    at = 0
    for vector in (qkv_bias, norm1_gain, norm1_shift, norm2_gain, norm2_shift):
        after = 8 * width - at - vector.shape[0]
        vectors = vectors + jnp.pad(vector.astype(f32), (at, after))
        at += vector.shape[0]
    vectors = vectors.reshape(8, width)
    weights = (qkv_weight, out_weight, gate_up_weight, down_weight)
    tables = (seg_rows, seg_columns, cosine, minus, plus)
    if copies == 8:
        outputs = layer_kernels(shards, tokens, cotangent, weights, vectors, tables)
    else:
        outputs = layer_plain(shards, tokens, cotangent, weights, vectors, tables)
    mixed, input_grad, small, grads = outputs
    bias_rows = 3 * width
    small = small.reshape(8 * width)
    out_dtype = tuple(grad.astype(f32) for grad in grads)
    return (
        mixed,
        input_grad,
        out_dtype[0],
        small[:bias_rows],
        out_dtype[1],
        out_dtype[2],
        out_dtype[3],
    ) + tuple(small[bias_rows + i * width : bias_rows + (i + 1) * width] for i in range(4))


def solution(mesh):
    placed = (
        P(("replica", "shard"), None),
        P(("replica", "shard"), None),
        P("shard", None),
        P("shard"),
        P("shard", None),
        P("shard", None),
        P("shard", None),
        P("shard"),
        P("shard"),
        P("shard"),
        P("shard"),
        P("replica", None),
    )
    return jax.shard_map(
        on_device,
        mesh=mesh,
        in_specs=placed,
        out_specs=(
            P(("replica", "shard"), None),
            P(("replica", "shard"), None),
            P("shard", None),
            P("shard"),
            P("shard", None),
            P("shard", None),
            P("shard", None),
            P("shard"),
            P("shard"),
            P("shard"),
            P("shard"),
        ),
        check_vma=False,
    )
```

```python
import functools

import jax
import jax.numpy as jnp
from jax import lax
from jax.experimental import pallas as pl
from jax.experimental.pallas import tpu as pltpu
from jax.sharding import PartitionSpec as P

D = 2048
FF = 5632
HEADS = 32
HEAD_DIM = 64
ROT_DIM = 16
MESH = pl.DeviceIdType.MESH


norm_eps = 1e-05
masked_score = -1000000000.0


def group_layout(lengths, token_index):
    segment = jnp.zeros_like(token_index)
    position = token_index
    end = jnp.int32(0)
    for i in range(lengths.shape[0]):
        end = end + lengths[i]
        passed = (token_index >= end).astype(jnp.int32)
        segment = segment + passed
        position = position - passed * lengths[i]
    return (segment, position)


def rope_tables(position, index):
    frequency = jnp.exp(-jnp.log(10000.0) * (2.0 * index.astype(jnp.float32) / ROT_DIM))
    angles = position.astype(jnp.float32)[:, None] * frequency
    return (jnp.cos(angles), jnp.sin(angles))


def contract_last(left, right):
    return lax.dot_general(
        left, right, (((1,), (1,)), ((), ())), preferred_element_type=jnp.float32
    )


def aligned(value, unit):
    return pl.multiple_of(value * unit, unit)


def greet(partners, count):
    barrier = pltpu.get_barrier_semaphore()
    for there, device in partners:
        @pl.when(there)
        def _():
            pl.semaphore_signal(barrier, inc=1, device_id=device, device_id_type=MESH)
    pl.semaphore_wait(barrier, count)


def greet_line(z, shards):
    count = (z + shards - 1) // shards + (2 * shards - 2 - z) // shards
    greet([(z >= 1, {"shard": z - 1}), (z + 1 < shards, {"shard": z + 1})], count)


def remote(source, target, send, recv, device):
    return pltpu.make_async_remote_copy(
        src_ref=source, dst_ref=target, send_sem=send, recv_sem=recv,
        device_id=device, device_id_type=MESH,
    )


class Cube:
    def __init__(self):
        r = lax.axis_index("replica")
        self.core, self.x, self.y = r % 2, (r // 2) % 2, r // 4
        self.place = 2 * self.y + self.x
        self.to_x = {"replica": r + 2 - 4 * self.x}
        self.to_y = {"replica": r + 4 - 8 * self.y}
        self.to_core = {"replica": r + 1 - 2 * self.core}

    def partners(self, shards):
        z = lax.axis_index("shard")
        return [((z != o), {"shard": o}) for o in range(shards)] + [
            (z >= 0, d) for d in (self.to_x, self.to_y, self.to_core)
        ]


def rows_of(ref, start, unit, count):
    return ref.at[pl.ds(pl.multiple_of(start, unit), count)]


class Spreader:
    def __init__(self, cube, shards, share, parts, source, out, sems):
        self.cube, self.shards, self.share, self.parts = cube, shards, share, parts
        self.source, self.out = source, out
        self.z_send, self.z_recv, self.send, self.recv, self.loc = sems
        self.cut = 16 * ((share // 16 + 1) // 2)
        self.z = lax.axis_index("shard")
        r = lax.axis_index("replica")
        self.who = (r, r + 2 - 4 * cube.x, r + 4 - 8 * cube.y, 4 * (1 - cube.y) + 2 * (1 - cube.x) + cube.core)

    def rows(self, o, kind, half=None):
        first, count = {None: (0, self.share), 0: (0, self.cut), 1: (self.cut, self.share - self.cut)}[half]
        return rows_of(self.out, (o * 8 + self.who[kind]) * self.share + first, 16, count)

    def target(self, o, part):
        width = self.out.shape[1] // self.parts
        return self.rows(o, 0).at[:, pl.ds(part * width, width)]

    def z_copy(self, o, part):
        return remote(self.source(o, part), self.target(self.z, part), self.z_send.at[o, part], self.z_recv.at[self.z, part], {"shard": o})

    def z_arrival(self, o, part):
        place = self.target(o, part)
        return remote(place, place, self.z_send.at[o, part], self.z_recv.at[o, part], {"shard": o})

    def local(self, o, part):
        return pltpu.make_async_copy(self.source(o, part), self.target(o, part), self.loc.at[part])

    def start_own(self):
        for part in range(self.parts):
            self.local(self.z, part).start()

    def start(self):
        for o in range(self.shards):
            for part in range(self.parts):
                @pl.when(self.z != o)
                def _():
                    self.z_copy(o, part).start()

    def sent(self):
        for o in range(self.shards):
            for part in range(self.parts):
                @pl.when(self.z != o)
                def _():
                    self.z_copy(o, part).wait_send()

    def copy(self, kind, o):
        c = self.cube
        block, device = (
            (self.rows(o, 0), c.to_x),
            (self.rows(o, 0), c.to_y),
            (self.rows(o, 1, 0), c.to_y),
            (self.rows(o, 2, 1), c.to_x),
            (self.rows(o, 0), c.to_core),
            (self.rows(o, 1), c.to_core),
            (self.rows(o, 2), c.to_core),
            (self.rows(o, 3), c.to_core),
        )[kind]
        return remote(block, block, self.send.at[kind, o], self.recv.at[kind, o], device)

    def arrive(self, distance):
        for o in range(self.shards):
            @pl.when((self.z - o == distance) | (o - self.z == distance))
            def _():
                for part in range(self.parts):
                    if distance == 0:
                        self.local(o, part).wait()
                    else:
                        self.z_arrival(o, part).wait_recv()
                for kind in (0, 1, 4):
                    self.copy(kind, o).start()

    def pass_on(self, o):
        self.copy(0, o).wait_recv()
        self.copy(2, o).start()
        self.copy(5, o).start()
        self.copy(1, o).wait_recv()
        self.copy(3, o).start()
        self.copy(6, o).start()

    def pass_last(self, o):
        self.copy(2, o).wait_recv()
        self.copy(3, o).wait_recv()
        self.copy(7, o).start()

    def landed(self):
        for o in range(self.shards):
            for kind in (4, 5, 6, 7):
                self.copy(kind, o).wait_recv()

    def finish(self):
        for o in range(self.shards):
            for kind in range(8):
                self.copy(kind, o).wait_send()


def spread_sems(shards, parts):
    dma = pltpu.SemaphoreType.DMA
    return [dma((shards, parts)), dma((shards, parts)), dma((8, shards)), dma((8, shards)), dma((parts,))]


class Line:
    def __init__(self, shards, pieces, own, buf, send, recv):
        self.z = lax.axis_index("shard")
        self.shards, self.pieces, self.own, self.buf, self.send, self.recv = shards, pieces, own, buf, send, recv
        self.rows = buf.shape[1] // pieces

    def copy(self, way, step, piece):
        target = self.z + 1 if way == 0 else self.z - 1
        owner = self.z - step if way == 0 else self.z + step
        block = pl.ds(piece * self.rows, self.rows)
        place = self.buf.at[owner, block]
        source = self.own.at[block] if step == 0 and self.own is not None else place
        return remote(source, place, self.send.at[way, step, piece], self.recv.at[way, step, piece], {"shard": target})

    def sends(self, way, step):
        if way == 0:
            return (self.z + 1 < self.shards) & (self.z - step >= 0)
        return (self.z >= 1) & (self.z + step < self.shards)

    def gets(self, way, step):
        return (self.z - step >= 1) if way == 0 else (self.z + step + 1 < self.shards)

    def start(self, piece):
        for way in (0, 1):
            @pl.when(self.sends(way, 0))
            def _():
                self.copy(way, 0, piece).start()

    def relay(self, step, piece):
        for way in (0, 1):
            @pl.when(self.gets(way, step))
            def _():
                self.copy(way, step, piece).wait_recv()
            if step + 1 < self.shards - 1:
                @pl.when(self.sends(way, step + 1))
                def _():
                    self.copy(way, step + 1, piece).start()

    def finish(self):
        for step in range(self.shards - 1):
            for piece in range(self.pieces):
                for way in (0, 1):
                    @pl.when(self.sends(way, step))
                    def _():
                        self.copy(way, step, piece).wait_send()


def line_sems(shards, pieces):
    dma = pltpu.SemaphoreType.DMA
    return [dma((2, shards - 1, pieces)), dma((2, shards - 1, pieces))]


def layer_norm_rows(values, gain, shift):
    centered = values - jnp.mean(values, axis=-1, keepdims=True)
    spread = jnp.mean(centered * centered, axis=-1, keepdims=True)
    return (centered * lax.rsqrt(spread + norm_eps) * gain + shift).astype(jnp.bfloat16)


def vector_row(vectors, i):
    return jnp.concatenate([vectors[o, i : i + 1, :] for o in range(vectors.shape[0])], axis=1)


def bias_piece(v_buf, z, t, tile, shards, per_part):
    flat = (t // per_part) * shards + z
    return v_buf[flat // 3, pl.ds(flat % 3, 1), pl.ds(aligned(t % per_part, tile), tile)]


def start_kernel(shards, tokens, vectors, weight, out_weight, cosine, minus, plus,
                 all_tokens, all_vectors, normed, qkv, kept_weight, all_out,
                 x_buf, v_buf, w_buf, n_buf, q_buf, *sems):
    cube = Cube()
    z = lax.axis_index("shard")
    r = lax.axis_index("replica")
    rows = tokens.shape[0]
    share = weight.shape[0] // 8
    width = w_buf.shape[1] // 3
    x_send, x_recv, v_send, v_recv, loc = sems[:5]
    line = Line(shards, 1, tokens, x_buf, x_send, x_recv)
    mine = pl.ds(aligned(r, share), share)
    spread = Spreader(
        cube, shards, share, 3,
        lambda o, part: weight.at[mine, pl.ds(aligned(part * shards + o, width), width)], w_buf, sems[5:10],
    )
    spread_out = Spreader(cube, shards, share, 1, lambda o, part: out_weight.at[mine], all_out, sems[10:15])
    greet(cube.partners(shards), shards + 2)

    def v_copy(o):
        return remote(vectors, v_buf.at[z], v_send.at[o], v_recv.at[z], {"shard": o})

    def v_arrival(o):
        return remote(vectors, v_buf.at[o], v_send.at[o], v_recv.at[o], {"shard": o})

    own_x = pltpu.make_async_copy(tokens, x_buf.at[z], loc.at[0, 0])
    own_v = pltpu.make_async_copy(vectors, v_buf.at[z], loc.at[1, 0])
    own_x.start()
    own_v.start()
    for o in range(shards):
        @pl.when(z != o)
        def _():
            v_copy(o).start()
    spread.start_own()
    spread_out.start_own()
    spread.start()
    spread.arrive(0)
    spread_out.arrive(0)
    line.start(0)
    spread_out.start()
    for distance in range(1, shards):
        spread.arrive(distance)
    own_x.wait()
    own_v.wait()
    for o in range(shards):
        @pl.when(z != o)
        def _():
            v_arrival(o).wait_recv()
    keep_v = pltpu.make_async_copy(v_buf, all_vectors, loc.at[2, 0])
    keep_v.start()
    gain, shift = vector_row(v_buf, 3), vector_row(v_buf, 4)

    def put(source, target, o, i):
        block = pl.ds(aligned(o, rows), rows)
        copy = pltpu.make_async_copy(source.at[block], target.at[block], loc.at[4 + i, o])
        copy.start()

    def normalize(o):
        @pl.loop(0, rows // 32)
        def _(i):
            values = x_buf[o, pl.ds(aligned(i, 32), 32), :].astype(jnp.float32)
            n_buf[pl.ds(pl.multiple_of(o * rows + i * 32, 32), 32), :] = layer_norm_rows(values, gain, shift)
        put(n_buf, normed, o, 0)
        pltpu.make_async_copy(x_buf.at[o], all_tokens.at[o], loc.at[6, o]).start()

    tile = 256
    per_part = width // tile

    def project(o):
        block = pl.ds(aligned(o, rows), rows)

        @pl.loop(0, 3 * per_part)
        def _(t):
            columns = pl.ds(aligned(t, tile), tile)
            value = jnp.dot(n_buf[block, :], w_buf[:, columns], preferred_element_type=jnp.float32)
            value = value + bias_piece(v_buf, z, t, tile, shards, per_part)

            @pl.when(t < 2 * per_part)
            def _():
                wide, wide_minus, wide_plus = (
                    jnp.concatenate([table[block, :]] * (tile // 128), axis=1) for table in (cosine, minus, plus)
                )
                turned = value * wide + pltpu.roll(value, tile - 8, 1) * wide_minus + pltpu.roll(value, 8, 1) * wide_plus
                q_buf[block, columns] = turned.astype(jnp.bfloat16)

            @pl.when(t >= 2 * per_part)
            def _():
                q_buf[block, columns] = value.astype(jnp.bfloat16)
        put(q_buf, qkv, o, 1)

    normalize(z)
    line.relay(0, 0)
    for o in range(shards):
        spread.pass_on(o)
    for o in range(shards):
        spread.pass_last(o)
    spread.landed()
    keep_w = pltpu.make_async_copy(w_buf, kept_weight, loc.at[3, 0])
    keep_w.start()
    project(z)
    for distance in range(1, shards):
        spread_out.arrive(distance)
    for step in range(shards - 1):
        if step > 0:
            line.relay(step, 0)
        for way in (0, 1):
            owner = z - step - 1 if way == 0 else z + step + 1

            @pl.when(line.gets(way, step))
            def _():
                normalize(owner)
                project(owner)
        if step == min(1, shards - 2):
            for o in range(shards):
                spread_out.pass_on(o)
    for o in range(shards):
        spread_out.pass_last(o)
    spread_out.landed()
    line.finish()
    spread.sent()
    spread.finish()
    spread_out.sent()
    spread_out.finish()
    for o in range(shards):
        block = pl.ds(o * rows, rows)

        @pl.when(z != o)
        def _():
            v_copy(o).wait_send()
        pltpu.make_async_copy(n_buf.at[block], normed.at[block], loc.at[4, o]).wait()
        pltpu.make_async_copy(q_buf.at[block], qkv.at[block], loc.at[5, o]).wait()
        pltpu.make_async_copy(x_buf.at[o], all_tokens.at[o], loc.at[6, o]).wait()
    keep_v.wait()
    keep_w.wait()


def start_call(shards, tokens, vectors, weight, out_weight, cosine, minus, plus):
    rows = tokens.shape[0]
    group = rows * shards
    depth = weight.shape[0]
    width = weight.shape[1] // shards
    any_ = pl.BlockSpec(memory_space=pl.ANY)
    vm = pl.BlockSpec(memory_space=pltpu.VMEM)
    low = jnp.bfloat16
    dma = pltpu.SemaphoreType.DMA
    return pl.pallas_call(
        functools.partial(start_kernel, shards),
        out_shape=[
            jax.ShapeDtypeStruct((shards, rows, D), low),
            jax.ShapeDtypeStruct((shards,) + vectors.shape, vectors.dtype),
            jax.ShapeDtypeStruct((group, D), low),
            jax.ShapeDtypeStruct((group, width), low),
            jax.ShapeDtypeStruct((depth * shards, width), low),
            jax.ShapeDtypeStruct((depth * shards, D), low),
        ],
        in_specs=[any_] * 4 + [vm] * 3,
        out_specs=[any_] * 6,
        scratch_shapes=[
            pltpu.VMEM((shards, rows, D), low),
            pltpu.VMEM((shards,) + vectors.shape, vectors.dtype),
            pltpu.VMEM((depth * shards, width), low),
            pltpu.VMEM((group, D), low),
            pltpu.VMEM((group, width), low),
        ] + line_sems(shards, 1) + [dma((shards,)), dma((shards,)), dma((7, shards))]
        + spread_sems(shards, 3) + spread_sems(shards, 1),
        compiler_params=pltpu.CompilerParams(
            collective_id=1, has_side_effects=True, vmem_limit_bytes=62 * 2**20
        ),
        name="start",
        cost_estimate=pl.CostEstimate(flops=2 * group * D * width, bytes_accessed=150 * 10**6, transcendentals=0),
    )(tokens, vectors, weight, out_weight, cosine, minus, plus)


def attend_spread_kernel(shards, rows, qkv, seg_rows, seg_columns, gate_up, attended, stats, all_gate_up, a_buf, *sems):
    cube = Cube()
    z = lax.axis_index("shard")
    r = lax.axis_index("replica")
    width = qkv.shape[1] // 3
    blocks = qkv.shape[0] // rows
    share = gate_up.shape[0] // 8
    half = all_gate_up.shape[1] // 2
    mine = pl.ds(aligned(r, share), share)
    spread = Spreader(
        cube, shards, share, 2,
        lambda o, part: gate_up.at[mine, pl.ds(aligned((part * shards + o) * (half // 128), 128), half)], all_gate_up, sems[3:8],
    )
    line = Line(shards, blocks, None, a_buf, sems[0], sems[1])
    loc = sems[2]
    greet(cube.partners(shards), shards + 2)
    spread.start_own()
    spread.start()
    spread.arrive(0)

    def done(block):
        line.start(block)
        if 0 < block < shards:
            spread.arrive(block)

    attend_body(rows, qkv, seg_rows, seg_columns, a_buf, stats, done)
    moves = [functools.partial(line.relay, step, block) for step in range(shards - 1) for block in range(blocks)]
    steps = [functools.partial(spread.pass_on, o) for o in range(shards)]
    steps += [functools.partial(spread.pass_last, o) for o in range(shards)]
    for i in range(max(len(moves), len(steps))):
        if i < len(moves):
            moves[i]()
        if i < len(steps):
            steps[i]()
    keep = [pltpu.make_async_copy(a_buf.at[o], attended.at[:, pl.ds(o * width, width)], loc.at[o]) for o in range(shards)]
    for copy in keep:
        copy.start()
    spread.landed()
    line.finish()
    spread.sent()
    spread.finish()
    for copy in keep:
        copy.wait()


def attend_spread_call(shards, rows, qkv, seg_rows, seg_columns, gate_up):
    group = qkv.shape[0]
    width = qkv.shape[1] // 3
    blocks = group // rows
    vm = pl.BlockSpec(memory_space=pltpu.VMEM)
    any_ = pl.BlockSpec(memory_space=pl.ANY)
    dma = pltpu.SemaphoreType.DMA
    low = jnp.bfloat16
    return pl.pallas_call(
        functools.partial(attend_spread_kernel, shards, rows),
        out_shape=[
            jax.ShapeDtypeStruct((group, shards * width), low),
            jax.ShapeDtypeStruct((group, 128), jnp.float32),
            jax.ShapeDtypeStruct((gate_up.shape[0] * shards, gate_up.shape[1] // shards), low),
        ],
        in_specs=[vm, vm, vm, any_],
        out_specs=[any_, vm, any_],
        scratch_shapes=[pltpu.VMEM((shards, group, width), low)] + line_sems(shards, blocks) + [dma((shards,))]
        + spread_sems(shards, 2),
        compiler_params=pltpu.CompilerParams(
            collective_id=2, has_side_effects=True, vmem_limit_bytes=48 * 2**20
        ),
        name="attend_spread",
        cost_estimate=pl.CostEstimate(flops=10**9, bytes_accessed=150 * 10**6, transcendentals=0),
    )(qkv, seg_rows, seg_columns, gate_up)


def hidden_kernel(shards, attended, tokens, out_weight, gate_up_weight, down_weight, cotangent, vectors,
                  middle_own, normed_two, hidden, slopes, all_cotangent, down_part,
                  a_buf, x_buf, o_buf, g_buf, d_buf, c_buf, mid, n_buf, gu, h_buf, s_buf, c_send, c_recv, loc):
    z = lax.axis_index("shard")
    greet_line(z, shards)
    rows = cotangent.shape[0]
    group = rows * shards
    inner = h_buf.shape[1]
    gain, shift = vector_row(vectors, 5), vector_row(vectors, 6)
    line = Line(shards, 1, cotangent, c_buf, c_send, c_recv)
    line.start(0)
    load = [pltpu.make_async_copy(source, target, loc.at[i]) for i, (source, target) in enumerate((
        (attended, a_buf), (out_weight, o_buf), (tokens, x_buf), (gate_up_weight, g_buf), (down_weight, d_buf),
        (cotangent, c_buf.at[z])))]
    for copy in load:
        copy.start()
    for copy in load[:3]:
        copy.wait()
    tile = 256
    span = 2 * rows
    for part in range(group // span):
        at = part * span

        @pl.loop(0, D // tile)
        def _(t):
            columns = pl.ds(aligned(t, tile), tile)
            value = jnp.dot(a_buf[at : at + span, :], o_buf[:, columns], preferred_element_type=jnp.float32)
            for k in range(2):
                mid[k * rows : (k + 1) * rows, columns] = (
                    value[k * rows : (k + 1) * rows] + x_buf[2 * part + k, :, columns].astype(jnp.float32)
                )

        @pl.loop(0, span // 32)
        def _(i):
            block = pl.ds(aligned(i, 32), 32)
            n_buf[pl.ds(pl.multiple_of(at + i * 32, 32), 32), :] = layer_norm_rows(mid[block, :], gain, shift)
        for k in range(2):
            @pl.when(z == 2 * part + k)
            def _():
                middle_own[...] = mid[k * rows : (k + 1) * rows, :]
    keep_n = pltpu.make_async_copy(n_buf, normed_two, loc.at[6])
    keep_n.start()
    line.relay(0, 0)
    load[3].wait()

    @pl.loop(0, 2 * inner // tile)
    def _(t):
        columns = pl.ds(aligned(t, tile), tile)
        gu[:, columns] = jnp.dot(n_buf[...], g_buf[:, columns], preferred_element_type=jnp.float32)

    @pl.loop(0, group // 32)
    def _(i):
        block = pl.ds(aligned(i, 32), 32)
        gate = gu[block, :inner]
        h_buf[block, :] = (gate / (1.0 + jnp.exp(-gate)) * gu[block, inner:]).astype(jnp.bfloat16)
    keep_h = pltpu.make_async_copy(h_buf, hidden, loc.at[7])
    keep_h.start()
    if shards > 2:
        line.relay(1, 0)
    load[4].wait()

    @pl.loop(0, D // tile)
    def _(t):
        columns = pl.ds(aligned(t, tile), tile)
        a_buf[:, columns] = jnp.dot(h_buf[...], d_buf[:, columns], preferred_element_type=jnp.float32).astype(jnp.bfloat16)
    keep_p = pltpu.make_async_copy(a_buf, down_part, loc.at[8])
    keep_p.start()
    load[5].wait()

    def back(o):
        mid[:rows, :inner] = contract_last(c_buf[o], d_buf[...])

        @pl.loop(0, rows // 32)
        def _(i):
            value = mid[pl.ds(aligned(i, 32), 32), :inner]
            place = pl.ds(pl.multiple_of(o * rows + i * 32, 32), 32)
            gate = gu[place, :inner]
            up = gu[place, inner:]
            sigmoid = 1.0 / (1.0 + jnp.exp(-gate))
            s_buf[place, :inner] = (value * up * (sigmoid * (1.0 + gate * (1.0 - sigmoid)))).astype(jnp.bfloat16)
            s_buf[place, inner:] = (value * (gate * sigmoid)).astype(jnp.bfloat16)

    back(z)
    for step in range(shards - 1):
        if step >= 2:
            line.relay(step, 0)
        for way in (0, 1):
            owner = z - step - 1 if way == 0 else z + step + 1

            @pl.when(line.gets(way, step))
            def _():
                back(owner)
    keep = [pltpu.make_async_copy(c_buf, all_cotangent, loc.at[9]), pltpu.make_async_copy(s_buf, slopes, loc.at[10])]
    for copy in keep:
        copy.start()
    line.finish()
    for copy in keep + [keep_n, keep_h, keep_p]:
        copy.wait()


def hidden_call(shards, attended, tokens, out_weight, gate_up_weight, down_weight, cotangent, vectors):
    rows = cotangent.shape[0]
    group = rows * shards
    inner = down_weight.shape[0]
    low = jnp.bfloat16
    f32 = jnp.float32
    vm = pl.BlockSpec(memory_space=pltpu.VMEM)
    any_ = pl.BlockSpec(memory_space=pl.ANY)
    return pl.pallas_call(
        functools.partial(hidden_kernel, shards),
        out_shape=[
            jax.ShapeDtypeStruct((rows, D), f32),
            jax.ShapeDtypeStruct((group, D), low),
            jax.ShapeDtypeStruct((group, inner), low),
            jax.ShapeDtypeStruct((group, 2 * inner), low),
            jax.ShapeDtypeStruct((shards, rows, D), low),
            jax.ShapeDtypeStruct((group, D), low),
        ],
        in_specs=[any_] * 6 + [vm],
        out_specs=[vm] + [any_] * 5,
        scratch_shapes=[
            pltpu.VMEM((group, D), low),
            pltpu.VMEM((shards, rows, D), low),
            pltpu.VMEM(out_weight.shape, low),
            pltpu.VMEM(gate_up_weight.shape, low),
            pltpu.VMEM(down_weight.shape, low),
            pltpu.VMEM((shards, rows, D), low),
            pltpu.VMEM((2 * rows, D), f32),
            pltpu.VMEM((group, D), low),
            pltpu.VMEM((group, 2 * inner), f32),
            pltpu.VMEM((group, inner), low),
            pltpu.VMEM((group, 2 * inner), low),
        ] + line_sems(shards, 1) + [pltpu.SemaphoreType.DMA((11,))],
        compiler_params=pltpu.CompilerParams(
            collective_id=9, has_side_effects=True, vmem_limit_bytes=63 * 2**20
        ),
        name="hidden",
        cost_estimate=pl.CostEstimate(flops=24 * 10**9, bytes_accessed=150 * 10**6, transcendentals=0),
    )(attended, tokens, out_weight, gate_up_weight, down_weight, cotangent, vectors)


def head_mask(even, rows):
    lane = lax.broadcasted_iota(jnp.int32, (rows, 128), 1)
    return (lane < HEAD_DIM) if even else (lane >= HEAD_DIM)


def only(values, keep):
    return jnp.where(keep, values.astype(jnp.float32), 0.0).astype(jnp.bfloat16)


def block_visible(at, rows, seg_rows, seg_columns):
    count = at + rows
    row = lax.broadcasted_iota(jnp.int32, (rows, count), 0) + at
    column = lax.broadcasted_iota(jnp.int32, (rows, count), 1)
    return (column <= row) & (seg_rows[at : at + rows, :1] == seg_columns[:1, :count])


def attend_body(rows, qkv, seg_rows, seg_columns, a_buf, stats, done):
    z = lax.axis_index("shard")
    width = qkv.shape[1] // 3
    pairs = width // 128
    scale = HEAD_DIM ** (-0.5)
    for block in range(qkv.shape[0] // rows):
        at = block * rows
        count = at + rows
        seen = block_visible(at, rows, seg_rows, seg_columns)
        for pair in range(pairs):
            lanes = slice(128 * pair, 128 * pair + 128)
            query = qkv[at:count, lanes]
            keys = qkv[:count, width + 128 * pair : width + 128 * pair + 128]
            values = qkv[:count, 2 * width + 128 * pair : 2 * width + 128 * pair + 128]
            results = []
            for odd in (0, 1):
                keep = head_mask(odd == 0, rows)
                scores = contract_last(only(query, keep), keys) * scale
                scores = jnp.where(seen, scores, masked_score)
                top = jnp.max(scores, axis=-1, keepdims=True)
                weights = jnp.exp(scores - top)
                total = jnp.sum(weights, axis=-1, keepdims=True)
                probs = (weights * (1.0 / total)).astype(jnp.bfloat16)
                results.append(jnp.dot(probs, values, preferred_element_type=jnp.float32))
                head = 2 * pair + odd
                stats[at:count, head : head + 1] = top
                stats[at:count, 64 + head : 65 + head] = 1.0 / total
            merged = jnp.where(head_mask(True, rows), results[0], results[1])
            a_buf[z, at:count, lanes] = merged.astype(jnp.bfloat16)
        done(block)


def attend_kernel(shards, rows, qkv, seg_rows, seg_columns, attended, stats, a_buf, a_send, a_recv, loc):
    z = lax.axis_index("shard")
    width = qkv.shape[1] // 3
    blocks = qkv.shape[0] // rows
    greet_line(z, shards)
    line = Line(shards, blocks, None, a_buf, a_send, a_recv)
    attend_body(rows, qkv, seg_rows, seg_columns, a_buf, stats, line.start)
    for step in range(shards - 1):
        for block in range(blocks):
            line.relay(step, block)
    keep = [pltpu.make_async_copy(a_buf.at[o], attended.at[:, pl.ds(o * width, width)], loc.at[o]) for o in range(shards)]
    for copy in keep:
        copy.start()
    line.finish()
    for copy in keep:
        copy.wait()


def attend_call(shards, rows, qkv, seg_rows, seg_columns):
    group = qkv.shape[0]
    width = qkv.shape[1] // 3
    blocks = group // rows
    vm = pl.BlockSpec(memory_space=pltpu.VMEM)
    any_ = pl.BlockSpec(memory_space=pl.ANY)
    dma = pltpu.SemaphoreType.DMA
    return pl.pallas_call(
        functools.partial(attend_kernel, shards, rows),
        out_shape=[
            jax.ShapeDtypeStruct((group, shards * width), jnp.bfloat16),
            jax.ShapeDtypeStruct((group, 128), jnp.float32),
        ],
        in_specs=[vm, vm, vm],
        out_specs=[any_, vm],
        scratch_shapes=[
            pltpu.VMEM((shards, group, width), jnp.bfloat16),
            dma((2, shards - 1, blocks)), dma((2, shards - 1, blocks)), dma((shards,)),
        ],
        compiler_params=pltpu.CompilerParams(
            collective_id=2, has_side_effects=True, vmem_limit_bytes=48 * 2**20
        ),
        name="attend",
        cost_estimate=pl.CostEstimate(flops=10**9, bytes_accessed=150 * 10**6, transcendentals=0),
    )(qkv, seg_rows, seg_columns)


def attend_back_kernel(rows, *refs):
    attend_back_body(rows, *refs, [])


def attend_back_body(rows, qkv, d_attended, stats, seg_rows, seg_columns, cosine, minus, plus,
                     d_qkv, bias_grad, d_keys, d_values, steps):
    width = qkv.shape[1] // 3
    group = qkv.shape[0]
    blocks = group // rows
    pairs = width // 128
    scale = HEAD_DIM ** (-0.5)

    def turned(value, at, count):
        return (value * cosine[at:count, :] - pltpu.roll(value, 120, 1) * minus[at:count, :]
                - pltpu.roll(value, 8, 1) * plus[at:count, :])

    for block in reversed(range(blocks)):
        at = block * rows
        count = at + rows
        seen = block_visible(at, rows, seg_rows, seg_columns)
        for pair in range(pairs):
            lanes = slice(128 * pair, 128 * pair + 128)
            query = qkv[at:count, lanes]
            keys = qkv[:count, width + 128 * pair : width + 128 * pair + 128]
            values = qkv[:count, 2 * width + 128 * pair : 2 * width + 128 * pair + 128]
            slope = d_attended[at:count, lanes]
            d_query, d_key, d_value = [], [], []
            for odd in (0, 1):
                keep = head_mask(odd == 0, rows)
                head = 2 * pair + odd
                own_query = only(query, keep)
                own_slope = only(slope, keep)
                scores = contract_last(own_query, keys) * scale
                scores = jnp.where(seen, scores, masked_score)
                probs = jnp.exp(scores - stats[at:count, head : head + 1]) * stats[at:count, 64 + head : 65 + head]
                d_probs = contract_last(own_slope, values)
                inner = jnp.sum(probs * d_probs, axis=-1, keepdims=True)
                d_scores = (probs * (d_probs - inner)).astype(jnp.bfloat16)
                d_query.append(jnp.dot(d_scores, keys, preferred_element_type=jnp.float32))
                d_key.append(contract_first(d_scores, own_query))
                d_value.append(contract_first(probs.astype(jnp.bfloat16), own_slope))
            keep = head_mask(True, rows)
            d_q = jnp.where(keep, d_query[0], d_query[1]) * scale
            d_q = turned(d_q, at, count).astype(jnp.bfloat16)
            d_qkv[at:count, lanes] = d_q
            d_k = (d_key[0] + d_key[1]) * scale
            d_v = d_value[0] + d_value[1]
            if block == blocks - 1:
                d_keys[:, lanes] = d_k
                d_values[:, lanes] = d_v
            else:
                d_keys[:count, lanes] += d_k
                d_values[:count, lanes] += d_v
            k_out = turned(d_keys[at:count, lanes], at, count).astype(jnp.bfloat16)
            d_qkv[at:count, width + 128 * pair : width + 128 * pair + 128] = k_out
            v_out = d_values[at:count, lanes].astype(jnp.bfloat16)
            d_qkv[at:count, 2 * width + 128 * pair : 2 * width + 128 * pair + 128] = v_out
            if steps:
                steps.pop(0)()
    for part in range(3 * pairs):
        lanes = slice(128 * part, 128 * part + 128)
        bias_grad[:, lanes] = jnp.broadcast_to(
            jnp.sum(d_qkv[:, lanes].astype(jnp.float32), axis=0, keepdims=True), (8, 128))


def contract_first(left, right):
    return lax.dot_general(
        left, right, (((0,), (0,)), ((), ())), preferred_element_type=jnp.float32
    )


def attend_back_call(rows, qkv, d_attended, stats, seg_rows, seg_columns, cosine, minus, plus):
    group = qkv.shape[0]
    width = qkv.shape[1] // 3
    vm = pl.BlockSpec(memory_space=pltpu.VMEM)
    return pl.pallas_call(
        functools.partial(attend_back_kernel, rows),
        out_shape=[
            jax.ShapeDtypeStruct((group, 3 * width), jnp.bfloat16),
            jax.ShapeDtypeStruct((8, 3 * width), jnp.float32),
        ],
        in_specs=[vm] * 8,
        out_specs=[vm, vm],
        scratch_shapes=[pltpu.VMEM((group, width), jnp.float32), pltpu.VMEM((group, width), jnp.float32)],
        compiler_params=pltpu.CompilerParams(vmem_limit_bytes=48 * 2**20),
        name="attend_back",
        cost_estimate=pl.CostEstimate(flops=3 * 10**9, bytes_accessed=100 * 10**6, transcendentals=0),
    )(qkv, d_attended, stats, seg_rows, seg_columns, cosine, minus, plus)


def scatter_kernel(shards, cuts, parts, total, own, got, load, send, recv):
    z = lax.axis_index("shard")
    rows = parts.shape[1]
    step_rows = rows // cuts
    greet_line(z, shards)

    def piece(cut):
        return pl.ds(cut * step_rows, step_rows)

    def moved(way, block, cut):
        target = z + 1 if way == 0 else z - 1
        place = got.at[way, block, piece(cut)]
        return remote(place, place, send.at[way, block, cut], recv.at[way, block, cut], {"shard": target})

    loads = [pltpu.make_async_copy(parts.at[j], own.at[j], load.at[j]) for j in range(shards)]
    for copy in loads:
        copy.start()
    for copy in loads:
        copy.wait()
    for far in range(shards - 1):
        for cut in range(cuts):
            for way in (0, 1):
                block = shards - 1 - far if way == 0 else far
                sends = z < block if way == 0 else z > block
                first = z == 0 if way == 0 else z == shards - 1

                @pl.when(sends)
                def _():
                    @pl.when(first)
                    def _():
                        got[way, block, piece(cut)] = own[block, piece(cut)]

                    @pl.when(jnp.logical_not(first))
                    def _():
                        moved(way, block, cut).wait_recv()
                        got[way, block, piece(cut)] = (
                            got[way, block, piece(cut)].astype(jnp.float32)
                            + own[block, piece(cut)].astype(jnp.float32)
                        ).astype(got.dtype)
                    moved(way, block, cut).start()
    total[...] = own[z].astype(jnp.float32)
    for way in (0, 1):
        @pl.when(z >= 1 if way == 0 else z + 1 < shards)
        def _():
            for cut in range(cuts):
                moved(way, z, cut).wait_recv()
            total[...] += got[way, z].astype(jnp.float32)
    for far in range(shards - 1):
        for cut in range(cuts):
            for way in (0, 1):
                block = shards - 1 - far if way == 0 else far

                @pl.when(z < block if way == 0 else z > block)
                def _():
                    moved(way, block, cut).wait_send()


def scatter_call(shards, parts, number):
    _, rows, columns = parts.shape
    cuts = 3
    dma = pltpu.SemaphoreType.DMA
    return pl.pallas_call(
        functools.partial(scatter_kernel, shards, cuts),
        out_shape=jax.ShapeDtypeStruct((rows, columns), jnp.float32),
        in_specs=[pl.BlockSpec(memory_space=pl.ANY)],
        out_specs=pl.BlockSpec(memory_space=pltpu.VMEM),
        scratch_shapes=[
            pltpu.VMEM(parts.shape, parts.dtype),
            pltpu.VMEM((2,) + parts.shape, parts.dtype),
            dma((shards,)), dma((2, shards, cuts)), dma((2, shards, cuts)),
        ],
        compiler_params=pltpu.CompilerParams(
            collective_id=number, has_side_effects=True, vmem_limit_bytes=32 * 2**20
        ),
        name="scatter",
        cost_estimate=pl.CostEstimate(flops=0, bytes_accessed=200 * 10**6, transcendentals=0),
    )(parts)


def exchange_kernel(shards, first, second, first_out, second_out, send, recv, loc):
    z = lax.axis_index("shard")
    width = first.shape[1] // shards
    greet([((z != o), {"shard": o}) for o in range(shards)], shards - 1)
    arrays = ((first, first_out), (second, second_out))

    def move(k, o):
        source, target = arrays[k]
        return remote(source.at[:, pl.ds(o * width, width)], target.at[z], send.at[k, o], recv.at[k, z], {"shard": o})

    def arrival(k, o):
        source, target = arrays[k]
        return remote(target.at[o], target.at[o], send.at[k, o], recv.at[k, o], {"shard": o})

    for k in (0, 1):
        for o in range(shards):
            @pl.when(z != o)
            def _():
                move(k, o).start()

            @pl.when(z == o)
            def _():
                source, target = arrays[k]
                pltpu.make_async_copy(source.at[:, pl.ds(o * width, width)], target.at[o], loc.at[k]).start()
    for k in (0, 1):
        for o in range(shards):
            @pl.when(z != o)
            def _():
                arrival(k, o).wait_recv()
                move(k, o).wait_send()

            @pl.when(z == o)
            def _():
                source, target = arrays[k]
                pltpu.make_async_copy(source.at[:, pl.ds(o * width, width)], target.at[o], loc.at[k]).wait()


def exchange_call(shards, first, second):
    rows, columns = first.shape
    shape = jax.ShapeDtypeStruct((shards, rows, columns // shards), first.dtype)
    any_ = pl.BlockSpec(memory_space=pl.ANY)
    dma = pltpu.SemaphoreType.DMA
    return pl.pallas_call(
        functools.partial(exchange_kernel, shards),
        out_shape=[shape, shape],
        in_specs=[any_, any_],
        out_specs=[any_, any_],
        scratch_shapes=[dma((2, shards)), dma((2, shards)), dma((2,))],
        compiler_params=pltpu.CompilerParams(collective_id=5, has_side_effects=True),
        name="exchange",
        cost_estimate=pl.CostEstimate(flops=0, bytes_accessed=100 * 10**6, transcendentals=0),
    )(first, second)


def add_rows(target, source, count):
    step = 16

    @pl.loop(0, count // step)
    def _(i):
        block = pl.ds(aligned(i, step), step)
        target[block, :] = (
            target[block, :].astype(jnp.float32) + source[block, :].astype(jnp.float32)
        ).astype(target.dtype)


class Reducer:
    def __init__(self, cube, share, term, core, near, last, send, recv):
        self.cube, self.share = cube, share
        self.cut = 16 * ((share // 16 + 1) // 2)
        self.term, self.core, self.near, self.last = term, core, near, last
        self.send, self.recv = send, recv
        self.chunks = term.shape[0]

    def share_rows(self, chunk, place, half):
        first, count = (0, self.cut) if half == 0 else (self.cut, self.share - self.cut)
        start = self.cube.core * 4 * self.share + place * self.share + first
        return rows_of(self.term.at[chunk], start, 16, count)

    def own(self, chunk):
        start = (self.cube.core * 4 + self.cube.place) * self.share
        return rows_of(self.term.at[chunk], start, 16, self.share)

    def core_copy(self, chunk):
        source = rows_of(self.term.at[chunk], (1 - self.cube.core) * 4 * self.share, 16, 4 * self.share)
        return remote(source, self.core.at[chunk], self.send.at[chunk, 0], self.recv.at[chunk, 0], self.cube.to_core)

    def near_place(self, half, other):
        c = self.cube
        if half == 0:
            return 2 * other + (1 - c.x), 2 * other + c.x
        return 2 * (1 - c.y) + other, 2 * c.y + other

    def near_slot(self, chunk, half, other):
        count = self.cut if half == 0 else self.share - self.cut
        start = other * count + (2 * self.cut if half == 1 else 0)
        return self.near.at[chunk, pl.ds(start, count)]

    def near_copy(self, chunk, half, other):
        source = self.share_rows(chunk, self.near_place(half, other)[0], half)
        slot = 1 + 2 * half + other
        device = self.cube.to_x if half == 0 else self.cube.to_y
        return remote(source, self.near_slot(chunk, half, other), self.send.at[chunk, slot], self.recv.at[chunk, slot], device)

    def last_slot(self, chunk, half):
        first, count = (0, self.cut) if half == 0 else (self.cut, self.share - self.cut)
        return self.last.at[chunk, pl.ds(first, count)]

    def last_copy(self, chunk, half):
        c = self.cube
        place = 2 * (1 - c.y) + c.x if half == 0 else 2 * c.y + (1 - c.x)
        device = c.to_y if half == 0 else c.to_x
        source = self.share_rows(chunk, place, half)
        return remote(source, self.last_slot(chunk, half), self.send.at[chunk, 5 + half], self.recv.at[chunk, 5 + half], device)

    def start(self, chunk):
        self.core_copy(chunk).start()

    def after_core(self, chunk):
        self.core_copy(chunk).wait_recv()
        mine = rows_of(self.term.at[chunk], self.cube.core * 4 * self.share, 16, 4 * self.share)
        add_rows(mine, self.core.at[chunk], 4 * self.share)
        for half in (0, 1):
            for other in (0, 1):
                self.near_copy(chunk, half, other).start()

    def after_near(self, chunk):
        for half in (0, 1):
            count = self.cut if half == 0 else self.share - self.cut
            for other in (0, 1):
                self.near_copy(chunk, half, other).wait_recv()
                stays = self.share_rows(chunk, self.near_place(half, other)[1], half)
                add_rows(stays, self.near_slot(chunk, half, other), count)
            self.last_copy(chunk, half).start()

    def after_last(self, chunk):
        c = self.cube
        for half in (0, 1):
            count = self.cut if half == 0 else self.share - self.cut
            self.last_copy(chunk, half).wait_recv()
            add_rows(self.share_rows(chunk, c.place, half), self.last_slot(chunk, half), count)

    def finish(self, chunk):
        self.core_copy(chunk).wait_send()
        for half in (0, 1):
            for other in (0, 1):
                self.near_copy(chunk, half, other).wait_send()
            self.last_copy(chunk, half).wait_send()


class Owners:
    def __init__(self, shards, parts, source, out, send, recv, loc):
        self.shards, self.parts, self.source, self.out = shards, parts, source, out
        self.send, self.recv, self.loc = send, recv, loc
        self.z = lax.axis_index("shard")
        self.width = out.shape[1] // (shards * parts)

    def target(self, shard, part):
        return self.out.at[:, pl.ds(aligned((part * self.shards + shard) * (self.width // 128), 128), self.width)]

    def piece(self, o, part):
        return self.source(o).at[:, pl.ds(part * self.width, self.width)]

    def copy(self, o, part):
        return remote(self.piece(o, part), self.target(self.z, part), self.send.at[o, part], self.recv.at[self.z, part], {"shard": o})

    def arrival(self, o, part):
        place = self.target(o, part)
        return remote(place, place, self.send.at[o, part], self.recv.at[o, part], {"shard": o})

    def local(self, o, part):
        return pltpu.make_async_copy(self.piece(o, part), self.target(o, part), self.loc.at[part])

    def start(self, k):
        o = lax.rem(self.z + k, self.shards)
        for part in range(self.parts):
            if k == 0:
                self.local(o, part).start()
            else:
                self.copy(o, part).start()

    def arrive(self):
        for k in range(self.shards):
            o = lax.rem(self.z + k, self.shards)
            for part in range(self.parts):
                if k == 0:
                    self.local(o, part).wait()
                else:
                    self.arrival(o, part).wait_recv()

    def finish(self):
        for k in range(1, self.shards):
            o = lax.rem(self.z + k, self.shards)
            for part in range(self.parts):
                self.copy(o, part).wait_send()


def owner_sems(shards, parts):
    dma = pltpu.SemaphoreType.DMA
    return [dma((shards, parts)), dma((shards, parts)), dma((parts,))]


class Gatherer:
    def __init__(self, cube, share, out, sems):
        self.cube, self.share, self.out = cube, share, out
        self.send, self.recv, self.loc = sems
        self.count = share.shape[0]
        self.cut = 16 * ((self.count // 16 + 1) // 2)

    def rows(self, place, half=None):
        first, count = {None: (0, self.count), 0: (0, self.cut), 1: (self.cut, self.count - self.cut)}[half]
        return rows_of(self.out, (self.cube.core * 4 + place) * self.count + first, 16, count)

    def copy(self, kind):
        c = self.cube
        at_x, at_y = 2 * c.y + 1 - c.x, 2 * (1 - c.y) + c.x
        block, device = (
            (self.rows(c.place), c.to_x),
            (self.rows(c.place), c.to_y),
            (self.rows(at_x, 0), c.to_y),
            (self.rows(at_y, 1), c.to_x),
            (self.rows(c.place), c.to_core),
            (self.rows(at_x), c.to_core),
            (self.rows(at_y), c.to_core),
            (self.rows(3 - c.place), c.to_core),
        )[kind]
        source = self.share if kind in (0, 1, 4) else block
        return remote(source, block, self.send.at[kind], self.recv.at[kind], device)

    def local(self):
        return pltpu.make_async_copy(self.share, self.rows(self.cube.place), self.loc.at[0])

    def start(self):
        for kind in (0, 1, 4):
            self.copy(kind).start()
        self.local().start()

    def pass_on(self):
        self.copy(0).wait_recv()
        self.copy(2).start()
        self.copy(5).start()
        self.copy(1).wait_recv()
        self.copy(3).start()
        self.copy(6).start()

    def pass_last(self):
        self.copy(2).wait_recv()
        self.copy(3).wait_recv()
        self.copy(7).start()

    def finish(self):
        for kind in (4, 5, 6, 7):
            self.copy(kind).wait_recv()
        for kind in range(8):
            self.copy(kind).wait_send()
        self.local().wait()


def gatherer_sems():
    dma = pltpu.SemaphoreType.DMA
    return [dma((8,)), dma((8,)), dma((1,))]


class LineSum:
    def __init__(self, shards, cuts, own, got, send, recv):
        self.z = lax.axis_index("shard")
        self.shards, self.cuts, self.own, self.got, self.send, self.recv = shards, cuts, own, got, send, recv
        self.step = own.shape[1] // cuts

    def piece(self, cut):
        return pl.ds(cut * self.step, self.step)

    def copy(self, way, block, cut, source=None):
        target = self.z + 1 if way == 0 else self.z - 1
        place = self.got.at[way, block, self.piece(cut)]
        return remote(place if source is None else source, place, self.send.at[way, block, cut], self.recv.at[way, block, cut], {"shard": target})

    def pair(self, t):
        half = self.shards // 2
        upper = self.z // half
        return half - 1 - t + upper * (2 * t - half + 1)

    def ready(self, pair):
        for way in (0, 1):
            for i in (0, 1):
                block = 2 * pair + (1 - i if way == 0 else i)

                @pl.when((self.z == (0 if way == 0 else self.shards - 1)) & (block != self.z))
                def _():
                    for cut in range(self.cuts):
                        self.copy(way, block, cut, self.own.at[block, self.piece(cut)]).start()

    def nearest(self):
        for way in (0, 1):
            block = 1 if way == 0 else self.shards - 2

            @pl.when(self.z == (0 if way == 0 else self.shards - 1))
            def _():
                for cut in range(self.cuts):
                    self.copy(way, block, cut, self.own.at[block, self.piece(cut)]).start()

    def step_on(self, hop, far, cut):
        for way in (0, 1):
            block = self.shards - 1 - far if way == 0 else far

            @pl.when(self.z == (hop if way == 0 else self.shards - 1 - hop))
            def _():
                self.copy(way, block, cut).wait_recv()
                place = self.got.at[way, block, self.piece(cut)]
                add_rows(place, self.own.at[block, self.piece(cut)], self.step)
                self.copy(way, block, cut).start()

    def steps(self):
        return [
            functools.partial(self.step_on, hop, far, cut)
            for far in range(self.shards - 2)
            for hop in range(1, self.shards - 1 - far)
            for cut in range(self.cuts)
        ]

    def result(self, total):
        rows = self.own.shape[1]
        for way in (0, 1):
            @pl.when(self.z >= 1 if way == 0 else self.z + 1 < self.shards)
            def _():
                for cut in range(self.cuts):
                    self.copy(way, self.z, cut).wait_recv()

        @pl.loop(0, rows // 16)
        def _(i):
            block = pl.ds(aligned(i, 16), 16)
            total[block, :] = self.own[self.z, block, :].astype(jnp.float32)

            @pl.when(self.z >= 1)
            def _():
                total[block, :] += self.got[0, self.z, block, :].astype(jnp.float32)

            @pl.when(self.z + 1 < self.shards)
            def _():
                total[block, :] += self.got[1, self.z, block, :].astype(jnp.float32)

    def finish(self):
        for far in range(self.shards - 1):
            for cut in range(self.cuts):
                for way in (0, 1):
                    block = self.shards - 1 - far if way == 0 else far

                    @pl.when(self.z < block if way == 0 else self.z > block)
                    def _():
                        self.copy(way, block, cut).wait_send()


def line_scratch(shards, rows, columns, cuts):
    dma = pltpu.SemaphoreType.DMA
    return [
        pltpu.VMEM((shards, rows, columns), jnp.bfloat16),
        pltpu.VMEM((2, shards, rows, columns), jnp.bfloat16),
        dma((2, shards, cuts)), dma((2, shards, cuts)),
    ]


def reducer_scratch(chunks, share, columns):
    dma = pltpu.SemaphoreType.DMA
    return [pltpu.VMEM((chunks, n * share, columns), jnp.bfloat16) for n in (8, 4, 2, 1)] + [
        dma((chunks, 7)), dma((chunks, 7)),
    ]


def pair_product(own, pair, slopes, weight, tile=512):
    rows = own.shape[1]

    @pl.loop(0, own.shape[2] // tile)
    def _(t):
        columns = pl.ds(aligned(t, tile), tile)
        value = contract_last(slopes[pl.ds(aligned(pair, 2 * rows), 2 * rows), :], weight[columns, :])
        own[2 * pair, :, columns] = value[:rows].astype(own.dtype)
        own[2 * pair + 1, :, columns] = value[rows:].astype(own.dtype)


def term_product(term, chunk, left, right):
    term.at[chunk][...] = contract_first(left[...], right[...]).astype(jnp.bfloat16)


def spaced(moves, steps, every):
    moves = list(moves)
    for i, step in enumerate(steps):
        step()
        if i % every == every - 1 and moves:
            moves.pop(0)()
    for move in moves:
        move()


def interleave(moves, steps):
    for i in range(max(len(moves), len(steps))):
        if i < len(moves):
            moves[i]()
        if i < len(steps):
            steps[i]()


def load_all(pairs, loc):
    copies = [pltpu.make_async_copy(source, target, loc.at[i]) for i, (source, target) in enumerate(pairs)]
    for copy in copies:
        copy.start()
    return copies


def further(shards):
    z = lax.axis_index("shard")
    return [(k, lax.rem(z + k, shards)) for k in (*range(1, shards), 0)]


class Chunks:
    def __init__(self, ref, chunks):
        self.ref, self.shape = ref, (chunks, ref.shape[0] // chunks, ref.shape[1])

    @property
    def at(self):
        return self

    def __getitem__(self, chunk):
        return self.ref.at[pl.ds(aligned(chunk, self.shape[1]), self.shape[1])]


def hidden_back_kernel(shards, slopes, weight, hidden, cotangent, normed_two, total, down_share, gate_up_rows,
                       s_buf, w_buf, h_buf, c_buf, n_buf, own, got, z_send, z_recv,
                       term, core, near, last, r_send, r_recv, g_core, g_near, g_last, g_send, g_recv, loc, *sems):
    cube = Cube()
    loads = load_all(((slopes, s_buf), (weight, w_buf), (hidden, h_buf), (cotangent, c_buf), (normed_two, n_buf)), loc)
    greet(cube.partners(shards), shards + 2)
    line = LineSum(shards, 3, own, got, z_send, z_recv)
    share = hidden.shape[1] // 8
    width = D // shards
    chunks, _, columns = term.shape
    g_term = Chunks(w_buf, shards)
    reducer = Reducer(cube, share, term, core, near, last, r_send, r_recv)
    g_reducer = Reducer(cube, width // 8, g_term, g_core, g_near, g_last, g_send, g_recv)
    owners = Owners(shards, 2, g_reducer.own, gate_up_rows, *sems)
    for copy in loads[:2]:
        copy.wait()
    for t in range(shards // 2):
        pair = line.pair(t)
        pair_product(own, pair, s_buf, w_buf)
        line.ready(pair)
    for copy in loads[2:]:
        copy.wait()

    def down_term(k):
        term_product(term, k, h_buf, c_buf.at[:, pl.ds(k * columns, columns)])
        reducer.start(k)

    def gate_up_term(k):
        term_product(g_term, k, n_buf.at[:, pl.ds(aligned(k, width), width)], s_buf)
        g_reducer.start(k)

    keep = []

    def keep_down(k):
        copy = pltpu.make_async_copy(reducer.own(k), down_share.at[:, pl.ds(k * columns, columns)], loc.at[5 + k])
        copy.start()
        keep.append(copy)

    def of(call, count):
        return [functools.partial(call, k) for k in range(count)]

    turn = further(shards)

    def each(call):
        return [functools.partial(call, o) for _, o in turn]

    moves = line.steps()

    def down_ending(k):
        reducer.after_last(k)
        keep_down(k)

    def g_ending(k, o):
        g_reducer.after_last(o)
        owners.start(k)

    cores = of(reducer.after_core, chunks) + each(g_reducer.after_core)
    nears = of(reducer.after_near, chunks) + each(g_reducer.after_near)
    lasts = of(down_ending, chunks) + [functools.partial(g_ending, k, o) for k, o in turn]
    g_terms = each(gate_up_term)
    sequence = of(down_term, chunks) + cores[:2] + g_terms[:2] + nears[:1] + cores[2:3] + g_terms[2:] + nears[1:2] + lasts[:1]
    sequence += cores[3:4] + moves[:5]
    for i in range(2, chunks + shards):
        sequence += nears[i : i + 1] + lasts[i - 1 : i] + cores[i + 2 : i + 3] + moves[i + 3 : i + 4]
    sequence += lasts[-1:] + moves[chunks + shards + 3 :]
    for step in sequence:
        step()
    line.result(total)
    line.finish()
    owners.arrive()
    for k in range(chunks):
        reducer.finish(k)
    for k in range(shards):
        g_reducer.finish(k)
    owners.finish()
    for copy in keep:
        copy.wait()


def hidden_back_call(shards, slopes, weight, hidden, cotangent, normed_two):
    group, inner = hidden.shape
    rows = group // shards
    share = inner // 8
    chunks = 4
    width = D // shards
    low = jnp.bfloat16
    any_ = pl.BlockSpec(memory_space=pl.ANY)
    dma = pltpu.SemaphoreType.DMA
    return pl.pallas_call(
        functools.partial(hidden_back_kernel, shards),
        out_shape=[
            jax.ShapeDtypeStruct((rows, D), jnp.float32),
            jax.ShapeDtypeStruct((share, D), low),
            jax.ShapeDtypeStruct((width // 8, shards * 2 * inner), low),
        ],
        in_specs=[any_] * 5,
        out_specs=[pl.BlockSpec(memory_space=pltpu.VMEM), any_, any_],
        scratch_shapes=[pltpu.VMEM(a.shape, low) for a in (slopes, weight, hidden, cotangent, normed_two)]
        + line_scratch(shards, rows, D, 3) + reducer_scratch(chunks, share, D // chunks)
        + reducer_scratch(shards, width // 8, 2 * inner)[1:] + [dma((5 + chunks,))] + owner_sems(shards, 2),
        compiler_params=pltpu.CompilerParams(collective_id=6, has_side_effects=True, vmem_limit_bytes=63 * 2**20),
        name="hidden_back",
        cost_estimate=pl.CostEstimate(flops=10**10, bytes_accessed=200 * 10**6, transcendentals=0),
    )(slopes, weight, hidden, cotangent, normed_two)


def norm_back_rows(slope, values, gain):
    centered = values - jnp.mean(values, axis=-1, keepdims=True)
    inverse = lax.rsqrt(jnp.mean(centered * centered, axis=-1, keepdims=True) + norm_eps)
    unit = centered * inverse
    scaled = slope * gain
    back = inverse * (
        scaled
        - jnp.mean(scaled, axis=-1, keepdims=True)
        - unit * jnp.mean(scaled * unit, axis=-1, keepdims=True)
    )
    return back, unit


def heads_back_kernel(shards, rows, d_normed_two, middle, cotangent, vectors, out_weight, qkv, stats, seg_rows, seg_columns,
                      cosine, minus, plus, down_part, down_share, gate_up_rows,
                      d_middle, norm_grads, d_qkv, bias_grad, mixed, m_columns, down_grad, gate_up_grad,
                      o_buf, m_low, da_own, d_attended, d_keys, d_values, total, own, got, z_send, z_recv, e_send, e_recv, loc, *sems):
    cube = Cube()
    z = lax.axis_index("shard")
    loads = load_all(((out_weight, o_buf), (down_part, own)), loc)
    gain = vector_row(vectors, 5)
    greet(cube.partners(shards), shards + 2)
    width = D // shards
    half = gate_up_rows.shape[1] // 2
    gatherers = [Gatherer(cube, down_share, down_grad, sems[0:3])] + [
        Gatherer(cube, gate_up_rows.at[:, pl.ds(i * half, half)], gate_up_grad.at[:, pl.ds(i * half, half)], sems[3 * i + 3 : 3 * i + 6])
        for i in (0, 1)
    ]
    line = LineSum(shards, 3, own, got, z_send, z_recv)
    gatherers[0].start()
    gatherers[1].start()
    arrays = ((da_own, d_attended), (m_low, m_columns))

    def move(k, o):
        source, target = arrays[k]
        return remote(source.at[:, pl.ds(o * width, width)], target.at[pl.ds(aligned(z, rows), rows)],
                      e_send.at[k, o], e_recv.at[k, z], {"shard": o})

    def arrival(k, o):
        place = arrays[k][1].at[pl.ds(o * rows, rows)]
        return remote(place, place, e_send.at[k, o], e_recv.at[k, o], {"shard": o})

    def here(k, o):
        source, target = arrays[k]
        return pltpu.make_async_copy(source.at[:, pl.ds(o * width, width)], target.at[pl.ds(o * rows, rows)], loc.at[2 + k])

    def begin(k, o):
        @pl.when(z != o)
        def _():
            move(k, o).start()

        @pl.when(z == o)
        def _():
            here(k, o).start()

    def arrive(k):
        for o in range(shards):
            @pl.when(z != o)
            def _():
                arrival(k, o).wait_recv()

            @pl.when(z == o)
            def _():
                here(k, o).wait()

    norm_grads[...] = jnp.zeros_like(norm_grads)

    @pl.loop(0, rows // 16)
    def _(i):
        block = pl.ds(aligned(i, 16), 16)
        slope = d_normed_two[block, :]
        back, unit = norm_back_rows(slope, middle[block, :], gain)
        value = cotangent[block, :].astype(jnp.float32) + back
        d_middle[block, :] = value
        m_low[block, :] = value.astype(jnp.bfloat16)
        norm_grads[0:8, :] += (slope * unit).reshape(2, 8, D).sum(axis=0)
        norm_grads[8:16, :] += slope.reshape(2, 8, D).sum(axis=0)

    loads[0].wait()
    for o in range(shards):
        da_own[:, o * width : (o + 1) * width] = contract_last(
            m_low[...], o_buf[o * width : (o + 1) * width, :]).astype(jnp.bfloat16)
        begin(0, o)
    loads[1].wait()
    for t in range(shards // 2):
        line.ready(line.pair(t))
    for o in range(shards):
        begin(1, o)
    arrive(0)
    gatherers[0].pass_on()

    def nothing():
        pass

    moves = line.steps()
    steps = [nothing, gatherers[1].pass_on, gatherers[2].start, nothing, moves[0], nothing, gatherers[0].pass_last]
    steps += [moves[1], nothing, moves[2], nothing] + [gatherers[1].pass_last] + moves[3:]
    attend_back_body(rows, qkv, d_attended, stats, seg_rows, seg_columns, cosine, minus, plus,
                     d_qkv, bias_grad, d_keys, d_values, steps)
    for step in steps:
        step()
    gatherers[2].pass_on()
    arrive(1)
    gatherers[2].pass_last()
    line.result(total)

    @pl.loop(0, rows // 16)
    def _(i):
        block = pl.ds(aligned(i, 16), 16)
        mixed[block, :] = (middle[block, :] + total[block, :]).astype(mixed.dtype)
    line.finish()
    for k in (0, 1):
        for o in range(shards):
            @pl.when(z != o)
            def _():
                move(k, o).wait_send()
    for gatherer in gatherers:
        gatherer.finish()


def heads_back_call(shards, rows, d_normed_two, middle, cotangent, vectors, out_weight, qkv, stats, seg_rows, seg_columns,
                    cosine, minus, plus, down_part, down_share, gate_up_rows):
    group = qkv.shape[0]
    width = D // shards
    vm = pl.BlockSpec(memory_space=pltpu.VMEM)
    any_ = pl.BlockSpec(memory_space=pl.ANY)
    dma = pltpu.SemaphoreType.DMA
    low = jnp.bfloat16
    f32 = jnp.float32
    return pl.pallas_call(
        functools.partial(heads_back_kernel, shards, rows),
        out_shape=[
            jax.ShapeDtypeStruct((rows, D), f32),
            jax.ShapeDtypeStruct((16, D), f32),
            jax.ShapeDtypeStruct((group, 3 * width), low),
            jax.ShapeDtypeStruct((8, 3 * width), f32),
            jax.ShapeDtypeStruct((rows, D), low),
            jax.ShapeDtypeStruct((group, width), low),
            jax.ShapeDtypeStruct((8 * down_share.shape[0], D), low),
            jax.ShapeDtypeStruct((8 * gate_up_rows.shape[0], gate_up_rows.shape[1]), low),
        ],
        in_specs=[vm] * 4 + [any_] + [vm] * 7 + [any_] * 3,
        out_specs=[vm] * 5 + [any_] * 3,
        scratch_shapes=[
            pltpu.VMEM(out_weight.shape, low), pltpu.VMEM((rows, D), low), pltpu.VMEM((rows, D), low),
            pltpu.VMEM((group, width), low),
            pltpu.VMEM((group, width), f32), pltpu.VMEM((group, width), f32), pltpu.VMEM((rows, D), f32),
        ] + line_scratch(shards, rows, D, 3) + [dma((2, shards)), dma((2, shards)), dma((4,))] + gatherer_sems() * 3,
        compiler_params=pltpu.CompilerParams(collective_id=7, has_side_effects=True, vmem_limit_bytes=60 * 2**20),
        name="heads_back",
        cost_estimate=pl.CostEstimate(flops=10**10, bytes_accessed=200 * 10**6, transcendentals=0),
    )(d_normed_two, middle, cotangent, vectors, out_weight, qkv, stats, seg_rows, seg_columns, cosine, minus, plus,
      down_part, down_share, gate_up_rows)


def input_back_kernel(shards, slopes, weight, normed, attended, d_middle_columns, tokens, vectors, d_middle, bias_grad, norm_grads,
                      input_grad, small, qkv_grad, out_grad,
                      w_buf, n_buf, a_buf, m_buf, total, part, part_in, own, got, z_send, z_recv,
                      term, core, near, last, r_send, r_recv, o_term, o_core, o_near, o_last, o_send, o_recv,
                      qkv_rows, out_rows, s_send, s_recv, loc, *sems):
    cube = Cube()
    z = lax.axis_index("shard")
    loads = load_all(((attended, a_buf), (d_middle_columns, m_buf), (weight, w_buf), (normed, n_buf)), loc)
    greet(cube.partners(shards), shards + 2)
    gain = vector_row(vectors, 3)
    rows = tokens.shape[0]
    width = D // shards
    share = width // 8
    line = LineSum(shards, 3, own, got, z_send, z_recv)
    reducer = Reducer(cube, share, term, core, near, last, r_send, r_recv)
    o_reducer = Reducer(cube, share, o_term, o_core, o_near, o_last, o_send, o_recv)
    owners = Owners(shards, 3, reducer.own, qkv_rows, *sems[0:3])
    o_owners = Owners(shards, 1, o_reducer.own, out_rows, *sems[3:6])
    gatherer = Gatherer(cube, qkv_rows, qkv_grad, sems[6:9])
    o_gatherer = Gatherer(cube, out_rows, out_grad, sems[9:12])

    def qkv_term(o):
        term_product(term, o, n_buf.at[:, pl.ds(aligned(o, width), width)], slopes)
        reducer.start(o)

    def out_term(o):
        term_product(o_term, o, a_buf.at[:, pl.ds(aligned(o, width), width)], m_buf)
        o_reducer.start(o)

    def product(t):
        pair = line.pair(t)
        pair_product(own, pair, slopes, w_buf)
        if t + 1 < shards // 2:
            line.ready(pair)

    turn = further(shards)

    def each(call):
        return [functools.partial(call, o) for _, o in turn]

    def ending(red, own_, k, o):
        red.after_last(o)
        own_.start(k)

    loads[0].wait()
    loads[1].wait()
    for _, o in turn:
        out_term(o)
    loads[2].wait()
    moves = line.steps()
    cores, nears = each(reducer.after_core), each(reducer.after_near)
    lasts = [functools.partial(ending, reducer, owners, k, o) for k, o in turn]
    terms = each(qkv_term)
    sequence = [functools.partial(product, 0)] + each(o_reducer.after_core)
    sequence += [functools.partial(product, t) for t in range(1, shards // 2)] + [loads[3].wait] + each(o_reducer.after_near)
    sequence += terms[:2] + cores[:1] + terms[2:3] + cores[1:2] + terms[3:]
    sequence += [functools.partial(ending, o_reducer, o_owners, k, o) for k, o in turn]
    sequence += moves[:2] + nears[:1] + cores[2:3] + moves[2:4] + nears[1:2] + lasts[:1] + cores[3:] + moves[4:6]
    for i in range(2, shards):
        sequence += nears[i : i + 1] + lasts[i - 1 : i] + moves[i + 4 : i + 5]
    sequence += lasts[-1:] + [line.nearest] + moves[shards + 4 :]
    sequence += [o_owners.arrive, o_gatherer.start]
    for step in sequence:
        step()
    owners.arrive()
    gatherer.start()
    line.result(total)

    part[...] = jnp.zeros_like(part)

    @pl.loop(0, rows // 16)
    def _(i):
        block = pl.ds(aligned(i, 16), 16)
        slope = total[block, :]
        back, unit = norm_back_rows(slope, tokens[block, :].astype(jnp.float32), gain)
        input_grad[block, :] = d_middle[block, :] + back
        ones = (slope * unit).reshape(2, 8, D).sum(axis=0).sum(axis=0, keepdims=True)
        twos = slope.reshape(2, 8, D).sum(axis=0).sum(axis=0, keepdims=True)
        for o in range(shards):
            part[o, 3:4, :] += ones[:, o * width : (o + 1) * width]
            part[o, 4:5, :] += twos[:, o * width : (o + 1) * width]
    for o in range(shards):
        for k in range(2):
            part[o, 5 + k : 6 + k, :] = jnp.sum(
                norm_grads[8 * k : 8 * k + 8, o * width : (o + 1) * width], axis=0, keepdims=True)
    for k in range(3):
        flat = k * shards + z
        part[flat // 3, pl.ds(flat % 3, 1), :] = bias_grad[0:1, k * width : (k + 1) * width]

    def small_copy(o):
        return remote(part.at[o], part_in.at[z], s_send.at[o], s_recv.at[z], {"shard": o})

    def small_arrival(o):
        return remote(part.at[o], part_in.at[o], s_send.at[o], s_recv.at[o], {"shard": o})

    for o in range(shards):
        @pl.when(z != o)
        def _():
            small_copy(o).start()
    small[...] = part[z]
    for o in range(shards):
        @pl.when(z != o)
        def _():
            small_arrival(o).wait_recv()
            small[...] += part_in[o]
    sums = [remote(small, part_in.at[shards + i], s_send.at[shards + i], s_recv.at[shards + i], device)
            for i, device in enumerate((cube.to_core, cube.to_x, cube.to_y))]

    def add_small(i):
        sums[i].start()
        sums[i].wait()
        small[...] += part_in[shards + i]

    add_small(0)
    o_gatherer.pass_on()
    gatherer.pass_on()
    add_small(1)
    add_small(2)
    o_gatherer.pass_last()
    gatherer.pass_last()
    for o in range(shards):
        @pl.when(z != o)
        def _():
            small_copy(o).wait_send()
    line.finish()
    for k in range(shards):
        reducer.finish(k)
        o_reducer.finish(k)
    owners.finish()
    o_owners.finish()
    gatherer.finish()
    o_gatherer.finish()


def input_back_call(shards, slopes, weight, normed, attended, d_middle_columns, tokens, vectors, d_middle, bias_grad, norm_grads):
    group = slopes.shape[0]
    rows = group // shards
    width = D // shards
    share = width // 8
    vm = pl.BlockSpec(memory_space=pltpu.VMEM)
    any_ = pl.BlockSpec(memory_space=pl.ANY)
    dma = pltpu.SemaphoreType.DMA
    low = jnp.bfloat16
    f32 = jnp.float32
    return pl.pallas_call(
        functools.partial(input_back_kernel, shards),
        out_shape=[
            jax.ShapeDtypeStruct((rows, D), f32),
            jax.ShapeDtypeStruct((8, width), f32),
            jax.ShapeDtypeStruct((width, 3 * D), low),
            jax.ShapeDtypeStruct((width, D), low),
        ],
        in_specs=[vm] + [any_] * 4 + [vm] * 5,
        out_specs=[vm, vm, any_, any_],
        scratch_shapes=[
            pltpu.VMEM(weight.shape, low), pltpu.VMEM(normed.shape, low), pltpu.VMEM(attended.shape, low),
            pltpu.VMEM(d_middle_columns.shape, low), pltpu.VMEM((rows, D), f32),
            pltpu.VMEM((shards, 8, width), f32), pltpu.VMEM((shards + 3, 8, width), f32),
        ] + line_scratch(shards, rows, D, 3) + reducer_scratch(shards, share, 3 * width) + reducer_scratch(shards, share, width)
        + [pltpu.VMEM((share, 3 * D), low), pltpu.VMEM((share, D), low), dma((shards + 3,)), dma((shards + 3,)), dma((4,))]
        + owner_sems(shards, 3) + owner_sems(shards, 1) + gatherer_sems() * 2,
        compiler_params=pltpu.CompilerParams(collective_id=8, has_side_effects=True, vmem_limit_bytes=60 * 2**20),
        name="input_back",
        cost_estimate=pl.CostEstimate(flops=10**10, bytes_accessed=200 * 10**6, transcendentals=0),
    )(slopes, weight, normed, attended, d_middle_columns, tokens, vectors, d_middle, bias_grad, norm_grads)


def swap_pieces(pieces):
    shards = lax.axis_size("shard")
    here = lax.axis_index("shard")
    out = pieces
    for k in range(1, shards):
        partner = jnp.bitwise_xor(here, k)
        piece = lax.dynamic_index_in_dim(pieces, partner, axis=0, keepdims=True)
        piece = lax.ppermute(piece, "shard", [(i, i ^ k) for i in range(shards)])
        out = lax.dynamic_update_slice_in_dim(out, piece, partner, axis=0)
    return out


def own_share(rows):
    own = rows.shape[0] // lax.axis_size("replica")
    return lax.dynamic_slice_in_dim(rows, lax.axis_index("replica") * own, own, axis=0)


def spread_rows(rows, columns):
    shards = lax.axis_size("shard")
    piece = own_share(rows)
    own = piece.shape[0]
    piece = piece.reshape(own, columns, shards, -1).transpose(2, 0, 1, 3).reshape(shards, own, -1)
    full = lax.all_gather(swap_pieces(piece), "replica", axis=0, tiled=False)
    return full.transpose(1, 0, 2, 3).reshape(rows.shape[0] * shards, -1)


def gather_rows(rows):
    shards = lax.axis_size("shard")
    piece = own_share(rows)
    moved = swap_pieces(jnp.broadcast_to(piece[None], (shards,) + piece.shape))
    full = lax.all_gather(moved, "replica", axis=0, tiled=False)
    return full.transpose(1, 0, 2, 3).reshape(rows.shape[0] * shards, -1)


def own_rows(features):
    copies = lax.axis_size("replica")
    shards = lax.axis_size("shard")
    count = features.shape[0]
    return (
        features.reshape(count, shards, copies, -1).transpose(0, 2, 1, 3).reshape(count, -1)
    )


def sum_columns(features, slopes, columns):
    shards = lax.axis_size("shard")
    term = contract_first(own_rows(features), slopes).astype(jnp.bfloat16)
    part = lax.psum_scatter(term, "replica", scatter_dimension=0, tiled=True)
    own = part.shape[0] // shards
    moved = swap_pieces(part.reshape(shards, own, -1))
    moved = moved.reshape(shards, own, columns, -1).transpose(1, 2, 0, 3).reshape(own, -1)
    return lax.all_gather(moved, "replica", axis=0, tiled=True)


def swiglu(gate_up):
    half = gate_up.shape[1] // 2
    return jax.nn.silu(gate_up[:, :half]) * gate_up[:, half:]


def norm_stats(values):
    mean = jnp.mean(values, axis=-1, keepdims=True)
    centered = values - mean
    inverse = lax.rsqrt(jnp.mean(centered * centered, axis=-1, keepdims=True) + norm_eps)
    return centered * inverse, inverse


def norm_back(slope, unit, inverse, gain):
    scaled = slope * gain
    return inverse * (
        scaled
        - jnp.mean(scaled, axis=-1, keepdims=True)
        - unit * jnp.mean(scaled * unit, axis=-1, keepdims=True)
    )


def start_plain(tokens, vectors, qkv_weight, cosine, minus, plus):
    shards = lax.axis_size("shard")
    here = lax.axis_index("shard")
    all_tokens = lax.all_gather(tokens, "shard", axis=0, tiled=False)
    all_vectors = lax.all_gather(vectors, "shard", axis=0, tiled=False)
    weight = spread_rows(qkv_weight, 3)
    width = D // shards
    gain, shift = (all_vectors[:, 3 + i].reshape(D) for i in (0, 1))
    unit, _ = norm_stats(all_tokens.reshape(-1, D).astype(jnp.float32))
    normed = (unit * gain + shift).astype(jnp.bfloat16)
    bias = all_vectors[:, :3].reshape(3, shards, width)
    bias = lax.dynamic_index_in_dim(bias, here, axis=1, keepdims=False).reshape(3 * width)
    value = jnp.dot(normed, weight, preferred_element_type=jnp.float32) + bias
    turned = value[:, : 2 * width]
    wide = [jnp.tile(t, (1, 2 * width // 128)) for t in (cosine, minus, plus)]
    turned = (
        turned * wide[0] + jnp.roll(turned, -8, 1) * wide[1] + jnp.roll(turned, 8, 1) * wide[2]
    )
    qkv = jnp.concatenate([turned, value[:, 2 * width :]], axis=1).astype(jnp.bfloat16)
    return all_tokens, all_vectors, normed, qkv, weight


def layer_kernels(shards, tokens, cotangent, weights, vectors, tables):
    qkv_weight, out_weight, gate_up_weight, down_weight = weights
    seg_rows, seg_columns, cosine, minus, plus = tables
    rows = tokens.shape[0]
    all_tokens, all_vectors, normed, qkv, weight_qkv, weight_out = start_call(
        shards, tokens, vectors, qkv_weight, out_weight, cosine, minus, plus
    )
    attended, stats, weight_gate_up = attend_spread_call(
        shards, rows, qkv, seg_rows, seg_columns, gate_up_weight
    )
    middle, normed_two, hidden, slopes, group_cotangent, down_part = hidden_call(
        shards, attended, all_tokens, weight_out, weight_gate_up, down_weight, cotangent, all_vectors
    )
    d_normed_two, down_share, gate_up_rows = hidden_back_call(
        shards, slopes, weight_gate_up, hidden, group_cotangent.reshape(shards * rows, D), normed_two
    )
    d_middle, norm_grads, d_qkv, bias_grad, mixed, d_middle_columns, down_grad, gate_up_grad = heads_back_call(
        shards, rows, d_normed_two, middle, cotangent, all_vectors, weight_out, qkv, stats, seg_rows, seg_columns,
        cosine, minus, plus, down_part.reshape(shards, rows, D), down_share, gate_up_rows,
    )
    input_grad, small, qkv_grad, out_grad = input_back_call(
        shards, d_qkv, weight_qkv, normed, attended, d_middle_columns, tokens, all_vectors, d_middle, bias_grad, norm_grads
    )
    return mixed, input_grad, small, (qkv_grad, out_grad, gate_up_grad, down_grad)


def layer_plain(shards, tokens, cotangent, weights, vectors, tables):
    qkv_weight, out_weight, gate_up_weight, down_weight = weights
    seg_rows, seg_columns, cosine, minus, plus = tables
    here = lax.axis_index("shard")
    row_count = tokens.shape[0]
    group_rows = row_count * shards
    width = D // shards
    f32 = jnp.float32
    low = jnp.bfloat16
    weight_out = gather_rows(out_weight)
    weight_gate_up = spread_rows(gate_up_weight, 2)
    all_tokens, all_vectors, normed_low, qkv, weight_qkv = start_plain(
        tokens, vectors, qkv_weight, cosine, minus, plus
    )
    gain_one, shift_one, gain_two, shift_two = (
        all_vectors[:, 3 + i].reshape(D) for i in range(4)
    )
    cotangent_later, qkv = lax.optimization_barrier((cotangent, qkv))
    group_cotangent = lax.all_gather(cotangent_later, "shard", axis=0, tiled=True)

    def local(array):
        return lax.dynamic_slice_in_dim(array, here * row_count, row_count, axis=0)

    attended, stats = attend_call(shards, row_count, qkv, seg_rows, seg_columns)
    inputs = all_tokens.reshape(group_rows, D).astype(f32)
    middle = inputs + jnp.dot(attended, weight_out, preferred_element_type=f32)
    unit_two, inverse_two = norm_stats(middle)
    normed_two_low = (unit_two * gain_two + shift_two).astype(low)
    gate_up = jnp.dot(normed_two_low, weight_gate_up, preferred_element_type=f32)
    hidden, swiglu_pull = jax.vjp(swiglu, gate_up)
    hidden_low = hidden.astype(low)
    d_hidden = contract_last(group_cotangent, down_weight)
    d_gate_up_low = swiglu_pull(d_hidden)[0].astype(low)
    down_part = jnp.dot(hidden_low, down_weight, preferred_element_type=f32).astype(low)
    unit_two_own = local(unit_two)
    inverse_two_own = local(inverse_two)
    middle_own = local(middle)

    d_normed_two_part = contract_last(d_gate_up_low, weight_gate_up).astype(low)
    d_normed_two = scatter_call(shards, d_normed_two_part.reshape(shards, row_count, D), 3)
    down_grad = lax.psum(contract_first(hidden_low, group_cotangent).astype(low), "replica")
    d_middle = cotangent.astype(f32) + norm_back(
        d_normed_two, unit_two_own, inverse_two_own, gain_two
    )
    d_gain_two = jnp.sum(d_normed_two * unit_two_own, axis=0)
    d_shift_two = jnp.sum(d_normed_two, axis=0)
    d_middle_low = d_middle.astype(low)
    d_attended_own = contract_last(d_middle_low, weight_out).astype(low)
    d_attended, d_middle_columns = exchange_call(shards, d_attended_own, d_middle_low)
    d_projected_low, bias_part = attend_back_call(
        row_count, qkv, d_attended.reshape(group_rows, width), stats, seg_rows, seg_columns,
        cosine, minus, plus,
    )
    down_own = lax.psum_scatter(down_part, "shard", scatter_dimension=0, tiled=True)
    mixed = (middle_own + down_own.astype(f32)).astype(low)
    d_normed_part = contract_last(d_projected_low, weight_qkv).astype(low)
    d_normed = scatter_call(shards, d_normed_part.reshape(shards, row_count, D), 4)
    gate_up_grad = sum_columns(normed_two_low, d_gate_up_low, 2)
    out_grad = sum_columns(attended, d_middle_columns.reshape(group_rows, width), 1)
    qkv_grad = sum_columns(normed_low, d_projected_low, 3)
    unit_one, inverse_one = norm_stats(tokens.astype(f32))
    input_grad = d_middle + norm_back(d_normed, unit_one, inverse_one, gain_one)
    d_gain_one = jnp.sum(d_normed * unit_one, axis=0)
    d_shift_one = jnp.sum(d_normed, axis=0)

    bias_part = bias_part[0].reshape(3, 1, width)
    bias_wide = lax.dynamic_update_slice(
        jnp.zeros((3, shards, width), f32), bias_part, (0, here, 0)
    ).reshape(shards, 3 * width)
    small = jnp.concatenate(
        [bias_wide]
        + [v.reshape(shards, width) for v in (d_gain_one, d_shift_one, d_gain_two, d_shift_two)],
        axis=1,
    )
    small = jnp.pad(small, ((0, 0), (0, width)))
    small = lax.psum(small, ("replica", "shard"))
    small = lax.dynamic_index_in_dim(small, here, axis=0, keepdims=False)
    return mixed, input_grad, small, (qkv_grad, out_grad, gate_up_grad, down_grad)


def on_device(
    tokens,
    cotangent,
    qkv_weight,
    qkv_bias,
    out_weight,
    gate_up_weight,
    down_weight,
    norm1_gain,
    norm1_shift,
    norm2_gain,
    norm2_shift,
    seq_lengths,
):
    shards = lax.axis_size("shard")
    copies = lax.axis_size("replica")
    row_count = tokens.shape[0]
    group_rows = row_count * shards
    width = D // shards
    f32 = jnp.float32
    low = jnp.bfloat16

    segment, position = group_layout(seq_lengths[0], jnp.arange(group_rows, dtype=jnp.int32))
    seg_rows = jnp.broadcast_to(segment[:, None], (group_rows, 128))
    seg_columns = jnp.broadcast_to(segment[None, :], (8, group_rows))
    lane = jnp.arange(128, dtype=jnp.int32)[None, :] % HEAD_DIM
    cosine, sine_value = rope_tables(position, lane % (ROT_DIM // 2))
    cosine = jnp.where(lane < ROT_DIM, cosine, 1.0)
    minus = jnp.where(lane < ROT_DIM // 2, -sine_value, 0.0)
    plus = jnp.where((lane >= ROT_DIM // 2) & (lane < ROT_DIM), sine_value, 0.0)

    vectors = jnp.zeros((8 * width,), f32)
    at = 0
    for vector in (qkv_bias, norm1_gain, norm1_shift, norm2_gain, norm2_shift):
        after = 8 * width - at - vector.shape[0]
        vectors = vectors + jnp.pad(vector.astype(f32), (at, after))
        at += vector.shape[0]
    vectors = vectors.reshape(8, width)
    weights = (qkv_weight, out_weight, gate_up_weight, down_weight)
    tables = (seg_rows, seg_columns, cosine, minus, plus)
    if copies == 8:
        outputs = layer_kernels(shards, tokens, cotangent, weights, vectors, tables)
    else:
        outputs = layer_plain(shards, tokens, cotangent, weights, vectors, tables)
    mixed, input_grad, small, grads = outputs
    bias_rows = 3 * width
    small = small.reshape(8 * width)
    out_dtype = tuple(grad.astype(f32) for grad in grads)
    return (
        mixed,
        input_grad,
        out_dtype[0],
        small[:bias_rows],
        out_dtype[1],
        out_dtype[2],
        out_dtype[3],
    ) + tuple(small[bias_rows + i * width : bias_rows + (i + 1) * width] for i in range(4))


def solution(mesh):
    placed = (
        P(("replica", "shard"), None),
        P(("replica", "shard"), None),
        P("shard", None),
        P("shard"),
        P("shard", None),
        P("shard", None),
        P("shard", None),
        P("shard"),
        P("shard"),
        P("shard"),
        P("shard"),
        P("replica", None),
    )
    return jax.shard_map(
        on_device,
        mesh=mesh,
        in_specs=placed,
        out_specs=(
            P(("replica", "shard"), None),
            P(("replica", "shard"), None),
            P("shard", None),
            P("shard"),
            P("shard", None),
            P("shard", None),
            P("shard", None),
            P("shard"),
            P("shard"),
            P("shard"),
            P("shard"),
        ),
        check_vma=False,
    )
```

```python
import functools

import jax
import jax.numpy as jnp
from jax import lax
from jax.experimental import pallas as pl
from jax.experimental.pallas import tpu as pltpu
from jax.sharding import PartitionSpec as P

D = 2048
FF = 5632
HEADS = 32
HEAD_DIM = 64
ROT_DIM = 16
MESH = pl.DeviceIdType.MESH


norm_eps = 1e-05
masked_score = -1000000000.0


def group_layout(lengths, token_index):
    segment = jnp.zeros_like(token_index)
    position = token_index
    end = jnp.int32(0)
    for i in range(lengths.shape[0]):
        end = end + lengths[i]
        passed = (token_index >= end).astype(jnp.int32)
        segment = segment + passed
        position = position - passed * lengths[i]
    return (segment, position)


def rope_tables(position, index):
    frequency = jnp.exp(-jnp.log(10000.0) * (2.0 * index.astype(jnp.float32) / ROT_DIM))
    angles = position.astype(jnp.float32)[:, None] * frequency
    return (jnp.cos(angles), jnp.sin(angles))


def contract_last(left, right):
    return lax.dot_general(
        left, right, (((1,), (1,)), ((), ())), preferred_element_type=jnp.float32
    )


def aligned(value, unit):
    return pl.multiple_of(value * unit, unit)


def greet(partners, count):
    barrier = pltpu.get_barrier_semaphore()
    for there, device in partners:
        @pl.when(there)
        def _():
            pl.semaphore_signal(barrier, inc=1, device_id=device, device_id_type=MESH)
    pl.semaphore_wait(barrier, count)


def greet_line(z, shards):
    count = (z + shards - 1) // shards + (2 * shards - 2 - z) // shards
    greet([(z >= 1, {"shard": z - 1}), (z + 1 < shards, {"shard": z + 1})], count)


def remote(source, target, send, recv, device):
    return pltpu.make_async_remote_copy(
        src_ref=source, dst_ref=target, send_sem=send, recv_sem=recv,
        device_id=device, device_id_type=MESH,
    )


class Cube:
    def __init__(self):
        r = lax.axis_index("replica")
        self.core, self.x, self.y = r % 2, (r // 2) % 2, r // 4
        self.place = 2 * self.y + self.x
        self.to_x = {"replica": r + 2 - 4 * self.x}
        self.to_y = {"replica": r + 4 - 8 * self.y}
        self.to_core = {"replica": r + 1 - 2 * self.core}

    def partners(self, shards):
        z = lax.axis_index("shard")
        return [((z != o), {"shard": o}) for o in range(shards)] + [
            (z >= 0, d) for d in (self.to_x, self.to_y, self.to_core)
        ]


def rows_of(ref, start, unit, count):
    return ref.at[pl.ds(pl.multiple_of(start, unit), count)]


class Spreader:
    def __init__(self, cube, shards, share, parts, source, out, sems):
        self.cube, self.shards, self.share, self.parts = cube, shards, share, parts
        self.source, self.out = source, out
        self.z_send, self.z_recv, self.send, self.recv, self.loc = sems
        self.cut = 16 * ((share // 16 + 1) // 2)
        self.z = lax.axis_index("shard")
        r = lax.axis_index("replica")
        self.who = (r, r + 2 - 4 * cube.x, r + 4 - 8 * cube.y, 4 * (1 - cube.y) + 2 * (1 - cube.x) + cube.core)

    def rows(self, o, kind, half=None):
        first, count = {None: (0, self.share), 0: (0, self.cut), 1: (self.cut, self.share - self.cut)}[half]
        return rows_of(self.out, (o * 8 + self.who[kind]) * self.share + first, 16, count)

    def target(self, o, part):
        width = self.out.shape[1] // self.parts
        return self.rows(o, 0).at[:, pl.ds(part * width, width)]

    def z_copy(self, o, part):
        return remote(self.source(o, part), self.target(self.z, part), self.z_send.at[o, part], self.z_recv.at[self.z, part], {"shard": o})

    def z_arrival(self, o, part):
        place = self.target(o, part)
        return remote(place, place, self.z_send.at[o, part], self.z_recv.at[o, part], {"shard": o})

    def local(self, o, part):
        return pltpu.make_async_copy(self.source(o, part), self.target(o, part), self.loc.at[part])

    def start_own(self):
        for part in range(self.parts):
            self.local(self.z, part).start()

    def start(self):
        for o in range(self.shards):
            for part in range(self.parts):
                @pl.when(self.z != o)
                def _():
                    self.z_copy(o, part).start()

    def sent(self):
        for o in range(self.shards):
            for part in range(self.parts):
                @pl.when(self.z != o)
                def _():
                    self.z_copy(o, part).wait_send()

    def copy(self, kind, o):
        c = self.cube
        block, device = (
            (self.rows(o, 0), c.to_x),
            (self.rows(o, 0), c.to_y),
            (self.rows(o, 1, 0), c.to_y),
            (self.rows(o, 2, 1), c.to_x),
            (self.rows(o, 0), c.to_core),
            (self.rows(o, 1), c.to_core),
            (self.rows(o, 2), c.to_core),
            (self.rows(o, 3), c.to_core),
        )[kind]
        return remote(block, block, self.send.at[kind, o], self.recv.at[kind, o], device)

    def arrive(self, distance):
        for o in range(self.shards):
            @pl.when((self.z - o == distance) | (o - self.z == distance))
            def _():
                for part in range(self.parts):
                    if distance == 0:
                        self.local(o, part).wait()
                    else:
                        self.z_arrival(o, part).wait_recv()
                for kind in (0, 1, 4):
                    self.copy(kind, o).start()

    def pass_on(self, o):
        self.copy(0, o).wait_recv()
        self.copy(2, o).start()
        self.copy(5, o).start()
        self.copy(1, o).wait_recv()
        self.copy(3, o).start()
        self.copy(6, o).start()

    def pass_last(self, o):
        self.copy(2, o).wait_recv()
        self.copy(3, o).wait_recv()
        self.copy(7, o).start()

    def landed(self):
        for o in range(self.shards):
            for kind in (4, 5, 6, 7):
                self.copy(kind, o).wait_recv()

    def finish(self):
        for o in range(self.shards):
            for kind in range(8):
                self.copy(kind, o).wait_send()


def spread_sems(shards, parts):
    dma = pltpu.SemaphoreType.DMA
    return [dma((shards, parts)), dma((shards, parts)), dma((8, shards)), dma((8, shards)), dma((parts,))]


class Line:
    def __init__(self, shards, pieces, own, buf, send, recv):
        self.z = lax.axis_index("shard")
        self.shards, self.pieces, self.own, self.buf, self.send, self.recv = shards, pieces, own, buf, send, recv
        self.rows = buf.shape[1] // pieces

    def copy(self, way, step, piece):
        target = self.z + 1 if way == 0 else self.z - 1
        owner = self.z - step if way == 0 else self.z + step
        block = pl.ds(piece * self.rows, self.rows)
        place = self.buf.at[owner, block]
        source = self.own.at[block] if step == 0 and self.own is not None else place
        return remote(source, place, self.send.at[way, step, piece], self.recv.at[way, step, piece], {"shard": target})

    def sends(self, way, step):
        if way == 0:
            return (self.z + 1 < self.shards) & (self.z - step >= 0)
        return (self.z >= 1) & (self.z + step < self.shards)

    def gets(self, way, step):
        return (self.z - step >= 1) if way == 0 else (self.z + step + 1 < self.shards)

    def start(self, piece):
        for way in (0, 1):
            @pl.when(self.sends(way, 0))
            def _():
                self.copy(way, 0, piece).start()

    def relay(self, step, piece):
        for way in (0, 1):
            @pl.when(self.gets(way, step))
            def _():
                self.copy(way, step, piece).wait_recv()
            if step + 1 < self.shards - 1:
                @pl.when(self.sends(way, step + 1))
                def _():
                    self.copy(way, step + 1, piece).start()

    def finish(self):
        for step in range(self.shards - 1):
            for piece in range(self.pieces):
                for way in (0, 1):
                    @pl.when(self.sends(way, step))
                    def _():
                        self.copy(way, step, piece).wait_send()


def line_sems(shards, pieces):
    dma = pltpu.SemaphoreType.DMA
    return [dma((2, shards - 1, pieces)), dma((2, shards - 1, pieces))]


def layer_norm_rows(values, gain, shift):
    centered = values - jnp.mean(values, axis=-1, keepdims=True)
    spread = jnp.mean(centered * centered, axis=-1, keepdims=True)
    return (centered * lax.rsqrt(spread + norm_eps) * gain + shift).astype(jnp.bfloat16)


def vector_row(vectors, i):
    return jnp.concatenate([vectors[o, i : i + 1, :] for o in range(vectors.shape[0])], axis=1)


def bias_piece(v_buf, z, t, tile, shards, per_part):
    flat = (t // per_part) * shards + z
    return v_buf[flat // 3, pl.ds(flat % 3, 1), pl.ds(aligned(t % per_part, tile), tile)]


def start_kernel(shards, tokens, vectors, weight, out_weight, cosine, minus, plus,
                 all_tokens, all_vectors, normed, qkv, kept_weight, all_out,
                 x_buf, v_buf, w_buf, n_buf, q_buf, *sems):
    cube = Cube()
    z = lax.axis_index("shard")
    r = lax.axis_index("replica")
    rows = tokens.shape[0]
    share = weight.shape[0] // 8
    width = w_buf.shape[1] // 3
    x_send, x_recv, v_send, v_recv, loc = sems[:5]
    line = Line(shards, 1, tokens, x_buf, x_send, x_recv)
    mine = pl.ds(aligned(r, share), share)
    spread = Spreader(
        cube, shards, share, 3,
        lambda o, part: weight.at[mine, pl.ds(aligned(part * shards + o, width), width)], w_buf, sems[5:10],
    )
    spread_out = Spreader(cube, shards, share, 1, lambda o, part: out_weight.at[mine], all_out, sems[10:15])
    greet(cube.partners(shards), shards + 2)

    def v_copy(o):
        return remote(vectors, v_buf.at[z], v_send.at[o], v_recv.at[z], {"shard": o})

    def v_arrival(o):
        return remote(vectors, v_buf.at[o], v_send.at[o], v_recv.at[o], {"shard": o})

    own_x = pltpu.make_async_copy(tokens, x_buf.at[z], loc.at[0, 0])
    own_v = pltpu.make_async_copy(vectors, v_buf.at[z], loc.at[1, 0])
    own_x.start()
    own_v.start()
    for o in range(shards):
        @pl.when(z != o)
        def _():
            v_copy(o).start()
    spread.start_own()
    spread_out.start_own()
    spread.start()
    spread.arrive(0)
    spread_out.arrive(0)
    line.start(0)
    spread_out.start()
    for distance in range(1, shards):
        spread.arrive(distance)
    own_x.wait()
    own_v.wait()
    for o in range(shards):
        @pl.when(z != o)
        def _():
            v_arrival(o).wait_recv()
    keep_v = pltpu.make_async_copy(v_buf, all_vectors, loc.at[2, 0])
    keep_v.start()
    gain, shift = vector_row(v_buf, 3), vector_row(v_buf, 4)

    def put(source, target, o, i):
        block = pl.ds(aligned(o, rows), rows)
        copy = pltpu.make_async_copy(source.at[block], target.at[block], loc.at[4 + i, o])
        copy.start()

    def normalize(o):
        @pl.loop(0, rows // 32)
        def _(i):
            values = x_buf[o, pl.ds(aligned(i, 32), 32), :].astype(jnp.float32)
            n_buf[pl.ds(pl.multiple_of(o * rows + i * 32, 32), 32), :] = layer_norm_rows(values, gain, shift)
        put(n_buf, normed, o, 0)
        pltpu.make_async_copy(x_buf.at[o], all_tokens.at[o], loc.at[6, o]).start()

    tile = 256
    per_part = width // tile

    def project(o):
        block = pl.ds(aligned(o, rows), rows)

        @pl.loop(0, 3 * per_part)
        def _(t):
            columns = pl.ds(aligned(t, tile), tile)
            value = jnp.dot(n_buf[block, :], w_buf[:, columns], preferred_element_type=jnp.float32)
            value = value + bias_piece(v_buf, z, t, tile, shards, per_part)

            @pl.when(t < 2 * per_part)
            def _():
                wide, wide_minus, wide_plus = (
                    jnp.concatenate([table[block, :]] * (tile // 128), axis=1) for table in (cosine, minus, plus)
                )
                turned = value * wide + pltpu.roll(value, tile - 8, 1) * wide_minus + pltpu.roll(value, 8, 1) * wide_plus
                q_buf[block, columns] = turned.astype(jnp.bfloat16)

            @pl.when(t >= 2 * per_part)
            def _():
                q_buf[block, columns] = value.astype(jnp.bfloat16)
        put(q_buf, qkv, o, 1)

    normalize(z)
    line.relay(0, 0)
    for o in range(shards):
        spread.pass_on(o)
    for o in range(shards):
        spread.pass_last(o)
    spread.landed()
    keep_w = pltpu.make_async_copy(w_buf, kept_weight, loc.at[3, 0])
    keep_w.start()
    project(z)
    for distance in range(1, shards):
        spread_out.arrive(distance)
    for step in range(shards - 1):
        if step > 0:
            line.relay(step, 0)
        for way in (0, 1):
            owner = z - step - 1 if way == 0 else z + step + 1

            @pl.when(line.gets(way, step))
            def _():
                normalize(owner)
                project(owner)
        if step == min(1, shards - 2):
            for o in range(shards):
                spread_out.pass_on(o)
    for o in range(shards):
        spread_out.pass_last(o)
    spread_out.landed()
    line.finish()
    spread.sent()
    spread.finish()
    spread_out.sent()
    spread_out.finish()
    for o in range(shards):
        block = pl.ds(o * rows, rows)

        @pl.when(z != o)
        def _():
            v_copy(o).wait_send()
        pltpu.make_async_copy(n_buf.at[block], normed.at[block], loc.at[4, o]).wait()
        pltpu.make_async_copy(q_buf.at[block], qkv.at[block], loc.at[5, o]).wait()
        pltpu.make_async_copy(x_buf.at[o], all_tokens.at[o], loc.at[6, o]).wait()
    keep_v.wait()
    keep_w.wait()


def start_call(shards, tokens, vectors, weight, out_weight, cosine, minus, plus):
    rows = tokens.shape[0]
    group = rows * shards
    depth = weight.shape[0]
    width = weight.shape[1] // shards
    any_ = pl.BlockSpec(memory_space=pl.ANY)
    vm = pl.BlockSpec(memory_space=pltpu.VMEM)
    low = jnp.bfloat16
    dma = pltpu.SemaphoreType.DMA
    return pl.pallas_call(
        functools.partial(start_kernel, shards),
        out_shape=[
            jax.ShapeDtypeStruct((shards, rows, D), low),
            jax.ShapeDtypeStruct((shards,) + vectors.shape, vectors.dtype),
            jax.ShapeDtypeStruct((group, D), low),
            jax.ShapeDtypeStruct((group, width), low),
            jax.ShapeDtypeStruct((depth * shards, width), low),
            jax.ShapeDtypeStruct((depth * shards, D), low),
        ],
        in_specs=[any_] * 4 + [vm] * 3,
        out_specs=[any_] * 6,
        scratch_shapes=[
            pltpu.VMEM((shards, rows, D), low),
            pltpu.VMEM((shards,) + vectors.shape, vectors.dtype),
            pltpu.VMEM((depth * shards, width), low),
            pltpu.VMEM((group, D), low),
            pltpu.VMEM((group, width), low),
        ] + line_sems(shards, 1) + [dma((shards,)), dma((shards,)), dma((7, shards))]
        + spread_sems(shards, 3) + spread_sems(shards, 1),
        compiler_params=pltpu.CompilerParams(
            collective_id=1, has_side_effects=True, vmem_limit_bytes=62 * 2**20
        ),
        name="start",
        cost_estimate=pl.CostEstimate(flops=2 * group * D * width, bytes_accessed=150 * 10**6, transcendentals=0),
    )(tokens, vectors, weight, out_weight, cosine, minus, plus)


def attend_spread_kernel(shards, rows, qkv, seg_rows, seg_columns, gate_up, attended, stats, all_gate_up, a_buf, *sems):
    cube = Cube()
    z = lax.axis_index("shard")
    r = lax.axis_index("replica")
    width = qkv.shape[1] // 3
    blocks = qkv.shape[0] // rows
    share = gate_up.shape[0] // 8
    half = all_gate_up.shape[1] // 2
    mine = pl.ds(aligned(r, share), share)
    spread = Spreader(
        cube, shards, share, 2,
        lambda o, part: gate_up.at[mine, pl.ds(aligned((part * shards + o) * (half // 128), 128), half)], all_gate_up, sems[3:8],
    )
    line = Line(shards, blocks, None, a_buf, sems[0], sems[1])
    loc = sems[2]
    greet(cube.partners(shards), shards + 2)
    spread.start_own()
    spread.start()
    spread.arrive(0)

    def done(block):
        line.start(block)
        if 0 < block < shards:
            spread.arrive(block)

    attend_body(rows, qkv, seg_rows, seg_columns, a_buf, stats, done)
    moves = [functools.partial(line.relay, step, block) for step in range(shards - 1) for block in range(blocks)]
    steps = [functools.partial(spread.pass_on, o) for o in range(shards)]
    steps += [functools.partial(spread.pass_last, o) for o in range(shards)]
    for i in range(max(len(moves), len(steps))):
        if i < len(moves):
            moves[i]()
        if i < len(steps):
            steps[i]()
    keep = [pltpu.make_async_copy(a_buf.at[o], attended.at[:, pl.ds(o * width, width)], loc.at[o]) for o in range(shards)]
    for copy in keep:
        copy.start()
    spread.landed()
    line.finish()
    spread.sent()
    spread.finish()
    for copy in keep:
        copy.wait()


def attend_spread_call(shards, rows, qkv, seg_rows, seg_columns, gate_up):
    group = qkv.shape[0]
    width = qkv.shape[1] // 3
    blocks = group // rows
    vm = pl.BlockSpec(memory_space=pltpu.VMEM)
    any_ = pl.BlockSpec(memory_space=pl.ANY)
    dma = pltpu.SemaphoreType.DMA
    low = jnp.bfloat16
    return pl.pallas_call(
        functools.partial(attend_spread_kernel, shards, rows),
        out_shape=[
            jax.ShapeDtypeStruct((group, shards * width), low),
            jax.ShapeDtypeStruct((group, 128), jnp.float32),
            jax.ShapeDtypeStruct((gate_up.shape[0] * shards, gate_up.shape[1] // shards), low),
        ],
        in_specs=[vm, vm, vm, any_],
        out_specs=[any_, vm, any_],
        scratch_shapes=[pltpu.VMEM((shards, group, width), low)] + line_sems(shards, blocks) + [dma((shards,))]
        + spread_sems(shards, 2),
        compiler_params=pltpu.CompilerParams(
            collective_id=2, has_side_effects=True, vmem_limit_bytes=48 * 2**20
        ),
        name="attend_spread",
        cost_estimate=pl.CostEstimate(flops=10**9, bytes_accessed=150 * 10**6, transcendentals=0),
    )(qkv, seg_rows, seg_columns, gate_up)


def hidden_kernel(shards, attended, tokens, out_weight, gate_up_weight, down_weight, cotangent, vectors,
                  middle_own, normed_two, hidden, slopes, all_cotangent, down_part,
                  a_buf, x_buf, o_buf, g_buf, d_buf, c_buf, mid, n_buf, gu, h_buf, s_buf, c_send, c_recv, loc):
    z = lax.axis_index("shard")
    greet_line(z, shards)
    rows = cotangent.shape[0]
    group = rows * shards
    inner = h_buf.shape[1]
    gain, shift = vector_row(vectors, 5), vector_row(vectors, 6)
    line = Line(shards, 1, cotangent, c_buf, c_send, c_recv)
    line.start(0)
    load = [pltpu.make_async_copy(source, target, loc.at[i]) for i, (source, target) in enumerate((
        (attended, a_buf), (out_weight, o_buf), (tokens, x_buf), (gate_up_weight, g_buf), (down_weight, d_buf),
        (cotangent, c_buf.at[z])))]
    for copy in load:
        copy.start()
    for copy in load[:3]:
        copy.wait()
    tile = 256
    span = 2 * rows
    for part in range(group // span):
        at = part * span

        @pl.loop(0, D // tile)
        def _(t):
            columns = pl.ds(aligned(t, tile), tile)
            value = jnp.dot(a_buf[at : at + span, :], o_buf[:, columns], preferred_element_type=jnp.float32)
            for k in range(2):
                mid[k * rows : (k + 1) * rows, columns] = (
                    value[k * rows : (k + 1) * rows] + x_buf[2 * part + k, :, columns].astype(jnp.float32)
                )

        @pl.loop(0, span // 32)
        def _(i):
            block = pl.ds(aligned(i, 32), 32)
            n_buf[pl.ds(pl.multiple_of(at + i * 32, 32), 32), :] = layer_norm_rows(mid[block, :], gain, shift)
        for k in range(2):
            @pl.when(z == 2 * part + k)
            def _():
                middle_own[...] = mid[k * rows : (k + 1) * rows, :]
    keep_n = pltpu.make_async_copy(n_buf, normed_two, loc.at[6])
    keep_n.start()
    line.relay(0, 0)
    load[3].wait()

    @pl.loop(0, 2 * inner // tile)
    def _(t):
        columns = pl.ds(aligned(t, tile), tile)
        gu[:, columns] = jnp.dot(n_buf[...], g_buf[:, columns], preferred_element_type=jnp.float32)

    @pl.loop(0, group // 32)
    def _(i):
        block = pl.ds(aligned(i, 32), 32)
        gate = gu[block, :inner]
        h_buf[block, :] = (gate / (1.0 + jnp.exp(-gate)) * gu[block, inner:]).astype(jnp.bfloat16)
    keep_h = pltpu.make_async_copy(h_buf, hidden, loc.at[7])
    keep_h.start()
    if shards > 2:
        line.relay(1, 0)
    load[4].wait()

    @pl.loop(0, D // tile)
    def _(t):
        columns = pl.ds(aligned(t, tile), tile)
        a_buf[:, columns] = jnp.dot(h_buf[...], d_buf[:, columns], preferred_element_type=jnp.float32).astype(jnp.bfloat16)
    keep_p = pltpu.make_async_copy(a_buf, down_part, loc.at[8])
    keep_p.start()
    load[5].wait()

    def back(o):
        mid[:rows, :inner] = contract_last(c_buf[o], d_buf[...])

        @pl.loop(0, rows // 32)
        def _(i):
            value = mid[pl.ds(aligned(i, 32), 32), :inner]
            place = pl.ds(pl.multiple_of(o * rows + i * 32, 32), 32)
            gate = gu[place, :inner]
            up = gu[place, inner:]
            sigmoid = 1.0 / (1.0 + jnp.exp(-gate))
            s_buf[place, :inner] = (value * up * (sigmoid * (1.0 + gate * (1.0 - sigmoid)))).astype(jnp.bfloat16)
            s_buf[place, inner:] = (value * (gate * sigmoid)).astype(jnp.bfloat16)

    back(z)
    for step in range(shards - 1):
        if step >= 2:
            line.relay(step, 0)
        for way in (0, 1):
            owner = z - step - 1 if way == 0 else z + step + 1

            @pl.when(line.gets(way, step))
            def _():
                back(owner)
    keep = [pltpu.make_async_copy(c_buf, all_cotangent, loc.at[9]), pltpu.make_async_copy(s_buf, slopes, loc.at[10])]
    for copy in keep:
        copy.start()
    line.finish()
    for copy in keep + [keep_n, keep_h, keep_p]:
        copy.wait()


def hidden_call(shards, attended, tokens, out_weight, gate_up_weight, down_weight, cotangent, vectors):
    rows = cotangent.shape[0]
    group = rows * shards
    inner = down_weight.shape[0]
    low = jnp.bfloat16
    f32 = jnp.float32
    vm = pl.BlockSpec(memory_space=pltpu.VMEM)
    any_ = pl.BlockSpec(memory_space=pl.ANY)
    return pl.pallas_call(
        functools.partial(hidden_kernel, shards),
        out_shape=[
            jax.ShapeDtypeStruct((rows, D), f32),
            jax.ShapeDtypeStruct((group, D), low),
            jax.ShapeDtypeStruct((group, inner), low),
            jax.ShapeDtypeStruct((group, 2 * inner), low),
            jax.ShapeDtypeStruct((shards, rows, D), low),
            jax.ShapeDtypeStruct((group, D), low),
        ],
        in_specs=[any_] * 6 + [vm],
        out_specs=[vm] + [any_] * 5,
        scratch_shapes=[
            pltpu.VMEM((group, D), low),
            pltpu.VMEM((shards, rows, D), low),
            pltpu.VMEM(out_weight.shape, low),
            pltpu.VMEM(gate_up_weight.shape, low),
            pltpu.VMEM(down_weight.shape, low),
            pltpu.VMEM((shards, rows, D), low),
            pltpu.VMEM((2 * rows, D), f32),
            pltpu.VMEM((group, D), low),
            pltpu.VMEM((group, 2 * inner), f32),
            pltpu.VMEM((group, inner), low),
            pltpu.VMEM((group, 2 * inner), low),
        ] + line_sems(shards, 1) + [pltpu.SemaphoreType.DMA((11,))],
        compiler_params=pltpu.CompilerParams(
            collective_id=9, has_side_effects=True, vmem_limit_bytes=63 * 2**20
        ),
        name="hidden",
        cost_estimate=pl.CostEstimate(flops=24 * 10**9, bytes_accessed=150 * 10**6, transcendentals=0),
    )(attended, tokens, out_weight, gate_up_weight, down_weight, cotangent, vectors)


def head_mask(even, rows):
    lane = lax.broadcasted_iota(jnp.int32, (rows, 128), 1)
    return (lane < HEAD_DIM) if even else (lane >= HEAD_DIM)


def only(values, keep):
    return jnp.where(keep, values.astype(jnp.float32), 0.0).astype(jnp.bfloat16)


def block_visible(at, rows, seg_rows, seg_columns):
    count = at + rows
    row = lax.broadcasted_iota(jnp.int32, (rows, count), 0) + at
    column = lax.broadcasted_iota(jnp.int32, (rows, count), 1)
    return (column <= row) & (seg_rows[at : at + rows, :1] == seg_columns[:1, :count])


def attend_body(rows, qkv, seg_rows, seg_columns, a_buf, stats, done):
    z = lax.axis_index("shard")
    width = qkv.shape[1] // 3
    pairs = width // 128
    scale = HEAD_DIM ** (-0.5)
    for block in range(qkv.shape[0] // rows):
        at = block * rows
        count = at + rows
        seen = block_visible(at, rows, seg_rows, seg_columns)
        for pair in range(pairs):
            lanes = slice(128 * pair, 128 * pair + 128)
            query = qkv[at:count, lanes]
            keys = qkv[:count, width + 128 * pair : width + 128 * pair + 128]
            values = qkv[:count, 2 * width + 128 * pair : 2 * width + 128 * pair + 128]
            results = []
            for odd in (0, 1):
                keep = head_mask(odd == 0, rows)
                scores = contract_last(only(query, keep), keys) * scale
                scores = jnp.where(seen, scores, masked_score)
                top = jnp.max(scores, axis=-1, keepdims=True)
                weights = jnp.exp(scores - top)
                total = jnp.sum(weights, axis=-1, keepdims=True)
                probs = (weights * (1.0 / total)).astype(jnp.bfloat16)
                results.append(jnp.dot(probs, values, preferred_element_type=jnp.float32))
                head = 2 * pair + odd
                stats[at:count, head : head + 1] = top
                stats[at:count, 64 + head : 65 + head] = 1.0 / total
            merged = jnp.where(head_mask(True, rows), results[0], results[1])
            a_buf[z, at:count, lanes] = merged.astype(jnp.bfloat16)
        done(block)


def attend_kernel(shards, rows, qkv, seg_rows, seg_columns, attended, stats, a_buf, a_send, a_recv, loc):
    z = lax.axis_index("shard")
    width = qkv.shape[1] // 3
    blocks = qkv.shape[0] // rows
    greet_line(z, shards)
    line = Line(shards, blocks, None, a_buf, a_send, a_recv)
    attend_body(rows, qkv, seg_rows, seg_columns, a_buf, stats, line.start)
    for step in range(shards - 1):
        for block in range(blocks):
            line.relay(step, block)
    keep = [pltpu.make_async_copy(a_buf.at[o], attended.at[:, pl.ds(o * width, width)], loc.at[o]) for o in range(shards)]
    for copy in keep:
        copy.start()
    line.finish()
    for copy in keep:
        copy.wait()


def attend_call(shards, rows, qkv, seg_rows, seg_columns):
    group = qkv.shape[0]
    width = qkv.shape[1] // 3
    blocks = group // rows
    vm = pl.BlockSpec(memory_space=pltpu.VMEM)
    any_ = pl.BlockSpec(memory_space=pl.ANY)
    dma = pltpu.SemaphoreType.DMA
    return pl.pallas_call(
        functools.partial(attend_kernel, shards, rows),
        out_shape=[
            jax.ShapeDtypeStruct((group, shards * width), jnp.bfloat16),
            jax.ShapeDtypeStruct((group, 128), jnp.float32),
        ],
        in_specs=[vm, vm, vm],
        out_specs=[any_, vm],
        scratch_shapes=[
            pltpu.VMEM((shards, group, width), jnp.bfloat16),
            dma((2, shards - 1, blocks)), dma((2, shards - 1, blocks)), dma((shards,)),
        ],
        compiler_params=pltpu.CompilerParams(
            collective_id=2, has_side_effects=True, vmem_limit_bytes=48 * 2**20
        ),
        name="attend",
        cost_estimate=pl.CostEstimate(flops=10**9, bytes_accessed=150 * 10**6, transcendentals=0),
    )(qkv, seg_rows, seg_columns)


def attend_back_kernel(rows, *refs):
    attend_back_body(rows, *refs, [])


def attend_back_body(rows, qkv, d_attended, stats, seg_rows, seg_columns, cosine, minus, plus,
                     d_qkv, bias_grad, d_keys, d_values, steps):
    width = qkv.shape[1] // 3
    group = qkv.shape[0]
    blocks = group // rows
    pairs = width // 128
    scale = HEAD_DIM ** (-0.5)

    def turned(value, at, count):
        return (value * cosine[at:count, :] - pltpu.roll(value, 120, 1) * minus[at:count, :]
                - pltpu.roll(value, 8, 1) * plus[at:count, :])

    for block in reversed(range(blocks)):
        at = block * rows
        count = at + rows
        seen = block_visible(at, rows, seg_rows, seg_columns)
        for pair in range(pairs):
            lanes = slice(128 * pair, 128 * pair + 128)
            query = qkv[at:count, lanes]
            keys = qkv[:count, width + 128 * pair : width + 128 * pair + 128]
            values = qkv[:count, 2 * width + 128 * pair : 2 * width + 128 * pair + 128]
            slope = d_attended[at:count, lanes]
            d_query, d_key, d_value = [], [], []
            for odd in (0, 1):
                keep = head_mask(odd == 0, rows)
                head = 2 * pair + odd
                own_query = only(query, keep)
                own_slope = only(slope, keep)
                scores = contract_last(own_query, keys) * scale
                scores = jnp.where(seen, scores, masked_score)
                probs = jnp.exp(scores - stats[at:count, head : head + 1]) * stats[at:count, 64 + head : 65 + head]
                d_probs = contract_last(own_slope, values)
                inner = jnp.sum(probs * d_probs, axis=-1, keepdims=True)
                d_scores = (probs * (d_probs - inner)).astype(jnp.bfloat16)
                d_query.append(jnp.dot(d_scores, keys, preferred_element_type=jnp.float32))
                d_key.append(contract_first(d_scores, own_query))
                d_value.append(contract_first(probs.astype(jnp.bfloat16), own_slope))
            keep = head_mask(True, rows)
            d_q = jnp.where(keep, d_query[0], d_query[1]) * scale
            d_q = turned(d_q, at, count).astype(jnp.bfloat16)
            d_qkv[at:count, lanes] = d_q
            d_k = (d_key[0] + d_key[1]) * scale
            d_v = d_value[0] + d_value[1]
            if block == blocks - 1:
                d_keys[:, lanes] = d_k
                d_values[:, lanes] = d_v
            else:
                d_keys[:count, lanes] += d_k
                d_values[:count, lanes] += d_v
            k_out = turned(d_keys[at:count, lanes], at, count).astype(jnp.bfloat16)
            d_qkv[at:count, width + 128 * pair : width + 128 * pair + 128] = k_out
            v_out = d_values[at:count, lanes].astype(jnp.bfloat16)
            d_qkv[at:count, 2 * width + 128 * pair : 2 * width + 128 * pair + 128] = v_out
            if steps:
                steps.pop(0)()
    for part in range(3 * pairs):
        lanes = slice(128 * part, 128 * part + 128)
        bias_grad[:, lanes] = jnp.broadcast_to(
            jnp.sum(d_qkv[:, lanes].astype(jnp.float32), axis=0, keepdims=True), (8, 128))


def contract_first(left, right):
    return lax.dot_general(
        left, right, (((0,), (0,)), ((), ())), preferred_element_type=jnp.float32
    )


def attend_back_call(rows, qkv, d_attended, stats, seg_rows, seg_columns, cosine, minus, plus):
    group = qkv.shape[0]
    width = qkv.shape[1] // 3
    vm = pl.BlockSpec(memory_space=pltpu.VMEM)
    return pl.pallas_call(
        functools.partial(attend_back_kernel, rows),
        out_shape=[
            jax.ShapeDtypeStruct((group, 3 * width), jnp.bfloat16),
            jax.ShapeDtypeStruct((8, 3 * width), jnp.float32),
        ],
        in_specs=[vm] * 8,
        out_specs=[vm, vm],
        scratch_shapes=[pltpu.VMEM((group, width), jnp.float32), pltpu.VMEM((group, width), jnp.float32)],
        compiler_params=pltpu.CompilerParams(vmem_limit_bytes=48 * 2**20),
        name="attend_back",
        cost_estimate=pl.CostEstimate(flops=3 * 10**9, bytes_accessed=100 * 10**6, transcendentals=0),
    )(qkv, d_attended, stats, seg_rows, seg_columns, cosine, minus, plus)


def scatter_kernel(shards, cuts, parts, total, own, got, load, send, recv):
    z = lax.axis_index("shard")
    rows = parts.shape[1]
    step_rows = rows // cuts
    greet_line(z, shards)

    def piece(cut):
        return pl.ds(cut * step_rows, step_rows)

    def moved(way, block, cut):
        target = z + 1 if way == 0 else z - 1
        place = got.at[way, block, piece(cut)]
        return remote(place, place, send.at[way, block, cut], recv.at[way, block, cut], {"shard": target})

    loads = [pltpu.make_async_copy(parts.at[j], own.at[j], load.at[j]) for j in range(shards)]
    for copy in loads:
        copy.start()
    for copy in loads:
        copy.wait()
    for far in range(shards - 1):
        for cut in range(cuts):
            for way in (0, 1):
                block = shards - 1 - far if way == 0 else far
                sends = z < block if way == 0 else z > block
                first = z == 0 if way == 0 else z == shards - 1

                @pl.when(sends)
                def _():
                    @pl.when(first)
                    def _():
                        got[way, block, piece(cut)] = own[block, piece(cut)]

                    @pl.when(jnp.logical_not(first))
                    def _():
                        moved(way, block, cut).wait_recv()
                        got[way, block, piece(cut)] = (
                            got[way, block, piece(cut)].astype(jnp.float32)
                            + own[block, piece(cut)].astype(jnp.float32)
                        ).astype(got.dtype)
                    moved(way, block, cut).start()
    total[...] = own[z].astype(jnp.float32)
    for way in (0, 1):
        @pl.when(z >= 1 if way == 0 else z + 1 < shards)
        def _():
            for cut in range(cuts):
                moved(way, z, cut).wait_recv()
            total[...] += got[way, z].astype(jnp.float32)
    for far in range(shards - 1):
        for cut in range(cuts):
            for way in (0, 1):
                block = shards - 1 - far if way == 0 else far

                @pl.when(z < block if way == 0 else z > block)
                def _():
                    moved(way, block, cut).wait_send()


def scatter_call(shards, parts, number):
    _, rows, columns = parts.shape
    cuts = 3
    dma = pltpu.SemaphoreType.DMA
    return pl.pallas_call(
        functools.partial(scatter_kernel, shards, cuts),
        out_shape=jax.ShapeDtypeStruct((rows, columns), jnp.float32),
        in_specs=[pl.BlockSpec(memory_space=pl.ANY)],
        out_specs=pl.BlockSpec(memory_space=pltpu.VMEM),
        scratch_shapes=[
            pltpu.VMEM(parts.shape, parts.dtype),
            pltpu.VMEM((2,) + parts.shape, parts.dtype),
            dma((shards,)), dma((2, shards, cuts)), dma((2, shards, cuts)),
        ],
        compiler_params=pltpu.CompilerParams(
            collective_id=number, has_side_effects=True, vmem_limit_bytes=32 * 2**20
        ),
        name="scatter",
        cost_estimate=pl.CostEstimate(flops=0, bytes_accessed=200 * 10**6, transcendentals=0),
    )(parts)


def exchange_kernel(shards, first, second, first_out, second_out, send, recv, loc):
    z = lax.axis_index("shard")
    width = first.shape[1] // shards
    greet([((z != o), {"shard": o}) for o in range(shards)], shards - 1)
    arrays = ((first, first_out), (second, second_out))

    def move(k, o):
        source, target = arrays[k]
        return remote(source.at[:, pl.ds(o * width, width)], target.at[z], send.at[k, o], recv.at[k, z], {"shard": o})

    def arrival(k, o):
        source, target = arrays[k]
        return remote(target.at[o], target.at[o], send.at[k, o], recv.at[k, o], {"shard": o})

    for k in (0, 1):
        for o in range(shards):
            @pl.when(z != o)
            def _():
                move(k, o).start()

            @pl.when(z == o)
            def _():
                source, target = arrays[k]
                pltpu.make_async_copy(source.at[:, pl.ds(o * width, width)], target.at[o], loc.at[k]).start()
    for k in (0, 1):
        for o in range(shards):
            @pl.when(z != o)
            def _():
                arrival(k, o).wait_recv()
                move(k, o).wait_send()

            @pl.when(z == o)
            def _():
                source, target = arrays[k]
                pltpu.make_async_copy(source.at[:, pl.ds(o * width, width)], target.at[o], loc.at[k]).wait()


def exchange_call(shards, first, second):
    rows, columns = first.shape
    shape = jax.ShapeDtypeStruct((shards, rows, columns // shards), first.dtype)
    any_ = pl.BlockSpec(memory_space=pl.ANY)
    dma = pltpu.SemaphoreType.DMA
    return pl.pallas_call(
        functools.partial(exchange_kernel, shards),
        out_shape=[shape, shape],
        in_specs=[any_, any_],
        out_specs=[any_, any_],
        scratch_shapes=[dma((2, shards)), dma((2, shards)), dma((2,))],
        compiler_params=pltpu.CompilerParams(collective_id=5, has_side_effects=True),
        name="exchange",
        cost_estimate=pl.CostEstimate(flops=0, bytes_accessed=100 * 10**6, transcendentals=0),
    )(first, second)


def add_rows(target, source, count):
    step = 16

    @pl.loop(0, count // step)
    def _(i):
        block = pl.ds(aligned(i, step), step)
        target[block, :] = (
            target[block, :].astype(jnp.float32) + source[block, :].astype(jnp.float32)
        ).astype(target.dtype)


class Reducer:
    def __init__(self, cube, share, term, core, near, last, send, recv):
        self.cube, self.share = cube, share
        self.cut = 16 * ((share // 16 + 1) // 2)
        self.term, self.core, self.near, self.last = term, core, near, last
        self.send, self.recv = send, recv
        self.chunks = term.shape[0]

    def share_rows(self, chunk, place, half):
        first, count = (0, self.cut) if half == 0 else (self.cut, self.share - self.cut)
        start = self.cube.core * 4 * self.share + place * self.share + first
        return rows_of(self.term.at[chunk], start, 16, count)

    def own(self, chunk):
        start = (self.cube.core * 4 + self.cube.place) * self.share
        return rows_of(self.term.at[chunk], start, 16, self.share)

    def core_copy(self, chunk):
        source = rows_of(self.term.at[chunk], (1 - self.cube.core) * 4 * self.share, 16, 4 * self.share)
        return remote(source, self.core.at[chunk], self.send.at[chunk, 0], self.recv.at[chunk, 0], self.cube.to_core)

    def near_place(self, half, other):
        c = self.cube
        if half == 0:
            return 2 * other + (1 - c.x), 2 * other + c.x
        return 2 * (1 - c.y) + other, 2 * c.y + other

    def near_slot(self, chunk, half, other):
        count = self.cut if half == 0 else self.share - self.cut
        start = other * count + (2 * self.cut if half == 1 else 0)
        return self.near.at[chunk, pl.ds(start, count)]

    def near_copy(self, chunk, half, other):
        source = self.share_rows(chunk, self.near_place(half, other)[0], half)
        slot = 1 + 2 * half + other
        device = self.cube.to_x if half == 0 else self.cube.to_y
        return remote(source, self.near_slot(chunk, half, other), self.send.at[chunk, slot], self.recv.at[chunk, slot], device)

    def last_slot(self, chunk, half):
        first, count = (0, self.cut) if half == 0 else (self.cut, self.share - self.cut)
        return self.last.at[chunk, pl.ds(first, count)]

    def last_copy(self, chunk, half):
        c = self.cube
        place = 2 * (1 - c.y) + c.x if half == 0 else 2 * c.y + (1 - c.x)
        device = c.to_y if half == 0 else c.to_x
        source = self.share_rows(chunk, place, half)
        return remote(source, self.last_slot(chunk, half), self.send.at[chunk, 5 + half], self.recv.at[chunk, 5 + half], device)

    def start(self, chunk):
        self.core_copy(chunk).start()

    def after_core(self, chunk):
        self.core_copy(chunk).wait_recv()
        mine = rows_of(self.term.at[chunk], self.cube.core * 4 * self.share, 16, 4 * self.share)
        add_rows(mine, self.core.at[chunk], 4 * self.share)
        for half in (0, 1):
            for other in (0, 1):
                self.near_copy(chunk, half, other).start()

    def after_near(self, chunk):
        for half in (0, 1):
            count = self.cut if half == 0 else self.share - self.cut
            for other in (0, 1):
                self.near_copy(chunk, half, other).wait_recv()
                stays = self.share_rows(chunk, self.near_place(half, other)[1], half)
                add_rows(stays, self.near_slot(chunk, half, other), count)
            self.last_copy(chunk, half).start()

    def after_last(self, chunk):
        c = self.cube
        for half in (0, 1):
            count = self.cut if half == 0 else self.share - self.cut
            self.last_copy(chunk, half).wait_recv()
            add_rows(self.share_rows(chunk, c.place, half), self.last_slot(chunk, half), count)

    def finish(self, chunk):
        self.core_copy(chunk).wait_send()
        for half in (0, 1):
            for other in (0, 1):
                self.near_copy(chunk, half, other).wait_send()
            self.last_copy(chunk, half).wait_send()


class Owners:
    def __init__(self, shards, parts, source, out, send, recv, loc):
        self.shards, self.parts, self.source, self.out = shards, parts, source, out
        self.send, self.recv, self.loc = send, recv, loc
        self.z = lax.axis_index("shard")
        self.width = out.shape[1] // (shards * parts)

    def target(self, shard, part):
        return self.out.at[:, pl.ds(aligned((part * self.shards + shard) * (self.width // 128), 128), self.width)]

    def piece(self, o, part):
        return self.source(o).at[:, pl.ds(part * self.width, self.width)]

    def copy(self, o, part):
        return remote(self.piece(o, part), self.target(self.z, part), self.send.at[o, part], self.recv.at[self.z, part], {"shard": o})

    def arrival(self, o, part):
        place = self.target(o, part)
        return remote(place, place, self.send.at[o, part], self.recv.at[o, part], {"shard": o})

    def local(self, o, part):
        return pltpu.make_async_copy(self.piece(o, part), self.target(o, part), self.loc.at[part])

    def start(self, k):
        o = lax.rem(self.z + k, self.shards)
        for part in range(self.parts):
            if k == 0:
                self.local(o, part).start()
            else:
                self.copy(o, part).start()

    def arrive_from(self, k):
        o = lax.rem(self.z + k, self.shards)
        for part in range(self.parts):
            if k == 0:
                self.local(o, part).wait()
            else:
                self.arrival(o, part).wait_recv()

    def arrive(self):
        for k in range(self.shards):
            self.arrive_from(k)

    def finish(self):
        for k in range(1, self.shards):
            o = lax.rem(self.z + k, self.shards)
            for part in range(self.parts):
                self.copy(o, part).wait_send()


def owner_sems(shards, parts):
    dma = pltpu.SemaphoreType.DMA
    return [dma((shards, parts)), dma((shards, parts)), dma((parts,))]


class Gatherer:
    def __init__(self, cube, share, out, sems):
        self.cube, self.share, self.out = cube, share, out
        self.send, self.recv, self.loc = sems
        self.count = share.shape[0]
        self.cut = 16 * ((self.count // 16 + 1) // 2)

    def rows(self, place, half=None):
        first, count = {None: (0, self.count), 0: (0, self.cut), 1: (self.cut, self.count - self.cut)}[half]
        return rows_of(self.out, (self.cube.core * 4 + place) * self.count + first, 16, count)

    def copy(self, kind):
        c = self.cube
        at_x, at_y = 2 * c.y + 1 - c.x, 2 * (1 - c.y) + c.x
        block, device = (
            (self.rows(c.place), c.to_x),
            (self.rows(c.place), c.to_y),
            (self.rows(at_x, 0), c.to_y),
            (self.rows(at_y, 1), c.to_x),
            (self.rows(c.place), c.to_core),
            (self.rows(at_x), c.to_core),
            (self.rows(at_y), c.to_core),
            (self.rows(3 - c.place), c.to_core),
        )[kind]
        source = self.share if kind in (0, 1, 4) else block
        return remote(source, block, self.send.at[kind], self.recv.at[kind], device)

    def local(self):
        return pltpu.make_async_copy(self.share, self.rows(self.cube.place), self.loc.at[0])

    def start(self):
        for kind in (0, 1, 4):
            self.copy(kind).start()
        self.local().start()

    def pass_on(self):
        self.copy(0).wait_recv()
        self.copy(2).start()
        self.copy(5).start()
        self.copy(1).wait_recv()
        self.copy(3).start()
        self.copy(6).start()

    def pass_last(self):
        self.copy(2).wait_recv()
        self.copy(3).wait_recv()
        self.copy(7).start()

    def finish(self):
        for kind in (4, 5, 6, 7):
            self.copy(kind).wait_recv()
        for kind in range(8):
            self.copy(kind).wait_send()
        self.local().wait()


def gatherer_sems():
    dma = pltpu.SemaphoreType.DMA
    return [dma((8,)), dma((8,)), dma((1,))]


class LineSum:
    def __init__(self, shards, cuts, own, got, send, recv):
        self.z = lax.axis_index("shard")
        self.shards, self.cuts, self.own, self.got, self.send, self.recv = shards, cuts, own, got, send, recv
        self.step = own.shape[1] // cuts

    def piece(self, cut):
        return pl.ds(cut * self.step, self.step)

    def copy(self, way, block, cut, source=None):
        target = self.z + 1 if way == 0 else self.z - 1
        place = self.got.at[way, block, self.piece(cut)]
        return remote(place if source is None else source, place, self.send.at[way, block, cut], self.recv.at[way, block, cut], {"shard": target})

    def pair(self, t):
        half = self.shards // 2
        upper = self.z // half
        return half - 1 - t + upper * (2 * t - half + 1)

    def ready(self, pair):
        for way in (0, 1):
            for i in (0, 1):
                block = 2 * pair + (1 - i if way == 0 else i)

                @pl.when((self.z == (0 if way == 0 else self.shards - 1)) & (block != self.z))
                def _():
                    for cut in range(self.cuts):
                        self.copy(way, block, cut, self.own.at[block, self.piece(cut)]).start()

    def ends(self, i):
        for way in (0, 1):
            block = self.shards - 1 - i if way == 0 else i

            @pl.when(self.z == (0 if way == 0 else self.shards - 1))
            def _():
                for cut in range(self.cuts):
                    self.copy(way, block, cut, self.own.at[block, self.piece(cut)]).start()

    def step_on(self, hop, far, cut):
        for way in (0, 1):
            block = self.shards - 1 - far if way == 0 else far

            @pl.when(self.z == (hop if way == 0 else self.shards - 1 - hop))
            def _():
                self.copy(way, block, cut).wait_recv()
                place = self.got.at[way, block, self.piece(cut)]
                add_rows(place, self.own.at[block, self.piece(cut)], self.step)
                self.copy(way, block, cut).start()

    def steps(self):
        return [
            functools.partial(self.step_on, hop, far, cut)
            for far in range(self.shards - 2)
            for hop in range(1, self.shards - 1 - far)
            for cut in range(self.cuts)
        ]

    def result(self, total):
        rows = self.own.shape[1]
        for way in (0, 1):
            @pl.when(self.z >= 1 if way == 0 else self.z + 1 < self.shards)
            def _():
                for cut in range(self.cuts):
                    self.copy(way, self.z, cut).wait_recv()

        @pl.loop(0, rows // 16)
        def _(i):
            block = pl.ds(aligned(i, 16), 16)
            total[block, :] = self.own[self.z, block, :].astype(jnp.float32)

            @pl.when(self.z >= 1)
            def _():
                total[block, :] += self.got[0, self.z, block, :].astype(jnp.float32)

            @pl.when(self.z + 1 < self.shards)
            def _():
                total[block, :] += self.got[1, self.z, block, :].astype(jnp.float32)

    def finish(self):
        for far in range(self.shards - 1):
            for cut in range(self.cuts):
                for way in (0, 1):
                    block = self.shards - 1 - far if way == 0 else far

                    @pl.when(self.z < block if way == 0 else self.z > block)
                    def _():
                        self.copy(way, block, cut).wait_send()


def line_scratch(shards, rows, columns, cuts):
    dma = pltpu.SemaphoreType.DMA
    return [
        pltpu.VMEM((shards, rows, columns), jnp.bfloat16),
        pltpu.VMEM((2, shards, rows, columns), jnp.bfloat16),
        dma((2, shards, cuts)), dma((2, shards, cuts)),
    ]


def reducer_scratch(chunks, share, columns):
    dma = pltpu.SemaphoreType.DMA
    return [pltpu.VMEM((chunks, n * share, columns), jnp.bfloat16) for n in (8, 4, 2, 1)] + [
        dma((chunks, 7)), dma((chunks, 7)),
    ]


def pair_product(own, pair, slopes, weight, tile=512):
    rows = own.shape[1]

    @pl.loop(0, own.shape[2] // tile)
    def _(t):
        columns = pl.ds(aligned(t, tile), tile)
        value = contract_last(slopes[pl.ds(aligned(pair, 2 * rows), 2 * rows), :], weight[columns, :])
        own[2 * pair, :, columns] = value[:rows].astype(own.dtype)
        own[2 * pair + 1, :, columns] = value[rows:].astype(own.dtype)


def term_product(term, chunk, left, right):
    term.at[chunk][...] = contract_first(left[...], right[...]).astype(jnp.bfloat16)


def spaced(moves, steps, every):
    moves = list(moves)
    for i, step in enumerate(steps):
        step()
        if i % every == every - 1 and moves:
            moves.pop(0)()
    for move in moves:
        move()


def interleave(moves, steps):
    for i in range(max(len(moves), len(steps))):
        if i < len(moves):
            moves[i]()
        if i < len(steps):
            steps[i]()


def load_all(pairs, loc):
    copies = [pltpu.make_async_copy(source, target, loc.at[i]) for i, (source, target) in enumerate(pairs)]
    for copy in copies:
        copy.start()
    return copies


def further(shards):
    z = lax.axis_index("shard")
    return [(k, lax.rem(z + k, shards)) for k in (*range(1, shards), 0)]


class Chunks:
    def __init__(self, ref, chunks):
        self.ref, self.shape = ref, (chunks, ref.shape[0] // chunks, ref.shape[1])

    @property
    def at(self):
        return self

    def __getitem__(self, chunk):
        return self.ref.at[pl.ds(aligned(chunk, self.shape[1]), self.shape[1])]


def hidden_back_kernel(shards, slopes, weight, hidden, cotangent, normed_two, total, down_share, gate_up_rows,
                       s_buf, w_buf, h_buf, c_buf, n_buf, own, got, z_send, z_recv,
                       term, core, near, last, r_send, r_recv, g_core, g_near, g_last, g_send, g_recv, loc, *sems):
    cube = Cube()
    loads = load_all(((hidden, h_buf), (cotangent, c_buf), (slopes, s_buf), (weight, w_buf), (normed_two, n_buf)), loc)
    greet(cube.partners(shards), shards + 2)
    line = LineSum(shards, 3, own, got, z_send, z_recv)
    share = hidden.shape[1] // 8
    width = D // shards
    chunks, _, columns = term.shape
    g_term = Chunks(w_buf, shards)
    reducer = Reducer(cube, share, term, core, near, last, r_send, r_recv)
    g_reducer = Reducer(cube, width // 8, g_term, g_core, g_near, g_last, g_send, g_recv)
    owners = Owners(shards, 2, g_reducer.own, gate_up_rows, *sems)
    def product(t):
        pair = line.pair(t)
        pair_product(own, pair, s_buf, w_buf)
        line.ready(pair)

    def down_term(k):
        term_product(term, k, h_buf, c_buf.at[:, pl.ds(k * columns, columns)])
        reducer.start(k)

    def gate_up_term(k):
        term_product(g_term, k, n_buf.at[:, pl.ds(aligned(k, width), width)], s_buf)
        g_reducer.start(k)

    keep = []

    def keep_down(k):
        copy = pltpu.make_async_copy(reducer.own(k), down_share.at[:, pl.ds(k * columns, columns)], loc.at[5 + k])
        copy.start()
        keep.append(copy)

    def of(call, count):
        return [functools.partial(call, k) for k in range(count)]

    turn = further(shards)

    def each(call):
        return [functools.partial(call, o) for _, o in turn]

    moves = line.steps()

    def down_ending(k):
        reducer.after_last(k)
        keep_down(k)

    def g_ending(k, o):
        g_reducer.after_last(o)
        owners.start(k)

    cores = of(reducer.after_core, chunks) + each(g_reducer.after_core)
    nears = of(reducer.after_near, chunks) + each(g_reducer.after_near)
    lasts = of(down_ending, chunks) + [functools.partial(g_ending, k, o) for k, o in turn]
    g_terms = each(gate_up_term)
    sequence = [copy.wait for copy in loads[:2]] + of(down_term, chunks) + [copy.wait for copy in loads[2:]]
    sequence += [functools.partial(product, 0)] + cores[:2]
    sequence += [functools.partial(product, t) for t in range(1, shards // 2)] + g_terms[:2] + nears[:1] + cores[2:3] + g_terms[2:] + nears[1:2] + lasts[:1]
    sequence += cores[3:4] + moves[:5]
    for i in range(2, chunks + shards):
        sequence += nears[i : i + 1] + lasts[i - 1 : i] + cores[i + 2 : i + 3] + moves[i + 3 : i + 4]
    sequence += lasts[-1:] + moves[chunks + shards + 3 :]
    for step in sequence:
        step()
    line.result(total)
    line.finish()
    owners.arrive()
    for k in range(chunks):
        reducer.finish(k)
    for k in range(shards):
        g_reducer.finish(k)
    owners.finish()
    for copy in keep:
        copy.wait()


def hidden_back_call(shards, slopes, weight, hidden, cotangent, normed_two):
    group, inner = hidden.shape
    rows = group // shards
    share = inner // 8
    chunks = 4
    width = D // shards
    low = jnp.bfloat16
    any_ = pl.BlockSpec(memory_space=pl.ANY)
    dma = pltpu.SemaphoreType.DMA
    return pl.pallas_call(
        functools.partial(hidden_back_kernel, shards),
        out_shape=[
            jax.ShapeDtypeStruct((rows, D), jnp.float32),
            jax.ShapeDtypeStruct((share, D), low),
            jax.ShapeDtypeStruct((width // 8, shards * 2 * inner), low),
        ],
        in_specs=[any_] * 5,
        out_specs=[pl.BlockSpec(memory_space=pltpu.VMEM), any_, any_],
        scratch_shapes=[pltpu.VMEM(a.shape, low) for a in (slopes, weight, hidden, cotangent, normed_two)]
        + line_scratch(shards, rows, D, 3) + reducer_scratch(chunks, share, D // chunks)
        + reducer_scratch(shards, width // 8, 2 * inner)[1:] + [dma((5 + chunks,))] + owner_sems(shards, 2),
        compiler_params=pltpu.CompilerParams(collective_id=6, has_side_effects=True, vmem_limit_bytes=63 * 2**20),
        name="hidden_back",
        cost_estimate=pl.CostEstimate(flops=10**10, bytes_accessed=200 * 10**6, transcendentals=0),
    )(slopes, weight, hidden, cotangent, normed_two)


def norm_back_rows(slope, values, gain):
    centered = values - jnp.mean(values, axis=-1, keepdims=True)
    inverse = lax.rsqrt(jnp.mean(centered * centered, axis=-1, keepdims=True) + norm_eps)
    unit = centered * inverse
    scaled = slope * gain
    back = inverse * (
        scaled
        - jnp.mean(scaled, axis=-1, keepdims=True)
        - unit * jnp.mean(scaled * unit, axis=-1, keepdims=True)
    )
    return back, unit


def heads_back_kernel(shards, rows, d_normed_two, middle, cotangent, vectors, out_weight, qkv, stats, seg_rows, seg_columns,
                      cosine, minus, plus, down_part, down_share, gate_up_rows,
                      d_middle, norm_grads, d_qkv, bias_grad, mixed, m_columns, down_grad, gate_up_grad,
                      o_buf, m_low, da_own, d_attended, d_keys, d_values, total, own, got, z_send, z_recv, e_send, e_recv, loc, *sems):
    cube = Cube()
    z = lax.axis_index("shard")
    loads = load_all(((out_weight, o_buf), (down_part, own)), loc)
    gain = vector_row(vectors, 5)
    greet(cube.partners(shards), shards + 2)
    width = D // shards
    half = gate_up_rows.shape[1] // 2
    gatherers = [Gatherer(cube, down_share, down_grad, sems[0:3])] + [
        Gatherer(cube, gate_up_rows.at[:, pl.ds(i * half, half)], gate_up_grad.at[:, pl.ds(i * half, half)], sems[3 * i + 3 : 3 * i + 6])
        for i in (0, 1)
    ]
    line = LineSum(shards, 3, own, got, z_send, z_recv)
    gatherers[0].start()
    gatherers[1].start()
    arrays = ((da_own, d_attended), (m_low, m_columns))

    def move(k, o):
        source, target = arrays[k]
        return remote(source.at[:, pl.ds(o * width, width)], target.at[pl.ds(aligned(z, rows), rows)],
                      e_send.at[k, o], e_recv.at[k, z], {"shard": o})

    def arrival(k, o):
        place = arrays[k][1].at[pl.ds(o * rows, rows)]
        return remote(place, place, e_send.at[k, o], e_recv.at[k, o], {"shard": o})

    def here(k, o):
        source, target = arrays[k]
        return pltpu.make_async_copy(source.at[:, pl.ds(o * width, width)], target.at[pl.ds(o * rows, rows)], loc.at[2 + k])

    def begin(k, o):
        @pl.when(z != o)
        def _():
            move(k, o).start()

        @pl.when(z == o)
        def _():
            here(k, o).start()

    def arrive(k):
        for o in range(shards):
            @pl.when(z != o)
            def _():
                arrival(k, o).wait_recv()

            @pl.when(z == o)
            def _():
                here(k, o).wait()

    norm_grads[...] = jnp.zeros_like(norm_grads)

    @pl.loop(0, rows // 16)
    def _(i):
        block = pl.ds(aligned(i, 16), 16)
        slope = d_normed_two[block, :]
        back, unit = norm_back_rows(slope, middle[block, :], gain)
        value = cotangent[block, :].astype(jnp.float32) + back
        d_middle[block, :] = value
        m_low[block, :] = value.astype(jnp.bfloat16)
        norm_grads[0:8, :] += (slope * unit).reshape(2, 8, D).sum(axis=0)
        norm_grads[8:16, :] += slope.reshape(2, 8, D).sum(axis=0)

    loads[0].wait()
    for o in range(shards):
        da_own[:, o * width : (o + 1) * width] = contract_last(
            m_low[...], o_buf[o * width : (o + 1) * width, :]).astype(jnp.bfloat16)
        begin(0, o)
    loads[1].wait()
    for t in range(shards // 2):
        line.ready(line.pair(t))
    for o in range(shards):
        begin(1, o)
    arrive(0)
    gatherers[0].pass_on()

    def nothing():
        pass

    moves = line.steps()
    steps = [nothing, gatherers[1].pass_on, gatherers[2].start, nothing, moves[0], nothing, gatherers[0].pass_last]
    steps += [moves[1], nothing, moves[2], nothing] + [gatherers[1].pass_last] + moves[3:]
    attend_back_body(rows, qkv, d_attended, stats, seg_rows, seg_columns, cosine, minus, plus,
                     d_qkv, bias_grad, d_keys, d_values, steps)
    for step in steps:
        step()
    gatherers[2].pass_on()
    arrive(1)
    gatherers[2].pass_last()
    line.result(total)

    @pl.loop(0, rows // 16)
    def _(i):
        block = pl.ds(aligned(i, 16), 16)
        mixed[block, :] = (middle[block, :] + total[block, :]).astype(mixed.dtype)
    line.finish()
    for k in (0, 1):
        for o in range(shards):
            @pl.when(z != o)
            def _():
                move(k, o).wait_send()
    for gatherer in gatherers:
        gatherer.finish()


def heads_back_call(shards, rows, d_normed_two, middle, cotangent, vectors, out_weight, qkv, stats, seg_rows, seg_columns,
                    cosine, minus, plus, down_part, down_share, gate_up_rows):
    group = qkv.shape[0]
    width = D // shards
    vm = pl.BlockSpec(memory_space=pltpu.VMEM)
    any_ = pl.BlockSpec(memory_space=pl.ANY)
    dma = pltpu.SemaphoreType.DMA
    low = jnp.bfloat16
    f32 = jnp.float32
    return pl.pallas_call(
        functools.partial(heads_back_kernel, shards, rows),
        out_shape=[
            jax.ShapeDtypeStruct((rows, D), f32),
            jax.ShapeDtypeStruct((16, D), f32),
            jax.ShapeDtypeStruct((group, 3 * width), low),
            jax.ShapeDtypeStruct((8, 3 * width), f32),
            jax.ShapeDtypeStruct((rows, D), low),
            jax.ShapeDtypeStruct((group, width), low),
            jax.ShapeDtypeStruct((8 * down_share.shape[0], D), low),
            jax.ShapeDtypeStruct((8 * gate_up_rows.shape[0], gate_up_rows.shape[1]), low),
        ],
        in_specs=[vm] * 4 + [any_] + [vm] * 7 + [any_] * 3,
        out_specs=[vm] * 5 + [any_] * 3,
        scratch_shapes=[
            pltpu.VMEM(out_weight.shape, low), pltpu.VMEM((rows, D), low), pltpu.VMEM((rows, D), low),
            pltpu.VMEM((group, width), low),
            pltpu.VMEM((group, width), f32), pltpu.VMEM((group, width), f32), pltpu.VMEM((rows, D), f32),
        ] + line_scratch(shards, rows, D, 3) + [dma((2, shards)), dma((2, shards)), dma((4,))] + gatherer_sems() * 3,
        compiler_params=pltpu.CompilerParams(collective_id=7, has_side_effects=True, vmem_limit_bytes=60 * 2**20),
        name="heads_back",
        cost_estimate=pl.CostEstimate(flops=10**10, bytes_accessed=200 * 10**6, transcendentals=0),
    )(d_normed_two, middle, cotangent, vectors, out_weight, qkv, stats, seg_rows, seg_columns, cosine, minus, plus,
      down_part, down_share, gate_up_rows)


def input_back_kernel(shards, slopes, weight, normed, attended, d_middle_columns, tokens, vectors, d_middle, bias_grad, norm_grads,
                      input_grad, small, qkv_grad, out_grad,
                      w_buf, n_buf, a_buf, m_buf, total, part, part_in, own, got, z_send, z_recv,
                      term, core, near, last, r_send, r_recv, o_term, o_core, o_near, o_last, o_send, o_recv,
                      qkv_rows, out_rows, s_send, s_recv, loc, *sems):
    cube = Cube()
    z = lax.axis_index("shard")
    loads = load_all(((normed, n_buf), (weight, w_buf), (attended, a_buf), (d_middle_columns, m_buf)), loc)
    r = lax.axis_index("replica")
    others = [lax.rem(r + i, 8) for i in range(1, 8)]
    greet([((z != o), {"shard": o}) for o in range(shards)] + [(z >= 0, {"replica": o}) for o in others], shards + 6)
    gain = vector_row(vectors, 3)
    rows = tokens.shape[0]
    width = D // shards
    share = width // 8
    line = LineSum(shards, 3, own, got, z_send, z_recv)
    reducer = Reducer(cube, share, term, core, near, last, r_send, r_recv)
    o_reducer = Reducer(cube, share, o_term, o_core, o_near, o_last, o_send, o_recv)
    owners = Owners(shards, 3, reducer.own, qkv_rows, *sems[0:3])
    o_owners = Owners(shards, 1, o_reducer.own, out_rows, *sems[3:6])
    gatherers = [
        [
            Gatherer(
                cube, *(ref.at[:, pl.ds(aligned(p * shards + lax.rem(z + k, shards), width), width)] for ref in (qkv_rows, qkv_grad)),
                [sem.at[3 * k + p] for sem in sems[6:9]],
            )
            for p in range(3)
        ]
        for k in range(shards)
    ]
    o_gatherer = Gatherer(cube, out_rows, out_grad, sems[9:12])

    def qkv_term(o):
        term_product(term, o, n_buf.at[:, pl.ds(aligned(o, width), width)], slopes)
        reducer.start(o)

    def out_term(o):
        term_product(o_term, o, a_buf.at[:, pl.ds(aligned(o, width), width)], m_buf)
        o_reducer.start(o)

    def product(t):
        pair = line.pair(t)
        pair_product(own, pair, slopes, w_buf)
        line.ends(t)

    turn = further(shards)

    def each(call):
        return [functools.partial(call, o) for _, o in turn]

    def ending(red, own_, k, o):
        red.after_last(o)
        own_.start(k)

    moves = line.steps()
    cores, nears = each(reducer.after_core), each(reducer.after_near)
    lasts = [functools.partial(ending, reducer, owners, k, o) for k, o in turn]
    terms = each(qkv_term)

    def begin_from(i):
        owners.arrive_from(i)
        for g in gatherers[i]:
            g.start()

    def pass_from(i):
        for g in gatherers[i]:
            g.pass_on()

    def pass_last_from(i):
        for g in gatherers[i]:
            g.pass_last()

    sequence = [loads[0].wait] + terms + [loads[1].wait, functools.partial(product, 0)] + cores[:2]
    sequence += [functools.partial(product, t) for t in range(1, shards // 2)] + [loads[2].wait, loads[3].wait] + each(out_term)
    sequence += moves[:1] + nears[:1] + cores[2:3] + each(o_reducer.after_core) + moves[1:3] + nears[1:2] + lasts[:1] + cores[3:] + moves[3:5]
    sequence += nears[2:3] + lasts[1:2] + moves[5:6] + nears[3:] + lasts[2:3] + [functools.partial(line.ends, i) for i in range(shards // 2, shards - 1)]
    sequence += each(o_reducer.after_near) + lasts[3:]
    sequence += [functools.partial(ending, o_reducer, o_owners, k, o) for k, o in turn]
    order = list(reversed(range(shards)))
    sequence += [functools.partial(begin_from, i) for i in order] + moves[6:7]
    sequence += [functools.partial(pass_from, i) for i in order[:2]] + moves[7:8] + [o_owners.arrive, o_gatherer.start]
    sequence += [functools.partial(pass_from, i) for i in order[2:]] + moves[8:] + [functools.partial(pass_last_from, i) for i in order[:2]]
    for step in sequence:
        step()
    line.result(total)

    part[...] = jnp.zeros_like(part)

    @pl.loop(0, rows // 16)
    def _(i):
        block = pl.ds(aligned(i, 16), 16)
        slope = total[block, :]
        back, unit = norm_back_rows(slope, tokens[block, :].astype(jnp.float32), gain)
        input_grad[block, :] = d_middle[block, :] + back
        ones = (slope * unit).reshape(2, 8, D).sum(axis=0).sum(axis=0, keepdims=True)
        twos = slope.reshape(2, 8, D).sum(axis=0).sum(axis=0, keepdims=True)
        for o in range(shards):
            part[o, 3:4, :] += ones[:, o * width : (o + 1) * width]
            part[o, 4:5, :] += twos[:, o * width : (o + 1) * width]
    for o in range(shards):
        for k in range(2):
            part[o, 5 + k : 6 + k, :] = jnp.sum(
                norm_grads[8 * k : 8 * k + 8, o * width : (o + 1) * width], axis=0, keepdims=True)
    for k in range(3):
        flat = k * shards + z
        part[flat // 3, pl.ds(flat % 3, 1), :] = bias_grad[0:1, k * width : (k + 1) * width]

    def small_copy(o):
        return remote(part.at[o], part_in.at[z], s_send.at[o], s_recv.at[z], {"shard": o})

    def small_arrival(o):
        return remote(part.at[o], part_in.at[o], s_send.at[o], s_recv.at[o], {"shard": o})

    for o in range(shards):
        @pl.when(z != o)
        def _():
            small_copy(o).start()
    small[...] = part[z]
    for o in range(shards):
        @pl.when(z != o)
        def _():
            small_arrival(o).wait_recv()
            small[...] += part_in[o]

    def sum_copy(o):
        return remote(small, part_in.at[shards + r], s_send.at[shards + o], s_recv.at[shards + r], {"replica": o})

    def sum_arrival(o):
        place = part_in.at[shards + o]
        return remote(place, place, s_send.at[shards + o], s_recv.at[shards + o], {"replica": o})

    for o in others:
        sum_copy(o).start()
    part_in[shards + r] = small[...]
    o_gatherer.pass_on()
    for o in others:
        sum_copy(o).wait_send()
        sum_arrival(o).wait_recv()
    small[...] = sum([part_in[shards + i] for i in range(1, 8)], part_in[shards])
    o_gatherer.pass_last()
    for i in order[2:]:
        pass_last_from(i)
    for o in range(shards):
        @pl.when(z != o)
        def _():
            small_copy(o).wait_send()
    line.finish()
    for k in range(shards):
        reducer.finish(k)
        o_reducer.finish(k)
    owners.finish()
    o_owners.finish()
    for g in sum(gatherers, [o_gatherer]):
        g.finish()


def input_back_call(shards, slopes, weight, normed, attended, d_middle_columns, tokens, vectors, d_middle, bias_grad, norm_grads):
    group = slopes.shape[0]
    rows = group // shards
    width = D // shards
    share = width // 8
    vm = pl.BlockSpec(memory_space=pltpu.VMEM)
    any_ = pl.BlockSpec(memory_space=pl.ANY)
    dma = pltpu.SemaphoreType.DMA
    low = jnp.bfloat16
    f32 = jnp.float32
    return pl.pallas_call(
        functools.partial(input_back_kernel, shards),
        out_shape=[
            jax.ShapeDtypeStruct((rows, D), f32),
            jax.ShapeDtypeStruct((8, width), f32),
            jax.ShapeDtypeStruct((width, 3 * D), low),
            jax.ShapeDtypeStruct((width, D), low),
        ],
        in_specs=[vm] + [any_] * 4 + [vm] * 5,
        out_specs=[vm, vm, any_, any_],
        scratch_shapes=[
            pltpu.VMEM(weight.shape, low), pltpu.VMEM(normed.shape, low), pltpu.VMEM(attended.shape, low),
            pltpu.VMEM(d_middle_columns.shape, low), pltpu.VMEM((rows, D), f32),
            pltpu.VMEM((shards, 8, width), f32), pltpu.VMEM((shards + 8, 8, width), f32),
        ] + line_scratch(shards, rows, D, 3) + reducer_scratch(shards, share, 3 * width) + reducer_scratch(shards, share, width)
        + [pltpu.VMEM((share, 3 * D), low), pltpu.VMEM((share, D), low), dma((shards + 8,)), dma((shards + 8,)), dma((4,))]
        + owner_sems(shards, 3) + owner_sems(shards, 1)
        + [dma((3 * shards, 8)), dma((3 * shards, 8)), dma((3 * shards, 1))] + gatherer_sems(),
        compiler_params=pltpu.CompilerParams(collective_id=8, has_side_effects=True, vmem_limit_bytes=60 * 2**20),
        name="input_back",
        cost_estimate=pl.CostEstimate(flops=10**10, bytes_accessed=200 * 10**6, transcendentals=0),
    )(slopes, weight, normed, attended, d_middle_columns, tokens, vectors, d_middle, bias_grad, norm_grads)


def swap_pieces(pieces):
    shards = lax.axis_size("shard")
    here = lax.axis_index("shard")
    out = pieces
    for k in range(1, shards):
        partner = jnp.bitwise_xor(here, k)
        piece = lax.dynamic_index_in_dim(pieces, partner, axis=0, keepdims=True)
        piece = lax.ppermute(piece, "shard", [(i, i ^ k) for i in range(shards)])
        out = lax.dynamic_update_slice_in_dim(out, piece, partner, axis=0)
    return out


def own_share(rows):
    own = rows.shape[0] // lax.axis_size("replica")
    return lax.dynamic_slice_in_dim(rows, lax.axis_index("replica") * own, own, axis=0)


def spread_rows(rows, columns):
    shards = lax.axis_size("shard")
    piece = own_share(rows)
    own = piece.shape[0]
    piece = piece.reshape(own, columns, shards, -1).transpose(2, 0, 1, 3).reshape(shards, own, -1)
    full = lax.all_gather(swap_pieces(piece), "replica", axis=0, tiled=False)
    return full.transpose(1, 0, 2, 3).reshape(rows.shape[0] * shards, -1)


def gather_rows(rows):
    shards = lax.axis_size("shard")
    piece = own_share(rows)
    moved = swap_pieces(jnp.broadcast_to(piece[None], (shards,) + piece.shape))
    full = lax.all_gather(moved, "replica", axis=0, tiled=False)
    return full.transpose(1, 0, 2, 3).reshape(rows.shape[0] * shards, -1)


def own_rows(features):
    copies = lax.axis_size("replica")
    shards = lax.axis_size("shard")
    count = features.shape[0]
    return (
        features.reshape(count, shards, copies, -1).transpose(0, 2, 1, 3).reshape(count, -1)
    )


def sum_columns(features, slopes, columns):
    shards = lax.axis_size("shard")
    term = contract_first(own_rows(features), slopes).astype(jnp.bfloat16)
    part = lax.psum_scatter(term, "replica", scatter_dimension=0, tiled=True)
    own = part.shape[0] // shards
    moved = swap_pieces(part.reshape(shards, own, -1))
    moved = moved.reshape(shards, own, columns, -1).transpose(1, 2, 0, 3).reshape(own, -1)
    return lax.all_gather(moved, "replica", axis=0, tiled=True)


def swiglu(gate_up):
    half = gate_up.shape[1] // 2
    return jax.nn.silu(gate_up[:, :half]) * gate_up[:, half:]


def norm_stats(values):
    mean = jnp.mean(values, axis=-1, keepdims=True)
    centered = values - mean
    inverse = lax.rsqrt(jnp.mean(centered * centered, axis=-1, keepdims=True) + norm_eps)
    return centered * inverse, inverse


def norm_back(slope, unit, inverse, gain):
    scaled = slope * gain
    return inverse * (
        scaled
        - jnp.mean(scaled, axis=-1, keepdims=True)
        - unit * jnp.mean(scaled * unit, axis=-1, keepdims=True)
    )


def start_plain(tokens, vectors, qkv_weight, cosine, minus, plus):
    shards = lax.axis_size("shard")
    here = lax.axis_index("shard")
    all_tokens = lax.all_gather(tokens, "shard", axis=0, tiled=False)
    all_vectors = lax.all_gather(vectors, "shard", axis=0, tiled=False)
    weight = spread_rows(qkv_weight, 3)
    width = D // shards
    gain, shift = (all_vectors[:, 3 + i].reshape(D) for i in (0, 1))
    unit, _ = norm_stats(all_tokens.reshape(-1, D).astype(jnp.float32))
    normed = (unit * gain + shift).astype(jnp.bfloat16)
    bias = all_vectors[:, :3].reshape(3, shards, width)
    bias = lax.dynamic_index_in_dim(bias, here, axis=1, keepdims=False).reshape(3 * width)
    value = jnp.dot(normed, weight, preferred_element_type=jnp.float32) + bias
    turned = value[:, : 2 * width]
    wide = [jnp.tile(t, (1, 2 * width // 128)) for t in (cosine, minus, plus)]
    turned = (
        turned * wide[0] + jnp.roll(turned, -8, 1) * wide[1] + jnp.roll(turned, 8, 1) * wide[2]
    )
    qkv = jnp.concatenate([turned, value[:, 2 * width :]], axis=1).astype(jnp.bfloat16)
    return all_tokens, all_vectors, normed, qkv, weight


def layer_kernels(shards, tokens, cotangent, weights, vectors, tables):
    qkv_weight, out_weight, gate_up_weight, down_weight = weights
    seg_rows, seg_columns, cosine, minus, plus = tables
    rows = tokens.shape[0]
    all_tokens, all_vectors, normed, qkv, weight_qkv, weight_out = start_call(
        shards, tokens, vectors, qkv_weight, out_weight, cosine, minus, plus
    )
    attended, stats, weight_gate_up = attend_spread_call(
        shards, rows, qkv, seg_rows, seg_columns, gate_up_weight
    )
    middle, normed_two, hidden, slopes, group_cotangent, down_part = hidden_call(
        shards, attended, all_tokens, weight_out, weight_gate_up, down_weight, cotangent, all_vectors
    )
    d_normed_two, down_share, gate_up_rows = hidden_back_call(
        shards, slopes, weight_gate_up, hidden, group_cotangent.reshape(shards * rows, D), normed_two
    )
    d_middle, norm_grads, d_qkv, bias_grad, mixed, d_middle_columns, down_grad, gate_up_grad = heads_back_call(
        shards, rows, d_normed_two, middle, cotangent, all_vectors, weight_out, qkv, stats, seg_rows, seg_columns,
        cosine, minus, plus, down_part.reshape(shards, rows, D), down_share, gate_up_rows,
    )
    input_grad, small, qkv_grad, out_grad = input_back_call(
        shards, d_qkv, weight_qkv, normed, attended, d_middle_columns, tokens, all_vectors, d_middle, bias_grad, norm_grads
    )
    return mixed, input_grad, small, (qkv_grad, out_grad, gate_up_grad, down_grad)


def layer_plain(shards, tokens, cotangent, weights, vectors, tables):
    qkv_weight, out_weight, gate_up_weight, down_weight = weights
    seg_rows, seg_columns, cosine, minus, plus = tables
    here = lax.axis_index("shard")
    row_count = tokens.shape[0]
    group_rows = row_count * shards
    width = D // shards
    f32 = jnp.float32
    low = jnp.bfloat16
    weight_out = gather_rows(out_weight)
    weight_gate_up = spread_rows(gate_up_weight, 2)
    all_tokens, all_vectors, normed_low, qkv, weight_qkv = start_plain(
        tokens, vectors, qkv_weight, cosine, minus, plus
    )
    gain_one, shift_one, gain_two, shift_two = (
        all_vectors[:, 3 + i].reshape(D) for i in range(4)
    )
    cotangent_later, qkv = lax.optimization_barrier((cotangent, qkv))
    group_cotangent = lax.all_gather(cotangent_later, "shard", axis=0, tiled=True)

    def local(array):
        return lax.dynamic_slice_in_dim(array, here * row_count, row_count, axis=0)

    attended, stats = attend_call(shards, row_count, qkv, seg_rows, seg_columns)
    inputs = all_tokens.reshape(group_rows, D).astype(f32)
    middle = inputs + jnp.dot(attended, weight_out, preferred_element_type=f32)
    unit_two, inverse_two = norm_stats(middle)
    normed_two_low = (unit_two * gain_two + shift_two).astype(low)
    gate_up = jnp.dot(normed_two_low, weight_gate_up, preferred_element_type=f32)
    hidden, swiglu_pull = jax.vjp(swiglu, gate_up)
    hidden_low = hidden.astype(low)
    d_hidden = contract_last(group_cotangent, down_weight)
    d_gate_up_low = swiglu_pull(d_hidden)[0].astype(low)
    down_part = jnp.dot(hidden_low, down_weight, preferred_element_type=f32).astype(low)
    unit_two_own = local(unit_two)
    inverse_two_own = local(inverse_two)
    middle_own = local(middle)

    d_normed_two_part = contract_last(d_gate_up_low, weight_gate_up).astype(low)
    d_normed_two = scatter_call(shards, d_normed_two_part.reshape(shards, row_count, D), 3)
    down_grad = lax.psum(contract_first(hidden_low, group_cotangent).astype(low), "replica")
    d_middle = cotangent.astype(f32) + norm_back(
        d_normed_two, unit_two_own, inverse_two_own, gain_two
    )
    d_gain_two = jnp.sum(d_normed_two * unit_two_own, axis=0)
    d_shift_two = jnp.sum(d_normed_two, axis=0)
    d_middle_low = d_middle.astype(low)
    d_attended_own = contract_last(d_middle_low, weight_out).astype(low)
    d_attended, d_middle_columns = exchange_call(shards, d_attended_own, d_middle_low)
    d_projected_low, bias_part = attend_back_call(
        row_count, qkv, d_attended.reshape(group_rows, width), stats, seg_rows, seg_columns,
        cosine, minus, plus,
    )
    down_own = lax.psum_scatter(down_part, "shard", scatter_dimension=0, tiled=True)
    mixed = (middle_own + down_own.astype(f32)).astype(low)
    d_normed_part = contract_last(d_projected_low, weight_qkv).astype(low)
    d_normed = scatter_call(shards, d_normed_part.reshape(shards, row_count, D), 4)
    gate_up_grad = sum_columns(normed_two_low, d_gate_up_low, 2)
    out_grad = sum_columns(attended, d_middle_columns.reshape(group_rows, width), 1)
    qkv_grad = sum_columns(normed_low, d_projected_low, 3)
    unit_one, inverse_one = norm_stats(tokens.astype(f32))
    input_grad = d_middle + norm_back(d_normed, unit_one, inverse_one, gain_one)
    d_gain_one = jnp.sum(d_normed * unit_one, axis=0)
    d_shift_one = jnp.sum(d_normed, axis=0)

    bias_part = bias_part[0].reshape(3, 1, width)
    bias_wide = lax.dynamic_update_slice(
        jnp.zeros((3, shards, width), f32), bias_part, (0, here, 0)
    ).reshape(shards, 3 * width)
    small = jnp.concatenate(
        [bias_wide]
        + [v.reshape(shards, width) for v in (d_gain_one, d_shift_one, d_gain_two, d_shift_two)],
        axis=1,
    )
    small = jnp.pad(small, ((0, 0), (0, width)))
    small = lax.psum(small, ("replica", "shard"))
    small = lax.dynamic_index_in_dim(small, here, axis=0, keepdims=False)
    return mixed, input_grad, small, (qkv_grad, out_grad, gate_up_grad, down_grad)


def on_device(
    tokens,
    cotangent,
    qkv_weight,
    qkv_bias,
    out_weight,
    gate_up_weight,
    down_weight,
    norm1_gain,
    norm1_shift,
    norm2_gain,
    norm2_shift,
    seq_lengths,
):
    shards = lax.axis_size("shard")
    copies = lax.axis_size("replica")
    row_count = tokens.shape[0]
    group_rows = row_count * shards
    width = D // shards
    f32 = jnp.float32
    low = jnp.bfloat16

    segment, position = group_layout(seq_lengths[0], jnp.arange(group_rows, dtype=jnp.int32))
    seg_rows = jnp.broadcast_to(segment[:, None], (group_rows, 128))
    seg_columns = jnp.broadcast_to(segment[None, :], (8, group_rows))
    lane = jnp.arange(128, dtype=jnp.int32)[None, :] % HEAD_DIM
    cosine, sine_value = rope_tables(position, lane % (ROT_DIM // 2))
    cosine = jnp.where(lane < ROT_DIM, cosine, 1.0)
    minus = jnp.where(lane < ROT_DIM // 2, -sine_value, 0.0)
    plus = jnp.where((lane >= ROT_DIM // 2) & (lane < ROT_DIM), sine_value, 0.0)

    vectors = jnp.zeros((8 * width,), f32)
    at = 0
    for vector in (qkv_bias, norm1_gain, norm1_shift, norm2_gain, norm2_shift):
        after = 8 * width - at - vector.shape[0]
        vectors = vectors + jnp.pad(vector.astype(f32), (at, after))
        at += vector.shape[0]
    vectors = vectors.reshape(8, width)
    weights = (qkv_weight, out_weight, gate_up_weight, down_weight)
    tables = (seg_rows, seg_columns, cosine, minus, plus)
    if copies == 8:
        outputs = layer_kernels(shards, tokens, cotangent, weights, vectors, tables)
    else:
        outputs = layer_plain(shards, tokens, cotangent, weights, vectors, tables)
    mixed, input_grad, small, grads = outputs
    bias_rows = 3 * width
    small = small.reshape(8 * width)
    out_dtype = tuple(grad.astype(f32) for grad in grads)
    return (
        mixed,
        input_grad,
        out_dtype[0],
        small[:bias_rows],
        out_dtype[1],
        out_dtype[2],
        out_dtype[3],
    ) + tuple(small[bias_rows + i * width : bias_rows + (i + 1) * width] for i in range(4))


def solution(mesh):
    placed = (
        P(("replica", "shard"), None),
        P(("replica", "shard"), None),
        P("shard", None),
        P("shard"),
        P("shard", None),
        P("shard", None),
        P("shard", None),
        P("shard"),
        P("shard"),
        P("shard"),
        P("shard"),
        P("replica", None),
    )
    return jax.shard_map(
        on_device,
        mesh=mesh,
        in_specs=placed,
        out_specs=(
            P(("replica", "shard"), None),
            P(("replica", "shard"), None),
            P("shard", None),
            P("shard"),
            P("shard", None),
            P("shard", None),
            P("shard", None),
            P("shard"),
            P("shard"),
            P("shard"),
            P("shard"),
        ),
        check_vma=False,
    )
```

```python
import functools

import jax
import jax.numpy as jnp
import numpy as np
from jax import lax
from jax.experimental import pallas as pl
from jax.experimental.pallas import tpu as pltpu
from jax.sharding import PartitionSpec as P

D = 2048
FF = 5632
HEADS = 32
HEAD_DIM = 64
ROT_DIM = 16
MESH = pl.DeviceIdType.MESH


norm_eps = 1e-05
masked_score = -1000000000.0


def group_layout(lengths, token_index):
    segment = jnp.zeros_like(token_index)
    position = token_index
    end = jnp.int32(0)
    for i in range(lengths.shape[0]):
        end = end + lengths[i]
        passed = (token_index >= end).astype(jnp.int32)
        segment = segment + passed
        position = position - passed * lengths[i]
    return (segment, position)


def contract_last(left, right):
    return lax.dot_general(
        left, right, (((1,), (1,)), ((), ())), preferred_element_type=jnp.float32
    )


def aligned(value, unit):
    return pl.multiple_of(value * unit, unit)


def greet(partners, count):
    barrier = pltpu.get_barrier_semaphore()
    for there, device in partners:
        @pl.when(there)
        def _():
            pl.semaphore_signal(barrier, inc=1, device_id=device, device_id_type=MESH)
    pl.semaphore_wait(barrier, count)


def greet_line(z, shards):
    count = (z + shards - 1) // shards + (2 * shards - 2 - z) // shards
    greet([(z >= 1, {"shard": z - 1}), (z + 1 < shards, {"shard": z + 1})], count)


def remote(source, target, send, recv, device):
    return pltpu.make_async_remote_copy(
        src_ref=source, dst_ref=target, send_sem=send, recv_sem=recv,
        device_id=device, device_id_type=MESH,
    )


class Cube:
    def __init__(self):
        r = lax.axis_index("replica")
        self.core, self.x, self.y = r % 2, (r // 2) % 2, r // 4
        self.place = 2 * self.y + self.x
        self.to_x = {"replica": r + 2 - 4 * self.x}
        self.to_y = {"replica": r + 4 - 8 * self.y}
        self.to_core = {"replica": r + 1 - 2 * self.core}

    def partners(self, shards):
        z = lax.axis_index("shard")
        return [((z != o), {"shard": o}) for o in range(shards)] + [
            (z >= 0, d) for d in (self.to_x, self.to_y, self.to_core)
        ]


def rows_of(ref, start, unit, count):
    return ref.at[pl.ds(pl.multiple_of(start, unit), count)]


class Spreader:
    def __init__(self, cube, shards, share, parts, source, out, sems):
        self.cube, self.shards, self.share, self.parts = cube, shards, share, parts
        self.source, self.out = source, out
        self.z_send, self.z_recv, self.send, self.recv, self.loc = sems
        self.cut = 16 * ((share // 16 + 1) // 2)
        self.z = lax.axis_index("shard")
        r = lax.axis_index("replica")
        self.who = (r, r + 2 - 4 * cube.x, r + 4 - 8 * cube.y, 4 * (1 - cube.y) + 2 * (1 - cube.x) + cube.core)

    def rows(self, o, kind, half=None):
        first, count = {None: (0, self.share), 0: (0, self.cut), 1: (self.cut, self.share - self.cut)}[half]
        return rows_of(self.out, (o * 8 + self.who[kind]) * self.share + first, 16, count)

    def target(self, o, part):
        width = self.out.shape[1] // self.parts
        return self.rows(o, 0).at[:, pl.ds(part * width, width)]

    def z_copy(self, o, part):
        return remote(self.source(o, part), self.target(self.z, part), self.z_send.at[o, part], self.z_recv.at[self.z, part], {"shard": o})

    def z_arrival(self, o, part):
        place = self.target(o, part)
        return remote(place, place, self.z_send.at[o, part], self.z_recv.at[o, part], {"shard": o})

    def local(self, o, part):
        return pltpu.make_async_copy(self.source(o, part), self.target(o, part), self.loc.at[part])

    def start_own(self):
        for part in range(self.parts):
            self.local(self.z, part).start()

    def start(self):
        for o in range(self.shards):
            for part in range(self.parts):
                @pl.when(self.z != o)
                def _():
                    self.z_copy(o, part).start()

    def sent(self):
        for o in range(self.shards):
            for part in range(self.parts):
                @pl.when(self.z != o)
                def _():
                    self.z_copy(o, part).wait_send()

    def copy(self, kind, o):
        c = self.cube
        block, device = (
            (self.rows(o, 0), c.to_x),
            (self.rows(o, 0), c.to_y),
            (self.rows(o, 1, 0), c.to_y),
            (self.rows(o, 2, 1), c.to_x),
            (self.rows(o, 0), c.to_core),
            (self.rows(o, 1), c.to_core),
            (self.rows(o, 2), c.to_core),
            (self.rows(o, 3), c.to_core),
        )[kind]
        return remote(block, block, self.send.at[kind, o], self.recv.at[kind, o], device)

    def arrive(self, distance):
        for o in range(self.shards):
            @pl.when((self.z - o == distance) | (o - self.z == distance))
            def _():
                for part in range(self.parts):
                    if distance == 0:
                        self.local(o, part).wait()
                    else:
                        self.z_arrival(o, part).wait_recv()
                for kind in (0, 1, 4):
                    self.copy(kind, o).start()

    def pass_on(self, o):
        self.copy(0, o).wait_recv()
        self.copy(2, o).start()
        self.copy(5, o).start()
        self.copy(1, o).wait_recv()
        self.copy(3, o).start()
        self.copy(6, o).start()

    def pass_last(self, o):
        self.copy(2, o).wait_recv()
        self.copy(3, o).wait_recv()
        self.copy(7, o).start()

    def landed(self):
        for o in range(self.shards):
            for kind in (4, 5, 6, 7):
                self.copy(kind, o).wait_recv()

    def finish(self):
        for o in range(self.shards):
            for kind in range(8):
                self.copy(kind, o).wait_send()


def spread_sems(shards, parts):
    dma = pltpu.SemaphoreType.DMA
    return [dma((shards, parts)), dma((shards, parts)), dma((8, shards)), dma((8, shards)), dma((parts,))]


class Line:
    def __init__(self, shards, pieces, own, buf, send, recv):
        self.z = lax.axis_index("shard")
        self.shards, self.pieces, self.own, self.buf, self.send, self.recv = shards, pieces, own, buf, send, recv
        self.rows = buf.shape[1] // pieces

    def copy(self, way, step, piece):
        target = self.z + 1 if way == 0 else self.z - 1
        owner = self.z - step if way == 0 else self.z + step
        block = pl.ds(piece * self.rows, self.rows)
        place = self.buf.at[owner, block]
        source = self.own.at[block] if step == 0 and self.own is not None else place
        return remote(source, place, self.send.at[way, step, piece], self.recv.at[way, step, piece], {"shard": target})

    def sends(self, way, step):
        if way == 0:
            return (self.z + 1 < self.shards) & (self.z - step >= 0)
        return (self.z >= 1) & (self.z + step < self.shards)

    def gets(self, way, step):
        return (self.z - step >= 1) if way == 0 else (self.z + step + 1 < self.shards)

    def start(self, piece):
        for way in (0, 1):
            @pl.when(self.sends(way, 0))
            def _():
                self.copy(way, 0, piece).start()

    def relay(self, step, piece):
        for way in (0, 1):
            @pl.when(self.gets(way, step))
            def _():
                self.copy(way, step, piece).wait_recv()
            if step + 1 < self.shards - 1:
                @pl.when(self.sends(way, step + 1))
                def _():
                    self.copy(way, step + 1, piece).start()

    def finish(self):
        for step in range(self.shards - 1):
            for piece in range(self.pieces):
                for way in (0, 1):
                    @pl.when(self.sends(way, step))
                    def _():
                        self.copy(way, step, piece).wait_send()


def line_sems(shards, pieces):
    dma = pltpu.SemaphoreType.DMA
    return [dma((2, shards - 1, pieces)), dma((2, shards - 1, pieces))]


def layer_norm_rows(values, gain, shift):
    centered = values - jnp.mean(values, axis=-1, keepdims=True)
    spread = jnp.mean(centered * centered, axis=-1, keepdims=True)
    return (centered * lax.rsqrt(spread + norm_eps) * gain + shift).astype(jnp.bfloat16)


def vector_row(vectors, i):
    return jnp.concatenate([vectors[o, i : i + 1, :] for o in range(vectors.shape[0])], axis=1)


def bias_piece(v_buf, z, t, tile, shards, per_part):
    flat = (t // per_part) * shards + z
    return v_buf[flat // 3, pl.ds(flat % 3, 1), pl.ds(aligned(t % per_part, tile), tile)]


def start_kernel(shards, tokens, vectors, weight, out_weight, cosine, minus, plus,
                 all_tokens, all_vectors, normed, qkv, kept_weight, all_out,
                 x_buf, v_buf, w_buf, n_buf, q_buf, *sems):
    cube = Cube()
    z = lax.axis_index("shard")
    r = lax.axis_index("replica")
    rows = tokens.shape[0]
    share = weight.shape[0] // 8
    width = w_buf.shape[1] // 3
    x_send, x_recv, v_send, v_recv, loc = sems[:5]
    line = Line(shards, 1, tokens, x_buf, x_send, x_recv)
    mine = pl.ds(aligned(r, share), share)
    spread = Spreader(
        cube, shards, share, 3,
        lambda o, part: weight.at[mine, pl.ds(aligned(part * shards + o, width), width)], w_buf, sems[5:10],
    )
    spread_out = Spreader(cube, shards, share, 1, lambda o, part: out_weight.at[mine], all_out, sems[10:15])
    greet(cube.partners(shards), shards + 2)

    def v_copy(o):
        return remote(vectors, v_buf.at[z], v_send.at[o], v_recv.at[z], {"shard": o})

    def v_arrival(o):
        return remote(vectors, v_buf.at[o], v_send.at[o], v_recv.at[o], {"shard": o})

    own_x = pltpu.make_async_copy(tokens, x_buf.at[z], loc.at[0, 0])
    own_v = pltpu.make_async_copy(vectors, v_buf.at[z], loc.at[1, 0])
    own_x.start()
    own_v.start()
    for o in range(shards):
        @pl.when(z != o)
        def _():
            v_copy(o).start()
    spread.start_own()
    spread_out.start_own()
    spread.start()
    spread.arrive(0)
    spread_out.arrive(0)
    line.start(0)
    spread_out.start()
    for distance in range(1, shards):
        spread.arrive(distance)
    own_x.wait()
    own_v.wait()
    for o in range(shards):
        @pl.when(z != o)
        def _():
            v_arrival(o).wait_recv()
    keep_v = pltpu.make_async_copy(v_buf, all_vectors, loc.at[2, 0])
    keep_v.start()
    gain, shift = vector_row(v_buf, 3), vector_row(v_buf, 4)

    def put(source, target, o, i):
        block = pl.ds(aligned(o, rows), rows)
        copy = pltpu.make_async_copy(source.at[block], target.at[block], loc.at[4 + i, o])
        copy.start()

    def normalize(o):
        @pl.loop(0, rows // 32)
        def _(i):
            values = x_buf[o, pl.ds(aligned(i, 32), 32), :].astype(jnp.float32)
            n_buf[pl.ds(pl.multiple_of(o * rows + i * 32, 32), 32), :] = layer_norm_rows(values, gain, shift)
        put(n_buf, normed, o, 0)
        pltpu.make_async_copy(x_buf.at[o], all_tokens.at[o], loc.at[6, o]).start()

    tile = 256
    per_part = width // tile

    def project(o):
        block = pl.ds(aligned(o, rows), rows)

        @pl.loop(0, 3 * per_part)
        def _(t):
            columns = pl.ds(aligned(t, tile), tile)
            value = jnp.dot(n_buf[block, :], w_buf[:, columns], preferred_element_type=jnp.float32)
            value = value + bias_piece(v_buf, z, t, tile, shards, per_part)

            @pl.when(t < 2 * per_part)
            def _():
                wide, wide_minus, wide_plus = (
                    jnp.concatenate([table[block, :]] * (tile // 128), axis=1) for table in (cosine, minus, plus)
                )
                turned = value * wide + pltpu.roll(value, tile - 8, 1) * wide_minus + pltpu.roll(value, 8, 1) * wide_plus
                q_buf[block, columns] = turned.astype(jnp.bfloat16)

            @pl.when(t >= 2 * per_part)
            def _():
                q_buf[block, columns] = value.astype(jnp.bfloat16)
        put(q_buf, qkv, o, 1)

    normalize(z)
    line.relay(0, 0)
    for o in range(shards):
        spread.pass_on(o)
    for o in range(shards):
        spread.pass_last(o)
    spread.landed()
    keep_w = pltpu.make_async_copy(w_buf, kept_weight, loc.at[3, 0])
    keep_w.start()
    project(z)
    for distance in range(1, shards):
        spread_out.arrive(distance)
    for step in range(shards - 1):
        if step > 0:
            line.relay(step, 0)
        if step == min(1, shards - 2):
            for o in range(shards):
                spread_out.pass_on(o)
        if step == shards - 2:
            for o in range(shards):
                spread_out.pass_last(o)
        for way in (0, 1):
            owner = z - step - 1 if way == 0 else z + step + 1

            @pl.when(line.gets(way, step))
            def _():
                normalize(owner)
                project(owner)
    spread_out.landed()
    line.finish()
    spread.sent()
    spread.finish()
    spread_out.sent()
    spread_out.finish()
    for o in range(shards):
        block = pl.ds(o * rows, rows)

        @pl.when(z != o)
        def _():
            v_copy(o).wait_send()
        pltpu.make_async_copy(n_buf.at[block], normed.at[block], loc.at[4, o]).wait()
        pltpu.make_async_copy(q_buf.at[block], qkv.at[block], loc.at[5, o]).wait()
        pltpu.make_async_copy(x_buf.at[o], all_tokens.at[o], loc.at[6, o]).wait()
    keep_v.wait()
    keep_w.wait()


def start_call(shards, tokens, vectors, weight, out_weight, cosine, minus, plus):
    rows = tokens.shape[0]
    group = rows * shards
    depth = weight.shape[0]
    width = weight.shape[1] // shards
    any_ = pl.BlockSpec(memory_space=pl.ANY)
    vm = pl.BlockSpec(memory_space=pltpu.VMEM)
    low = jnp.bfloat16
    dma = pltpu.SemaphoreType.DMA
    return pl.pallas_call(
        functools.partial(start_kernel, shards),
        out_shape=[
            jax.ShapeDtypeStruct((shards, rows, D), low),
            jax.ShapeDtypeStruct((shards,) + vectors.shape, vectors.dtype),
            jax.ShapeDtypeStruct((group, D), low),
            jax.ShapeDtypeStruct((group, width), low),
            jax.ShapeDtypeStruct((depth * shards, width), low),
            jax.ShapeDtypeStruct((depth * shards, D), low),
        ],
        in_specs=[any_] * 4 + [vm] * 3,
        out_specs=[any_] * 6,
        scratch_shapes=[
            pltpu.VMEM((shards, rows, D), low),
            pltpu.VMEM((shards,) + vectors.shape, vectors.dtype),
            pltpu.VMEM((depth * shards, width), low),
            pltpu.VMEM((group, D), low),
            pltpu.VMEM((group, width), low),
        ] + line_sems(shards, 1) + [dma((shards,)), dma((shards,)), dma((7, shards))]
        + spread_sems(shards, 3) + spread_sems(shards, 1),
        compiler_params=pltpu.CompilerParams(
            collective_id=1, has_side_effects=True, vmem_limit_bytes=62 * 2**20
        ),
        name="start",
        cost_estimate=pl.CostEstimate(flops=2 * group * D * width, bytes_accessed=150 * 10**6, transcendentals=0),
    )(tokens, vectors, weight, out_weight, cosine, minus, plus)


def attend_spread_kernel(shards, rows, qkv, seg_rows, seg_columns, gate_up, attended, stats, all_gate_up, a_buf, *sems):
    cube = Cube()
    z = lax.axis_index("shard")
    r = lax.axis_index("replica")
    width = qkv.shape[1] // 3
    blocks = qkv.shape[0] // rows
    share = gate_up.shape[0] // 8
    half = all_gate_up.shape[1] // 2
    mine = pl.ds(aligned(r, share), share)
    spread = Spreader(
        cube, shards, share, 2,
        lambda o, part: gate_up.at[mine, pl.ds(aligned((part * shards + o) * (half // 128), 128), half)], all_gate_up, sems[3:8],
    )
    line = Line(shards, blocks, None, a_buf, sems[0], sems[1])
    loc = sems[2]
    greet(cube.partners(shards), shards + 2)
    spread.start_own()
    spread.start()
    spread.arrive(0)

    def done(block):
        line.start(block)
        if 0 < block < shards:
            spread.arrive(block)

    attend_body(rows, qkv, seg_rows, seg_columns, a_buf, stats, done)
    moves = [functools.partial(line.relay, step, block) for step in range(shards - 1) for block in range(blocks)]
    steps = [functools.partial(spread.pass_on, o) for o in range(shards)]
    steps += [functools.partial(spread.pass_last, o) for o in range(shards)]
    for i in range(max(len(moves), len(steps))):
        if i < len(moves):
            moves[i]()
        if i < len(steps):
            steps[i]()
    keep = [pltpu.make_async_copy(a_buf.at[o], attended.at[:, pl.ds(o * width, width)], loc.at[o]) for o in range(shards)]
    for copy in keep:
        copy.start()
    spread.landed()
    line.finish()
    spread.sent()
    spread.finish()
    for copy in keep:
        copy.wait()


def attend_spread_call(shards, rows, qkv, seg_rows, seg_columns, gate_up):
    group = qkv.shape[0]
    width = qkv.shape[1] // 3
    blocks = group // rows
    vm = pl.BlockSpec(memory_space=pltpu.VMEM)
    any_ = pl.BlockSpec(memory_space=pl.ANY)
    dma = pltpu.SemaphoreType.DMA
    low = jnp.bfloat16
    return pl.pallas_call(
        functools.partial(attend_spread_kernel, shards, rows),
        out_shape=[
            jax.ShapeDtypeStruct((group, shards * width), low),
            jax.ShapeDtypeStruct((group, 128), jnp.float32),
            jax.ShapeDtypeStruct((gate_up.shape[0] * shards, gate_up.shape[1] // shards), low),
        ],
        in_specs=[vm, vm, vm, any_],
        out_specs=[any_, vm, any_],
        scratch_shapes=[pltpu.VMEM((shards, group, width), low)] + line_sems(shards, blocks) + [dma((shards,))]
        + spread_sems(shards, 2),
        compiler_params=pltpu.CompilerParams(
            collective_id=2, has_side_effects=True, vmem_limit_bytes=48 * 2**20
        ),
        name="attend_spread",
        cost_estimate=pl.CostEstimate(flops=10**9, bytes_accessed=150 * 10**6, transcendentals=0),
    )(qkv, seg_rows, seg_columns, gate_up)


def hidden_kernel(shards, attended, tokens, out_weight, gate_up_weight, down_weight, cotangent, vectors,
                  middle_own, normed_two, hidden, slopes, all_cotangent, down_part,
                  a_buf, x_buf, o_buf, g_buf, d_buf, c_buf, mid, n_buf, gu, h_buf, s_buf, c_send, c_recv, loc):
    z = lax.axis_index("shard")
    greet_line(z, shards)
    rows = cotangent.shape[0]
    group = rows * shards
    inner = h_buf.shape[1]
    gain, shift = vector_row(vectors, 5), vector_row(vectors, 6)
    line = Line(shards, 1, cotangent, c_buf, c_send, c_recv)
    line.start(0)
    load = [pltpu.make_async_copy(source, target, loc.at[i]) for i, (source, target) in enumerate((
        (attended, a_buf), (out_weight, o_buf), (tokens, x_buf), (gate_up_weight, g_buf), (down_weight, d_buf),
        (cotangent, c_buf.at[z])))]
    for copy in load:
        copy.start()
    for copy in load[:3]:
        copy.wait()
    tile = 256
    span = 2 * rows
    for part in range(group // span):
        at = part * span

        @pl.loop(0, D // tile)
        def _(t):
            columns = pl.ds(aligned(t, tile), tile)
            value = jnp.dot(a_buf[at : at + span, :], o_buf[:, columns], preferred_element_type=jnp.float32)
            for k in range(2):
                mid[k * rows : (k + 1) * rows, columns] = (
                    value[k * rows : (k + 1) * rows] + x_buf[2 * part + k, :, columns].astype(jnp.float32)
                )

        @pl.loop(0, span // 32)
        def _(i):
            block = pl.ds(aligned(i, 32), 32)
            n_buf[pl.ds(pl.multiple_of(at + i * 32, 32), 32), :] = layer_norm_rows(mid[block, :], gain, shift)
        for k in range(2):
            @pl.when(z == 2 * part + k)
            def _():
                middle_own[...] = mid[k * rows : (k + 1) * rows, :]
    keep_n = pltpu.make_async_copy(n_buf, normed_two, loc.at[6])
    keep_n.start()
    line.relay(0, 0)
    load[3].wait()

    @pl.loop(0, 2 * inner // tile)
    def _(t):
        columns = pl.ds(aligned(t, tile), tile)
        gu[:, columns] = jnp.dot(n_buf[...], g_buf[:, columns], preferred_element_type=jnp.float32)

    @pl.loop(0, group // 32)
    def _(i):
        block = pl.ds(aligned(i, 32), 32)
        gate = gu[block, :inner]
        h_buf[block, :] = (gate / (1.0 + jnp.exp(-gate)) * gu[block, inner:]).astype(jnp.bfloat16)
    keep_h = pltpu.make_async_copy(h_buf, hidden, loc.at[7])
    keep_h.start()
    if shards > 2:
        line.relay(1, 0)
    load[4].wait()

    @pl.loop(0, D // tile)
    def _(t):
        columns = pl.ds(aligned(t, tile), tile)
        a_buf[:, columns] = jnp.dot(h_buf[...], d_buf[:, columns], preferred_element_type=jnp.float32).astype(jnp.bfloat16)
    keep_p = pltpu.make_async_copy(a_buf, down_part, loc.at[8])
    keep_p.start()
    load[5].wait()

    def back(o):
        mid[:rows, :inner] = contract_last(c_buf[o], d_buf[...])

        @pl.loop(0, rows // 32)
        def _(i):
            value = mid[pl.ds(aligned(i, 32), 32), :inner]
            place = pl.ds(pl.multiple_of(o * rows + i * 32, 32), 32)
            gate = gu[place, :inner]
            up = gu[place, inner:]
            sigmoid = 1.0 / (1.0 + jnp.exp(-gate))
            s_buf[place, :inner] = (value * up * (sigmoid * (1.0 + gate * (1.0 - sigmoid)))).astype(jnp.bfloat16)
            s_buf[place, inner:] = (value * (gate * sigmoid)).astype(jnp.bfloat16)

    back(z)
    for step in range(shards - 1):
        if step >= 2:
            line.relay(step, 0)
        for way in (0, 1):
            owner = z - step - 1 if way == 0 else z + step + 1

            @pl.when(line.gets(way, step))
            def _():
                back(owner)
    keep = [pltpu.make_async_copy(c_buf, all_cotangent, loc.at[9]), pltpu.make_async_copy(s_buf, slopes, loc.at[10])]
    for copy in keep:
        copy.start()
    line.finish()
    for copy in keep + [keep_n, keep_h, keep_p]:
        copy.wait()


def hidden_call(shards, attended, tokens, out_weight, gate_up_weight, down_weight, cotangent, vectors):
    rows = cotangent.shape[0]
    group = rows * shards
    inner = down_weight.shape[0]
    low = jnp.bfloat16
    f32 = jnp.float32
    vm = pl.BlockSpec(memory_space=pltpu.VMEM)
    any_ = pl.BlockSpec(memory_space=pl.ANY)
    return pl.pallas_call(
        functools.partial(hidden_kernel, shards),
        out_shape=[
            jax.ShapeDtypeStruct((rows, D), f32),
            jax.ShapeDtypeStruct((group, D), low),
            jax.ShapeDtypeStruct((group, inner), low),
            jax.ShapeDtypeStruct((group, 2 * inner), low),
            jax.ShapeDtypeStruct((shards, rows, D), low),
            jax.ShapeDtypeStruct((group, D), low),
        ],
        in_specs=[any_] * 6 + [vm],
        out_specs=[vm] + [any_] * 5,
        scratch_shapes=[
            pltpu.VMEM((group, D), low),
            pltpu.VMEM((shards, rows, D), low),
            pltpu.VMEM(out_weight.shape, low),
            pltpu.VMEM(gate_up_weight.shape, low),
            pltpu.VMEM(down_weight.shape, low),
            pltpu.VMEM((shards, rows, D), low),
            pltpu.VMEM((2 * rows, D), f32),
            pltpu.VMEM((group, D), low),
            pltpu.VMEM((group, 2 * inner), f32),
            pltpu.VMEM((group, inner), low),
            pltpu.VMEM((group, 2 * inner), low),
        ] + line_sems(shards, 1) + [pltpu.SemaphoreType.DMA((11,))],
        compiler_params=pltpu.CompilerParams(
            collective_id=9, has_side_effects=True, vmem_limit_bytes=63 * 2**20
        ),
        name="hidden",
        cost_estimate=pl.CostEstimate(flops=24 * 10**9, bytes_accessed=150 * 10**6, transcendentals=0),
    )(attended, tokens, out_weight, gate_up_weight, down_weight, cotangent, vectors)


def head_mask(even, rows):
    lane = lax.broadcasted_iota(jnp.int32, (rows, 128), 1)
    return (lane < HEAD_DIM) if even else (lane >= HEAD_DIM)


def only(values, keep):
    return jnp.where(keep, values.astype(jnp.float32), 0.0).astype(jnp.bfloat16)


def block_visible(at, rows, seg_rows, seg_columns):
    count = at + rows
    row = lax.broadcasted_iota(jnp.int32, (rows, count), 0) + at
    column = lax.broadcasted_iota(jnp.int32, (rows, count), 1)
    return (column <= row) & (seg_rows[at : at + rows, :1] == seg_columns[:1, :count])


def attend_body(rows, qkv, seg_rows, seg_columns, a_buf, stats, done):
    z = lax.axis_index("shard")
    width = qkv.shape[1] // 3
    pairs = width // 128
    scale = HEAD_DIM ** (-0.5)
    for block in range(qkv.shape[0] // rows):
        at = block * rows
        count = at + rows
        seen = block_visible(at, rows, seg_rows, seg_columns)
        for pair in range(pairs):
            lanes = slice(128 * pair, 128 * pair + 128)
            query = qkv[at:count, lanes]
            keys = qkv[:count, width + 128 * pair : width + 128 * pair + 128]
            values = qkv[:count, 2 * width + 128 * pair : 2 * width + 128 * pair + 128]
            results = []
            for odd in (0, 1):
                keep = head_mask(odd == 0, rows)
                scores = contract_last(only(query, keep), keys) * scale
                scores = jnp.where(seen, scores, masked_score)
                top = jnp.max(scores, axis=-1, keepdims=True)
                weights = jnp.exp(scores - top)
                total = jnp.sum(weights, axis=-1, keepdims=True)
                probs = (weights * (1.0 / total)).astype(jnp.bfloat16)
                results.append(jnp.dot(probs, values, preferred_element_type=jnp.float32))
                head = 2 * pair + odd
                stats[at:count, head : head + 1] = top
                stats[at:count, 64 + head : 65 + head] = 1.0 / total
            merged = jnp.where(head_mask(True, rows), results[0], results[1])
            a_buf[z, at:count, lanes] = merged.astype(jnp.bfloat16)
        done(block)


def attend_kernel(shards, rows, qkv, seg_rows, seg_columns, attended, stats, a_buf, a_send, a_recv, loc):
    z = lax.axis_index("shard")
    width = qkv.shape[1] // 3
    blocks = qkv.shape[0] // rows
    greet_line(z, shards)
    line = Line(shards, blocks, None, a_buf, a_send, a_recv)
    attend_body(rows, qkv, seg_rows, seg_columns, a_buf, stats, line.start)
    for step in range(shards - 1):
        for block in range(blocks):
            line.relay(step, block)
    keep = [pltpu.make_async_copy(a_buf.at[o], attended.at[:, pl.ds(o * width, width)], loc.at[o]) for o in range(shards)]
    for copy in keep:
        copy.start()
    line.finish()
    for copy in keep:
        copy.wait()


def attend_call(shards, rows, qkv, seg_rows, seg_columns):
    group = qkv.shape[0]
    width = qkv.shape[1] // 3
    blocks = group // rows
    vm = pl.BlockSpec(memory_space=pltpu.VMEM)
    any_ = pl.BlockSpec(memory_space=pl.ANY)
    dma = pltpu.SemaphoreType.DMA
    return pl.pallas_call(
        functools.partial(attend_kernel, shards, rows),
        out_shape=[
            jax.ShapeDtypeStruct((group, shards * width), jnp.bfloat16),
            jax.ShapeDtypeStruct((group, 128), jnp.float32),
        ],
        in_specs=[vm, vm, vm],
        out_specs=[any_, vm],
        scratch_shapes=[
            pltpu.VMEM((shards, group, width), jnp.bfloat16),
            dma((2, shards - 1, blocks)), dma((2, shards - 1, blocks)), dma((shards,)),
        ],
        compiler_params=pltpu.CompilerParams(
            collective_id=2, has_side_effects=True, vmem_limit_bytes=48 * 2**20
        ),
        name="attend",
        cost_estimate=pl.CostEstimate(flops=10**9, bytes_accessed=150 * 10**6, transcendentals=0),
    )(qkv, seg_rows, seg_columns)


def attend_back_kernel(rows, *refs):
    attend_back_body(rows, *refs, [])


def attend_back_body(rows, qkv, d_attended, stats, seg_rows, seg_columns, cosine, minus, plus,
                     d_qkv, bias_grad, d_keys, d_values, steps):
    width = qkv.shape[1] // 3
    group = qkv.shape[0]
    blocks = group // rows
    pairs = width // 128
    scale = HEAD_DIM ** (-0.5)

    def turned(value, at, count):
        return (value * cosine[at:count, :] - pltpu.roll(value, 120, 1) * minus[at:count, :]
                - pltpu.roll(value, 8, 1) * plus[at:count, :])

    for block in reversed(range(blocks)):
        at = block * rows
        count = at + rows
        seen = block_visible(at, rows, seg_rows, seg_columns)
        for pair in range(pairs):
            lanes = slice(128 * pair, 128 * pair + 128)
            query = qkv[at:count, lanes]
            keys = qkv[:count, width + 128 * pair : width + 128 * pair + 128]
            values = qkv[:count, 2 * width + 128 * pair : 2 * width + 128 * pair + 128]
            slope = d_attended[at:count, lanes]
            d_query, d_key, d_value = [], [], []
            for odd in (0, 1):
                keep = head_mask(odd == 0, rows)
                head = 2 * pair + odd
                own_query = only(query, keep)
                own_slope = only(slope, keep)
                scores = contract_last(own_query, keys) * scale
                scores = jnp.where(seen, scores, masked_score)
                probs = jnp.exp(scores - stats[at:count, head : head + 1]) * stats[at:count, 64 + head : 65 + head]
                d_probs = contract_last(own_slope, values)
                inner = jnp.sum(probs * d_probs, axis=-1, keepdims=True)
                d_scores = (probs * (d_probs - inner)).astype(jnp.bfloat16)
                d_query.append(jnp.dot(d_scores, keys, preferred_element_type=jnp.float32))
                d_key.append(contract_first(d_scores, own_query))
                d_value.append(contract_first(probs.astype(jnp.bfloat16), own_slope))
            keep = head_mask(True, rows)
            d_q = jnp.where(keep, d_query[0], d_query[1]) * scale
            d_q = turned(d_q, at, count).astype(jnp.bfloat16)
            d_qkv[at:count, lanes] = d_q
            d_k = (d_key[0] + d_key[1]) * scale
            d_v = d_value[0] + d_value[1]
            if block == blocks - 1:
                d_keys[:, lanes] = d_k
                d_values[:, lanes] = d_v
            else:
                d_keys[:count, lanes] += d_k
                d_values[:count, lanes] += d_v
            k_out = turned(d_keys[at:count, lanes], at, count).astype(jnp.bfloat16)
            d_qkv[at:count, width + 128 * pair : width + 128 * pair + 128] = k_out
            v_out = d_values[at:count, lanes].astype(jnp.bfloat16)
            d_qkv[at:count, 2 * width + 128 * pair : 2 * width + 128 * pair + 128] = v_out
            if steps:
                steps.pop(0)()
    for part in range(3 * pairs):
        lanes = slice(128 * part, 128 * part + 128)
        bias_grad[:, lanes] = jnp.broadcast_to(
            jnp.sum(d_qkv[:, lanes].astype(jnp.float32), axis=0, keepdims=True), (8, 128))


def contract_first(left, right):
    return lax.dot_general(
        left, right, (((0,), (0,)), ((), ())), preferred_element_type=jnp.float32
    )


def attend_back_call(rows, qkv, d_attended, stats, seg_rows, seg_columns, cosine, minus, plus):
    group = qkv.shape[0]
    width = qkv.shape[1] // 3
    vm = pl.BlockSpec(memory_space=pltpu.VMEM)
    return pl.pallas_call(
        functools.partial(attend_back_kernel, rows),
        out_shape=[
            jax.ShapeDtypeStruct((group, 3 * width), jnp.bfloat16),
            jax.ShapeDtypeStruct((8, 3 * width), jnp.float32),
        ],
        in_specs=[vm] * 8,
        out_specs=[vm, vm],
        scratch_shapes=[pltpu.VMEM((group, width), jnp.float32), pltpu.VMEM((group, width), jnp.float32)],
        compiler_params=pltpu.CompilerParams(vmem_limit_bytes=48 * 2**20),
        name="attend_back",
        cost_estimate=pl.CostEstimate(flops=3 * 10**9, bytes_accessed=100 * 10**6, transcendentals=0),
    )(qkv, d_attended, stats, seg_rows, seg_columns, cosine, minus, plus)


def scatter_kernel(shards, cuts, parts, total, own, got, load, send, recv):
    z = lax.axis_index("shard")
    rows = parts.shape[1]
    step_rows = rows // cuts
    greet_line(z, shards)

    def piece(cut):
        return pl.ds(cut * step_rows, step_rows)

    def moved(way, block, cut):
        target = z + 1 if way == 0 else z - 1
        place = got.at[way, block, piece(cut)]
        return remote(place, place, send.at[way, block, cut], recv.at[way, block, cut], {"shard": target})

    loads = [pltpu.make_async_copy(parts.at[j], own.at[j], load.at[j]) for j in range(shards)]
    for copy in loads:
        copy.start()
    for copy in loads:
        copy.wait()
    for far in range(shards - 1):
        for cut in range(cuts):
            for way in (0, 1):
                block = shards - 1 - far if way == 0 else far
                sends = z < block if way == 0 else z > block
                first = z == 0 if way == 0 else z == shards - 1

                @pl.when(sends)
                def _():
                    @pl.when(first)
                    def _():
                        got[way, block, piece(cut)] = own[block, piece(cut)]

                    @pl.when(jnp.logical_not(first))
                    def _():
                        moved(way, block, cut).wait_recv()
                        got[way, block, piece(cut)] = (
                            got[way, block, piece(cut)].astype(jnp.float32)
                            + own[block, piece(cut)].astype(jnp.float32)
                        ).astype(got.dtype)
                    moved(way, block, cut).start()
    total[...] = own[z].astype(jnp.float32)
    for way in (0, 1):
        @pl.when(z >= 1 if way == 0 else z + 1 < shards)
        def _():
            for cut in range(cuts):
                moved(way, z, cut).wait_recv()
            total[...] += got[way, z].astype(jnp.float32)
    for far in range(shards - 1):
        for cut in range(cuts):
            for way in (0, 1):
                block = shards - 1 - far if way == 0 else far

                @pl.when(z < block if way == 0 else z > block)
                def _():
                    moved(way, block, cut).wait_send()


def scatter_call(shards, parts, number):
    _, rows, columns = parts.shape
    cuts = 3
    dma = pltpu.SemaphoreType.DMA
    return pl.pallas_call(
        functools.partial(scatter_kernel, shards, cuts),
        out_shape=jax.ShapeDtypeStruct((rows, columns), jnp.float32),
        in_specs=[pl.BlockSpec(memory_space=pl.ANY)],
        out_specs=pl.BlockSpec(memory_space=pltpu.VMEM),
        scratch_shapes=[
            pltpu.VMEM(parts.shape, parts.dtype),
            pltpu.VMEM((2,) + parts.shape, parts.dtype),
            dma((shards,)), dma((2, shards, cuts)), dma((2, shards, cuts)),
        ],
        compiler_params=pltpu.CompilerParams(
            collective_id=number, has_side_effects=True, vmem_limit_bytes=32 * 2**20
        ),
        name="scatter",
        cost_estimate=pl.CostEstimate(flops=0, bytes_accessed=200 * 10**6, transcendentals=0),
    )(parts)


def exchange_kernel(shards, first, second, first_out, second_out, send, recv, loc):
    z = lax.axis_index("shard")
    width = first.shape[1] // shards
    greet([((z != o), {"shard": o}) for o in range(shards)], shards - 1)
    arrays = ((first, first_out), (second, second_out))

    def move(k, o):
        source, target = arrays[k]
        return remote(source.at[:, pl.ds(o * width, width)], target.at[z], send.at[k, o], recv.at[k, z], {"shard": o})

    def arrival(k, o):
        source, target = arrays[k]
        return remote(target.at[o], target.at[o], send.at[k, o], recv.at[k, o], {"shard": o})

    for k in (0, 1):
        for o in range(shards):
            @pl.when(z != o)
            def _():
                move(k, o).start()

            @pl.when(z == o)
            def _():
                source, target = arrays[k]
                pltpu.make_async_copy(source.at[:, pl.ds(o * width, width)], target.at[o], loc.at[k]).start()
    for k in (0, 1):
        for o in range(shards):
            @pl.when(z != o)
            def _():
                arrival(k, o).wait_recv()
                move(k, o).wait_send()

            @pl.when(z == o)
            def _():
                source, target = arrays[k]
                pltpu.make_async_copy(source.at[:, pl.ds(o * width, width)], target.at[o], loc.at[k]).wait()


def exchange_call(shards, first, second):
    rows, columns = first.shape
    shape = jax.ShapeDtypeStruct((shards, rows, columns // shards), first.dtype)
    any_ = pl.BlockSpec(memory_space=pl.ANY)
    dma = pltpu.SemaphoreType.DMA
    return pl.pallas_call(
        functools.partial(exchange_kernel, shards),
        out_shape=[shape, shape],
        in_specs=[any_, any_],
        out_specs=[any_, any_],
        scratch_shapes=[dma((2, shards)), dma((2, shards)), dma((2,))],
        compiler_params=pltpu.CompilerParams(collective_id=5, has_side_effects=True),
        name="exchange",
        cost_estimate=pl.CostEstimate(flops=0, bytes_accessed=100 * 10**6, transcendentals=0),
    )(first, second)


def add_rows(target, source, count):
    step = 16

    @pl.loop(0, count // step)
    def _(i):
        block = pl.ds(aligned(i, step), step)
        target[block, :] = (
            target[block, :].astype(jnp.float32) + source[block, :].astype(jnp.float32)
        ).astype(target.dtype)


class Reducer:
    def __init__(self, cube, share, term, core, near, last, send, recv):
        self.cube, self.share = cube, share
        self.cut = 16 * ((share // 16 + 1) // 2)
        self.term, self.core, self.near, self.last = term, core, near, last
        self.send, self.recv = send, recv
        self.chunks = term.shape[0]

    def share_rows(self, chunk, place, half):
        first, count = (0, self.cut) if half == 0 else (self.cut, self.share - self.cut)
        start = self.cube.core * 4 * self.share + place * self.share + first
        return rows_of(self.term.at[chunk], start, 16, count)

    def own(self, chunk):
        start = (self.cube.core * 4 + self.cube.place) * self.share
        return rows_of(self.term.at[chunk], start, 16, self.share)

    def core_copy(self, chunk):
        source = rows_of(self.term.at[chunk], (1 - self.cube.core) * 4 * self.share, 16, 4 * self.share)
        return remote(source, self.core.at[chunk], self.send.at[chunk, 0], self.recv.at[chunk, 0], self.cube.to_core)

    def near_place(self, half, other):
        c = self.cube
        if half == 0:
            return 2 * other + (1 - c.x), 2 * other + c.x
        return 2 * (1 - c.y) + other, 2 * c.y + other

    def near_slot(self, chunk, half, other):
        count = self.cut if half == 0 else self.share - self.cut
        start = other * count + (2 * self.cut if half == 1 else 0)
        return self.near.at[chunk, pl.ds(start, count)]

    def near_copy(self, chunk, half, other):
        source = self.share_rows(chunk, self.near_place(half, other)[0], half)
        slot = 1 + 2 * half + other
        device = self.cube.to_x if half == 0 else self.cube.to_y
        return remote(source, self.near_slot(chunk, half, other), self.send.at[chunk, slot], self.recv.at[chunk, slot], device)

    def last_slot(self, chunk, half):
        first, count = (0, self.cut) if half == 0 else (self.cut, self.share - self.cut)
        return self.last.at[chunk, pl.ds(first, count)]

    def last_copy(self, chunk, half):
        c = self.cube
        place = 2 * (1 - c.y) + c.x if half == 0 else 2 * c.y + (1 - c.x)
        device = c.to_y if half == 0 else c.to_x
        source = self.share_rows(chunk, place, half)
        return remote(source, self.last_slot(chunk, half), self.send.at[chunk, 5 + half], self.recv.at[chunk, 5 + half], device)

    def start(self, chunk):
        self.core_copy(chunk).start()

    def after_core(self, chunk):
        self.core_copy(chunk).wait_recv()
        mine = rows_of(self.term.at[chunk], self.cube.core * 4 * self.share, 16, 4 * self.share)
        add_rows(mine, self.core.at[chunk], 4 * self.share)
        for half in (0, 1):
            for other in (0, 1):
                self.near_copy(chunk, half, other).start()

    def after_near(self, chunk):
        for half in (0, 1):
            count = self.cut if half == 0 else self.share - self.cut
            for other in (0, 1):
                self.near_copy(chunk, half, other).wait_recv()
                stays = self.share_rows(chunk, self.near_place(half, other)[1], half)
                add_rows(stays, self.near_slot(chunk, half, other), count)
            self.last_copy(chunk, half).start()

    def after_last(self, chunk):
        c = self.cube
        for half in (0, 1):
            count = self.cut if half == 0 else self.share - self.cut
            self.last_copy(chunk, half).wait_recv()
            add_rows(self.share_rows(chunk, c.place, half), self.last_slot(chunk, half), count)

    def finish(self, chunk):
        self.core_copy(chunk).wait_send()
        for half in (0, 1):
            for other in (0, 1):
                self.near_copy(chunk, half, other).wait_send()
            self.last_copy(chunk, half).wait_send()


class Owners:
    def __init__(self, shards, parts, source, out, send, recv, loc):
        self.shards, self.parts, self.source, self.out = shards, parts, source, out
        self.send, self.recv, self.loc = send, recv, loc
        self.z = lax.axis_index("shard")
        self.width = out.shape[1] // (shards * parts)

    def target(self, shard, part):
        return self.out.at[:, pl.ds(aligned((part * self.shards + shard) * (self.width // 128), 128), self.width)]

    def piece(self, o, part):
        return self.source(o).at[:, pl.ds(part * self.width, self.width)]

    def copy(self, o, part):
        return remote(self.piece(o, part), self.target(self.z, part), self.send.at[o, part], self.recv.at[self.z, part], {"shard": o})

    def arrival(self, o, part):
        place = self.target(o, part)
        return remote(place, place, self.send.at[o, part], self.recv.at[o, part], {"shard": o})

    def local(self, o, part):
        return pltpu.make_async_copy(self.piece(o, part), self.target(o, part), self.loc.at[part])

    def start(self, k):
        o = lax.rem(self.z + k, self.shards)
        for part in range(self.parts):
            if k == 0:
                self.local(o, part).start()
            else:
                self.copy(o, part).start()

    def arrive_from(self, k):
        o = lax.rem(self.z + k, self.shards)
        for part in range(self.parts):
            if k == 0:
                self.local(o, part).wait()
            else:
                self.arrival(o, part).wait_recv()

    def arrive(self):
        for k in range(self.shards):
            self.arrive_from(k)

    def finish(self):
        for k in range(1, self.shards):
            o = lax.rem(self.z + k, self.shards)
            for part in range(self.parts):
                self.copy(o, part).wait_send()


def owner_sems(shards, parts):
    dma = pltpu.SemaphoreType.DMA
    return [dma((shards, parts)), dma((shards, parts)), dma((parts,))]


class Gatherer:
    def __init__(self, cube, share, out, sems):
        self.cube, self.share, self.out = cube, share, out
        self.send, self.recv, self.loc = sems
        self.count = share.shape[0]
        self.cut = 16 * ((self.count // 16 + 1) // 2)

    def rows(self, place, half=None):
        first, count = {None: (0, self.count), 0: (0, self.cut), 1: (self.cut, self.count - self.cut)}[half]
        return rows_of(self.out, (self.cube.core * 4 + place) * self.count + first, 16, count)

    def copy(self, kind):
        c = self.cube
        at_x, at_y = 2 * c.y + 1 - c.x, 2 * (1 - c.y) + c.x
        block, device = (
            (self.rows(c.place), c.to_x),
            (self.rows(c.place), c.to_y),
            (self.rows(at_x, 0), c.to_y),
            (self.rows(at_y, 1), c.to_x),
            (self.rows(c.place), c.to_core),
            (self.rows(at_x), c.to_core),
            (self.rows(at_y), c.to_core),
            (self.rows(3 - c.place), c.to_core),
        )[kind]
        source = self.share if kind in (0, 1, 4) else block
        return remote(source, block, self.send.at[kind], self.recv.at[kind], device)

    def local(self):
        return pltpu.make_async_copy(self.share, self.rows(self.cube.place), self.loc.at[0])

    def start(self):
        for kind in (0, 1, 4):
            self.copy(kind).start()
        self.local().start()

    def pass_on(self):
        self.copy(0).wait_recv()
        self.copy(2).start()
        self.copy(5).start()
        self.copy(1).wait_recv()
        self.copy(3).start()
        self.copy(6).start()

    def pass_last(self):
        self.copy(2).wait_recv()
        self.copy(3).wait_recv()
        self.copy(7).start()

    def finish(self):
        for kind in (4, 5, 6, 7):
            self.copy(kind).wait_recv()
        for kind in range(8):
            self.copy(kind).wait_send()
        self.local().wait()


def gatherer_sems():
    dma = pltpu.SemaphoreType.DMA
    return [dma((8,)), dma((8,)), dma((1,))]


class LineSum:
    def __init__(self, shards, cuts, own, got, send, recv):
        self.z = lax.axis_index("shard")
        self.shards, self.cuts, self.own, self.got, self.send, self.recv = shards, cuts, own, got, send, recv
        self.step = own.shape[1] // cuts

    def piece(self, cut):
        return pl.ds(cut * self.step, self.step)

    def copy(self, way, block, cut, source=None):
        target = self.z + 1 if way == 0 else self.z - 1
        place = self.got.at[way, block, self.piece(cut)]
        return remote(place if source is None else source, place, self.send.at[way, block, cut], self.recv.at[way, block, cut], {"shard": target})

    def pair(self, t):
        half = self.shards // 2
        upper = self.z // half
        return half - 1 - t + upper * (2 * t - half + 1)

    def ready(self, pair):
        for way in (0, 1):
            for i in (0, 1):
                block = 2 * pair + (1 - i if way == 0 else i)

                @pl.when((self.z == (0 if way == 0 else self.shards - 1)) & (block != self.z))
                def _():
                    for cut in range(self.cuts):
                        self.copy(way, block, cut, self.own.at[block, self.piece(cut)]).start()

    def ends(self, i):
        for way in (0, 1):
            block = self.shards - 1 - i if way == 0 else i

            @pl.when(self.z == (0 if way == 0 else self.shards - 1))
            def _():
                for cut in range(self.cuts):
                    self.copy(way, block, cut, self.own.at[block, self.piece(cut)]).start()

    def step_on(self, hop, far, cut):
        for way in (0, 1):
            block = self.shards - 1 - far if way == 0 else far

            @pl.when(self.z == (hop if way == 0 else self.shards - 1 - hop))
            def _():
                self.copy(way, block, cut).wait_recv()
                place = self.got.at[way, block, self.piece(cut)]
                add_rows(place, self.own.at[block, self.piece(cut)], self.step)
                self.copy(way, block, cut).start()

    def steps(self):
        return [
            functools.partial(self.step_on, hop, far, cut)
            for far in range(self.shards - 2)
            for hop in range(1, self.shards - 1 - far)
            for cut in range(self.cuts)
        ]

    def result(self, total):
        rows = self.own.shape[1]
        for way in (0, 1):
            @pl.when(self.z >= 1 if way == 0 else self.z + 1 < self.shards)
            def _():
                for cut in range(self.cuts):
                    self.copy(way, self.z, cut).wait_recv()

        @pl.loop(0, rows // 16)
        def _(i):
            block = pl.ds(aligned(i, 16), 16)
            total[block, :] = self.own[self.z, block, :].astype(jnp.float32)

            @pl.when(self.z >= 1)
            def _():
                total[block, :] += self.got[0, self.z, block, :].astype(jnp.float32)

            @pl.when(self.z + 1 < self.shards)
            def _():
                total[block, :] += self.got[1, self.z, block, :].astype(jnp.float32)

    def finish(self):
        for far in range(self.shards - 1):
            for cut in range(self.cuts):
                for way in (0, 1):
                    block = self.shards - 1 - far if way == 0 else far

                    @pl.when(self.z < block if way == 0 else self.z > block)
                    def _():
                        self.copy(way, block, cut).wait_send()


def line_scratch(shards, rows, columns, cuts):
    dma = pltpu.SemaphoreType.DMA
    return [
        pltpu.VMEM((shards, rows, columns), jnp.bfloat16),
        pltpu.VMEM((2, shards, rows, columns), jnp.bfloat16),
        dma((2, shards, cuts)), dma((2, shards, cuts)),
    ]


def reducer_scratch(chunks, share, columns):
    dma = pltpu.SemaphoreType.DMA
    return [pltpu.VMEM((chunks, n * share, columns), jnp.bfloat16) for n in (8, 4, 2, 1)] + [
        dma((chunks, 7)), dma((chunks, 7)),
    ]


def pair_product(own, pair, slopes, weight, tile=512):
    rows = own.shape[1]

    @pl.loop(0, own.shape[2] // tile)
    def _(t):
        columns = pl.ds(aligned(t, tile), tile)
        value = contract_last(slopes[pl.ds(aligned(pair, 2 * rows), 2 * rows), :], weight[columns, :])
        own[2 * pair, :, columns] = value[:rows].astype(own.dtype)
        own[2 * pair + 1, :, columns] = value[rows:].astype(own.dtype)


def term_product(term, chunk, left, right):
    term.at[chunk][...] = contract_first(left[...], right[...]).astype(jnp.bfloat16)


def spaced(moves, steps, every):
    moves = list(moves)
    for i, step in enumerate(steps):
        step()
        if i % every == every - 1 and moves:
            moves.pop(0)()
    for move in moves:
        move()


def interleave(moves, steps):
    for i in range(max(len(moves), len(steps))):
        if i < len(moves):
            moves[i]()
        if i < len(steps):
            steps[i]()


def load_all(pairs, loc):
    copies = [pltpu.make_async_copy(source, target, loc.at[i]) for i, (source, target) in enumerate(pairs)]
    for copy in copies:
        copy.start()
    return copies


def further(shards):
    z = lax.axis_index("shard")
    return [(k, lax.rem(z + k, shards)) for k in (*range(1, shards), 0)]


class Chunks:
    def __init__(self, ref, chunks):
        self.ref, self.shape = ref, (chunks, ref.shape[0] // chunks, ref.shape[1])

    @property
    def at(self):
        return self

    def __getitem__(self, chunk):
        return self.ref.at[pl.ds(aligned(chunk, self.shape[1]), self.shape[1])]


def hidden_back_kernel(shards, slopes, weight, hidden, cotangent, normed_two, total, down_share, gate_up_rows,
                       s_buf, w_buf, h_buf, c_buf, n_buf, own, got, z_send, z_recv,
                       term, core, near, last, r_send, r_recv, g_core, g_near, g_last, g_send, g_recv, loc, *sems):
    cube = Cube()
    loads = load_all(((hidden, h_buf), (cotangent, c_buf), (slopes, s_buf), (weight, w_buf), (normed_two, n_buf)), loc)
    greet(cube.partners(shards), shards + 2)
    line = LineSum(shards, 3, own, got, z_send, z_recv)
    share = hidden.shape[1] // 8
    width = D // shards
    chunks, _, columns = term.shape
    g_term = Chunks(w_buf, shards)
    reducer = Reducer(cube, share, term, core, near, last, r_send, r_recv)
    g_reducer = Reducer(cube, width // 8, g_term, g_core, g_near, g_last, g_send, g_recv)
    owners = Owners(shards, 2, g_reducer.own, gate_up_rows, *sems)
    def product(t):
        pair = line.pair(t)
        pair_product(own, pair, s_buf, w_buf)
        line.ready(pair)

    def down_term(k):
        term_product(term, k, h_buf, c_buf.at[:, pl.ds(k * columns, columns)])
        reducer.start(k)

    def gate_up_term(k):
        term_product(g_term, k, n_buf.at[:, pl.ds(aligned(k, width), width)], s_buf)
        g_reducer.start(k)

    keep = []

    def keep_down(k):
        copy = pltpu.make_async_copy(reducer.own(k), down_share.at[:, pl.ds(k * columns, columns)], loc.at[5 + k])
        copy.start()
        keep.append(copy)

    def of(call, count):
        return [functools.partial(call, k) for k in range(count)]

    turn = further(shards)

    def each(call):
        return [functools.partial(call, o) for _, o in turn]

    moves = line.steps()

    def down_ending(k):
        reducer.after_last(k)
        keep_down(k)

    def g_ending(k, o):
        g_reducer.after_last(o)
        owners.start(k)

    cores = of(reducer.after_core, chunks) + each(g_reducer.after_core)
    nears = of(reducer.after_near, chunks) + each(g_reducer.after_near)
    lasts = of(down_ending, chunks) + [functools.partial(g_ending, k, o) for k, o in turn]
    g_terms = each(gate_up_term)
    sequence = [copy.wait for copy in loads[:2]] + of(down_term, chunks) + [copy.wait for copy in loads[2:]]
    sequence += [functools.partial(product, 0)] + cores[:2]
    sequence += [functools.partial(product, t) for t in range(1, shards // 2)] + g_terms[:2] + nears[:1] + cores[2:3] + g_terms[2:] + nears[1:2] + lasts[:1]
    sequence += cores[3:4] + moves[:5]
    for i in range(2, chunks + shards):
        sequence += nears[i : i + 1] + lasts[i - 1 : i] + cores[i + 2 : i + 3] + moves[i + 3 : i + 4]
    sequence += lasts[-1:] + moves[chunks + shards + 3 :]
    for step in sequence:
        step()
    line.result(total)
    line.finish()
    owners.arrive()
    for k in range(chunks):
        reducer.finish(k)
    for k in range(shards):
        g_reducer.finish(k)
    owners.finish()
    for copy in keep:
        copy.wait()


def hidden_back_call(shards, slopes, weight, hidden, cotangent, normed_two):
    group, inner = hidden.shape
    rows = group // shards
    share = inner // 8
    chunks = 4
    width = D // shards
    low = jnp.bfloat16
    any_ = pl.BlockSpec(memory_space=pl.ANY)
    dma = pltpu.SemaphoreType.DMA
    return pl.pallas_call(
        functools.partial(hidden_back_kernel, shards),
        out_shape=[
            jax.ShapeDtypeStruct((rows, D), jnp.float32),
            jax.ShapeDtypeStruct((share, D), low),
            jax.ShapeDtypeStruct((width // 8, shards * 2 * inner), low),
        ],
        in_specs=[any_] * 5,
        out_specs=[pl.BlockSpec(memory_space=pltpu.VMEM), any_, any_],
        scratch_shapes=[pltpu.VMEM(a.shape, low) for a in (slopes, weight, hidden, cotangent, normed_two)]
        + line_scratch(shards, rows, D, 3) + reducer_scratch(chunks, share, D // chunks)
        + reducer_scratch(shards, width // 8, 2 * inner)[1:] + [dma((5 + chunks,))] + owner_sems(shards, 2),
        compiler_params=pltpu.CompilerParams(collective_id=6, has_side_effects=True, vmem_limit_bytes=63 * 2**20),
        name="hidden_back",
        cost_estimate=pl.CostEstimate(flops=10**10, bytes_accessed=200 * 10**6, transcendentals=0),
    )(slopes, weight, hidden, cotangent, normed_two)


def norm_back_rows(slope, values, gain):
    centered = values - jnp.mean(values, axis=-1, keepdims=True)
    inverse = lax.rsqrt(jnp.mean(centered * centered, axis=-1, keepdims=True) + norm_eps)
    unit = centered * inverse
    scaled = slope * gain
    back = inverse * (
        scaled
        - jnp.mean(scaled, axis=-1, keepdims=True)
        - unit * jnp.mean(scaled * unit, axis=-1, keepdims=True)
    )
    return back, unit


def heads_back_kernel(shards, rows, d_normed_two, middle, cotangent, vectors, out_weight, qkv, stats, seg_rows, seg_columns,
                      cosine, minus, plus, down_part, down_share, gate_up_rows,
                      d_middle, norm_grads, d_qkv, bias_grad, mixed, m_columns, down_grad, gate_up_grad,
                      o_buf, m_low, da_own, d_attended, d_keys, d_values, total, own, got, z_send, z_recv, e_send, e_recv, loc, *sems):
    cube = Cube()
    z = lax.axis_index("shard")
    loads = load_all(((out_weight, o_buf), (down_part, own)), loc)
    gain = vector_row(vectors, 5)
    greet(cube.partners(shards), shards + 2)
    width = D // shards
    half = gate_up_rows.shape[1] // 2
    gatherers = [Gatherer(cube, down_share, down_grad, sems[0:3])] + [
        Gatherer(cube, gate_up_rows.at[:, pl.ds(i * half, half)], gate_up_grad.at[:, pl.ds(i * half, half)], sems[3 * i + 3 : 3 * i + 6])
        for i in (0, 1)
    ]
    line = LineSum(shards, 3, own, got, z_send, z_recv)
    gatherers[0].start()
    gatherers[1].start()
    arrays = ((da_own, d_attended), (m_low, m_columns))

    def move(k, o):
        source, target = arrays[k]
        return remote(source.at[:, pl.ds(o * width, width)], target.at[pl.ds(aligned(z, rows), rows)],
                      e_send.at[k, o], e_recv.at[k, z], {"shard": o})

    def arrival(k, o):
        place = arrays[k][1].at[pl.ds(o * rows, rows)]
        return remote(place, place, e_send.at[k, o], e_recv.at[k, o], {"shard": o})

    def here(k, o):
        source, target = arrays[k]
        return pltpu.make_async_copy(source.at[:, pl.ds(o * width, width)], target.at[pl.ds(o * rows, rows)], loc.at[2 + k])

    def begin(k, o):
        @pl.when(z != o)
        def _():
            move(k, o).start()

        @pl.when(z == o)
        def _():
            here(k, o).start()

    def arrive(k):
        for o in range(shards):
            @pl.when(z != o)
            def _():
                arrival(k, o).wait_recv()

            @pl.when(z == o)
            def _():
                here(k, o).wait()

    norm_grads[...] = jnp.zeros_like(norm_grads)

    @pl.loop(0, rows // 16)
    def _(i):
        block = pl.ds(aligned(i, 16), 16)
        slope = d_normed_two[block, :]
        back, unit = norm_back_rows(slope, middle[block, :], gain)
        value = cotangent[block, :].astype(jnp.float32) + back
        d_middle[block, :] = value
        m_low[block, :] = value.astype(jnp.bfloat16)
        norm_grads[0:8, :] += (slope * unit).reshape(2, 8, D).sum(axis=0)
        norm_grads[8:16, :] += slope.reshape(2, 8, D).sum(axis=0)

    loads[0].wait()
    for o in range(shards):
        da_own[:, o * width : (o + 1) * width] = contract_last(
            m_low[...], o_buf[o * width : (o + 1) * width, :]).astype(jnp.bfloat16)
        begin(0, o)
    loads[1].wait()
    for t in range(shards // 2):
        line.ready(line.pair(t))
    for o in range(shards):
        begin(1, o)
    arrive(0)
    gatherers[0].pass_on()

    def nothing():
        pass

    moves = line.steps()
    steps = [nothing, gatherers[1].pass_on, gatherers[2].start, nothing, moves[0], nothing, gatherers[0].pass_last]
    steps += [moves[1], nothing, moves[2], nothing] + [gatherers[1].pass_last] + moves[3:]
    attend_back_body(rows, qkv, d_attended, stats, seg_rows, seg_columns, cosine, minus, plus,
                     d_qkv, bias_grad, d_keys, d_values, steps)
    for step in steps:
        step()
    gatherers[2].pass_on()
    arrive(1)
    gatherers[2].pass_last()
    line.result(total)

    @pl.loop(0, rows // 16)
    def _(i):
        block = pl.ds(aligned(i, 16), 16)
        mixed[block, :] = (middle[block, :] + total[block, :]).astype(mixed.dtype)
    line.finish()
    for k in (0, 1):
        for o in range(shards):
            @pl.when(z != o)
            def _():
                move(k, o).wait_send()
    for gatherer in gatherers:
        gatherer.finish()


def heads_back_call(shards, rows, d_normed_two, middle, cotangent, vectors, out_weight, qkv, stats, seg_rows, seg_columns,
                    cosine, minus, plus, down_part, down_share, gate_up_rows):
    group = qkv.shape[0]
    width = D // shards
    vm = pl.BlockSpec(memory_space=pltpu.VMEM)
    any_ = pl.BlockSpec(memory_space=pl.ANY)
    dma = pltpu.SemaphoreType.DMA
    low = jnp.bfloat16
    f32 = jnp.float32
    return pl.pallas_call(
        functools.partial(heads_back_kernel, shards, rows),
        out_shape=[
            jax.ShapeDtypeStruct((rows, D), f32),
            jax.ShapeDtypeStruct((16, D), f32),
            jax.ShapeDtypeStruct((group, 3 * width), low),
            jax.ShapeDtypeStruct((8, 3 * width), f32),
            jax.ShapeDtypeStruct((rows, D), low),
            jax.ShapeDtypeStruct((group, width), low),
            jax.ShapeDtypeStruct((8 * down_share.shape[0], D), low),
            jax.ShapeDtypeStruct((8 * gate_up_rows.shape[0], gate_up_rows.shape[1]), low),
        ],
        in_specs=[vm] * 4 + [any_] + [vm] * 7 + [any_] * 3,
        out_specs=[vm] * 5 + [any_] * 3,
        scratch_shapes=[
            pltpu.VMEM(out_weight.shape, low), pltpu.VMEM((rows, D), low), pltpu.VMEM((rows, D), low),
            pltpu.VMEM((group, width), low),
            pltpu.VMEM((group, width), f32), pltpu.VMEM((group, width), f32), pltpu.VMEM((rows, D), f32),
        ] + line_scratch(shards, rows, D, 3) + [dma((2, shards)), dma((2, shards)), dma((4,))] + gatherer_sems() * 3,
        compiler_params=pltpu.CompilerParams(collective_id=7, has_side_effects=True, vmem_limit_bytes=60 * 2**20),
        name="heads_back",
        cost_estimate=pl.CostEstimate(flops=10**10, bytes_accessed=200 * 10**6, transcendentals=0),
    )(d_normed_two, middle, cotangent, vectors, out_weight, qkv, stats, seg_rows, seg_columns, cosine, minus, plus,
      down_part, down_share, gate_up_rows)


def input_back_kernel(shards, slopes, weight, normed, attended, d_middle_columns, tokens, vectors, d_middle, bias_grad, norm_grads,
                      input_grad, small, qkv_grad, out_grad,
                      w_buf, n_buf, a_buf, m_buf, total, part, part_in, own, got, z_send, z_recv,
                      term, core, near, last, r_send, r_recv, o_term, o_core, o_near, o_last, o_send, o_recv,
                      qkv_rows, out_rows, s_send, s_recv, loc, *sems):
    cube = Cube()
    z = lax.axis_index("shard")
    loads = load_all(((normed, n_buf), (weight, w_buf), (attended, a_buf), (d_middle_columns, m_buf)), loc)
    r = lax.axis_index("replica")
    others = [lax.rem(r + i, 8) for i in range(1, 8)]
    greet([((z != o), {"shard": o}) for o in range(shards)] + [(z >= 0, {"replica": o}) for o in others], shards + 6)
    gain = vector_row(vectors, 3)
    rows = tokens.shape[0]
    width = D // shards
    share = width // 8
    line = LineSum(shards, 3, own, got, z_send, z_recv)
    reducer = Reducer(cube, share, term, core, near, last, r_send, r_recv)
    o_reducer = Reducer(cube, share, o_term, o_core, o_near, o_last, o_send, o_recv)
    owners = Owners(shards, 3, reducer.own, qkv_rows, *sems[0:3])
    o_owners = Owners(shards, 1, o_reducer.own, out_rows, *sems[3:6])
    gatherers = [
        [
            Gatherer(
                cube, *(ref.at[:, pl.ds(aligned(p * shards + lax.rem(z + k, shards), width), width)] for ref in (qkv_rows, qkv_grad)),
                [sem.at[3 * k + p] for sem in sems[6:9]],
            )
            for p in range(3)
        ]
        for k in range(shards)
    ]
    o_gatherer = Gatherer(cube, out_rows, out_grad, sems[9:12])

    def qkv_term(o):
        term_product(term, o, n_buf.at[:, pl.ds(aligned(o, width), width)], slopes)
        reducer.start(o)

    def out_term(o):
        term_product(o_term, o, a_buf.at[:, pl.ds(aligned(o, width), width)], m_buf)
        o_reducer.start(o)

    def product(t):
        pair = line.pair(t)
        pair_product(own, pair, slopes, w_buf)
        line.ends(t)

    turn = further(shards)

    def each(call):
        return [functools.partial(call, o) for _, o in turn]

    def ending(red, own_, k, o):
        red.after_last(o)
        own_.start(k)

    moves = line.steps()
    cores, nears = each(reducer.after_core), each(reducer.after_near)
    lasts = [functools.partial(ending, reducer, owners, k, o) for k, o in turn]
    terms = each(qkv_term)

    def begin_from(i):
        owners.arrive_from(i)
        for g in gatherers[i]:
            g.start()

    def pass_from(i):
        for g in gatherers[i]:
            g.pass_on()

    def pass_last_from(i):
        for g in gatherers[i]:
            g.pass_last()

    sequence = [loads[0].wait] + terms + [loads[1].wait, functools.partial(product, 0)] + cores[:2]
    sequence += [functools.partial(product, t) for t in range(1, shards // 2)] + [loads[2].wait, loads[3].wait] + each(out_term)
    sequence += moves[:1] + nears[:1] + cores[2:3] + each(o_reducer.after_core) + moves[1:3] + nears[1:2] + lasts[:1] + cores[3:] + moves[3:5]
    sequence += nears[2:3] + lasts[1:2] + moves[5:6] + nears[3:] + lasts[2:3] + [functools.partial(line.ends, i) for i in range(shards // 2, shards - 1)]
    sequence += each(o_reducer.after_near) + lasts[3:]
    sequence += [functools.partial(ending, o_reducer, o_owners, k, o) for k, o in turn]
    order = list(reversed(range(shards)))
    sequence += [functools.partial(begin_from, i) for i in order] + moves[6:7]
    sequence += [functools.partial(pass_from, i) for i in order[:2]] + moves[7:8] + [o_owners.arrive, o_gatherer.start]
    sequence += [functools.partial(pass_from, i) for i in order[2:]] + moves[8:] + [functools.partial(pass_last_from, i) for i in order[:2]]
    for step in sequence:
        step()
    line.result(total)

    part[...] = jnp.zeros_like(part)

    @pl.loop(0, rows // 16)
    def _(i):
        block = pl.ds(aligned(i, 16), 16)
        slope = total[block, :]
        back, unit = norm_back_rows(slope, tokens[block, :].astype(jnp.float32), gain)
        input_grad[block, :] = d_middle[block, :] + back
        ones = (slope * unit).reshape(2, 8, D).sum(axis=0).sum(axis=0, keepdims=True)
        twos = slope.reshape(2, 8, D).sum(axis=0).sum(axis=0, keepdims=True)
        for o in range(shards):
            part[o, 3:4, :] += ones[:, o * width : (o + 1) * width]
            part[o, 4:5, :] += twos[:, o * width : (o + 1) * width]
    for o in range(shards):
        for k in range(2):
            part[o, 5 + k : 6 + k, :] = jnp.sum(
                norm_grads[8 * k : 8 * k + 8, o * width : (o + 1) * width], axis=0, keepdims=True)
    for k in range(3):
        flat = k * shards + z
        part[flat // 3, pl.ds(flat % 3, 1), :] = bias_grad[0:1, k * width : (k + 1) * width]

    def small_copy(o):
        return remote(part.at[o], part_in.at[z], s_send.at[o], s_recv.at[z], {"shard": o})

    def small_arrival(o):
        return remote(part.at[o], part_in.at[o], s_send.at[o], s_recv.at[o], {"shard": o})

    for o in range(shards):
        @pl.when(z != o)
        def _():
            small_copy(o).start()
    small[...] = part[z]
    for o in range(shards):
        @pl.when(z != o)
        def _():
            small_arrival(o).wait_recv()
            small[...] += part_in[o]

    def sum_copy(o):
        return remote(small, part_in.at[shards + r], s_send.at[shards + o], s_recv.at[shards + r], {"replica": o})

    def sum_arrival(o):
        place = part_in.at[shards + o]
        return remote(place, place, s_send.at[shards + o], s_recv.at[shards + o], {"replica": o})

    for o in others:
        sum_copy(o).start()
    part_in[shards + r] = small[...]
    o_gatherer.pass_on()
    for o in others:
        sum_copy(o).wait_send()
        sum_arrival(o).wait_recv()
    small[...] = sum([part_in[shards + i] for i in range(1, 8)], part_in[shards])
    o_gatherer.pass_last()
    for i in order[2:]:
        pass_last_from(i)
    for o in range(shards):
        @pl.when(z != o)
        def _():
            small_copy(o).wait_send()
    line.finish()
    for k in range(shards):
        reducer.finish(k)
        o_reducer.finish(k)
    owners.finish()
    o_owners.finish()
    for g in sum(gatherers, [o_gatherer]):
        g.finish()


def input_back_call(shards, slopes, weight, normed, attended, d_middle_columns, tokens, vectors, d_middle, bias_grad, norm_grads):
    group = slopes.shape[0]
    rows = group // shards
    width = D // shards
    share = width // 8
    vm = pl.BlockSpec(memory_space=pltpu.VMEM)
    any_ = pl.BlockSpec(memory_space=pl.ANY)
    dma = pltpu.SemaphoreType.DMA
    low = jnp.bfloat16
    f32 = jnp.float32
    return pl.pallas_call(
        functools.partial(input_back_kernel, shards),
        out_shape=[
            jax.ShapeDtypeStruct((rows, D), f32),
            jax.ShapeDtypeStruct((8, width), f32),
            jax.ShapeDtypeStruct((width, 3 * D), low),
            jax.ShapeDtypeStruct((width, D), low),
        ],
        in_specs=[vm] + [any_] * 4 + [vm] * 5,
        out_specs=[vm, vm, any_, any_],
        scratch_shapes=[
            pltpu.VMEM(weight.shape, low), pltpu.VMEM(normed.shape, low), pltpu.VMEM(attended.shape, low),
            pltpu.VMEM(d_middle_columns.shape, low), pltpu.VMEM((rows, D), f32),
            pltpu.VMEM((shards, 8, width), f32), pltpu.VMEM((shards + 8, 8, width), f32),
        ] + line_scratch(shards, rows, D, 3) + reducer_scratch(shards, share, 3 * width) + reducer_scratch(shards, share, width)
        + [pltpu.VMEM((share, 3 * D), low), pltpu.VMEM((share, D), low), dma((shards + 8,)), dma((shards + 8,)), dma((4,))]
        + owner_sems(shards, 3) + owner_sems(shards, 1)
        + [dma((3 * shards, 8)), dma((3 * shards, 8)), dma((3 * shards, 1))] + gatherer_sems(),
        compiler_params=pltpu.CompilerParams(collective_id=8, has_side_effects=True, vmem_limit_bytes=60 * 2**20),
        name="input_back",
        cost_estimate=pl.CostEstimate(flops=10**10, bytes_accessed=200 * 10**6, transcendentals=0),
    )(slopes, weight, normed, attended, d_middle_columns, tokens, vectors, d_middle, bias_grad, norm_grads)


def swap_pieces(pieces):
    shards = lax.axis_size("shard")
    here = lax.axis_index("shard")
    out = pieces
    for k in range(1, shards):
        partner = jnp.bitwise_xor(here, k)
        piece = lax.dynamic_index_in_dim(pieces, partner, axis=0, keepdims=True)
        piece = lax.ppermute(piece, "shard", [(i, i ^ k) for i in range(shards)])
        out = lax.dynamic_update_slice_in_dim(out, piece, partner, axis=0)
    return out


def own_share(rows):
    own = rows.shape[0] // lax.axis_size("replica")
    return lax.dynamic_slice_in_dim(rows, lax.axis_index("replica") * own, own, axis=0)


def spread_rows(rows, columns):
    shards = lax.axis_size("shard")
    piece = own_share(rows)
    own = piece.shape[0]
    piece = piece.reshape(own, columns, shards, -1).transpose(2, 0, 1, 3).reshape(shards, own, -1)
    full = lax.all_gather(swap_pieces(piece), "replica", axis=0, tiled=False)
    return full.transpose(1, 0, 2, 3).reshape(rows.shape[0] * shards, -1)


def gather_rows(rows):
    shards = lax.axis_size("shard")
    piece = own_share(rows)
    moved = swap_pieces(jnp.broadcast_to(piece[None], (shards,) + piece.shape))
    full = lax.all_gather(moved, "replica", axis=0, tiled=False)
    return full.transpose(1, 0, 2, 3).reshape(rows.shape[0] * shards, -1)


def own_rows(features):
    copies = lax.axis_size("replica")
    shards = lax.axis_size("shard")
    count = features.shape[0]
    return (
        features.reshape(count, shards, copies, -1).transpose(0, 2, 1, 3).reshape(count, -1)
    )


def sum_columns(features, slopes, columns):
    shards = lax.axis_size("shard")
    term = contract_first(own_rows(features), slopes).astype(jnp.bfloat16)
    part = lax.psum_scatter(term, "replica", scatter_dimension=0, tiled=True)
    own = part.shape[0] // shards
    moved = swap_pieces(part.reshape(shards, own, -1))
    moved = moved.reshape(shards, own, columns, -1).transpose(1, 2, 0, 3).reshape(own, -1)
    return lax.all_gather(moved, "replica", axis=0, tiled=True)


def swiglu(gate_up):
    half = gate_up.shape[1] // 2
    return jax.nn.silu(gate_up[:, :half]) * gate_up[:, half:]


def norm_stats(values):
    mean = jnp.mean(values, axis=-1, keepdims=True)
    centered = values - mean
    inverse = lax.rsqrt(jnp.mean(centered * centered, axis=-1, keepdims=True) + norm_eps)
    return centered * inverse, inverse


def norm_back(slope, unit, inverse, gain):
    scaled = slope * gain
    return inverse * (
        scaled
        - jnp.mean(scaled, axis=-1, keepdims=True)
        - unit * jnp.mean(scaled * unit, axis=-1, keepdims=True)
    )


def start_plain(tokens, vectors, qkv_weight, cosine, minus, plus):
    shards = lax.axis_size("shard")
    here = lax.axis_index("shard")
    all_tokens = lax.all_gather(tokens, "shard", axis=0, tiled=False)
    all_vectors = lax.all_gather(vectors, "shard", axis=0, tiled=False)
    weight = spread_rows(qkv_weight, 3)
    width = D // shards
    gain, shift = (all_vectors[:, 3 + i].reshape(D) for i in (0, 1))
    unit, _ = norm_stats(all_tokens.reshape(-1, D).astype(jnp.float32))
    normed = (unit * gain + shift).astype(jnp.bfloat16)
    bias = all_vectors[:, :3].reshape(3, shards, width)
    bias = lax.dynamic_index_in_dim(bias, here, axis=1, keepdims=False).reshape(3 * width)
    value = jnp.dot(normed, weight, preferred_element_type=jnp.float32) + bias
    turned = value[:, : 2 * width]
    wide = [jnp.tile(t, (1, 2 * width // 128)) for t in (cosine, minus, plus)]
    turned = (
        turned * wide[0] + jnp.roll(turned, -8, 1) * wide[1] + jnp.roll(turned, 8, 1) * wide[2]
    )
    qkv = jnp.concatenate([turned, value[:, 2 * width :]], axis=1).astype(jnp.bfloat16)
    return all_tokens, all_vectors, normed, qkv, weight


def layer_kernels(shards, tokens, cotangent, weights, vectors, tables):
    qkv_weight, out_weight, gate_up_weight, down_weight = weights
    seg_rows, seg_columns, cosine, minus, plus = tables
    rows = tokens.shape[0]
    all_tokens, all_vectors, normed, qkv, weight_qkv, weight_out = start_call(
        shards, tokens, vectors, qkv_weight, out_weight, cosine, minus, plus
    )
    attended, stats, weight_gate_up = attend_spread_call(
        shards, rows, qkv, seg_rows, seg_columns, gate_up_weight
    )
    middle, normed_two, hidden, slopes, group_cotangent, down_part = hidden_call(
        shards, attended, all_tokens, weight_out, weight_gate_up, down_weight, cotangent, all_vectors
    )
    d_normed_two, down_share, gate_up_rows = hidden_back_call(
        shards, slopes, weight_gate_up, hidden, group_cotangent.reshape(shards * rows, D), normed_two
    )
    d_middle, norm_grads, d_qkv, bias_grad, mixed, d_middle_columns, down_grad, gate_up_grad = heads_back_call(
        shards, rows, d_normed_two, middle, cotangent, all_vectors, weight_out, qkv, stats, seg_rows, seg_columns,
        cosine, minus, plus, down_part.reshape(shards, rows, D), down_share, gate_up_rows,
    )
    input_grad, small, qkv_grad, out_grad = input_back_call(
        shards, d_qkv, weight_qkv, normed, attended, d_middle_columns, tokens, all_vectors, d_middle, bias_grad, norm_grads
    )
    return mixed, input_grad, small, (qkv_grad, out_grad, gate_up_grad, down_grad)


def layer_plain(shards, tokens, cotangent, weights, vectors, tables):
    qkv_weight, out_weight, gate_up_weight, down_weight = weights
    seg_rows, seg_columns, cosine, minus, plus = tables
    here = lax.axis_index("shard")
    row_count = tokens.shape[0]
    group_rows = row_count * shards
    width = D // shards
    f32 = jnp.float32
    low = jnp.bfloat16
    weight_out = gather_rows(out_weight)
    weight_gate_up = spread_rows(gate_up_weight, 2)
    all_tokens, all_vectors, normed_low, qkv, weight_qkv = start_plain(
        tokens, vectors, qkv_weight, cosine, minus, plus
    )
    gain_one, shift_one, gain_two, shift_two = (
        all_vectors[:, 3 + i].reshape(D) for i in range(4)
    )
    cotangent_later, qkv = lax.optimization_barrier((cotangent, qkv))
    group_cotangent = lax.all_gather(cotangent_later, "shard", axis=0, tiled=True)

    def local(array):
        return lax.dynamic_slice_in_dim(array, here * row_count, row_count, axis=0)

    attended, stats = attend_call(shards, row_count, qkv, seg_rows, seg_columns)
    inputs = all_tokens.reshape(group_rows, D).astype(f32)
    middle = inputs + jnp.dot(attended, weight_out, preferred_element_type=f32)
    unit_two, inverse_two = norm_stats(middle)
    normed_two_low = (unit_two * gain_two + shift_two).astype(low)
    gate_up = jnp.dot(normed_two_low, weight_gate_up, preferred_element_type=f32)
    hidden, swiglu_pull = jax.vjp(swiglu, gate_up)
    hidden_low = hidden.astype(low)
    d_hidden = contract_last(group_cotangent, down_weight)
    d_gate_up_low = swiglu_pull(d_hidden)[0].astype(low)
    down_part = jnp.dot(hidden_low, down_weight, preferred_element_type=f32).astype(low)
    unit_two_own = local(unit_two)
    inverse_two_own = local(inverse_two)
    middle_own = local(middle)

    d_normed_two_part = contract_last(d_gate_up_low, weight_gate_up).astype(low)
    d_normed_two = scatter_call(shards, d_normed_two_part.reshape(shards, row_count, D), 3)
    down_grad = lax.psum(contract_first(hidden_low, group_cotangent).astype(low), "replica")
    d_middle = cotangent.astype(f32) + norm_back(
        d_normed_two, unit_two_own, inverse_two_own, gain_two
    )
    d_gain_two = jnp.sum(d_normed_two * unit_two_own, axis=0)
    d_shift_two = jnp.sum(d_normed_two, axis=0)
    d_middle_low = d_middle.astype(low)
    d_attended_own = contract_last(d_middle_low, weight_out).astype(low)
    d_attended, d_middle_columns = exchange_call(shards, d_attended_own, d_middle_low)
    d_projected_low, bias_part = attend_back_call(
        row_count, qkv, d_attended.reshape(group_rows, width), stats, seg_rows, seg_columns,
        cosine, minus, plus,
    )
    down_own = lax.psum_scatter(down_part, "shard", scatter_dimension=0, tiled=True)
    mixed = (middle_own + down_own.astype(f32)).astype(low)
    d_normed_part = contract_last(d_projected_low, weight_qkv).astype(low)
    d_normed = scatter_call(shards, d_normed_part.reshape(shards, row_count, D), 4)
    gate_up_grad = sum_columns(normed_two_low, d_gate_up_low, 2)
    out_grad = sum_columns(attended, d_middle_columns.reshape(group_rows, width), 1)
    qkv_grad = sum_columns(normed_low, d_projected_low, 3)
    unit_one, inverse_one = norm_stats(tokens.astype(f32))
    input_grad = d_middle + norm_back(d_normed, unit_one, inverse_one, gain_one)
    d_gain_one = jnp.sum(d_normed * unit_one, axis=0)
    d_shift_one = jnp.sum(d_normed, axis=0)

    bias_part = bias_part[0].reshape(3, 1, width)
    bias_wide = lax.dynamic_update_slice(
        jnp.zeros((3, shards, width), f32), bias_part, (0, here, 0)
    ).reshape(shards, 3 * width)
    small = jnp.concatenate(
        [bias_wide]
        + [v.reshape(shards, width) for v in (d_gain_one, d_shift_one, d_gain_two, d_shift_two)],
        axis=1,
    )
    small = jnp.pad(small, ((0, 0), (0, width)))
    small = lax.psum(small, ("replica", "shard"))
    small = lax.dynamic_index_in_dim(small, here, axis=0, keepdims=False)
    return mixed, input_grad, small, (qkv_grad, out_grad, gate_up_grad, down_grad)


def on_device(
    tokens,
    cotangent,
    qkv_weight,
    qkv_bias,
    out_weight,
    gate_up_weight,
    down_weight,
    norm1_gain,
    norm1_shift,
    norm2_gain,
    norm2_shift,
    seq_lengths,
):
    shards = lax.axis_size("shard")
    copies = lax.axis_size("replica")
    row_count = tokens.shape[0]
    group_rows = row_count * shards
    width = D // shards
    f32 = jnp.float32
    low = jnp.bfloat16

    segment, position = group_layout(seq_lengths[0], jnp.arange(group_rows, dtype=jnp.int32))
    seg_rows = jnp.broadcast_to(segment[:, None], (group_rows, 128))
    seg_columns = jnp.broadcast_to(segment[None, :], (8, group_rows))
    lane = np.arange(128)[None, :] % HEAD_DIM
    half_rot = ROT_DIM // 2
    frequency = (10000.0 ** (-2.0 * (lane % half_rot) / ROT_DIM)).astype(np.float32)
    first = (lane < half_rot).astype(np.float32)
    second = ((lane >= half_rot) & (lane < ROT_DIM)).astype(np.float32)
    angles = position.astype(f32)[:, None] * frequency
    cosine = jnp.cos(angles) * (first + second) + (1.0 - first - second)
    sine_value = jnp.sin(angles)
    minus = -sine_value * first
    plus = sine_value * second

    vectors = jnp.zeros((8 * width,), f32)
    at = 0
    for vector in (qkv_bias, norm1_gain, norm1_shift, norm2_gain, norm2_shift):
        after = 8 * width - at - vector.shape[0]
        vectors = vectors + jnp.pad(vector.astype(f32), (at, after))
        at += vector.shape[0]
    vectors = vectors.reshape(8, width)
    weights = (qkv_weight, out_weight, gate_up_weight, down_weight)
    tables = (seg_rows, seg_columns, cosine, minus, plus)
    if copies == 8:
        outputs = layer_kernels(shards, tokens, cotangent, weights, vectors, tables)
    else:
        outputs = layer_plain(shards, tokens, cotangent, weights, vectors, tables)
    mixed, input_grad, small, grads = outputs
    bias_rows = 3 * width
    small = small.reshape(8 * width)
    out_dtype = tuple(grad.astype(f32) for grad in grads)
    return (
        mixed,
        input_grad,
        out_dtype[0],
        small[:bias_rows],
        out_dtype[1],
        out_dtype[2],
        out_dtype[3],
    ) + tuple(small[bias_rows + i * width : bias_rows + (i + 1) * width] for i in range(4))


def solution(mesh):
    placed = (
        P(("replica", "shard"), None),
        P(("replica", "shard"), None),
        P("shard", None),
        P("shard"),
        P("shard", None),
        P("shard", None),
        P("shard", None),
        P("shard"),
        P("shard"),
        P("shard"),
        P("shard"),
        P("replica", None),
    )
    return jax.shard_map(
        on_device,
        mesh=mesh,
        in_specs=placed,
        out_specs=(
            P(("replica", "shard"), None),
            P(("replica", "shard"), None),
            P("shard", None),
            P("shard"),
            P("shard", None),
            P("shard", None),
            P("shard", None),
            P("shard"),
            P("shard"),
            P("shard"),
            P("shard"),
        ),
        check_vma=False,
    )
```
